32 devices in a mesh: fsdp: 8 (over y, x, core), rep: 4 (over z).
Axes of the slice: x: 2, y: 2, z: 4, core: 2. Of those that a mesh axis runs over, the one named last changes fastest.
Arguments:
- images: bfloat16 [2, 32, 256, 768], P(None, ('fsdp', 'rep')), may hold values from -6 to 6
- cotangent: bfloat16 [2, 32, 256, 768], P(None, ('fsdp', 'rep')), may hold values from -6 to 6
- slot_flags: int32 [2, 32], P(None, ('fsdp', 'rep')), may hold values 0 or 1
- heads_weight: bfloat16 [2, 3, 768, 768], P(None, None, 'fsdp'), may hold values from -0.21875 to 0.21875
- heads_bias: bfloat16 [2, 2, 768], P(None, None, 'fsdp'), may hold values from -4 to 4
- merge_weight: bfloat16 [2, 768, 768], P(None, 'fsdp'), may hold values from -1.75 to 1.75
- merge_bias: bfloat16 [2, 768], P(None, 'fsdp'), may hold values from -4 to 4
- first_gain: bfloat16 [2, 768], P(None, 'fsdp'), may hold values from 0.5 to 1.5
- first_shift: bfloat16 [2, 768], P(None, 'fsdp'), may hold values from -4 to 4
- second_gain: bfloat16 [2, 768], P(None, 'fsdp'), may hold values from 0.5 to 1.5
- second_shift: bfloat16 [2, 768], P(None, 'fsdp'), may hold values from -4 to 4
- expand_weight: bfloat16 [2, 3072, 768], P(None, 'fsdp'), may hold values from -0.21875 to 0.21875
- expand_bias: bfloat16 [2, 3072], P(None, 'fsdp'), may hold values from -6 to 6
- reduce_weight: bfloat16 [2, 768, 3072], P(None, 'fsdp'), may hold values from -0.15625 to 0.15625
- reduce_bias: bfloat16 [2, 768], P(None, 'fsdp'), may hold values from -4 to 4
Outputs:
- outputs: bfloat16 [2, 32, 256, 768], P(None, ('fsdp', 'rep'))
- images_grad: bfloat16 [2, 32, 256, 768], P(None, ('fsdp', 'rep'))
- heads_weight_grad: float32 [2, 3, 768, 768], P(None, None, 'fsdp')
- heads_bias_grad: float32 [2, 2, 768], P(None, None, 'fsdp')
- merge_weight_grad: float32 [2, 768, 768], P(None, 'fsdp')
- merge_bias_grad: float32 [2, 768], P(None, 'fsdp')
- first_gain_grad: float32 [2, 768], P(None, 'fsdp')
- first_shift_grad: float32 [2, 768], P(None, 'fsdp')
- second_gain_grad: float32 [2, 768], P(None, 'fsdp')
- second_shift_grad: float32 [2, 768], P(None, 'fsdp')
- expand_weight_grad: float32 [2, 3072, 768], P(None, 'fsdp')
- expand_bias_grad: float32 [2, 3072], P(None, 'fsdp')
- reduce_weight_grad: float32 [2, 768, 3072], P(None, 'fsdp')
- reduce_bias_grad: float32 [2, 768], P(None, 'fsdp')
The draws below stay inside these ranges and needn't reach their ends.
Inputs may be any that keep to these rules, and one draw needn't show every extreme that they name: `slot_flags`: 1 marks a slot that holds an image, 0 an empty slot.
All inputs are finite; a program needn't handle non-finite values. No bound on the sum of `slot_flags` on one device may be relied on, other than what follows from the above.
Results may differ from the reference program's by a relative error of at most 0.017.
Values may be sent and summed in bfloat16 or wider, within the bound.
No kernel may reach another device: no remote copies, remote signals or barrier semaphores. Data moves between devices by JAX's collectives and lax.ppermute only.
A program may use at most 256 MiB of HBM per device.

```python
import math
import jax
import jax.numpy as jnp
from jax import lax

D = 768
HEADS = 12
HEAD_DIM = 64
FF = 3072
LEN = 256
MICRO = 2
LAYERS = 2
SLOTS = 32


def with_ends(result, rng, smallest, top_value):
    dims = result.shape
    place = [jax.random.randint(jax.random.fold_in(rng, axis), (), 0, dims[axis]) for axis in range(len(dims))]
    result = result.at[tuple(place)].set(smallest)
    longest = dims.index(max(dims))
    place[longest] = (place[longest] + 1) % dims[longest]
    return result.at[tuple(place)].set(top_value)


def level_of(stream_key, shape, pieces, least, high):
    level, own = 1.0, jax.random.fold_in(stream_key, 6)
    for axis_at, parts in pieces:
        draws = jnp.exp(jax.random.uniform(jax.random.fold_in(own, axis_at), (parts,), jnp.float32, least / len(pieces), high / len(pieces)))
        level = level * jnp.repeat(draws, shape[axis_at] // parts).reshape([-1 if axis == axis_at else 1 for axis in range(len(shape))])
    return level


def normal_values(own_key, dims, deviation, limit, shards=(), held_as=jnp.bfloat16):
    drawn = jax.random.normal(own_key, dims, jnp.float32) * deviation
    if len(shards) > 0:
        drawn = level_of(own_key, dims, shards, -0.22, 0.18) * drawn
    return jnp.clip(drawn, min=-limit, max=limit).astype(held_as)


def setup_inputs(seed: int = 0) -> dict:
    splits = jax.random.split(jax.random.key(seed), 16)
    return {
        "images": normal_values(splits[0], (MICRO, SLOTS, LEN, D), 1.0, 6.0, ((1, 32),)),
        "cotangent": normal_values(splits[1], (MICRO, SLOTS, LEN, D), 1.0, 6.0, ((1, 32),)),
        "slot_flags": with_ends((jax.random.randint(splits[2], (MICRO, SLOTS), 0, 8) < 5).astype(jnp.int32), jax.random.fold_in(splits[2], 1), 0, 1),
        "heads_weight": normal_values(splits[3], (LAYERS, 3, D, D), D ** -0.5, 0.21875, ((2, 8),)),
        "heads_bias": normal_values(splits[4], (LAYERS, 2, D), 0.3, 4.0, ((2, 8),)),
        "merge_weight": normal_values(splits[5], (LAYERS, D, D), (D * 4 // LEN) ** -0.5, 1.75, ((1, 8),)),
        "merge_bias": normal_values(splits[6], (LAYERS, D), 0.3, 4.0, ((1, 8),)),
        "first_gain": jnp.clip(1.0 + 0.1 * jax.random.normal(splits[7], (LAYERS, D), jnp.float32), 0.5, 1.5).astype(jnp.bfloat16),
        "first_shift": normal_values(splits[8], (LAYERS, D), 0.3, 4.0, ((1, 8),)),
        "second_gain": jnp.clip(1.0 + 0.1 * jax.random.normal(splits[9], (LAYERS, D), jnp.float32), 0.5, 1.5).astype(jnp.bfloat16),
        "second_shift": normal_values(splits[10], (LAYERS, D), 0.3, 4.0, ((1, 8),)),
        "expand_weight": normal_values(splits[11], (LAYERS, FF, D), D ** -0.5, 0.21875, ((1, 8),)),
        "expand_bias": normal_values(splits[12], (LAYERS, FF), 0.5, 6.0, ((1, 8),)),
        "reduce_weight": normal_values(splits[13], (LAYERS, D, FF), (FF // 2) ** -0.5, 0.15625, ((1, 8),)),
        "reduce_bias": normal_values(splits[14], (LAYERS, D), 0.3, 4.0, ((1, 8),)),
    }


@jax.custom_vjp
def low(v):
    return lax.optimization_barrier(v.astype(jnp.bfloat16)).astype(jnp.float32)

@jax.custom_vjp
def low_back(v):
    return v

def low_keep(v):
    return (low(v), None)

def low_pass(kept, grad):
    return (grad,)

def back_keep(v):
    return (v, None)

def back_low(kept, grad):
    return (low(grad),)
low.defvjp(low_keep, low_pass)
low_back.defvjp(back_keep, back_low)
norm_eps = 1e-06
highest = lax.Precision.HIGHEST

def layer_norm(token_rows, scale_row, offset_row):
    centre = token_rows - lax.optimization_barrier(jnp.mean(token_rows, axis=-1, keepdims=True))
    spread = lax.optimization_barrier(jnp.mean(centre * centre, axis=-1, keepdims=True))
    return centre * lax.rsqrt(spread + norm_eps) * scale_row + offset_row

def project(token_rows, weight):
    return jnp.einsum('ti,oi->to', token_rows, weight, precision=highest)

def one_layer(hidden, params):
    heads_weight, heads_bias, merge_weight, merge_bias, first_gain, first_shift, second_gain, second_shift, expand_weight, expand_bias, reduce_weight, reduce_bias = params
    shaped = (LEN, HEADS, HEAD_DIM)
    normed = low(layer_norm(hidden, first_gain, first_shift))
    queries = low_back(low(project(normed, heads_weight[0]) + heads_bias[0]))
    key_rows = low_back(low(project(normed, heads_weight[1])))
    values = low_back(low(project(normed, heads_weight[2]) + heads_bias[1]))
    scores = low_back(jnp.einsum('qhd,khd->hqk', queries.reshape(shaped), key_rows.reshape(shaped), precision=highest) * HEAD_DIM ** (-0.5))
    attend = low(jax.nn.softmax(scores, axis=-1))
    mixed_rows = jnp.einsum('hqk,khd->qhd', attend, values.reshape(shaped), precision=highest)
    mixed_rows = low_back(low(mixed_rows.reshape(LEN, D)))
    middle = hidden + low_back(project(mixed_rows, merge_weight) + merge_bias)
    second = low(layer_norm(middle, second_gain, second_shift))
    pre_act = low_back(project(second, expand_weight) + expand_bias)
    activated = low(jax.nn.gelu(pre_act, approximate=True))
    return middle + low_back(project(activated, reduce_weight) + reduce_bias)

def both_layers(token_rows, params):
    for layer_at in range(LAYERS):
        token_rows = one_layer(token_rows, tuple((array_in[layer_at] for array_in in params)))
    return token_rows

def reference(images, cotangent, slot_flags, heads_weight, heads_bias, merge_weight, merge_bias, first_gain, first_shift, second_gain, second_shift, expand_weight, expand_bias, reduce_weight, reduce_bias):
    weights = tuple((array_in.astype(jnp.float32) for array_in in (heads_weight, heads_bias, merge_weight, merge_bias, first_gain, first_shift, second_gain, second_shift, expand_weight, expand_bias, reduce_weight, reduce_bias)))
    images_total = MICRO * SLOTS
    per_step = math.gcd(images_total, max(1, 4096 // LEN))
    steps_total = images_total // per_step
    shape_steps = (steps_total, per_step, LEN, D)
    inputs = images.astype(jnp.float32).reshape(shape_steps)
    live_flags = slot_flags.astype(jnp.float32).reshape(steps_total, per_step, 1, 1)

    def forward(token_blocks, params):

        def run_block(image_block):
            return jax.vmap(lambda token_rows: both_layers(token_rows, params))(image_block)
        return live_flags * lax.map(jax.checkpoint(run_block), token_blocks)
    finals, pullback = jax.vjp(forward, inputs, weights)
    input_grad, weight_grads = pullback(cotangent.astype(jnp.float32).reshape(shape_steps))
    grad_scale = (MICRO * SLOTS * LEN) ** (-0.5)
    outputs = finals.reshape(MICRO, SLOTS, LEN, D).astype(jnp.bfloat16)
    images_grad = input_grad.reshape(MICRO, SLOTS, LEN, D).astype(jnp.bfloat16)
    return (outputs, images_grad, weight_grads[0] * grad_scale, weight_grads[1] * grad_scale, weight_grads[2] * grad_scale, weight_grads[3] * grad_scale, weight_grads[4] * grad_scale, weight_grads[5] * grad_scale, weight_grads[6] * grad_scale, weight_grads[7] * grad_scale, weight_grads[8] * grad_scale, weight_grads[9] * grad_scale, weight_grads[10] * grad_scale, weight_grads[11] * grad_scale)
```

```python
import jax
import jax.numpy as jnp
from jax import lax
from jax.experimental import pallas as pl
from jax.experimental.pallas import tpu as pltpu
from jax.sharding import PartitionSpec as P

HEADS = 12
HEAD_DIM = 64


norm_eps = 1e-06


def layer_norm(token_rows, scale_row, offset_row):
    centre = token_rows - jnp.mean(token_rows, axis=-1, keepdims=True)
    spread = jnp.mean(centre * centre, axis=-1, keepdims=True)
    return centre * lax.rsqrt(spread + norm_eps) * scale_row + offset_row


def project(token_rows, weight):
    return lax.dot_general(
        token_rows, weight, (((1,), (1,)), ((), ())), preferred_element_type=jnp.float32
    )


def outer_sum(grad_rows, token_rows):
    return lax.dot_general(
        grad_rows, token_rows, (((0,), (0,)), ((), ())), preferred_element_type=jnp.float32
    )


def carry_back(grad_rows, weight):
    return jnp.dot(grad_rows, weight, preferred_element_type=jnp.float32)


def forward_layer(hidden, params):
    (
        heads_weight,
        heads_bias,
        merge_weight,
        merge_bias,
        first_gain,
        first_shift,
        second_gain,
        second_shift,
        expand_weight,
        expand_bias,
        reduce_weight,
        reduce_bias,
    ) = params
    seq_len, model_width = hidden.shape
    shaped = (seq_len, HEADS, HEAD_DIM)
    score_scale = HEAD_DIM ** (-0.5)
    normed = layer_norm(
        hidden, first_gain.astype(jnp.float32), first_shift.astype(jnp.float32)
    ).astype(jnp.bfloat16)
    queries = (project(normed, heads_weight[0]) + heads_bias[0].astype(jnp.float32)).astype(
        jnp.bfloat16
    )
    key_rows = project(normed, heads_weight[1]).astype(jnp.bfloat16)
    values = (project(normed, heads_weight[2]) + heads_bias[1].astype(jnp.float32)).astype(
        jnp.bfloat16
    )
    scores = (
        jnp.einsum(
            "qhd,khd->hqk",
            queries.reshape(shaped),
            key_rows.reshape(shaped),
            preferred_element_type=jnp.float32,
        )
        * score_scale
    )
    row_peak = jnp.max(scores, axis=-1, keepdims=True)
    exponent = jnp.exp(scores - row_peak)
    row_total = jnp.sum(exponent, axis=-1, keepdims=True)
    attend = exponent / row_total
    log_total = row_peak + jnp.log(row_total)
    mixed_rows = jnp.einsum(
        "hqk,khd->qhd",
        attend.astype(jnp.bfloat16),
        values.reshape(shaped),
        preferred_element_type=jnp.float32,
    )
    mixed_rows = mixed_rows.reshape(seq_len, model_width).astype(jnp.bfloat16)
    middle = hidden + (project(mixed_rows, merge_weight) + merge_bias.astype(jnp.float32))
    second = layer_norm(
        middle, second_gain.astype(jnp.float32), second_shift.astype(jnp.float32)
    ).astype(jnp.bfloat16)
    pre_act = project(second, expand_weight) + expand_bias.astype(jnp.float32)
    activated = jax.nn.gelu(pre_act, approximate=True).astype(jnp.bfloat16)
    result = middle + (project(activated, reduce_weight) + reduce_bias.astype(jnp.float32))
    saved = (
        hidden,
        normed,
        queries,
        key_rows,
        values,
        log_total,
        mixed_rows,
        middle,
        second,
        pre_act,
        activated,
    )
    return (result, saved)


def backward_layer(grad_out, params, saved):
    (
        heads_weight,
        heads_bias,
        merge_weight,
        merge_bias,
        first_gain,
        first_shift,
        second_gain,
        second_shift,
        expand_weight,
        expand_bias,
        reduce_weight,
        reduce_bias,
    ) = params
    (
        hidden,
        normed,
        queries,
        key_rows,
        values,
        log_total,
        mixed_rows,
        middle,
        second,
        pre_act,
        activated,
    ) = saved
    seq_len, model_width = hidden.shape
    shaped = (seq_len, HEADS, HEAD_DIM)
    score_scale = HEAD_DIM ** (-0.5)
    branch_low = grad_out.astype(jnp.bfloat16)
    reduce_weight_term = outer_sum(branch_low, activated)
    reduce_bias_term = jnp.sum(branch_low.astype(jnp.float32), axis=0)
    grad_act = carry_back(branch_low, reduce_weight)
    unused_value, gelu_back = jax.vjp(lambda point: jax.nn.gelu(point, approximate=True), pre_act)
    grad_pre = gelu_back(grad_act)[0].astype(jnp.bfloat16)
    expand_weight_term = outer_sum(grad_pre, second)
    expand_bias_term = jnp.sum(grad_pre.astype(jnp.float32), axis=0)
    grad_second = carry_back(grad_pre, expand_weight)
    unused_norm, second_back = jax.vjp(
        layer_norm, middle, second_gain.astype(jnp.float32), second_shift.astype(jnp.float32)
    )
    middle_part, second_gain_term, second_shift_term = second_back(grad_second)
    grad_middle = grad_out + middle_part
    attn_low = grad_middle.astype(jnp.bfloat16)
    merge_weight_term = outer_sum(attn_low, mixed_rows)
    merge_bias_term = jnp.sum(attn_low.astype(jnp.float32), axis=0)
    grad_mixed = carry_back(attn_low, merge_weight).astype(jnp.bfloat16).reshape(shaped)
    queries_heads = queries.reshape(shaped)
    keys_heads = key_rows.reshape(shaped)
    values_heads = values.reshape(shaped)
    scores = (
        jnp.einsum("qhd,khd->hqk", queries_heads, keys_heads, preferred_element_type=jnp.float32)
        * score_scale
    )
    attend = jnp.exp(scores - log_total)
    grad_values = jnp.einsum(
        "hqk,qhd->khd", attend.astype(jnp.bfloat16), grad_mixed, preferred_element_type=jnp.float32
    ).astype(jnp.bfloat16)
    grad_attend = jnp.einsum(
        "qhd,khd->hqk", grad_mixed, values_heads, preferred_element_type=jnp.float32
    )
    grad_scores = attend * (grad_attend - jnp.sum(grad_attend * attend, axis=-1, keepdims=True))
    grad_scores = grad_scores.astype(jnp.bfloat16)
    grad_queries = (
        jnp.einsum("hqk,khd->qhd", grad_scores, keys_heads, preferred_element_type=jnp.float32)
        * score_scale
    ).astype(jnp.bfloat16)
    grad_keys = (
        jnp.einsum("hqk,qhd->khd", grad_scores, queries_heads, preferred_element_type=jnp.float32)
        * score_scale
    ).astype(jnp.bfloat16)
    stacked_grads = jnp.stack(
        [
            grad_queries.reshape(seq_len, model_width),
            grad_keys.reshape(seq_len, model_width),
            grad_values.reshape(seq_len, model_width),
        ]
    )
    heads_weight_term = jnp.einsum(
        "jto,ti->joi", stacked_grads, normed, preferred_element_type=jnp.float32
    )
    grad_normed = jnp.einsum(
        "jto,joi->ti", stacked_grads, heads_weight, preferred_element_type=jnp.float32
    )
    heads_bias_term = jnp.stack(
        [
            jnp.sum(stacked_grads[0].astype(jnp.float32), axis=0),
            jnp.sum(stacked_grads[2].astype(jnp.float32), axis=0),
        ]
    )
    unused_first, first_back = jax.vjp(
        layer_norm, hidden, first_gain.astype(jnp.float32), first_shift.astype(jnp.float32)
    )
    hidden_part, first_gain_term, first_shift_term = first_back(grad_normed)
    grad_hidden = grad_middle + hidden_part
    terms = (
        heads_weight_term,
        heads_bias_term,
        merge_weight_term,
        merge_bias_term,
        first_gain_term,
        first_shift_term,
        second_gain_term,
        second_shift_term,
        expand_weight_term,
        expand_bias_term,
        reduce_weight_term,
        reduce_bias_term,
    )
    return (grad_hidden, terms)


def plain_shards(
    images,
    cotangent,
    slot_flags,
    heads_weight,
    heads_bias,
    merge_weight,
    merge_bias,
    first_gain,
    first_shift,
    second_gain,
    second_shift,
    expand_weight,
    expand_bias,
    reduce_weight,
    reduce_bias,
):
    micro_count = images.shape[0]
    seq_len = images.shape[2]
    layers = heads_weight.shape[0]
    live_flags = slot_flags.astype(jnp.float32)
    states = [images[batch_at, 0].astype(jnp.float32) for batch_at in range(micro_count)]
    saved_all = []
    for layer_at in range(layers):
        saved_row = []
        for batch_at in range(micro_count):
            params = (
                lax.all_gather(heads_weight[layer_at], "fsdp", axis=1, tiled=True),
                lax.all_gather(heads_bias[layer_at], "fsdp", axis=1, tiled=True),
                lax.all_gather(merge_weight[layer_at], "fsdp", axis=0, tiled=True),
                lax.all_gather(merge_bias[layer_at], "fsdp", axis=0, tiled=True),
                lax.all_gather(first_gain[layer_at], "fsdp", axis=0, tiled=True),
                lax.all_gather(first_shift[layer_at], "fsdp", axis=0, tiled=True),
                lax.all_gather(second_gain[layer_at], "fsdp", axis=0, tiled=True),
                lax.all_gather(second_shift[layer_at], "fsdp", axis=0, tiled=True),
                lax.all_gather(expand_weight[layer_at], "fsdp", axis=0, tiled=True),
                lax.all_gather(expand_bias[layer_at], "fsdp", axis=0, tiled=True),
                lax.all_gather(reduce_weight[layer_at], "fsdp", axis=0, tiled=True),
                lax.all_gather(reduce_bias[layer_at], "fsdp", axis=0, tiled=True),
            )
            states[batch_at], saved = forward_layer(states[batch_at], params)
            saved_row.append(saved)
        saved_all.append(saved_row)
    outputs = jnp.stack(
        [live_flags[batch_at, 0] * states[batch_at] for batch_at in range(micro_count)]
    )[:, None].astype(jnp.bfloat16)
    grads_back = [
        cotangent[batch_at, 0].astype(jnp.float32) * live_flags[batch_at, 0]
        for batch_at in range(micro_count)
    ]
    collected = [None] * layers
    for layer_at in reversed(range(layers)):
        totals = None
        for batch_at in range(micro_count):
            params = (
                lax.all_gather(heads_weight[layer_at], "fsdp", axis=1, tiled=True),
                lax.all_gather(heads_bias[layer_at], "fsdp", axis=1, tiled=True),
                lax.all_gather(merge_weight[layer_at], "fsdp", axis=0, tiled=True),
                lax.all_gather(merge_bias[layer_at], "fsdp", axis=0, tiled=True),
                lax.all_gather(first_gain[layer_at], "fsdp", axis=0, tiled=True),
                lax.all_gather(first_shift[layer_at], "fsdp", axis=0, tiled=True),
                lax.all_gather(second_gain[layer_at], "fsdp", axis=0, tiled=True),
                lax.all_gather(second_shift[layer_at], "fsdp", axis=0, tiled=True),
                lax.all_gather(expand_weight[layer_at], "fsdp", axis=0, tiled=True),
                lax.all_gather(expand_bias[layer_at], "fsdp", axis=0, tiled=True),
                lax.all_gather(reduce_weight[layer_at], "fsdp", axis=0, tiled=True),
                lax.all_gather(reduce_bias[layer_at], "fsdp", axis=0, tiled=True),
            )
            grads_back[batch_at], terms = backward_layer(
                grads_back[batch_at], params, saved_all[layer_at][batch_at]
            )
            if totals is None:
                totals = terms
            else:
                totals = tuple((earlier + current for earlier, current in zip(totals, terms)))
        collected[layer_at] = totals
    images_grad = jnp.stack(grads_back)[:, None].astype(jnp.bfloat16)
    stacked = [
        jnp.stack([collected[layer_at][member] for layer_at in range(layers)])
        for member in range(12)
    ]
    shares = (
        lax.psum_scatter(
            stacked[0].astype(jnp.bfloat16), "fsdp", scatter_dimension=2, tiled=True
        ).astype(jnp.float32),
        lax.psum_scatter(
            stacked[1].astype(jnp.bfloat16), "fsdp", scatter_dimension=2, tiled=True
        ).astype(jnp.float32),
        lax.psum_scatter(
            stacked[2].astype(jnp.bfloat16), "fsdp", scatter_dimension=1, tiled=True
        ).astype(jnp.float32),
        lax.psum_scatter(
            stacked[3].astype(jnp.bfloat16), "fsdp", scatter_dimension=1, tiled=True
        ).astype(jnp.float32),
        lax.psum_scatter(
            stacked[4].astype(jnp.bfloat16), "fsdp", scatter_dimension=1, tiled=True
        ).astype(jnp.float32),
        lax.psum_scatter(
            stacked[5].astype(jnp.bfloat16), "fsdp", scatter_dimension=1, tiled=True
        ).astype(jnp.float32),
        lax.psum_scatter(
            stacked[6].astype(jnp.bfloat16), "fsdp", scatter_dimension=1, tiled=True
        ).astype(jnp.float32),
        lax.psum_scatter(
            stacked[7].astype(jnp.bfloat16), "fsdp", scatter_dimension=1, tiled=True
        ).astype(jnp.float32),
        lax.psum_scatter(
            stacked[8].astype(jnp.bfloat16), "fsdp", scatter_dimension=1, tiled=True
        ).astype(jnp.float32),
        lax.psum_scatter(
            stacked[9].astype(jnp.bfloat16), "fsdp", scatter_dimension=1, tiled=True
        ).astype(jnp.float32),
        lax.psum_scatter(
            stacked[10].astype(jnp.bfloat16), "fsdp", scatter_dimension=1, tiled=True
        ).astype(jnp.float32),
        lax.psum_scatter(
            stacked[11].astype(jnp.bfloat16), "fsdp", scatter_dimension=1, tiled=True
        ).astype(jnp.float32),
    )
    reduced = (
        lax.psum(shares[0].astype(jnp.bfloat16), "rep").astype(jnp.float32),
        lax.psum(shares[1].astype(jnp.bfloat16), "rep").astype(jnp.float32),
        lax.psum(shares[2].astype(jnp.bfloat16), "rep").astype(jnp.float32),
        lax.psum(shares[3].astype(jnp.bfloat16), "rep").astype(jnp.float32),
        lax.psum(shares[4].astype(jnp.bfloat16), "rep").astype(jnp.float32),
        lax.psum(shares[5].astype(jnp.bfloat16), "rep").astype(jnp.float32),
        lax.psum(shares[6].astype(jnp.bfloat16), "rep").astype(jnp.float32),
        lax.psum(shares[7].astype(jnp.bfloat16), "rep").astype(jnp.float32),
        lax.psum(shares[8].astype(jnp.bfloat16), "rep").astype(jnp.float32),
        lax.psum(shares[9].astype(jnp.bfloat16), "rep").astype(jnp.float32),
        lax.psum(shares[10].astype(jnp.bfloat16), "rep").astype(jnp.float32),
        lax.psum(shares[11].astype(jnp.bfloat16), "rep").astype(jnp.float32),
    )
    grad_scale = (micro_count * lax.axis_size("fsdp") * lax.axis_size("rep") * seq_len) ** (-0.5)
    finals = tuple((member_sum * grad_scale for member_sum in reduced))
    return (outputs, images_grad) + finals


ROWS = 256
WIDTH = 768
FF_PARTS = 4
f32 = jnp.float32
bf16 = jnp.bfloat16
VMEM_BYTES = 56 * 1024 * 1024


def dot_nt(left, right):
    return lax.dot_general(left, right, (((1,), (1,)), ((), ())), preferred_element_type=f32)


def dot_nn(left, right):
    return lax.dot_general(left, right, (((1,), (0,)), ((), ())), preferred_element_type=f32)


def swap_core(value):
    return lax.ppermute(value, "fsdp", [(at, at ^ 1) for at in range(8)])


def swap_x(value):
    return lax.ppermute(value, "fsdp", [(at, at ^ 2) for at in range(8)])


def swap_y(value):
    return lax.ppermute(value, "fsdp", [(at, at ^ 4) for at in range(8)])


def gather_pack(own, cut):
    along_x = swap_x(own)
    along_y = swap_y(own)
    across_low = swap_x(along_y[:cut])
    across_high = swap_y(along_x[cut:])
    even = (own, along_x, along_y, across_low, across_high)
    return even + tuple(swap_core(piece) for piece in even)


def piece_plan(cut, first, count):
    plan = []
    for odd in range(2):
        for place, delta in ((0, 0), (1, 2), (2, 4)):
            plan.append((5 * odd + place, first, count, delta ^ odd, 0))
        low = min(max(cut - first, 0), count)
        if low > 0:
            plan.append((5 * odd + 3, first, low, 6 ^ odd, 0))
        if low < count:
            plan.append((5 * odd + 4, first + low - cut, count - low, 6 ^ odd, low))
    return plan


def block_copies(place, refs, plan, block, sems):
    return [
        pltpu.make_async_copy(
            refs[array_at].at[pl.ds(row, count)],
            block.at[place ^ delta, pl.ds(into, count)],
            sems.at[at],
        )
        for at, (array_at, row, count, delta, into) in enumerate(plan)
    ]


def run_all(copies, what):
    for copy in copies:
        getattr(copy, what)()


def in_any():
    return pl.BlockSpec(memory_space=pl.ANY)


def in_smem():
    return pl.BlockSpec(memory_space=pltpu.SMEM)


def params(steps=1):
    return pltpu.CompilerParams(
        dimension_semantics=("arbitrary",) * steps, vmem_limit_bytes=VMEM_BYTES
    )


def cost(flops, moved):
    return pl.CostEstimate(flops=int(flops), bytes_accessed=int(moved), transcendentals=0)


def rows_spec(width):
    return pl.BlockSpec((ROWS, width), lambda image: (image, 0))


def fixed(shape):
    return pl.BlockSpec(shape, lambda image: (0,) * len(shape))


def normalise(rows):
    centre = rows - jnp.mean(rows, axis=-1, keepdims=True)
    root = lax.rsqrt(jnp.mean(centre * centre, axis=-1, keepdims=True) + norm_eps)
    return centre * root, root


SM_HB0, SM_HB1, SM_MB, SM_G1, SM_S1, SM_G2, SM_S2, SM_RB = range(8)


def attn_forward(place, hidden, small, pack, cut):
    plans = [piece_plan(cut, 96 * at, 96) for at in range(4)]
    copies_in_all = sum(len(plan) for plan in plans)

    def kernel(place_ref, hidden_ref, small_ref, *rest):
        packs = rest[:10]
        middle_ref, normed_ref, qkv_ref, mixed_ref, blocks, sems = rest[10:]
        place_now = place_ref[0]
        image = pl.program_id(0)
        copies = []
        at = 0
        for member, plan in enumerate(plans):
            copies.append(
                block_copies(
                    place_now, packs, plan, blocks.at[member], sems.at[pl.ds(at, len(plan))]
                )
            )
            at += len(plan)

        @pl.when(image == 0)
        def begin():
            for group in copies:
                run_all(group, "start")

        rows = hidden_ref[...].astype(f32)
        unit, root = normalise(rows)
        normed = (unit * small_ref[SM_G1 : SM_G1 + 1] + small_ref[SM_S1 : SM_S1 + 1]).astype(bf16)
        normed_ref[...] = normed

        @pl.when(image == 0)
        def arrive():
            for group in copies:
                run_all(group, "wait")

        for member, bias in ((0, SM_HB0), (1, None), (2, SM_HB1)):
            block = blocks[member].reshape(WIDTH, WIDTH)
            made = dot_nt(normed, block)
            if bias is not None:
                made = made + small_ref[bias : bias + 1]
            qkv_ref[:, WIDTH * member : WIDTH * (member + 1)] = made.astype(bf16)
        lane = lax.broadcasted_iota(jnp.int32, (ROWS, 128), 1)
        for pair in range(HEADS // 2):
            q_pair = qkv_ref[:, 128 * pair : 128 * pair + 128]
            k_pair = qkv_ref[:, WIDTH + 128 * pair : WIDTH + 128 * pair + 128]
            v_pair = qkv_ref[:, 2 * WIDTH + 128 * pair : 2 * WIDTH + 128 * pair + 128]
            parts = []
            for half in range(2):
                q_one = jnp.where((lane < 64) == (half == 0), q_pair, jnp.zeros_like(q_pair))
                scores = dot_nt(q_one, k_pair) * (HEAD_DIM**-0.5)
                peak = jnp.max(scores, axis=-1, keepdims=True)
                powers = jnp.exp(scores - peak)
                total = jnp.sum(powers, axis=-1, keepdims=True)
                attend = (powers / total).astype(bf16)
                parts.append(dot_nn(attend, v_pair))
            mixed_ref[:, 128 * pair : 128 * pair + 128] = jnp.where(
                lane < 64, parts[0], parts[1]
            ).astype(bf16)
        merged = dot_nt(mixed_ref[...], blocks[3].reshape(WIDTH, WIDTH))
        middle_ref[...] = rows + (merged + small_ref[SM_MB : SM_MB + 1])

    tokens = hidden.shape[0]
    shape = jax.ShapeDtypeStruct
    return pl.pallas_call(
        kernel,
        grid=(tokens // ROWS,),
        in_specs=[in_smem(), rows_spec(WIDTH), fixed(small.shape)] + [in_any()] * 10,
        out_specs=[rows_spec(WIDTH), rows_spec(WIDTH), rows_spec(3 * WIDTH), rows_spec(WIDTH)],
        out_shape=[
            shape((tokens, WIDTH), f32),
            shape((tokens, WIDTH), bf16),
            shape((tokens, 3 * WIDTH), bf16),
            shape((tokens, WIDTH), bf16),
        ],
        scratch_shapes=[
            pltpu.VMEM((4, 8, 96, WIDTH), bf16),
            pltpu.SemaphoreType.DMA((copies_in_all,)),
        ],
        compiler_params=params(),
        cost_estimate=cost(8 * tokens * WIDTH * WIDTH * 1.5, 12e6),
        name="attn_forward",
    )(place, hidden, small, *pack)


def expand_forward(place, middle, small, expand_bias, pack, cut, first):
    plan = piece_plan(cut, first, 384)

    def kernel(place_ref, middle_ref, small_ref, bias_ref, *rest):
        packs = rest[:10]
        normed_ref, active_ref, slope_ref, block, sems = rest[10:]
        image = pl.program_id(0)
        copies = block_copies(place_ref[0], packs, plan, block, sems)

        @pl.when(image == 0)
        def begin():
            run_all(copies, "start")

        unit, root = normalise(middle_ref[...])
        normed = (unit * small_ref[SM_G2 : SM_G2 + 1] + small_ref[SM_S2 : SM_S2 + 1]).astype(bf16)
        normed_ref[...] = normed

        @pl.when(image == 0)
        def arrive():
            run_all(copies, "wait")

        for part in range(FF_PARTS):
            weight = block[2 * part : 2 * part + 2].reshape(WIDTH, WIDTH)
            point = dot_nt(normed, weight) + bias_ref[part : part + 1]
            square = point * point
            slant = jnp.tanh(0.7978845608028654 * point * (1.0 + 0.044715 * square))
            upper = 0.5 + 0.5 * slant
            columns = slice(WIDTH * part, WIDTH * (part + 1))
            active_ref[:, columns] = (point * upper).astype(bf16)
            bend = point * (0.7978845608028654 + (3 * 0.044715 * 0.7978845608028654) * square)
            slope_ref[:, columns] = (upper + 0.5 * bend * (1.0 - slant * slant)).astype(bf16)

    tokens = middle.shape[0]
    hidden_units = FF_PARTS * WIDTH
    shape = jax.ShapeDtypeStruct
    return pl.pallas_call(
        kernel,
        grid=(tokens // ROWS,),
        in_specs=[
            in_smem(),
            rows_spec(WIDTH),
            fixed(small.shape),
            fixed(expand_bias.shape),
        ]
        + [in_any()] * 10,
        out_specs=[rows_spec(WIDTH), rows_spec(hidden_units), rows_spec(hidden_units)],
        out_shape=[
            shape((tokens, WIDTH), bf16),
            shape((tokens, hidden_units), bf16),
            shape((tokens, hidden_units), bf16),
        ],
        scratch_shapes=[
            pltpu.VMEM((8, 384, WIDTH), bf16),
            pltpu.SemaphoreType.DMA((len(plan),)),
        ],
        compiler_params=params(),
        cost_estimate=cost(8 * tokens * WIDTH * WIDTH, 14e6),
        name="expand_forward",
    )(place, middle, small, expand_bias, *pack)


def reduce_plans(cut, first):
    return [piece_plan(cut, first + 96 * part, 96) for part in range(FF_PARTS)]


def reduce_forward(place, live, middle, active, small, pack, cut, first, last):
    plans = reduce_plans(cut, first)
    copies_in_all = sum(len(plan) for plan in plans)

    def kernel(place_ref, live_ref, middle_ref, active_ref, small_ref, *rest):
        packs = rest[:10]
        result_ref, blocks, sems = rest[10:]
        image = pl.program_id(0)
        copies = []
        for part, plan in enumerate(plans):
            at = sum(len(earlier) for earlier in plans[:part])
            copies += block_copies(
                place_ref[0], packs, plan, blocks.at[part], sems.at[pl.ds(at, len(plan))]
            )

        @pl.when(image == 0)
        def arrive():
            run_all(copies, "start")
            run_all(copies, "wait")

        total = middle_ref[...] + small_ref[SM_RB : SM_RB + 1]
        for part in range(FF_PARTS):
            total = total + dot_nt(
                active_ref[:, WIDTH * part : WIDTH * (part + 1)],
                blocks[part].reshape(WIDTH, WIDTH),
            )
        if last:
            total = total * live_ref[image, 0].astype(f32)
        result_ref[...] = total.astype(result_ref.dtype)

    tokens = middle.shape[0]
    return pl.pallas_call(
        kernel,
        grid=(tokens // ROWS,),
        in_specs=[
            in_smem(),
            in_smem(),
            rows_spec(WIDTH),
            rows_spec(FF_PARTS * WIDTH),
            fixed(small.shape),
        ]
        + [in_any()] * 10,
        out_specs=rows_spec(WIDTH),
        out_shape=jax.ShapeDtypeStruct((tokens, WIDTH), bf16 if last else f32),
        scratch_shapes=[
            pltpu.VMEM((FF_PARTS, 8, 96, WIDTH), bf16),
            pltpu.SemaphoreType.DMA((copies_in_all,)),
        ],
        compiler_params=params(),
        cost_estimate=cost(8 * tokens * WIDTH * WIDTH, 12e6),
        name="reduce_forward",
    )(place, live, middle, active, small, *pack)


def split_owners(place_now, turned, mine_ref, theirs_ref, count, lead=()):
    core = place_now & 1
    chip = place_now >> 1
    for owner in range(4):
        mine_ref[lead + (owner ^ chip,)] = turned[2 * owner + core]
        theirs_ref[lead + (owner ^ chip,)] = turned[2 * owner + 1 - core]


def halves_spec(count):
    return pl.BlockSpec((4, count, ROWS), lambda image: (0, 0, image))


def start_grad(place, live, cotangent):
    def kernel(place_ref, live_ref, cot_ref, grad_ref, mine_ref, theirs_ref, turned):
        image = pl.program_id(0)
        grad = cot_ref[...].astype(f32) * live_ref[image, 0].astype(f32)
        grad_ref[...] = grad.astype(bf16)
        turned[...] = grad.T.astype(bf16).reshape(8, 96, ROWS)
        split_owners(place_ref[0], turned, mine_ref, theirs_ref, 96)

    tokens = cotangent.shape[0]
    shape = jax.ShapeDtypeStruct
    return pl.pallas_call(
        kernel,
        grid=(tokens // ROWS,),
        in_specs=[in_smem(), in_smem(), rows_spec(WIDTH)],
        out_specs=[rows_spec(WIDTH), halves_spec(96), halves_spec(96)],
        out_shape=[shape((tokens, WIDTH), bf16)] + [shape((4, 96, tokens), bf16)] * 2,
        scratch_shapes=[pltpu.VMEM((8, 96, ROWS), bf16)],
        compiler_params=params(),
        cost_estimate=cost(1e6, 4e6),
        name="start_grad",
    )(place, live, cotangent)


def ff_backward(place, grad, slope, middle, small, packs_and_plans):
    (expand_pack, expand_cut, expand_first), (reduce_pack, reduce_cut, reduce_first) = (
        packs_and_plans
    )
    expand_plan = piece_plan(expand_cut, expand_first, 384)
    plans = reduce_plans(reduce_cut, reduce_first)
    copies_in_all = sum(len(plan) for plan in plans)

    def kernel(place_ref, grad_ref, slope_ref, middle_ref, small_ref, *rest):
        expand_packs, reduce_packs = rest[:10], rest[10:20]
        (
            out_ref,
            pre_mine,
            pre_theirs,
            attn_mine,
            attn_theirs,
            sums_ref,
            expand_block,
            reduce_blocks,
            turned_pre,
            turned_attn,
            expand_sems,
            reduce_sems,
        ) = rest[20:]
        place_now = place_ref[0]
        image = pl.program_id(0)
        reduce_copies = []
        for part, plan in enumerate(plans):
            at = sum(len(earlier) for earlier in plans[:part])
            reduce_copies.append(
                block_copies(
                    place_now,
                    reduce_packs,
                    plan,
                    reduce_blocks.at[part],
                    reduce_sems.at[pl.ds(at, len(plan))],
                )
            )
        expand_copies = block_copies(
            place_now, expand_packs, expand_plan, expand_block, expand_sems
        )

        @pl.when(image == 0)
        def begin():
            for group in reduce_copies:
                run_all(group, "start")
            run_all(expand_copies, "start")
            sums_ref[...] = jnp.zeros_like(sums_ref)

        grad_rows = grad_ref[...].astype(f32)
        low = grad_rows.astype(bf16)
        sums_ref[0:1] += jnp.sum(low.astype(f32), axis=0, keepdims=True)
        core = place_now & 1
        chip = place_now >> 1
        back = jnp.zeros((ROWS, WIDTH), f32)
        for part in range(FF_PARTS):

            @pl.when(image == 0)
            def arrive():
                run_all(reduce_copies[part], "wait")
                if part == 0:
                    run_all(expand_copies, "wait")

            columns = slice(WIDTH * part, WIDTH * (part + 1))
            up = dot_nn(low, reduce_blocks[part].reshape(WIDTH, WIDTH))
            pre = up * slope_ref[:, columns].astype(f32)
            pre_low = pre.astype(bf16)
            sums_ref[4 + part : 5 + part] += jnp.sum(
                pre_low.astype(f32), axis=0, keepdims=True
            )
            turned_pre[...] = pre_low.T.reshape(2, 384, ROWS)
            pre_mine[part ^ chip] = turned_pre[core]
            pre_theirs[part ^ chip] = turned_pre[1 - core]
            back = back + dot_nn(
                pre_low, expand_block[2 * part : 2 * part + 2].reshape(WIDTH, WIDTH)
            )
        unit, root = normalise(middle_ref[...])
        sums_ref[1:2] += jnp.sum(back * unit, axis=0, keepdims=True)
        sums_ref[2:3] += jnp.sum(back, axis=0, keepdims=True)
        scaled = back * small_ref[SM_G2 : SM_G2 + 1]
        result = grad_rows + root * (
            scaled
            - jnp.mean(scaled, axis=-1, keepdims=True)
            - unit * jnp.mean(scaled * unit, axis=-1, keepdims=True)
        )
        out_ref[...] = result
        result_low = result.astype(bf16)
        sums_ref[3:4] += jnp.sum(result_low.astype(f32), axis=0, keepdims=True)
        turned_attn[...] = result_low.T.reshape(8, 96, ROWS)
        split_owners(place_now, turned_attn, attn_mine, attn_theirs, 96)

    tokens = middle.shape[0]
    shape = jax.ShapeDtypeStruct
    return pl.pallas_call(
        kernel,
        grid=(tokens // ROWS,),
        in_specs=[
            in_smem(),
            rows_spec(WIDTH),
            rows_spec(FF_PARTS * WIDTH),
            rows_spec(WIDTH),
            fixed(small.shape),
        ]
        + [in_any()] * 20,
        out_specs=[
            rows_spec(WIDTH),
            halves_spec(384),
            halves_spec(384),
            halves_spec(96),
            halves_spec(96),
            fixed((8, WIDTH)),
        ],
        out_shape=[shape((tokens, WIDTH), f32)]
        + [shape((4, 384, tokens), bf16)] * 2
        + [shape((4, 96, tokens), bf16)] * 2
        + [shape((8, WIDTH), f32)],
        scratch_shapes=[
            pltpu.VMEM((8, 384, WIDTH), bf16),
            pltpu.VMEM((FF_PARTS, 8, 96, WIDTH), bf16),
            pltpu.VMEM((2, 384, ROWS), bf16),
            pltpu.VMEM((8, 96, ROWS), bf16),
            pltpu.SemaphoreType.DMA((len(expand_plan),)),
            pltpu.SemaphoreType.DMA((copies_in_all,)),
        ],
        compiler_params=params(),
        cost_estimate=cost(16 * tokens * WIDTH * WIDTH, 22e6),
        name="ff_backward",
    )(place, grad, slope, middle, small, *expand_pack, *reduce_pack)


def attn_backward(place, grad, hidden, qkv, small, pack, cut, last):
    plans = [piece_plan(cut, 96 * at, 96) for at in range(4)]
    copies_in_all = sum(len(plan) for plan in plans)

    def kernel(place_ref, grad_ref, hidden_ref, qkv_ref, small_ref, *rest):
        packs = rest[:10]
        if last:
            out_ref, qkv_mine, qkv_theirs, sums_ref = rest[10:14]
        else:
            out_ref, qkv_mine, qkv_theirs, sums_ref, low_mine, low_theirs = rest[10:16]
        blocks, turned, straight, sems = rest[-4:]
        place_now = place_ref[0]
        image = pl.program_id(0)
        copies = []
        at = 0
        for member, plan in enumerate(plans):
            copies.append(
                block_copies(
                    place_now, packs, plan, blocks.at[member], sems.at[pl.ds(at, len(plan))]
                )
            )
            at += len(plan)

        @pl.when(image == 0)
        def begin():
            for member in (3, 0, 1, 2):
                run_all(copies[member], "start")
            sums_ref[...] = jnp.zeros_like(sums_ref)

        grad_rows = grad_ref[...]

        @pl.when(image == 0)
        def arrive():
            for member in (3, 0, 1, 2):
                run_all(copies[member], "wait")

        mixed_back = dot_nn(grad_rows.astype(bf16), blocks[3].reshape(WIDTH, WIDTH)).astype(bf16)
        lane = lax.broadcasted_iota(jnp.int32, (ROWS, 128), 1)
        line = lax.broadcasted_iota(jnp.int32, (128, ROWS), 0)
        for pair in range(HEADS // 2):
            q_pair = qkv_ref[:, 128 * pair : 128 * pair + 128]
            k_pair = qkv_ref[:, WIDTH + 128 * pair : WIDTH + 128 * pair + 128]
            v_pair = qkv_ref[:, 2 * WIDTH + 128 * pair : 2 * WIDTH + 128 * pair + 128]
            g_pair = mixed_back[:, 128 * pair : 128 * pair + 128]
            q_turned = q_pair.T
            k_turned = k_pair.T
            g_turned = g_pair.T
            made = []
            for half in range(2):
                here = (lane < 64) == (half == 0)
                k_one = jnp.where(here, k_pair, jnp.zeros_like(k_pair))
                v_one = jnp.where(here, v_pair, jnp.zeros_like(v_pair))
                scores = dot_nt(k_one, q_pair) * (HEAD_DIM**-0.5)
                peak = jnp.max(scores, axis=0, keepdims=True)
                powers = jnp.exp(scores - peak)
                attend = powers / jnp.sum(powers, axis=0, keepdims=True)
                back = dot_nt(v_one, g_pair)
                inner = jnp.sum(back * attend, axis=0, keepdims=True)
                scores_back = (attend * (back - inner)).astype(bf16)
                made.append(
                    (
                        dot_nn(k_turned, scores_back) * (HEAD_DIM**-0.5),
                        dot_nt(q_turned, scores_back) * (HEAD_DIM**-0.5),
                        dot_nt(g_turned, attend.astype(bf16)),
                    )
                )
            for member in range(3):
                both = jnp.where(line < 64, made[0][member], made[1][member]).astype(bf16)
                turned[member, pl.ds(128 * pair, 128)] = both
                straight[:, WIDTH * member + 128 * pair : WIDTH * member + 128 * pair + 128] = (
                    both.T
                )
        core = place_now & 1
        chip = place_now >> 1
        back = jnp.zeros((ROWS, WIDTH), f32)
        for member in range(3):
            for owner in range(4):
                for odd in range(2):
                    rows = turned[
                        member,
                        pl.ds(pl.multiple_of(192 * owner + 96 * (core ^ odd), 96), 96),
                    ]
                    target = qkv_theirs if odd else qkv_mine
                    target[member, owner ^ chip] = rows
            straight_one = straight[:, WIDTH * member : WIDTH * (member + 1)]
            back = back + dot_nn(straight_one, blocks[member].reshape(WIDTH, WIDTH))
            if member != 1:
                row = 0 if member == 0 else 1
                sums_ref[row : row + 1] += jnp.sum(
                    straight_one.astype(f32), axis=0, keepdims=True
                )
        unit, root = normalise(hidden_ref[...].astype(f32))
        sums_ref[2:3] += jnp.sum(back * unit, axis=0, keepdims=True)
        sums_ref[3:4] += jnp.sum(back, axis=0, keepdims=True)
        scaled = back * small_ref[SM_G1 : SM_G1 + 1]
        result = grad_rows + root * (
            scaled
            - jnp.mean(scaled, axis=-1, keepdims=True)
            - unit * jnp.mean(scaled * unit, axis=-1, keepdims=True)
        )
        out_ref[...] = result.astype(out_ref.dtype)
        if not last:
            turned[0] = result.astype(bf16).T
            for owner in range(4):
                for odd in range(2):
                    rows = turned[
                        0, pl.ds(pl.multiple_of(192 * owner + 96 * (core ^ odd), 96), 96)
                    ]
                    target = low_theirs if odd else low_mine
                    target[owner ^ chip] = rows

    tokens = grad.shape[0]
    shape = jax.ShapeDtypeStruct
    heads_spec = pl.BlockSpec((3, 4, 96, ROWS), lambda image: (0, 0, 0, image))
    out_specs = [rows_spec(WIDTH), heads_spec, heads_spec, fixed((8, WIDTH))]
    out_shape = (
        [shape((tokens, WIDTH), bf16 if last else f32)]
        + [shape((3, 4, 96, tokens), bf16)] * 2
        + [shape((8, WIDTH), f32)]
    )
    if not last:
        out_specs += [halves_spec(96)] * 2
        out_shape += [shape((4, 96, tokens), bf16)] * 2
    return pl.pallas_call(
        kernel,
        grid=(tokens // ROWS,),
        in_specs=[
            in_smem(),
            rows_spec(WIDTH),
            rows_spec(WIDTH),
            rows_spec(3 * WIDTH),
            fixed(small.shape),
        ]
        + [in_any()] * 10,
        out_specs=out_specs,
        out_shape=out_shape,
        scratch_shapes=[
            pltpu.VMEM((4, 8, 96, WIDTH), bf16),
            pltpu.VMEM((3, WIDTH, ROWS), bf16),
            pltpu.VMEM((ROWS, 3 * WIDTH), bf16),
            pltpu.SemaphoreType.DMA((copies_in_all,)),
        ],
        compiler_params=params(),
        cost_estimate=cost(8 * tokens * WIDTH * WIDTH * 2.5, 16e6),
        name="attn_backward",
    )(place, grad, hidden, qkv, small, *pack)


def spread(result, owner, rows, out_refs, half):
    go_x, go_y, stay_x, stay_y = out_refs
    low, high = result[:, :half].astype(bf16), result[:, half:].astype(bf16)
    target, at = ((stay_x, 0), (go_x, 0), (stay_x, 1), (go_x, 1))[owner]
    target[at, rows] = low
    target, at = ((stay_y, 0), (stay_y, 1), (go_y, 0), (go_y, 1))[owner]
    target[at, rows] = high


def travel_shapes(rows_low, rows_high, half):
    shape = jax.ShapeDtypeStruct
    return [
        shape((2, rows_low, half), bf16),
        shape((2, rows_high, half), bf16),
        shape((2, rows_low, half), bf16),
        shape((2, rows_high, half), bf16),
    ]


def reduce_terms(grad_mine, grad_other, active_mine, active_other):
    tokens, columns = active_mine.shape
    half = columns // 2
    chunk = min(half, WIDTH)

    def kernel(grad_a, grad_b, low_a, low_b, high_a, high_b, go_x, go_y, stay_x, stay_y):
        left_a = grad_a[...].reshape(384, tokens)
        left_b = grad_b[...].reshape(384, tokens)
        low = dot_nn(left_a, low_a[...]) + dot_nn(left_b, low_b[...])
        low = low.astype(bf16).reshape(4, 96, chunk)
        stay_x[0], go_x[0], stay_x[1], go_x[1] = low[0], low[1], low[2], low[3]
        high = dot_nn(left_a, high_a[...]) + dot_nn(left_b, high_b[...])
        high = high.astype(bf16).reshape(4, 96, chunk)
        stay_y[0], stay_y[1], go_y[0], go_y[1] = high[0], high[1], high[2], high[3]

    steps = half // chunk
    grads_spec = pl.BlockSpec((4, 96, tokens), lambda at: (0, 0, 0))
    low_spec = pl.BlockSpec((tokens, chunk), lambda at: (0, at))
    high_spec = pl.BlockSpec((tokens, chunk), lambda at: (0, at + steps))
    return pl.pallas_call(
        kernel,
        grid=(steps,),
        in_specs=[grads_spec, grads_spec, low_spec, low_spec, high_spec, high_spec],
        out_specs=[pl.BlockSpec((2, 96, chunk), lambda at: (0, 0, at))] * 4,
        out_shape=travel_shapes(96, 96, half),
        compiler_params=params(),
        cost_estimate=cost(4 * 384 * tokens * columns, 12e6),
        name="reduce_terms",
    )(grad_mine, grad_other, active_mine, active_other, active_mine, active_other)


def expand_terms(grad_mine, grad_other, normed_mine, normed_other):
    tokens = normed_mine.shape[0]

    def kernel(grad_a, grad_b, rows_a, rows_b, *out_refs):
        for owner in range(4):
            result = dot_nn(grad_a[owner], rows_a[...]) + dot_nn(grad_b[owner], rows_b[...])
            spread(result, owner, slice(None), out_refs, WIDTH // 2)

    return pl.pallas_call(
        kernel,
        out_shape=travel_shapes(384, 384, WIDTH // 2),
        compiler_params=pltpu.CompilerParams(vmem_limit_bytes=VMEM_BYTES),
        cost_estimate=cost(4 * 1536 * tokens * WIDTH, 9e6),
        name="expand_terms",
    )(grad_mine, grad_other, normed_mine, normed_other)


def attn_terms(
    qkv_mine,
    qkv_other,
    normed_mine,
    normed_other,
    attn_mine,
    attn_other,
    mixed_mine,
    mixed_other,
    small_terms,
):
    tokens = normed_mine.shape[0]

    def kernel(
        qkv_a, qkv_b, normed_a, normed_b, attn_a, attn_b, mixed_a, mixed_b, small_ref, *out_refs
    ):
        go_x, go_y, stay_x, stay_y = out_refs
        for member in range(4):
            if member < 3:
                left_a, left_b, right_a, right_b = qkv_a[member], qkv_b[member], normed_a, normed_b
            else:
                left_a, left_b, right_a, right_b = attn_a[...], attn_b[...], mixed_a, mixed_b
            result = dot_nn(left_a.reshape(384, tokens), right_a[...]) + dot_nn(
                left_b.reshape(384, tokens), right_b[...]
            )
            for owner in range(4):
                spread(
                    result[96 * owner : 96 * owner + 96],
                    owner,
                    slice(96 * member, 96 * member + 96),
                    out_refs,
                    WIDTH // 2,
                )
        for owner in range(4):
            target, at = ((stay_x, 0), (go_x, 0), (stay_x, 1), (go_x, 1))[owner]
            target[at, 384:400] = small_ref[owner]

    return pl.pallas_call(
        kernel,
        out_shape=travel_shapes(400, 384, WIDTH // 2),
        compiler_params=pltpu.CompilerParams(vmem_limit_bytes=VMEM_BYTES),
        cost_estimate=cost(4 * 1536 * tokens * WIDTH, 10e6),
        name="attn_terms",
    )(
        qkv_mine,
        qkv_other,
        normed_mine,
        normed_other,
        attn_mine,
        attn_other,
        mixed_mine,
        mixed_other,
        small_terms,
    )


def by_difference(place_at, rows):
    shape = rows.shape
    for bit in range(3):
        halves = rows.reshape((8 >> (bit + 1), 2, 1 << bit) + shape[1:])
        rows = jnp.where((place_at >> bit) & 1 == 1, halves[:, ::-1], halves).reshape(shape)
    return rows


def add_low(*parts):
    total = parts[0].astype(f32)
    for part in parts[1:]:
        total = total + part.astype(f32)
    return total.astype(bf16)


def sum_chips(go_x, go_y, stay_x, stay_y):
    from_x, from_y = swap_x(go_x), swap_y(go_y)
    low_on = swap_y(add_low(stay_x[1], from_x[1]))
    high_on = swap_x(add_low(stay_y[1], from_y[1]))
    return jnp.concatenate(
        [add_low(stay_x[0], from_x[0], low_on), add_low(stay_y[0], from_y[0], high_on)]
    )


def sum_replicas(part):
    inward = add_low(part, lax.ppermute(part, "rep", [(0, 1), (3, 2)]))
    total = add_low(inward, lax.ppermute(inward, "rep", [(1, 2), (2, 1)]))
    outward = lax.ppermute(total, "rep", [(1, 0), (2, 3)])
    rep_at = lax.axis_index("rep")
    return jnp.where((rep_at == 0) | (rep_at == 3), outward, total).astype(f32)


def shards(
    images,
    cotangent,
    slot_flags,
    heads_weight,
    heads_bias,
    merge_weight,
    merge_bias,
    first_gain,
    first_shift,
    second_gain,
    second_shift,
    expand_weight,
    expand_bias,
    reduce_weight,
    reduce_bias,
):
    micro_count, unused_slots, seq_len, width = images.shape
    layers = heads_weight.shape[0]
    tokens = micro_count * seq_len
    place_at = lax.axis_index("fsdp").astype(jnp.int32)
    place = place_at[None]

    def small_rows(layer):
        rows = jnp.concatenate(
            [
                heads_bias[layer],
                merge_bias[layer][None],
                first_gain[layer][None],
                first_shift[layer][None],
                second_gain[layer][None],
                second_shift[layer][None],
                reduce_bias[layer][None],
                expand_bias[layer].reshape(4, 96),
            ]
        )
        return jnp.pad(rows, ((0, 4), (0, width - 96)))

    def reduce_rows(layer):
        return [reduce_weight[layer][:, width * part : width * (part + 1)] for part in range(4)]

    attn_cut, ff_cut = 192, 384
    attn_packs, ff_packs = [], []
    for layer in range(layers):
        own = jnp.concatenate(
            [
                heads_weight[layer].reshape(288, width),
                merge_weight[layer],
                small_rows(layer),
            ]
        )
        attn_packs.append(gather_pack(own, attn_cut))
        own = jnp.concatenate([expand_weight[layer]] + reduce_rows(layer))
        ff_packs.append(gather_pack(own, ff_cut))

    smalls, expand_biases = [], []
    for pack in attn_packs:
        own, along_x, along_y, unused, across, own_c, x_c, y_c, unused_c, across_c = pack
        rows = [
            own[384:396, :96],
            own_c[384:396, :96],
            along_x[384:396, :96],
            x_c[384:396, :96],
            along_y[384:396, :96],
            y_c[384:396, :96],
            across[192:204, :96],
            across_c[192:204, :96],
        ]
        ordered = by_difference(place_at, jnp.stack(rows).astype(f32))
        smalls.append(ordered[:, :8].transpose(1, 0, 2).reshape(8, width))
        expand_biases.append(ordered[:, 8:].reshape(4, width))

    hidden = images.reshape(tokens, width)
    saved = []
    grad, low_mine, low_theirs = start_grad(place, slot_flags, cotangent.reshape(tokens, width))
    for layer in range(layers):
        last = layer == layers - 1
        small = smalls[layer]
        middle, normed, qkv, mixed = attn_forward(
            place, hidden, small, attn_packs[layer], attn_cut
        )
        second, active, slope = expand_forward(
            place, middle, small, expand_biases[layer], ff_packs[layer], ff_cut, 0
        )
        following = reduce_forward(
            place, slot_flags, middle, active, small, ff_packs[layer], ff_cut, 384, last
        )
        others = tuple(swap_core(rows) for rows in (normed, mixed, second, active))
        saved.append((hidden, normed, qkv, mixed, middle, second, active, slope, others))
        hidden = following
    outputs = hidden.reshape(images.shape)

    sums = [None] * layers
    for layer in reversed(range(layers)):
        last = layer == 0
        small = smalls[layer]
        before, normed, qkv, mixed, middle, second, active, slope, others = saved[layer]
        normed_other, mixed_other, second_other, active_other = others
        reduce_sum = sum_replicas(
            sum_chips(*reduce_terms(low_mine, swap_core(low_theirs), active, active_other))
        )
        grad, pre_mine, pre_theirs, attn_mine, attn_theirs, ff_sums = ff_backward(
            place,
            grad,
            slope,
            middle,
            small,
            ((ff_packs[layer], ff_cut, 0), (ff_packs[layer], ff_cut, 384)),
        )
        expand_sum = sum_replicas(
            sum_chips(*expand_terms(pre_mine, swap_core(pre_theirs), second, second_other))
        )
        made = attn_backward(place, grad, before, qkv, small, attn_packs[layer], attn_cut, last)
        grad, qkv_mine, qkv_theirs, attn_sums = made[:4]
        if not last:
            low_mine, low_theirs = made[4:]
        vectors = jnp.concatenate(
            [
                attn_sums[0:2],
                ff_sums[3:4],
                attn_sums[2:4],
                ff_sums[1:3],
                ff_sums[0:1],
            ]
        )
        terms = jnp.concatenate(
            [
                vectors.reshape(8, 8, 96).transpose(1, 0, 2),
                ff_sums[4:8].reshape(8, 4, 96),
            ],
            axis=1,
        )
        terms = by_difference(place_at, terms).reshape(4, 2, 12, 96)
        terms = terms[:, 0] + swap_core(terms[:, 1])
        terms = jnp.pad(terms, ((0, 0), (0, 4), (0, width // 2 - 96))).astype(bf16)
        attn_sum = sum_replicas(
            sum_chips(
                *attn_terms(
                    qkv_mine,
                    swap_core(qkv_theirs),
                    normed,
                    normed_other,
                    attn_mine,
                    swap_core(attn_theirs),
                    mixed,
                    mixed_other,
                    terms,
                )
            )
        )
        sums[layer] = (reduce_sum, expand_sum, attn_sum)
    images_grad = grad.reshape(images.shape)

    grad_scale = (
        micro_count * images.shape[1] * lax.axis_size("fsdp") * lax.axis_size("rep") * seq_len
    ) ** (-0.5)
    finals = []
    for reduce_sum, expand_sum, attn_sum in sums:
        low, high = attn_sum[:400] * grad_scale, attn_sum[400:] * grad_scale
        whole = jnp.concatenate([low[:384], high], axis=1)
        vectors = low[384:396, :96]
        finals.append(
            (
                whole[:288].reshape(3, 96, width),
                vectors[SM_HB0 : SM_HB1 + 1],
                whole[288:],
                vectors[SM_MB],
                vectors[SM_G1],
                vectors[SM_S1],
                vectors[SM_G2],
                vectors[SM_S2],
                jnp.concatenate([expand_sum[:384], expand_sum[384:]], axis=1) * grad_scale,
                vectors[8:12].reshape(384),
                jnp.concatenate([reduce_sum[:96], reduce_sum[96:]], axis=1) * grad_scale,
                vectors[SM_RB],
            )
        )
    stacked = tuple(jnp.stack(member) for member in zip(*finals))
    return (outputs, images_grad) + stacked


def solution(mesh):
    body = shards if (mesh.shape["fsdp"], mesh.shape["rep"]) == (8, 4) else plain_shards
    placed = (
        P(None, ("fsdp", "rep"), None, None),
        P(None, ("fsdp", "rep"), None, None),
        P(None, ("fsdp", "rep")),
        P(None, None, "fsdp", None),
        P(None, None, "fsdp"),
        P(None, "fsdp", None),
        P(None, "fsdp"),
        P(None, "fsdp"),
        P(None, "fsdp"),
        P(None, "fsdp"),
        P(None, "fsdp"),
        P(None, "fsdp", None),
        P(None, "fsdp"),
        P(None, "fsdp", None),
        P(None, "fsdp"),
    )
    return jax.shard_map(
        body,
        mesh=mesh,
        in_specs=placed,
        out_specs=(
            P(None, ("fsdp", "rep"), None, None),
            P(None, ("fsdp", "rep"), None, None),
            P(None, None, "fsdp", None),
            P(None, None, "fsdp"),
            P(None, "fsdp", None),
            P(None, "fsdp"),
            P(None, "fsdp"),
            P(None, "fsdp"),
            P(None, "fsdp"),
            P(None, "fsdp"),
            P(None, "fsdp", None),
            P(None, "fsdp"),
            P(None, "fsdp", None),
            P(None, "fsdp"),
        ),
        check_vma=False,
    )
```

```python
import jax
import jax.numpy as jnp
from jax import lax
from jax.experimental import pallas as pl
from jax.experimental.pallas import tpu as pltpu
from jax.sharding import PartitionSpec as P

HEADS = 12
HEAD_DIM = 64


norm_eps = 1e-06


def layer_norm(token_rows, scale_row, offset_row):
    centre = token_rows - jnp.mean(token_rows, axis=-1, keepdims=True)
    spread = jnp.mean(centre * centre, axis=-1, keepdims=True)
    return centre * lax.rsqrt(spread + norm_eps) * scale_row + offset_row


def project(token_rows, weight):
    return lax.dot_general(
        token_rows, weight, (((1,), (1,)), ((), ())), preferred_element_type=jnp.float32
    )


def outer_sum(grad_rows, token_rows):
    return lax.dot_general(
        grad_rows, token_rows, (((0,), (0,)), ((), ())), preferred_element_type=jnp.float32
    )


def carry_back(grad_rows, weight):
    return jnp.dot(grad_rows, weight, preferred_element_type=jnp.float32)


def forward_layer(hidden, params):
    (
        heads_weight,
        heads_bias,
        merge_weight,
        merge_bias,
        first_gain,
        first_shift,
        second_gain,
        second_shift,
        expand_weight,
        expand_bias,
        reduce_weight,
        reduce_bias,
    ) = params
    seq_len, model_width = hidden.shape
    shaped = (seq_len, HEADS, HEAD_DIM)
    score_scale = HEAD_DIM ** (-0.5)
    normed = layer_norm(
        hidden, first_gain.astype(jnp.float32), first_shift.astype(jnp.float32)
    ).astype(jnp.bfloat16)
    queries = (project(normed, heads_weight[0]) + heads_bias[0].astype(jnp.float32)).astype(
        jnp.bfloat16
    )
    key_rows = project(normed, heads_weight[1]).astype(jnp.bfloat16)
    values = (project(normed, heads_weight[2]) + heads_bias[1].astype(jnp.float32)).astype(
        jnp.bfloat16
    )
    scores = (
        jnp.einsum(
            "qhd,khd->hqk",
            queries.reshape(shaped),
            key_rows.reshape(shaped),
            preferred_element_type=jnp.float32,
        )
        * score_scale
    )
    row_peak = jnp.max(scores, axis=-1, keepdims=True)
    exponent = jnp.exp(scores - row_peak)
    row_total = jnp.sum(exponent, axis=-1, keepdims=True)
    attend = exponent / row_total
    log_total = row_peak + jnp.log(row_total)
    mixed_rows = jnp.einsum(
        "hqk,khd->qhd",
        attend.astype(jnp.bfloat16),
        values.reshape(shaped),
        preferred_element_type=jnp.float32,
    )
    mixed_rows = mixed_rows.reshape(seq_len, model_width).astype(jnp.bfloat16)
    middle = hidden + (project(mixed_rows, merge_weight) + merge_bias.astype(jnp.float32))
    second = layer_norm(
        middle, second_gain.astype(jnp.float32), second_shift.astype(jnp.float32)
    ).astype(jnp.bfloat16)
    pre_act = project(second, expand_weight) + expand_bias.astype(jnp.float32)
    activated = jax.nn.gelu(pre_act, approximate=True).astype(jnp.bfloat16)
    result = middle + (project(activated, reduce_weight) + reduce_bias.astype(jnp.float32))
    saved = (
        hidden,
        normed,
        queries,
        key_rows,
        values,
        log_total,
        mixed_rows,
        middle,
        second,
        pre_act,
        activated,
    )
    return (result, saved)


def backward_layer(grad_out, params, saved):
    (
        heads_weight,
        heads_bias,
        merge_weight,
        merge_bias,
        first_gain,
        first_shift,
        second_gain,
        second_shift,
        expand_weight,
        expand_bias,
        reduce_weight,
        reduce_bias,
    ) = params
    (
        hidden,
        normed,
        queries,
        key_rows,
        values,
        log_total,
        mixed_rows,
        middle,
        second,
        pre_act,
        activated,
    ) = saved
    seq_len, model_width = hidden.shape
    shaped = (seq_len, HEADS, HEAD_DIM)
    score_scale = HEAD_DIM ** (-0.5)
    branch_low = grad_out.astype(jnp.bfloat16)
    reduce_weight_term = outer_sum(branch_low, activated)
    reduce_bias_term = jnp.sum(branch_low.astype(jnp.float32), axis=0)
    grad_act = carry_back(branch_low, reduce_weight)
    unused_value, gelu_back = jax.vjp(lambda point: jax.nn.gelu(point, approximate=True), pre_act)
    grad_pre = gelu_back(grad_act)[0].astype(jnp.bfloat16)
    expand_weight_term = outer_sum(grad_pre, second)
    expand_bias_term = jnp.sum(grad_pre.astype(jnp.float32), axis=0)
    grad_second = carry_back(grad_pre, expand_weight)
    unused_norm, second_back = jax.vjp(
        layer_norm, middle, second_gain.astype(jnp.float32), second_shift.astype(jnp.float32)
    )
    middle_part, second_gain_term, second_shift_term = second_back(grad_second)
    grad_middle = grad_out + middle_part
    attn_low = grad_middle.astype(jnp.bfloat16)
    merge_weight_term = outer_sum(attn_low, mixed_rows)
    merge_bias_term = jnp.sum(attn_low.astype(jnp.float32), axis=0)
    grad_mixed = carry_back(attn_low, merge_weight).astype(jnp.bfloat16).reshape(shaped)
    queries_heads = queries.reshape(shaped)
    keys_heads = key_rows.reshape(shaped)
    values_heads = values.reshape(shaped)
    scores = (
        jnp.einsum("qhd,khd->hqk", queries_heads, keys_heads, preferred_element_type=jnp.float32)
        * score_scale
    )
    attend = jnp.exp(scores - log_total)
    grad_values = jnp.einsum(
        "hqk,qhd->khd", attend.astype(jnp.bfloat16), grad_mixed, preferred_element_type=jnp.float32
    ).astype(jnp.bfloat16)
    grad_attend = jnp.einsum(
        "qhd,khd->hqk", grad_mixed, values_heads, preferred_element_type=jnp.float32
    )
    grad_scores = attend * (grad_attend - jnp.sum(grad_attend * attend, axis=-1, keepdims=True))
    grad_scores = grad_scores.astype(jnp.bfloat16)
    grad_queries = (
        jnp.einsum("hqk,khd->qhd", grad_scores, keys_heads, preferred_element_type=jnp.float32)
        * score_scale
    ).astype(jnp.bfloat16)
    grad_keys = (
        jnp.einsum("hqk,qhd->khd", grad_scores, queries_heads, preferred_element_type=jnp.float32)
        * score_scale
    ).astype(jnp.bfloat16)
    stacked_grads = jnp.stack(
        [
            grad_queries.reshape(seq_len, model_width),
            grad_keys.reshape(seq_len, model_width),
            grad_values.reshape(seq_len, model_width),
        ]
    )
    heads_weight_term = jnp.einsum(
        "jto,ti->joi", stacked_grads, normed, preferred_element_type=jnp.float32
    )
    grad_normed = jnp.einsum(
        "jto,joi->ti", stacked_grads, heads_weight, preferred_element_type=jnp.float32
    )
    heads_bias_term = jnp.stack(
        [
            jnp.sum(stacked_grads[0].astype(jnp.float32), axis=0),
            jnp.sum(stacked_grads[2].astype(jnp.float32), axis=0),
        ]
    )
    unused_first, first_back = jax.vjp(
        layer_norm, hidden, first_gain.astype(jnp.float32), first_shift.astype(jnp.float32)
    )
    hidden_part, first_gain_term, first_shift_term = first_back(grad_normed)
    grad_hidden = grad_middle + hidden_part
    terms = (
        heads_weight_term,
        heads_bias_term,
        merge_weight_term,
        merge_bias_term,
        first_gain_term,
        first_shift_term,
        second_gain_term,
        second_shift_term,
        expand_weight_term,
        expand_bias_term,
        reduce_weight_term,
        reduce_bias_term,
    )
    return (grad_hidden, terms)


def plain_shards(
    images,
    cotangent,
    slot_flags,
    heads_weight,
    heads_bias,
    merge_weight,
    merge_bias,
    first_gain,
    first_shift,
    second_gain,
    second_shift,
    expand_weight,
    expand_bias,
    reduce_weight,
    reduce_bias,
):
    micro_count = images.shape[0]
    seq_len = images.shape[2]
    layers = heads_weight.shape[0]
    live_flags = slot_flags.astype(jnp.float32)
    states = [images[batch_at, 0].astype(jnp.float32) for batch_at in range(micro_count)]
    saved_all = []
    for layer_at in range(layers):
        saved_row = []
        for batch_at in range(micro_count):
            params = (
                lax.all_gather(heads_weight[layer_at], "fsdp", axis=1, tiled=True),
                lax.all_gather(heads_bias[layer_at], "fsdp", axis=1, tiled=True),
                lax.all_gather(merge_weight[layer_at], "fsdp", axis=0, tiled=True),
                lax.all_gather(merge_bias[layer_at], "fsdp", axis=0, tiled=True),
                lax.all_gather(first_gain[layer_at], "fsdp", axis=0, tiled=True),
                lax.all_gather(first_shift[layer_at], "fsdp", axis=0, tiled=True),
                lax.all_gather(second_gain[layer_at], "fsdp", axis=0, tiled=True),
                lax.all_gather(second_shift[layer_at], "fsdp", axis=0, tiled=True),
                lax.all_gather(expand_weight[layer_at], "fsdp", axis=0, tiled=True),
                lax.all_gather(expand_bias[layer_at], "fsdp", axis=0, tiled=True),
                lax.all_gather(reduce_weight[layer_at], "fsdp", axis=0, tiled=True),
                lax.all_gather(reduce_bias[layer_at], "fsdp", axis=0, tiled=True),
            )
            states[batch_at], saved = forward_layer(states[batch_at], params)
            saved_row.append(saved)
        saved_all.append(saved_row)
    outputs = jnp.stack(
        [live_flags[batch_at, 0] * states[batch_at] for batch_at in range(micro_count)]
    )[:, None].astype(jnp.bfloat16)
    grads_back = [
        cotangent[batch_at, 0].astype(jnp.float32) * live_flags[batch_at, 0]
        for batch_at in range(micro_count)
    ]
    collected = [None] * layers
    for layer_at in reversed(range(layers)):
        totals = None
        for batch_at in range(micro_count):
            params = (
                lax.all_gather(heads_weight[layer_at], "fsdp", axis=1, tiled=True),
                lax.all_gather(heads_bias[layer_at], "fsdp", axis=1, tiled=True),
                lax.all_gather(merge_weight[layer_at], "fsdp", axis=0, tiled=True),
                lax.all_gather(merge_bias[layer_at], "fsdp", axis=0, tiled=True),
                lax.all_gather(first_gain[layer_at], "fsdp", axis=0, tiled=True),
                lax.all_gather(first_shift[layer_at], "fsdp", axis=0, tiled=True),
                lax.all_gather(second_gain[layer_at], "fsdp", axis=0, tiled=True),
                lax.all_gather(second_shift[layer_at], "fsdp", axis=0, tiled=True),
                lax.all_gather(expand_weight[layer_at], "fsdp", axis=0, tiled=True),
                lax.all_gather(expand_bias[layer_at], "fsdp", axis=0, tiled=True),
                lax.all_gather(reduce_weight[layer_at], "fsdp", axis=0, tiled=True),
                lax.all_gather(reduce_bias[layer_at], "fsdp", axis=0, tiled=True),
            )
            grads_back[batch_at], terms = backward_layer(
                grads_back[batch_at], params, saved_all[layer_at][batch_at]
            )
            if totals is None:
                totals = terms
            else:
                totals = tuple((earlier + current for earlier, current in zip(totals, terms)))
        collected[layer_at] = totals
    images_grad = jnp.stack(grads_back)[:, None].astype(jnp.bfloat16)
    stacked = [
        jnp.stack([collected[layer_at][member] for layer_at in range(layers)])
        for member in range(12)
    ]
    shares = (
        lax.psum_scatter(
            stacked[0].astype(jnp.bfloat16), "fsdp", scatter_dimension=2, tiled=True
        ).astype(jnp.float32),
        lax.psum_scatter(
            stacked[1].astype(jnp.bfloat16), "fsdp", scatter_dimension=2, tiled=True
        ).astype(jnp.float32),
        lax.psum_scatter(
            stacked[2].astype(jnp.bfloat16), "fsdp", scatter_dimension=1, tiled=True
        ).astype(jnp.float32),
        lax.psum_scatter(
            stacked[3].astype(jnp.bfloat16), "fsdp", scatter_dimension=1, tiled=True
        ).astype(jnp.float32),
        lax.psum_scatter(
            stacked[4].astype(jnp.bfloat16), "fsdp", scatter_dimension=1, tiled=True
        ).astype(jnp.float32),
        lax.psum_scatter(
            stacked[5].astype(jnp.bfloat16), "fsdp", scatter_dimension=1, tiled=True
        ).astype(jnp.float32),
        lax.psum_scatter(
            stacked[6].astype(jnp.bfloat16), "fsdp", scatter_dimension=1, tiled=True
        ).astype(jnp.float32),
        lax.psum_scatter(
            stacked[7].astype(jnp.bfloat16), "fsdp", scatter_dimension=1, tiled=True
        ).astype(jnp.float32),
        lax.psum_scatter(
            stacked[8].astype(jnp.bfloat16), "fsdp", scatter_dimension=1, tiled=True
        ).astype(jnp.float32),
        lax.psum_scatter(
            stacked[9].astype(jnp.bfloat16), "fsdp", scatter_dimension=1, tiled=True
        ).astype(jnp.float32),
        lax.psum_scatter(
            stacked[10].astype(jnp.bfloat16), "fsdp", scatter_dimension=1, tiled=True
        ).astype(jnp.float32),
        lax.psum_scatter(
            stacked[11].astype(jnp.bfloat16), "fsdp", scatter_dimension=1, tiled=True
        ).astype(jnp.float32),
    )
    reduced = (
        lax.psum(shares[0].astype(jnp.bfloat16), "rep").astype(jnp.float32),
        lax.psum(shares[1].astype(jnp.bfloat16), "rep").astype(jnp.float32),
        lax.psum(shares[2].astype(jnp.bfloat16), "rep").astype(jnp.float32),
        lax.psum(shares[3].astype(jnp.bfloat16), "rep").astype(jnp.float32),
        lax.psum(shares[4].astype(jnp.bfloat16), "rep").astype(jnp.float32),
        lax.psum(shares[5].astype(jnp.bfloat16), "rep").astype(jnp.float32),
        lax.psum(shares[6].astype(jnp.bfloat16), "rep").astype(jnp.float32),
        lax.psum(shares[7].astype(jnp.bfloat16), "rep").astype(jnp.float32),
        lax.psum(shares[8].astype(jnp.bfloat16), "rep").astype(jnp.float32),
        lax.psum(shares[9].astype(jnp.bfloat16), "rep").astype(jnp.float32),
        lax.psum(shares[10].astype(jnp.bfloat16), "rep").astype(jnp.float32),
        lax.psum(shares[11].astype(jnp.bfloat16), "rep").astype(jnp.float32),
    )
    grad_scale = (micro_count * lax.axis_size("fsdp") * lax.axis_size("rep") * seq_len) ** (-0.5)
    finals = tuple((member_sum * grad_scale for member_sum in reduced))
    return (outputs, images_grad) + finals


ROWS = 256
WIDTH = 768
FF_PARTS = 4
f32 = jnp.float32
bf16 = jnp.bfloat16
VMEM_BYTES = 56 * 1024 * 1024
SMALL_VMEM_BYTES = 24 * 1024 * 1024


def dot_nt(left, right):
    return lax.dot_general(left, right, (((1,), (1,)), ((), ())), preferred_element_type=f32)


def dot_nn(left, right):
    return lax.dot_general(left, right, (((1,), (0,)), ((), ())), preferred_element_type=f32)


def swap_core(value):
    return lax.ppermute(value, "fsdp", [(at, at ^ 1) for at in range(8)])


def swap_x(value):
    return lax.ppermute(value, "fsdp", [(at, at ^ 2) for at in range(8)])


def swap_y(value):
    return lax.ppermute(value, "fsdp", [(at, at ^ 4) for at in range(8)])


PIECES = 10


def regions_of(rows, cut, x_row, y_row):
    return [
        region
        for odd in range(2)
        for region in (
            (5 * odd, odd, 0, rows, 0),
            (5 * odd + 1, 2 ^ odd, 0, rows, x_row),
            (5 * odd + 2, 4 ^ odd, 0, rows, y_row),
            (5 * odd + 3, 6 ^ odd, 0, cut, 0),
            (5 * odd + 4, 6 ^ odd, cut, rows, 0),
        )
    ]


def block_copies(place, refs, regions, first, count, block, sems):
    copies = []
    for array_at, delta, low, high, start in regions:
        begin, end = max(low, first), min(high, first + count)
        if begin < end:
            copies.append(
                pltpu.make_async_copy(
                    refs[array_at].at[pl.ds(start + begin - low, end - begin)],
                    block.at[place ^ delta, pl.ds(begin - first, end - begin)],
                    sems.at[len(copies)],
                )
            )
    return copies


def run_all(copies, what):
    for copy in copies:
        getattr(copy, what)()


def in_any():
    return pl.BlockSpec(memory_space=pl.ANY)


def in_smem():
    return pl.BlockSpec(memory_space=pltpu.SMEM)


def params(steps=1):
    return pltpu.CompilerParams(
        dimension_semantics=("arbitrary",) * steps, vmem_limit_bytes=VMEM_BYTES
    )


def cost(micros):
    return pl.CostEstimate(flops=int(micros * 1.1e9), bytes_accessed=1 << 10, transcendentals=0)


def rows_spec(width):
    return pl.BlockSpec((ROWS, width), lambda image: (image, 0))


def fixed(shape):
    return pl.BlockSpec(shape, lambda image: (0,) * len(shape))


def normalise(rows):
    centre = rows - jnp.mean(rows, axis=-1, keepdims=True)
    root = lax.rsqrt(jnp.mean(centre * centre, axis=-1, keepdims=True) + norm_eps)
    return centre * root, root


def own_copies(sources, target, sems, kind, layer):
    if kind == "attn":
        heads, merge = sources[:2]
        pairs = [(heads.at[layer, at], target.at[pl.ds(96 * at, 96)]) for at in range(3)]
        pairs.append((merge.at[layer], target.at[pl.ds(288, 96)]))
    else:
        expand, reduce = sources[2:]
        pairs = [(expand.at[layer], target.at[pl.ds(0, 384)])]
        for part in range(FF_PARTS):
            pairs.append(
                (
                    reduce.at[layer, :, pl.ds(WIDTH * part, WIDTH)],
                    target.at[pl.ds(384 + 96 * part, 96)],
                )
            )
    return [pltpu.make_async_copy(*pair, sems.at[at]) for at, pair in enumerate(pairs)]


def own_packs(wanted, matrices, vectors):
    count = len(wanted)

    def kernel(*refs):
        sources, vector_refs = refs[:4], refs[4:12]
        outs = refs[12 : 12 + count]
        rows, low_rows, sems, vector_sems = refs[12 + count :]
        copies = []
        for at, (kind, layer) in enumerate(wanted):
            copies += own_copies(sources, outs[at], sems.at[at], kind, layer)
        run_all(copies, "start")
        vector_copies = []
        for at, (kind, layer) in enumerate(wanted):
            if kind == "attn":
                rows[...] = jnp.zeros_like(rows)
                rows[0:2, 0:96] = vector_refs[0][layer].astype(f32)
                for row in range(2, 8):
                    values = vector_refs[row - 1][...].astype(f32)
                    rows[row : row + 1, 0:96] = values[layer : layer + 1]
                rows[8:9, 0:384] = vector_refs[7][...].astype(f32)[layer : layer + 1]
                low_rows[at] = rows[...].astype(bf16)
                vector_copies.append(
                    pltpu.make_async_copy(
                        low_rows.at[at], outs[at].at[pl.ds(384, 16)], vector_sems.at[at]
                    )
                )
        run_all(vector_copies, "start")
        run_all(copies + vector_copies, "wait")

    return pl.pallas_call(
        kernel,
        in_specs=[in_any()] * 4 + [pl.BlockSpec(memory_space=pltpu.VMEM)] * 8,
        out_specs=[in_any()] * count,
        out_shape=[
            jax.ShapeDtypeStruct((400 if kind == "attn" else 768, WIDTH), bf16)
            for kind, layer in wanted
        ],
        scratch_shapes=[
            pltpu.VMEM((16, WIDTH), f32),
            pltpu.VMEM((count, 16, WIDTH), bf16),
            pltpu.SemaphoreType.DMA((count, 5)),
            pltpu.SemaphoreType.DMA((count,)),
        ],
        compiler_params=pltpu.CompilerParams(vmem_limit_bytes=SMALL_VMEM_BYTES),
        cost_estimate=cost(0.01),
        name="own_packs",
    )(*matrices, *vectors)


def join_rows(pieces_of):
    flat = [piece for pieces in pieces_of for piece in pieces]
    heights = [sum(rows for unused, unused_first, rows in pieces) for pieces in pieces_of]

    def kernel(*refs):
        ins, outs, sems = refs[: len(flat)], refs[len(flat) : -1], refs[-1]
        copies = []
        for out, pieces in zip(outs, pieces_of):
            into = 0
            for unused, first, rows in pieces:
                at = len(copies)
                copies.append(
                    pltpu.make_async_copy(
                        ins[at].at[pl.ds(first, rows)], out.at[pl.ds(into, rows)], sems.at[at]
                    )
                )
                into += rows
        run_all(copies, "start")
        run_all(copies, "wait")

    return pl.pallas_call(
        kernel,
        in_specs=[in_any()] * len(flat),
        out_specs=[in_any()] * len(heights),
        out_shape=[jax.ShapeDtypeStruct((rows, WIDTH), bf16) for rows in heights],
        scratch_shapes=[pltpu.SemaphoreType.DMA((len(flat),))],
        compiler_params=pltpu.CompilerParams(vmem_limit_bytes=SMALL_VMEM_BYTES),
        cost_estimate=cost(0.01),
        name="join_rows",
    )(*[array for array, unused, unused_rows in flat])


def gathered_vectors(place, pack):
    arrays, regions = pack
    used = {}
    for array_at, delta, low, high, start in regions:
        if low <= 384 and 400 <= high:
            used[delta] = (arrays[array_at], start + 384 - low)
    deltas = sorted(used)

    def kernel(place_ref, *refs):
        ins, small_ref, expand_ref, rows, sems = refs[:8], refs[8], refs[9], refs[10], refs[11]
        copies = [
            pltpu.make_async_copy(
                ins[at].at[pl.ds(used[delta][1], 16)], rows.at[at], sems.at[at]
            )
            for at, delta in enumerate(deltas)
        ]
        run_all(copies, "start")
        here = place_ref[0]
        row = lax.broadcasted_iota(jnp.int32, (1024, WIDTH), 0)
        column = lax.broadcasted_iota(jnp.int32, (1024, WIDTH), 1)
        at = row & 127
        wanted = 96 * ((row >> 7) ^ here) + at
        chosen = jnp.where((column == wanted) & (at < 96), 1.0, 0.0).astype(bf16)
        run_all(copies, "wait")
        flat = jnp.concatenate([rows[at, 0:8, 0:128].astype(f32) for at in range(8)], axis=1)
        small_ref[...] = dot_nn(flat.astype(bf16), chosen)
        for at, delta in enumerate(deltas):
            owner = here ^ delta
            line = rows[at].astype(f32)[8:9, 0:384]

            @pl.when((owner & 1) == 0)
            def left():
                expand_ref[owner >> 1, :, 0:384] = line

            @pl.when((owner & 1) == 1)
            def right():
                expand_ref[owner >> 1, :, 384:768] = line

    shape = jax.ShapeDtypeStruct
    return pl.pallas_call(
        kernel,
        in_specs=[in_smem()] + [in_any()] * 8,
        out_specs=[pl.BlockSpec(memory_space=pltpu.VMEM)] * 2,
        out_shape=[shape((8, WIDTH), f32), shape((4, 1, WIDTH), f32)],
        scratch_shapes=[pltpu.VMEM((8, 16, WIDTH), bf16), pltpu.SemaphoreType.DMA((8,))],
        compiler_params=pltpu.CompilerParams(vmem_limit_bytes=SMALL_VMEM_BYTES),
        cost_estimate=cost(0.01),
        name="gathered_vectors",
    )(place, *[used[delta][0] for delta in deltas])


def elementwise(name, body, ins, out_shapes):
    def kernel(*refs):
        body(refs[: len(ins)], refs[len(ins) :])

    return pl.pallas_call(
        kernel,
        in_specs=[pl.BlockSpec(memory_space=pltpu.VMEM)] * len(ins),
        out_specs=[pl.BlockSpec(memory_space=pltpu.VMEM)] * len(out_shapes),
        out_shape=[jax.ShapeDtypeStruct(shape, bf16) for shape in out_shapes],
        compiler_params=pltpu.CompilerParams(vmem_limit_bytes=SMALL_VMEM_BYTES),
        cost_estimate=cost(0.01),
        name=name,
    )(*ins)


def add_low(*parts):
    total = parts[0].astype(f32)
    for part in parts[1:]:
        total = total + part.astype(f32)
    return total.astype(bf16)


def first_steps(travel):
    go_x, go_y, stay_x, stay_y = travel
    return swap_x(go_x), swap_y(go_y), stay_x, stay_y


def second_steps(state):
    def body(ins, outs):
        from_x, from_y, stay_x, stay_y = ins
        outs[0][...] = add_low(stay_x[1], from_x[1])
        outs[1][...] = add_low(stay_y[1], from_y[1])
        outs[2][...] = add_low(stay_x[0], from_x[0])
        outs[3][...] = add_low(stay_y[0], from_y[0])

    low, high = state[0].shape[1:], state[1].shape[1:]
    low_on, high_on, kept_low, kept_high = elementwise(
        "second_steps", body, state, [low, high, low, high]
    )
    return swap_y(low_on), swap_x(high_on), kept_low, kept_high


def ends(state):
    from_y, from_x, kept_low, kept_high = state
    low, high = kept_low.shape[0], kept_high.shape[0]

    def body(ins, outs):
        outs[0][0:low] = add_low(ins[2][...], ins[0][...])
        outs[0][low : low + high] = add_low(ins[3][...], ins[1][...])

    return elementwise("ends", body, state, [(low + high, WIDTH // 2)])[0]


def to_middle(part):
    return part, lax.ppermute(part, "rep", [(0, 1), (3, 2)])


def plus(parts):
    def body(ins, outs):
        outs[0][...] = add_low(ins[0][...], ins[1][...])

    return elementwise("plus", body, parts, [parts[0].shape])[0]


def across_middle(parts):
    inward = plus(parts)
    return inward, lax.ppermute(inward, "rep", [(1, 2), (2, 1)])


def to_ends(parts):
    total = plus(parts)
    return total, lax.ppermute(total, "rep", [(1, 0), (2, 3)])


SM_HB0, SM_HB1, SM_MB, SM_G1, SM_S1, SM_G2, SM_S2, SM_RB = range(8)


def heads_copies(place_now, packs, regions, blocks, sems):
    return [
        block_copies(place_now, packs, regions, 96 * at, 96, blocks.at[at], sems.at[at])
        for at in range(4)
    ]


def attn_forward(place, hidden, small, pack):

    def kernel(place_ref, hidden_ref, small_ref, *rest):
        packs = rest[:PIECES]
        middle_ref, normed_ref, qkv_ref, mixed_ref, blocks, sems = rest[PIECES:]
        place_now = place_ref[0]
        image = pl.program_id(0)
        copies = heads_copies(place_now, packs, pack[1], blocks, sems)

        @pl.when(image == 0)
        def begin():
            for group in copies:
                run_all(group, "start")

        rows = hidden_ref[...].astype(f32)
        unit, root = normalise(rows)
        normed = (unit * small_ref[SM_G1 : SM_G1 + 1] + small_ref[SM_S1 : SM_S1 + 1]).astype(bf16)
        normed_ref[...] = normed

        @pl.when(image == 0)
        def arrive():
            for group in copies:
                run_all(group, "wait")

        for member, bias in ((0, SM_HB0), (1, None), (2, SM_HB1)):
            block = blocks[member].reshape(WIDTH, WIDTH)
            made = dot_nt(normed, block)
            if bias is not None:
                made = made + small_ref[bias : bias + 1]
            qkv_ref[:, WIDTH * member : WIDTH * (member + 1)] = made.astype(bf16)
        lane = lax.broadcasted_iota(jnp.int32, (ROWS, 128), 1)
        for pair in range(HEADS // 2):
            q_pair = qkv_ref[:, 128 * pair : 128 * pair + 128]
            k_pair = qkv_ref[:, WIDTH + 128 * pair : WIDTH + 128 * pair + 128]
            v_pair = qkv_ref[:, 2 * WIDTH + 128 * pair : 2 * WIDTH + 128 * pair + 128]
            parts = []
            for half in range(2):
                q_one = jnp.where((lane < 64) == (half == 0), q_pair, jnp.zeros_like(q_pair))
                scores = dot_nt(q_one, k_pair) * (HEAD_DIM**-0.5)
                peak = jnp.max(scores, axis=-1, keepdims=True)
                powers = jnp.exp(scores - peak)
                total = jnp.sum(powers, axis=-1, keepdims=True)
                attend = (powers / total).astype(bf16)
                parts.append(dot_nn(attend, v_pair))
            mixed_ref[:, 128 * pair : 128 * pair + 128] = jnp.where(
                lane < 64, parts[0], parts[1]
            ).astype(bf16)
        merged = dot_nt(mixed_ref[...], blocks[3].reshape(WIDTH, WIDTH))
        middle_ref[...] = rows + (merged + small_ref[SM_MB : SM_MB + 1])

    tokens = hidden.shape[0]
    shape = jax.ShapeDtypeStruct
    return pl.pallas_call(
        kernel,
        grid=(tokens // ROWS,),
        in_specs=[in_smem(), rows_spec(WIDTH), fixed(small.shape)] + [in_any()] * PIECES,
        out_specs=[rows_spec(WIDTH), rows_spec(WIDTH), rows_spec(3 * WIDTH), rows_spec(WIDTH)],
        out_shape=[
            shape((tokens, WIDTH), f32),
            shape((tokens, WIDTH), bf16),
            shape((tokens, 3 * WIDTH), bf16),
            shape((tokens, WIDTH), bf16),
        ],
        scratch_shapes=[
            pltpu.VMEM((4, 8, 96, WIDTH), bf16),
            pltpu.SemaphoreType.DMA((4, PIECES)),
        ],
        compiler_params=params(),
        cost_estimate=cost(0.01),
        name="attn_forward",
    )(place, hidden, small, *pack[0])


def expand_forward(place, middle, small, expand_bias, pack, first):

    def kernel(place_ref, middle_ref, small_ref, bias_ref, *rest):
        packs = rest[:PIECES]
        normed_ref, active_ref, slope_ref, block, sems = rest[PIECES:]
        image = pl.program_id(0)
        copies = block_copies(place_ref[0], packs, pack[1], first, 384, block, sems)

        @pl.when(image == 0)
        def begin():
            run_all(copies, "start")

        unit, root = normalise(middle_ref[...])
        normed = (unit * small_ref[SM_G2 : SM_G2 + 1] + small_ref[SM_S2 : SM_S2 + 1]).astype(bf16)
        normed_ref[...] = normed

        @pl.when(image == 0)
        def arrive():
            run_all(copies, "wait")

        for part in range(FF_PARTS):
            weight = block[2 * part : 2 * part + 2].reshape(WIDTH, WIDTH)
            point = dot_nt(normed, weight) + bias_ref[part]
            square = point * point
            slant = jnp.tanh(0.7978845608028654 * point * (1.0 + 0.044715 * square))
            upper = 0.5 + 0.5 * slant
            columns = slice(WIDTH * part, WIDTH * (part + 1))
            active_ref[:, columns] = (point * upper).astype(bf16)
            bend = point * (0.7978845608028654 + (3 * 0.044715 * 0.7978845608028654) * square)
            slope_ref[:, columns] = (upper + 0.5 * bend * (1.0 - slant * slant)).astype(bf16)

    tokens = middle.shape[0]
    hidden_units = FF_PARTS * WIDTH
    shape = jax.ShapeDtypeStruct
    return pl.pallas_call(
        kernel,
        grid=(tokens // ROWS,),
        in_specs=[
            in_smem(),
            rows_spec(WIDTH),
            fixed(small.shape),
            fixed(expand_bias.shape),
        ]
        + [in_any()] * PIECES,
        out_specs=[rows_spec(WIDTH), rows_spec(hidden_units), rows_spec(hidden_units)],
        out_shape=[
            shape((tokens, WIDTH), bf16),
            shape((tokens, hidden_units), bf16),
            shape((tokens, hidden_units), bf16),
        ],
        scratch_shapes=[
            pltpu.VMEM((8, 384, WIDTH), bf16),
            pltpu.SemaphoreType.DMA((PIECES,)),
        ],
        compiler_params=params(),
        cost_estimate=cost(0.01),
        name="expand_forward",
    )(place, middle, small, expand_bias, *pack[0])


def reduce_copies(place_now, packs, regions, first, blocks, sems):
    return [
        block_copies(
            place_now, packs, regions, first + 96 * part, 96, blocks.at[part], sems.at[part]
        )
        for part in range(FF_PARTS)
    ]


def reduce_forward(place, live, middle, active, small, pack, first, last):

    def kernel(place_ref, live_ref, middle_ref, active_ref, small_ref, *rest):
        packs = rest[:PIECES]
        result_ref, blocks, sems = rest[PIECES:]
        image = pl.program_id(0)
        copies = reduce_copies(place_ref[0], packs, pack[1], first, blocks, sems)

        @pl.when(image == 0)
        def begin():
            for group in copies:
                run_all(group, "start")

        total = middle_ref[...] + small_ref[SM_RB : SM_RB + 1]
        for part in range(FF_PARTS):

            @pl.when(image == 0)
            def arrive():
                run_all(copies[part], "wait")

            total = total + dot_nt(
                active_ref[:, WIDTH * part : WIDTH * (part + 1)],
                blocks[part].reshape(WIDTH, WIDTH),
            )
        if last:
            total = total * live_ref[image, 0].astype(f32)
        result_ref[...] = total.astype(result_ref.dtype)

    tokens = middle.shape[0]
    return pl.pallas_call(
        kernel,
        grid=(tokens // ROWS,),
        in_specs=[
            in_smem(),
            in_smem(),
            rows_spec(WIDTH),
            rows_spec(FF_PARTS * WIDTH),
            fixed(small.shape),
        ]
        + [in_any()] * PIECES,
        out_specs=rows_spec(WIDTH),
        out_shape=jax.ShapeDtypeStruct((tokens, WIDTH), bf16 if last else f32),
        scratch_shapes=[
            pltpu.VMEM((FF_PARTS, 8, 96, WIDTH), bf16),
            pltpu.SemaphoreType.DMA((4, PIECES)),
        ],
        compiler_params=params(),
        cost_estimate=cost(0.01),
        name="reduce_forward",
    )(place, live, middle, active, small, *pack[0])


def split_owners(place_now, turned, mine_ref, theirs_ref, count, lead=()):
    core = place_now & 1
    chip = place_now >> 1
    for owner in range(4):
        mine_ref[lead + (owner ^ chip,)] = turned[2 * owner + core]
        theirs_ref[lead + (owner ^ chip,)] = turned[2 * owner + 1 - core]


def halves_spec(count):
    return pl.BlockSpec((4, count, ROWS), lambda image: (0, 0, image))


def start_grad(place, live, cotangent):
    def kernel(place_ref, live_ref, cot_ref, grad_ref, mine_ref, theirs_ref, turned):
        image = pl.program_id(0)
        grad = cot_ref[...].astype(f32) * live_ref[image, 0].astype(f32)
        grad_ref[...] = grad.astype(bf16)
        turned[...] = grad.T.astype(bf16).reshape(8, 96, ROWS)
        split_owners(place_ref[0], turned, mine_ref, theirs_ref, 96)

    tokens = cotangent.shape[0]
    shape = jax.ShapeDtypeStruct
    return pl.pallas_call(
        kernel,
        grid=(tokens // ROWS,),
        in_specs=[in_smem(), in_smem(), rows_spec(WIDTH)],
        out_specs=[rows_spec(WIDTH), halves_spec(96), halves_spec(96)],
        out_shape=[shape((tokens, WIDTH), bf16)] + [shape((4, 96, tokens), bf16)] * 2,
        scratch_shapes=[pltpu.VMEM((8, 96, ROWS), bf16)],
        compiler_params=params(),
        cost_estimate=cost(0.01),
        name="start_grad",
    )(place, live, cotangent)


def ff_backward(place, grad, slope, middle, small, pack):
    def kernel(place_ref, grad_ref, slope_ref, middle_ref, small_ref, *rest):
        packs = rest[:PIECES]
        (
            out_ref,
            pre_mine,
            pre_theirs,
            attn_mine,
            attn_theirs,
            sums_ref,
            expand_block,
            reduce_blocks,
            turned_pre,
            turned_attn,
            expand_sems,
            reduce_sems,
        ) = rest[PIECES:]
        place_now = place_ref[0]
        image = pl.program_id(0)
        copies = reduce_copies(place_now, packs, pack[1], 384, reduce_blocks, reduce_sems)
        expand_copies = block_copies(
            place_now, packs, pack[1], 0, 384, expand_block, expand_sems
        )

        @pl.when(image == 0)
        def begin():
            for group in copies:
                run_all(group, "start")
            run_all(expand_copies, "start")
            sums_ref[...] = jnp.zeros_like(sums_ref)

        grad_rows = grad_ref[...].astype(f32)
        low = grad_rows.astype(bf16)
        sums_ref[2:3] += jnp.sum(low.astype(f32), axis=0, keepdims=True)
        core = place_now & 1
        chip = place_now >> 1
        back = jnp.zeros((ROWS, WIDTH), f32)
        for part in range(FF_PARTS):

            @pl.when(image == 0)
            def arrive():
                run_all(copies[part], "wait")
                if part == 0:
                    run_all(expand_copies, "wait")

            columns = slice(WIDTH * part, WIDTH * (part + 1))
            up = dot_nn(low, reduce_blocks[part].reshape(WIDTH, WIDTH))
            pre = up * slope_ref[:, columns].astype(f32)
            pre_low = pre.astype(bf16)
            sums_ref[4 + part : 5 + part] += jnp.sum(
                pre_low.astype(f32), axis=0, keepdims=True
            )
            turned_pre[...] = pre_low.T.reshape(2, 384, ROWS)
            pre_mine[part ^ chip] = turned_pre[core]
            pre_theirs[part ^ chip] = turned_pre[1 - core]
            back = back + dot_nn(
                pre_low, expand_block[2 * part : 2 * part + 2].reshape(WIDTH, WIDTH)
            )
        unit, root = normalise(middle_ref[...])
        sums_ref[0:1] += jnp.sum(back * unit, axis=0, keepdims=True)
        sums_ref[1:2] += jnp.sum(back, axis=0, keepdims=True)
        scaled = back * small_ref[SM_G2 : SM_G2 + 1]
        result = grad_rows + root * (
            scaled
            - jnp.mean(scaled, axis=-1, keepdims=True)
            - unit * jnp.mean(scaled * unit, axis=-1, keepdims=True)
        )
        out_ref[...] = result
        result_low = result.astype(bf16)
        sums_ref[3:4] += jnp.sum(result_low.astype(f32), axis=0, keepdims=True)
        turned_attn[...] = result_low.T.reshape(8, 96, ROWS)
        split_owners(place_now, turned_attn, attn_mine, attn_theirs, 96)

    tokens = middle.shape[0]
    shape = jax.ShapeDtypeStruct
    return pl.pallas_call(
        kernel,
        grid=(tokens // ROWS,),
        in_specs=[
            in_smem(),
            rows_spec(WIDTH),
            rows_spec(FF_PARTS * WIDTH),
            rows_spec(WIDTH),
            fixed(small.shape),
        ]
        + [in_any()] * PIECES,
        out_specs=[
            rows_spec(WIDTH),
            halves_spec(384),
            halves_spec(384),
            halves_spec(96),
            halves_spec(96),
            fixed((8, WIDTH)),
        ],
        out_shape=[shape((tokens, WIDTH), f32)]
        + [shape((4, 384, tokens), bf16)] * 2
        + [shape((4, 96, tokens), bf16)] * 2
        + [shape((8, WIDTH), f32)],
        scratch_shapes=[
            pltpu.VMEM((8, 384, WIDTH), bf16),
            pltpu.VMEM((FF_PARTS, 8, 96, WIDTH), bf16),
            pltpu.VMEM((2, 384, ROWS), bf16),
            pltpu.VMEM((8, 96, ROWS), bf16),
            pltpu.SemaphoreType.DMA((PIECES,)),
            pltpu.SemaphoreType.DMA((4, PIECES)),
        ],
        compiler_params=params(),
        cost_estimate=cost(0.01),
        name="ff_backward",
    )(place, grad, slope, middle, small, *pack[0])


def attn_backward(place, grad, hidden, qkv, small, ff_sums, pack, last):
    def kernel(place_ref, grad_ref, hidden_ref, qkv_ref, small_ref, ff_sums_ref, *rest):
        packs = rest[:PIECES]
        if last:
            out_ref, qkv_mine, qkv_theirs, vec_mine, vec_theirs = rest[PIECES : PIECES + 5]
        else:
            (
                out_ref,
                qkv_mine,
                qkv_theirs,
                vec_mine,
                vec_theirs,
                low_mine,
                low_theirs,
            ) = rest[PIECES : PIECES + 7]
        blocks, turned, straight, sums_ref, sems = rest[-5:]
        place_now = place_ref[0]
        image = pl.program_id(0)
        copies = heads_copies(place_now, packs, pack[1], blocks, sems)

        @pl.when(image == 0)
        def begin():
            for member in (3, 0, 1, 2):
                run_all(copies[member], "start")
            sums_ref[...] = jnp.zeros_like(sums_ref)

        grad_rows = grad_ref[...]

        @pl.when(image == 0)
        def arrive():
            for member in (3, 0, 1, 2):
                run_all(copies[member], "wait")

        mixed_back = dot_nn(grad_rows.astype(bf16), blocks[3].reshape(WIDTH, WIDTH)).astype(bf16)
        lane = lax.broadcasted_iota(jnp.int32, (ROWS, 128), 1)
        line = lax.broadcasted_iota(jnp.int32, (128, ROWS), 0)
        for pair in range(HEADS // 2):
            q_pair = qkv_ref[:, 128 * pair : 128 * pair + 128]
            k_pair = qkv_ref[:, WIDTH + 128 * pair : WIDTH + 128 * pair + 128]
            v_pair = qkv_ref[:, 2 * WIDTH + 128 * pair : 2 * WIDTH + 128 * pair + 128]
            g_pair = mixed_back[:, 128 * pair : 128 * pair + 128]
            q_turned = q_pair.T
            k_turned = k_pair.T
            g_turned = g_pair.T
            made = []
            for half in range(2):
                here = (lane < 64) == (half == 0)
                k_one = jnp.where(here, k_pair, jnp.zeros_like(k_pair))
                v_one = jnp.where(here, v_pair, jnp.zeros_like(v_pair))
                scores = dot_nt(k_one, q_pair) * (HEAD_DIM**-0.5)
                peak = jnp.max(scores, axis=0, keepdims=True)
                powers = jnp.exp(scores - peak)
                attend = powers / jnp.sum(powers, axis=0, keepdims=True)
                back = dot_nt(v_one, g_pair)
                inner = jnp.sum(back * attend, axis=0, keepdims=True)
                scores_back = (attend * (back - inner)).astype(bf16)
                made.append(
                    (
                        dot_nn(k_turned, scores_back) * (HEAD_DIM**-0.5),
                        dot_nt(q_turned, scores_back) * (HEAD_DIM**-0.5),
                        dot_nt(g_turned, attend.astype(bf16)),
                    )
                )
            for member in range(3):
                both = jnp.where(line < 64, made[0][member], made[1][member]).astype(bf16)
                turned[member, pl.ds(128 * pair, 128)] = both
                straight[:, WIDTH * member + 128 * pair : WIDTH * member + 128 * pair + 128] = (
                    both.T
                )
        core = place_now & 1
        chip = place_now >> 1
        back = jnp.zeros((ROWS, WIDTH), f32)
        for member in range(3):
            for owner in range(4):
                for odd in range(2):
                    rows = turned[
                        member,
                        pl.ds(pl.multiple_of(192 * owner + 96 * (core ^ odd), 96), 96),
                    ]
                    target = qkv_theirs if odd else qkv_mine
                    target[member, owner ^ chip] = rows
            straight_one = straight[:, WIDTH * member : WIDTH * (member + 1)]
            back = back + dot_nn(straight_one, blocks[member].reshape(WIDTH, WIDTH))
            if member != 1:
                row = 0 if member == 0 else 1
                sums_ref[row : row + 1] += jnp.sum(
                    straight_one.astype(f32), axis=0, keepdims=True
                )
        unit, root = normalise(hidden_ref[...].astype(f32))
        sums_ref[3:4] += jnp.sum(back * unit, axis=0, keepdims=True)
        sums_ref[4:5] += jnp.sum(back, axis=0, keepdims=True)

        @pl.when(image == pl.num_programs(0) - 1)
        def vectors():
            sums_ref[2:3] = ff_sums_ref[3:4]
            sums_ref[5:8] = ff_sums_ref[0:3]
            row = lax.broadcasted_iota(jnp.int32, (WIDTH, 1024), 0)
            column = lax.broadcasted_iota(jnp.int32, (WIDTH, 1024), 1)
            at = column & 127
            wanted = 96 * ((column >> 7) ^ place_now) + at
            chosen = jnp.where((row == wanted) & (at < 96), 1.0, 0.0)
            cut = jnp.dot(
                sums_ref[...],
                chosen,
                preferred_element_type=f32,
                precision=lax.Precision.HIGHEST,
            )
            for delta in range(8):
                owner = place_now ^ delta
                target = vec_theirs if delta & 1 else vec_mine
                target[delta >> 1] = jnp.zeros((16, WIDTH // 2), f32)
                target[delta >> 1, 0:8, 0:128] = cut[:, 128 * delta : 128 * delta + 128]
                line = ff_sums_ref[pl.ds(4 + (owner >> 1), 1)]
                target[delta >> 1, 8:9] = jnp.where(
                    (owner & 1) == 0, line[:, : WIDTH // 2], line[:, WIDTH // 2 :]
                )

        scaled = back * small_ref[SM_G1 : SM_G1 + 1]
        result = grad_rows + root * (
            scaled
            - jnp.mean(scaled, axis=-1, keepdims=True)
            - unit * jnp.mean(scaled * unit, axis=-1, keepdims=True)
        )
        out_ref[...] = result.astype(out_ref.dtype)
        if not last:
            turned[0] = result.astype(bf16).T
            for owner in range(4):
                for odd in range(2):
                    rows = turned[
                        0, pl.ds(pl.multiple_of(192 * owner + 96 * (core ^ odd), 96), 96)
                    ]
                    target = low_theirs if odd else low_mine
                    target[owner ^ chip] = rows

    tokens = grad.shape[0]
    shape = jax.ShapeDtypeStruct
    heads_spec = pl.BlockSpec((3, 4, 96, ROWS), lambda image: (0, 0, 0, image))
    vector_shape = (4, 16, WIDTH // 2)
    out_specs = [rows_spec(WIDTH), heads_spec, heads_spec, fixed(vector_shape), fixed(vector_shape)]
    out_shape = (
        [shape((tokens, WIDTH), bf16 if last else f32)]
        + [shape((3, 4, 96, tokens), bf16)] * 2
        + [shape(vector_shape, f32)] * 2
    )
    if not last:
        out_specs += [halves_spec(96)] * 2
        out_shape += [shape((4, 96, tokens), bf16)] * 2
    return pl.pallas_call(
        kernel,
        grid=(tokens // ROWS,),
        in_specs=[
            in_smem(),
            rows_spec(WIDTH),
            rows_spec(WIDTH),
            rows_spec(3 * WIDTH),
            fixed(small.shape),
            fixed(ff_sums.shape),
        ]
        + [in_any()] * PIECES,
        out_specs=out_specs,
        out_shape=out_shape,
        scratch_shapes=[
            pltpu.VMEM((4, 8, 96, WIDTH), bf16),
            pltpu.VMEM((3, WIDTH, ROWS), bf16),
            pltpu.VMEM((ROWS, 3 * WIDTH), bf16),
            pltpu.VMEM((8, WIDTH), f32),
            pltpu.SemaphoreType.DMA((4, PIECES)),
        ],
        compiler_params=params(),
        cost_estimate=cost(0.01),
        name="attn_backward",
    )(place, grad, hidden, qkv, small, ff_sums, *pack[0])


def spread(result, owner, rows, out_refs):
    go_x, go_y, stay_x, stay_y = out_refs
    half = WIDTH // 2
    low, high = result[:, :half].astype(bf16), result[:, half:].astype(bf16)
    target, at = ((stay_x, 0), (go_x, 0), (stay_x, 1), (go_x, 1))[owner]
    target[at, rows] = low
    target, at = ((stay_y, 0), (stay_y, 1), (go_y, 0), (go_y, 1))[owner]
    target[at, rows] = high


def travel_shapes(rows_low, rows_high):
    shape = jax.ShapeDtypeStruct
    half = WIDTH // 2
    return [shape((2, rows, half), bf16) for rows in (rows_low, rows_high, rows_low, rows_high)]


def owner_terms(reduce=None, expand=None, merge=None, heads=None, small_terms=None):
    given, in_specs, sections = [], [], []
    rows = 0
    tokens = (reduce or expand or heads)[1][0].shape[0]
    whole = pl.BlockSpec((tokens, WIDTH), lambda at: (0, 0))
    four = pl.BlockSpec((4, 96, tokens), lambda at: (0, 0, 0))
    for name, pair, left, right, taken in (
        ("reduce", reduce, four, pl.BlockSpec((tokens, WIDTH), lambda at: (0, at)), 384),
        ("expand", expand, pl.BlockSpec((1, 384, tokens), lambda at: (at, 0, 0)), whole, 384),
        ("merge", merge, four, whole, 96),
        (
            "heads",
            heads,
            pl.BlockSpec((1, 4, 96, tokens), lambda at: (jnp.minimum(at, 2), 0, 0, 0)),
            whole,
            288,
        ),
    ):
        if pair is not None:
            given += [*pair[0], *pair[1]]
            in_specs += [left, left, right, right]
            sections.append((name, rows))
            rows += taken
    extra = 0
    if small_terms is not None:
        given += small_terms
        in_specs += [pl.BlockSpec(small_terms[0].shape, lambda at: (0, 0, 0))] * 2
        extra = 16

    def kernel(*refs):
        ins, out_refs = refs[: len(given)], refs[len(given) :]
        go_x, go_y, stay_x, stay_y = out_refs
        part = pl.program_id(0)

        def multiply(place, first):
            left_a, left_b, right_a, right_b = ins[4 * place : 4 * place + 4]
            result = dot_nn(left_a[...].reshape(384, tokens), right_a[...]) + dot_nn(
                left_b[...].reshape(384, tokens), right_b[...]
            )
            if first is None:
                return result
            for owner in range(4):
                spread(
                    result[96 * owner : 96 * owner + 96], owner, pl.ds(first, 96), out_refs
                )

        for place, (name, first) in enumerate(sections):
            if name == "reduce":
                multiply(place, pl.multiple_of(first + 96 * part, 96))
            elif name == "heads":

                @pl.when(part < 3)
                def one_head_block():
                    multiply(place, pl.multiple_of(first + 96 * part, 96))

            elif name == "merge":

                @pl.when(part == 3)
                def merge_block():
                    multiply(place, first)

            else:
                result = multiply(place, None)
                for owner in range(4):

                    @pl.when(part == owner)
                    def keep():
                        spread(result, owner, slice(first, first + 384), out_refs)

        if small_terms is not None:

            @pl.when(part == 3)
            def vectors():
                for owner in range(4):
                    target, at = ((stay_x, 0), (go_x, 0), (stay_x, 1), (go_x, 1))[owner]
                    target[at, rows : rows + 16] = (ins[-2][owner] + ins[-1][owner]).astype(bf16)

    half = WIDTH // 2
    heights = (rows + extra, rows, rows + extra, rows)
    return pl.pallas_call(
        kernel,
        grid=(4,),
        in_specs=in_specs,
        out_specs=[pl.BlockSpec((2, height, half), lambda at: (0, 0, 0)) for height in heights],
        out_shape=[jax.ShapeDtypeStruct((2, height, half), bf16) for height in heights],
        compiler_params=params(),
        cost_estimate=cost(0.01),
        name="owner_terms",
    )(*given)


def shards(
    images,
    cotangent,
    slot_flags,
    heads_weight,
    heads_bias,
    merge_weight,
    merge_bias,
    first_gain,
    first_shift,
    second_gain,
    second_shift,
    expand_weight,
    expand_bias,
    reduce_weight,
    reduce_bias,
):
    micro_count, unused_slots, seq_len, width = images.shape
    layers = heads_weight.shape[0]
    tokens = micro_count * seq_len
    place_at = lax.axis_index("fsdp").astype(jnp.int32)
    place = place_at[None]

    matrices = (heads_weight, merge_weight, expand_weight, reduce_weight)
    vectors = (
        heads_bias,
        merge_bias,
        first_gain,
        first_shift,
        second_gain,
        second_shift,
        reduce_bias,
        expand_bias,
    )
    kinds = [(kind, layer) for layer in range(layers) for kind in ("attn", "ff")]
    rows_of = [400 if kind == "attn" else 768 for kind, layer in kinds]
    cut_of = [192 if kind == "attn" else 384 for kind, layer in kinds]
    x_rows = [0] + cut_of
    y_rows = [0] + [rows - cut for rows, cut in zip(rows_of, cut_of)]
    count = len(kinds)

    def send_round(at, own_now, x_before, y_before):
        if at == 0:
            return swap_x(own_now), swap_y(own_now)
        rows, cut = rows_of[at - 1], cut_of[at - 1]
        to_x = [(y_before, y_rows[at - 1], cut)]
        to_y = [(x_before, x_rows[at - 1] + cut, rows - cut)]
        if at < count:
            to_x.append((own_now, 0, rows_of[at]))
            to_y.append((own_now, 0, rows_of[at]))
        to_x, to_y = join_rows([to_x, to_y])
        return swap_x(to_x), swap_y(to_y)

    def pack_of(at, own_pair, came):
        (x_0, y_0, cx_0, cy_0), (x_1, y_1, cx_1, cy_1) = came[at], came[at + 1]
        return (
            (own_pair[0], x_0, y_0, x_1, y_1, own_pair[1], cx_0, cy_0, cx_1, cy_1),
            regions_of(rows_of[at], cut_of[at], x_rows[at], y_rows[at]),
        )

    def both(values):
        return tuple(swap_core(value) for value in values)

    hidden = images.reshape(tokens, width)
    seal = lax.optimization_barrier

    came = []
    own = own_packs(kinds[:1], matrices, vectors)
    new = send_round(0, own[0], None, None)
    own += own_packs(kinds[1:], matrices, vectors)
    own_other = both(own)
    grad, low_mine, low_theirs = start_grad(place, slot_flags, cotangent.reshape(tokens, width))
    own, own_other, new, grad, low_mine, low_theirs = seal(
        (own, own_other, new, grad, low_mine, low_theirs)
    )

    got, new = new, send_round(1, own[1], *new)
    came.append(got + both(got))
    low = (low_mine, swap_core(low_theirs))
    own, own_other, came, new, low, grad = seal((own, own_other, came, new, low, grad))

    got, new = new, send_round(2, own[2], *new)
    came.append(got + both(got))
    pack_a0 = pack_of(0, (own[0], own_other[0]), came)
    small_0, expand_rows_0 = gathered_vectors(place, pack_a0)
    middle_0, normed_0, qkv_0, mixed_0 = attn_forward(place, hidden, small_0, pack_a0)
    own, came, new, small_0, expand_rows_0, middle_0, normed_0, qkv_0, mixed_0 = seal(
        (own, came, new, small_0, expand_rows_0, middle_0, normed_0, qkv_0, mixed_0)
    )

    got, new = new, send_round(3, own[3], *new)
    came.append(got + both(got))
    pack_f0 = pack_of(1, (own[1], own_other[1]), came)
    second_0, active_0, slope_0 = expand_forward(
        place, middle_0, small_0, expand_rows_0, pack_f0, 0
    )
    hidden_1 = reduce_forward(
        place, slot_flags, middle_0, active_0, small_0, pack_f0, 384, False
    )
    others_a0 = both((normed_0, mixed_0))
    own, came, new, second_0, active_0, slope_0, hidden_1, others_a0 = seal(
        (own, came, new, second_0, active_0, slope_0, hidden_1, others_a0)
    )

    got, new = new, send_round(4, None, *new)
    came.append(got + both(got))
    pack_a1 = pack_of(2, (own[2], own_other[2]), came)
    small_1, expand_rows_1 = gathered_vectors(place, pack_a1)
    middle_1, normed_1, qkv_1, mixed_1 = attn_forward(place, hidden_1, small_1, pack_a1)
    second_other_0 = swap_core(second_0)
    came, new, small_1, expand_rows_1, middle_1, normed_1, qkv_1, mixed_1, second_other_0 = seal(
        (came, new, small_1, expand_rows_1, middle_1, normed_1, qkv_1, mixed_1, second_other_0)
    )

    came.append(new + both(new))
    pack_f1 = pack_of(3, (own[3], own_other[3]), came)
    second_1, active_1, slope_1 = expand_forward(
        place, middle_1, small_1, expand_rows_1, pack_f1, 0
    )
    others_a1 = both((normed_1, mixed_1))
    active_other_0 = swap_core(active_0)
    second_1, active_1, slope_1, others_a1, active_other_0, came = seal(
        (second_1, active_1, slope_1, others_a1, active_other_0, came)
    )
    pack_f1 = pack_of(3, (own[3], own_other[3]), came)

    grad, pre_mine, pre_theirs, attn_mine, attn_theirs, ff_sums = ff_backward(
        place, grad, slope_1, middle_1, small_1, pack_f1
    )
    others_f1 = both((second_1, active_1))
    grad, pre_mine, pre_theirs, attn_mine, attn_theirs, ff_sums, others_f1 = seal(
        (grad, pre_mine, pre_theirs, attn_mine, attn_theirs, ff_sums, others_f1)
    )

    travel_r1 = owner_terms(reduce=(low, (active_1, others_f1[1])))
    pre_other, attn_other = both((pre_theirs, attn_theirs))
    travel_r1, pre_other, attn_other, grad = seal((travel_r1, pre_other, attn_other, grad))

    state_r1 = first_steps(travel_r1)
    travel_em1 = owner_terms(
        expand=((pre_mine, pre_other), (second_1, others_f1[0])),
        merge=((attn_mine, attn_other), (mixed_1, others_a1[1])),
    )
    state_r1, travel_em1, grad = seal((state_r1, travel_em1, grad))

    state_r1 = second_steps(state_r1)
    state_em1 = first_steps(travel_em1)
    grad, qkv_mine, qkv_theirs, vec_mine, vec_theirs, low_mine, low_theirs = attn_backward(
        place, grad, hidden_1, qkv_1, small_1, ff_sums, pack_a1, False
    )
    made = (grad, qkv_mine, qkv_theirs, vec_mine, vec_theirs, low_mine, low_theirs)
    state_r1, state_em1, made = seal((state_r1, state_em1, made))
    grad, qkv_mine, qkv_theirs, vec_mine, vec_theirs, low_mine, low_theirs = made

    sum_r1 = to_middle(ends(state_r1))
    state_em1 = second_steps(state_em1)
    low_other, qkv_other, vec_other = both((low_theirs, qkv_theirs, vec_theirs))
    travel_hr = owner_terms(
        reduce=((low_mine, low_other), (active_0, active_other_0)),
        heads=((qkv_mine, qkv_other), (normed_1, others_a1[0])),
        small_terms=(vec_mine, vec_other),
    )
    sum_r1, state_em1, travel_hr, grad = seal((sum_r1, state_em1, travel_hr, grad))

    state_hr = first_steps(travel_hr)
    sum_em1 = to_middle(ends(state_em1))
    sum_r1 = across_middle(sum_r1)
    grad, pre_mine, pre_theirs, attn_mine, attn_theirs, ff_sums = ff_backward(
        place, grad, slope_0, middle_0, small_0, pack_f0
    )
    made = (grad, pre_mine, pre_theirs, attn_mine, attn_theirs, ff_sums)
    state_hr, sum_em1, sum_r1, made = seal((state_hr, sum_em1, sum_r1, made))
    grad, pre_mine, pre_theirs, attn_mine, attn_theirs, ff_sums = made

    state_hr = second_steps(state_hr)
    sum_em1 = across_middle(sum_em1)
    pre_other, attn_other = both((pre_theirs, attn_theirs))
    travel_em0 = owner_terms(
        expand=((pre_mine, pre_other), (second_0, second_other_0)),
        merge=((attn_mine, attn_other), (mixed_0, others_a0[1])),
    )
    state_hr, sum_em1, travel_em0, grad = seal((state_hr, sum_em1, travel_em0, grad))

    state_em0 = first_steps(travel_em0)
    sum_hr = to_middle(ends(state_hr))
    final_r1, final_em1 = to_ends(sum_r1), to_ends(sum_em1)
    images_grad, qkv_mine, qkv_theirs, vec_mine, vec_theirs = attn_backward(
        place, grad, hidden, qkv_0, small_0, ff_sums, pack_a0, True
    )
    made = (images_grad, qkv_mine, qkv_theirs, vec_mine, vec_theirs)
    state_em0, sum_hr, final_r1, final_em1, made = seal(
        (state_em0, sum_hr, final_r1, final_em1, made)
    )
    images_grad, qkv_mine, qkv_theirs, vec_mine, vec_theirs = made

    state_em0 = second_steps(state_em0)
    sum_hr = across_middle(sum_hr)
    qkv_other, vec_other = both((qkv_theirs, vec_theirs))
    travel_h0 = owner_terms(
        heads=((qkv_mine, qkv_other), (normed_0, others_a0[0])), small_terms=(vec_mine, vec_other)
    )
    state_em0, sum_hr, travel_h0 = seal((state_em0, sum_hr, travel_h0))

    state_h0 = first_steps(travel_h0)
    sum_em0 = to_middle(ends(state_em0))
    final_hr = to_ends(sum_hr)
    middle_last, active_last, travel_h0 = seal((middle_1, active_1, travel_h0))
    outputs = reduce_forward(
        place, slot_flags, middle_last, active_last, small_1, pack_f1, 384, True
    ).reshape(images.shape)
    state_h0, outputs = seal((state_h0, outputs))

    state_h0 = second_steps(state_h0)
    sum_em0 = across_middle(sum_em0)
    state_h0 = seal(state_h0)
    sum_h0 = to_middle(ends(state_h0))
    sum_h0, sum_em0 = seal((sum_h0, sum_em0))
    sum_h0 = across_middle(sum_h0)
    final_em0 = to_ends(sum_em0)
    final_h0 = to_ends(sum_h0)
    rep_at = lax.axis_index("rep")
    at_end = (rep_at == 0) | (rep_at == lax.axis_size("rep") - 1)
    final_r1, final_em1, final_hr, final_em0, final_h0 = (
        jnp.where(at_end, outward, total)
        for total, outward in (final_r1, final_em1, final_hr, final_em0, final_h0)
    )
    images_grad = images_grad.reshape(images.shape)

    grad_scale = (
        micro_count * images.shape[1] * lax.axis_size("fsdp") * lax.axis_size("rep") * seq_len
    ) ** (-0.5)

    def halves(low_half, high_half):
        return jnp.concatenate([low_half, high_half], axis=1).astype(f32) * grad_scale

    def as_reduce(rows):
        return rows.reshape(4, 96, width).transpose(1, 0, 2).reshape(96, 4 * width)

    def layer_grads(reduce_sum, em_sum, heads_sum, vectors):
        vectors = vectors.astype(f32) * grad_scale
        short = vectors[:, :96]
        return (
            heads_sum.reshape(3, 96, width),
            short[SM_HB0 : SM_HB1 + 1],
            em_sum[384:480],
            short[SM_MB],
            short[SM_G1],
            short[SM_S1],
            short[SM_G2],
            short[SM_S2],
            em_sum[:384],
            vectors[8],
            as_reduce(reduce_sum),
            short[SM_RB],
        )

    hr_low, hr_high = final_hr[:688], final_hr[688:]
    hr_sum = halves(hr_low[:672], hr_high)
    h0_low, h0_high = final_h0[:304], final_h0[304:]
    finals = [
        layer_grads(
            hr_sum[:384],
            halves(final_em0[:480], final_em0[480:]),
            halves(h0_low[:288], h0_high),
            h0_low[288:],
        ),
        layer_grads(
            halves(final_r1[:384], final_r1[384:]),
            halves(final_em1[:480], final_em1[480:]),
            hr_sum[384:],
            hr_low[672:],
        ),
    ]
    stacked = tuple(jnp.stack(member) for member in zip(*finals))
    return (outputs, images_grad) + stacked


def solution(mesh):
    body = shards if (mesh.shape["fsdp"], mesh.shape["rep"]) == (8, 4) else plain_shards
    placed = (
        P(None, ("fsdp", "rep"), None, None),
        P(None, ("fsdp", "rep"), None, None),
        P(None, ("fsdp", "rep")),
        P(None, None, "fsdp", None),
        P(None, None, "fsdp"),
        P(None, "fsdp", None),
        P(None, "fsdp"),
        P(None, "fsdp"),
        P(None, "fsdp"),
        P(None, "fsdp"),
        P(None, "fsdp"),
        P(None, "fsdp", None),
        P(None, "fsdp"),
        P(None, "fsdp", None),
        P(None, "fsdp"),
    )
    return jax.shard_map(
        body,
        mesh=mesh,
        in_specs=placed,
        out_specs=(
            P(None, ("fsdp", "rep"), None, None),
            P(None, ("fsdp", "rep"), None, None),
            P(None, None, "fsdp", None),
            P(None, None, "fsdp"),
            P(None, "fsdp", None),
            P(None, "fsdp"),
            P(None, "fsdp"),
            P(None, "fsdp"),
            P(None, "fsdp"),
            P(None, "fsdp"),
            P(None, "fsdp", None),
            P(None, "fsdp"),
            P(None, "fsdp", None),
            P(None, "fsdp"),
        ),
        check_vma=False,
    )
```

```python
import jax
import jax.numpy as jnp
from jax import lax
from jax.experimental import pallas as pl
from jax.experimental.pallas import tpu as pltpu
from jax.sharding import PartitionSpec as P

HEADS = 12
HEAD_DIM = 64


norm_eps = 1e-06


def layer_norm(token_rows, scale_row, offset_row):
    centre = token_rows - jnp.mean(token_rows, axis=-1, keepdims=True)
    spread = jnp.mean(centre * centre, axis=-1, keepdims=True)
    return centre * lax.rsqrt(spread + norm_eps) * scale_row + offset_row


def project(token_rows, weight):
    return lax.dot_general(
        token_rows, weight, (((1,), (1,)), ((), ())), preferred_element_type=jnp.float32
    )


def outer_sum(grad_rows, token_rows):
    return lax.dot_general(
        grad_rows, token_rows, (((0,), (0,)), ((), ())), preferred_element_type=jnp.float32
    )


def carry_back(grad_rows, weight):
    return jnp.dot(grad_rows, weight, preferred_element_type=jnp.float32)


def forward_layer(hidden, params):
    (
        heads_weight,
        heads_bias,
        merge_weight,
        merge_bias,
        first_gain,
        first_shift,
        second_gain,
        second_shift,
        expand_weight,
        expand_bias,
        reduce_weight,
        reduce_bias,
    ) = params
    seq_len, model_width = hidden.shape
    shaped = (seq_len, HEADS, HEAD_DIM)
    score_scale = HEAD_DIM ** (-0.5)
    normed = layer_norm(
        hidden, first_gain.astype(jnp.float32), first_shift.astype(jnp.float32)
    ).astype(jnp.bfloat16)
    queries = (project(normed, heads_weight[0]) + heads_bias[0].astype(jnp.float32)).astype(
        jnp.bfloat16
    )
    key_rows = project(normed, heads_weight[1]).astype(jnp.bfloat16)
    values = (project(normed, heads_weight[2]) + heads_bias[1].astype(jnp.float32)).astype(
        jnp.bfloat16
    )
    scores = (
        jnp.einsum(
            "qhd,khd->hqk",
            queries.reshape(shaped),
            key_rows.reshape(shaped),
            preferred_element_type=jnp.float32,
        )
        * score_scale
    )
    row_peak = jnp.max(scores, axis=-1, keepdims=True)
    exponent = jnp.exp(scores - row_peak)
    row_total = jnp.sum(exponent, axis=-1, keepdims=True)
    attend = exponent / row_total
    log_total = row_peak + jnp.log(row_total)
    mixed_rows = jnp.einsum(
        "hqk,khd->qhd",
        attend.astype(jnp.bfloat16),
        values.reshape(shaped),
        preferred_element_type=jnp.float32,
    )
    mixed_rows = mixed_rows.reshape(seq_len, model_width).astype(jnp.bfloat16)
    middle = hidden + (project(mixed_rows, merge_weight) + merge_bias.astype(jnp.float32))
    second = layer_norm(
        middle, second_gain.astype(jnp.float32), second_shift.astype(jnp.float32)
    ).astype(jnp.bfloat16)
    pre_act = project(second, expand_weight) + expand_bias.astype(jnp.float32)
    activated = jax.nn.gelu(pre_act, approximate=True).astype(jnp.bfloat16)
    result = middle + (project(activated, reduce_weight) + reduce_bias.astype(jnp.float32))
    saved = (
        hidden,
        normed,
        queries,
        key_rows,
        values,
        log_total,
        mixed_rows,
        middle,
        second,
        pre_act,
        activated,
    )
    return (result, saved)


def backward_layer(grad_out, params, saved):
    (
        heads_weight,
        heads_bias,
        merge_weight,
        merge_bias,
        first_gain,
        first_shift,
        second_gain,
        second_shift,
        expand_weight,
        expand_bias,
        reduce_weight,
        reduce_bias,
    ) = params
    (
        hidden,
        normed,
        queries,
        key_rows,
        values,
        log_total,
        mixed_rows,
        middle,
        second,
        pre_act,
        activated,
    ) = saved
    seq_len, model_width = hidden.shape
    shaped = (seq_len, HEADS, HEAD_DIM)
    score_scale = HEAD_DIM ** (-0.5)
    branch_low = grad_out.astype(jnp.bfloat16)
    reduce_weight_term = outer_sum(branch_low, activated)
    reduce_bias_term = jnp.sum(branch_low.astype(jnp.float32), axis=0)
    grad_act = carry_back(branch_low, reduce_weight)
    unused_value, gelu_back = jax.vjp(lambda point: jax.nn.gelu(point, approximate=True), pre_act)
    grad_pre = gelu_back(grad_act)[0].astype(jnp.bfloat16)
    expand_weight_term = outer_sum(grad_pre, second)
    expand_bias_term = jnp.sum(grad_pre.astype(jnp.float32), axis=0)
    grad_second = carry_back(grad_pre, expand_weight)
    unused_norm, second_back = jax.vjp(
        layer_norm, middle, second_gain.astype(jnp.float32), second_shift.astype(jnp.float32)
    )
    middle_part, second_gain_term, second_shift_term = second_back(grad_second)
    grad_middle = grad_out + middle_part
    attn_low = grad_middle.astype(jnp.bfloat16)
    merge_weight_term = outer_sum(attn_low, mixed_rows)
    merge_bias_term = jnp.sum(attn_low.astype(jnp.float32), axis=0)
    grad_mixed = carry_back(attn_low, merge_weight).astype(jnp.bfloat16).reshape(shaped)
    queries_heads = queries.reshape(shaped)
    keys_heads = key_rows.reshape(shaped)
    values_heads = values.reshape(shaped)
    scores = (
        jnp.einsum("qhd,khd->hqk", queries_heads, keys_heads, preferred_element_type=jnp.float32)
        * score_scale
    )
    attend = jnp.exp(scores - log_total)
    grad_values = jnp.einsum(
        "hqk,qhd->khd", attend.astype(jnp.bfloat16), grad_mixed, preferred_element_type=jnp.float32
    ).astype(jnp.bfloat16)
    grad_attend = jnp.einsum(
        "qhd,khd->hqk", grad_mixed, values_heads, preferred_element_type=jnp.float32
    )
    grad_scores = attend * (grad_attend - jnp.sum(grad_attend * attend, axis=-1, keepdims=True))
    grad_scores = grad_scores.astype(jnp.bfloat16)
    grad_queries = (
        jnp.einsum("hqk,khd->qhd", grad_scores, keys_heads, preferred_element_type=jnp.float32)
        * score_scale
    ).astype(jnp.bfloat16)
    grad_keys = (
        jnp.einsum("hqk,qhd->khd", grad_scores, queries_heads, preferred_element_type=jnp.float32)
        * score_scale
    ).astype(jnp.bfloat16)
    stacked_grads = jnp.stack(
        [
            grad_queries.reshape(seq_len, model_width),
            grad_keys.reshape(seq_len, model_width),
            grad_values.reshape(seq_len, model_width),
        ]
    )
    heads_weight_term = jnp.einsum(
        "jto,ti->joi", stacked_grads, normed, preferred_element_type=jnp.float32
    )
    grad_normed = jnp.einsum(
        "jto,joi->ti", stacked_grads, heads_weight, preferred_element_type=jnp.float32
    )
    heads_bias_term = jnp.stack(
        [
            jnp.sum(stacked_grads[0].astype(jnp.float32), axis=0),
            jnp.sum(stacked_grads[2].astype(jnp.float32), axis=0),
        ]
    )
    unused_first, first_back = jax.vjp(
        layer_norm, hidden, first_gain.astype(jnp.float32), first_shift.astype(jnp.float32)
    )
    hidden_part, first_gain_term, first_shift_term = first_back(grad_normed)
    grad_hidden = grad_middle + hidden_part
    terms = (
        heads_weight_term,
        heads_bias_term,
        merge_weight_term,
        merge_bias_term,
        first_gain_term,
        first_shift_term,
        second_gain_term,
        second_shift_term,
        expand_weight_term,
        expand_bias_term,
        reduce_weight_term,
        reduce_bias_term,
    )
    return (grad_hidden, terms)


def plain_shards(
    images,
    cotangent,
    slot_flags,
    heads_weight,
    heads_bias,
    merge_weight,
    merge_bias,
    first_gain,
    first_shift,
    second_gain,
    second_shift,
    expand_weight,
    expand_bias,
    reduce_weight,
    reduce_bias,
):
    micro_count = images.shape[0]
    seq_len = images.shape[2]
    layers = heads_weight.shape[0]
    live_flags = slot_flags.astype(jnp.float32)
    states = [images[batch_at, 0].astype(jnp.float32) for batch_at in range(micro_count)]
    saved_all = []
    for layer_at in range(layers):
        saved_row = []
        for batch_at in range(micro_count):
            params = (
                lax.all_gather(heads_weight[layer_at], "fsdp", axis=1, tiled=True),
                lax.all_gather(heads_bias[layer_at], "fsdp", axis=1, tiled=True),
                lax.all_gather(merge_weight[layer_at], "fsdp", axis=0, tiled=True),
                lax.all_gather(merge_bias[layer_at], "fsdp", axis=0, tiled=True),
                lax.all_gather(first_gain[layer_at], "fsdp", axis=0, tiled=True),
                lax.all_gather(first_shift[layer_at], "fsdp", axis=0, tiled=True),
                lax.all_gather(second_gain[layer_at], "fsdp", axis=0, tiled=True),
                lax.all_gather(second_shift[layer_at], "fsdp", axis=0, tiled=True),
                lax.all_gather(expand_weight[layer_at], "fsdp", axis=0, tiled=True),
                lax.all_gather(expand_bias[layer_at], "fsdp", axis=0, tiled=True),
                lax.all_gather(reduce_weight[layer_at], "fsdp", axis=0, tiled=True),
                lax.all_gather(reduce_bias[layer_at], "fsdp", axis=0, tiled=True),
            )
            states[batch_at], saved = forward_layer(states[batch_at], params)
            saved_row.append(saved)
        saved_all.append(saved_row)
    outputs = jnp.stack(
        [live_flags[batch_at, 0] * states[batch_at] for batch_at in range(micro_count)]
    )[:, None].astype(jnp.bfloat16)
    grads_back = [
        cotangent[batch_at, 0].astype(jnp.float32) * live_flags[batch_at, 0]
        for batch_at in range(micro_count)
    ]
    collected = [None] * layers
    for layer_at in reversed(range(layers)):
        totals = None
        for batch_at in range(micro_count):
            params = (
                lax.all_gather(heads_weight[layer_at], "fsdp", axis=1, tiled=True),
                lax.all_gather(heads_bias[layer_at], "fsdp", axis=1, tiled=True),
                lax.all_gather(merge_weight[layer_at], "fsdp", axis=0, tiled=True),
                lax.all_gather(merge_bias[layer_at], "fsdp", axis=0, tiled=True),
                lax.all_gather(first_gain[layer_at], "fsdp", axis=0, tiled=True),
                lax.all_gather(first_shift[layer_at], "fsdp", axis=0, tiled=True),
                lax.all_gather(second_gain[layer_at], "fsdp", axis=0, tiled=True),
                lax.all_gather(second_shift[layer_at], "fsdp", axis=0, tiled=True),
                lax.all_gather(expand_weight[layer_at], "fsdp", axis=0, tiled=True),
                lax.all_gather(expand_bias[layer_at], "fsdp", axis=0, tiled=True),
                lax.all_gather(reduce_weight[layer_at], "fsdp", axis=0, tiled=True),
                lax.all_gather(reduce_bias[layer_at], "fsdp", axis=0, tiled=True),
            )
            grads_back[batch_at], terms = backward_layer(
                grads_back[batch_at], params, saved_all[layer_at][batch_at]
            )
            if totals is None:
                totals = terms
            else:
                totals = tuple((earlier + current for earlier, current in zip(totals, terms)))
        collected[layer_at] = totals
    images_grad = jnp.stack(grads_back)[:, None].astype(jnp.bfloat16)
    stacked = [
        jnp.stack([collected[layer_at][member] for layer_at in range(layers)])
        for member in range(12)
    ]
    shares = (
        lax.psum_scatter(
            stacked[0].astype(jnp.bfloat16), "fsdp", scatter_dimension=2, tiled=True
        ).astype(jnp.float32),
        lax.psum_scatter(
            stacked[1].astype(jnp.bfloat16), "fsdp", scatter_dimension=2, tiled=True
        ).astype(jnp.float32),
        lax.psum_scatter(
            stacked[2].astype(jnp.bfloat16), "fsdp", scatter_dimension=1, tiled=True
        ).astype(jnp.float32),
        lax.psum_scatter(
            stacked[3].astype(jnp.bfloat16), "fsdp", scatter_dimension=1, tiled=True
        ).astype(jnp.float32),
        lax.psum_scatter(
            stacked[4].astype(jnp.bfloat16), "fsdp", scatter_dimension=1, tiled=True
        ).astype(jnp.float32),
        lax.psum_scatter(
            stacked[5].astype(jnp.bfloat16), "fsdp", scatter_dimension=1, tiled=True
        ).astype(jnp.float32),
        lax.psum_scatter(
            stacked[6].astype(jnp.bfloat16), "fsdp", scatter_dimension=1, tiled=True
        ).astype(jnp.float32),
        lax.psum_scatter(
            stacked[7].astype(jnp.bfloat16), "fsdp", scatter_dimension=1, tiled=True
        ).astype(jnp.float32),
        lax.psum_scatter(
            stacked[8].astype(jnp.bfloat16), "fsdp", scatter_dimension=1, tiled=True
        ).astype(jnp.float32),
        lax.psum_scatter(
            stacked[9].astype(jnp.bfloat16), "fsdp", scatter_dimension=1, tiled=True
        ).astype(jnp.float32),
        lax.psum_scatter(
            stacked[10].astype(jnp.bfloat16), "fsdp", scatter_dimension=1, tiled=True
        ).astype(jnp.float32),
        lax.psum_scatter(
            stacked[11].astype(jnp.bfloat16), "fsdp", scatter_dimension=1, tiled=True
        ).astype(jnp.float32),
    )
    reduced = (
        lax.psum(shares[0].astype(jnp.bfloat16), "rep").astype(jnp.float32),
        lax.psum(shares[1].astype(jnp.bfloat16), "rep").astype(jnp.float32),
        lax.psum(shares[2].astype(jnp.bfloat16), "rep").astype(jnp.float32),
        lax.psum(shares[3].astype(jnp.bfloat16), "rep").astype(jnp.float32),
        lax.psum(shares[4].astype(jnp.bfloat16), "rep").astype(jnp.float32),
        lax.psum(shares[5].astype(jnp.bfloat16), "rep").astype(jnp.float32),
        lax.psum(shares[6].astype(jnp.bfloat16), "rep").astype(jnp.float32),
        lax.psum(shares[7].astype(jnp.bfloat16), "rep").astype(jnp.float32),
        lax.psum(shares[8].astype(jnp.bfloat16), "rep").astype(jnp.float32),
        lax.psum(shares[9].astype(jnp.bfloat16), "rep").astype(jnp.float32),
        lax.psum(shares[10].astype(jnp.bfloat16), "rep").astype(jnp.float32),
        lax.psum(shares[11].astype(jnp.bfloat16), "rep").astype(jnp.float32),
    )
    grad_scale = (micro_count * lax.axis_size("fsdp") * lax.axis_size("rep") * seq_len) ** (-0.5)
    finals = tuple((member_sum * grad_scale for member_sum in reduced))
    return (outputs, images_grad) + finals


ROWS = 256
WIDTH = 768
FF_PARTS = 4
f32 = jnp.float32
bf16 = jnp.bfloat16
VMEM_BYTES = 58 * 1024 * 1024
SMALL_VMEM_BYTES = 24 * 1024 * 1024
LARGE_VMEM_BYTES = 60 * 1024 * 1024


def dot_nt(left, right):
    return lax.dot_general(left, right, (((1,), (1,)), ((), ())), preferred_element_type=f32)


def dot_nn(left, right):
    return lax.dot_general(left, right, (((1,), (0,)), ((), ())), preferred_element_type=f32)


def swap_core(value):
    return lax.ppermute(value, "fsdp", [(at, at ^ 1) for at in range(8)])


def swap_x(value):
    return lax.ppermute(value, "fsdp", [(at, at ^ 2) for at in range(8)])


def swap_y(value):
    return lax.ppermute(value, "fsdp", [(at, at ^ 4) for at in range(8)])


PIECES = 10


def regions_of(rows, cut, x_row, y_row):
    return [
        region
        for odd in range(2)
        for region in (
            (5 * odd, odd, 0, rows, 0),
            (5 * odd + 1, 2 ^ odd, 0, rows, x_row),
            (5 * odd + 2, 4 ^ odd, 0, rows, y_row),
            (5 * odd + 3, 6 ^ odd, 0, cut, 0),
            (5 * odd + 4, 6 ^ odd, cut, rows, 0),
        )
    ]


def block_copies(place, refs, regions, first, count, block, sems):
    copies = []
    for array_at, delta, low, high, start in regions:
        begin, end = max(low, first), min(high, first + count)
        if begin < end:
            copies.append(
                pltpu.make_async_copy(
                    refs[array_at].at[pl.ds(start + begin - low, end - begin)],
                    block.at[place ^ delta, pl.ds(begin - first, end - begin)],
                    sems.at[len(copies)],
                )
            )
    return copies


def run_all(copies, what):
    for copy in copies:
        getattr(copy, what)()


def in_any():
    return pl.BlockSpec(memory_space=pltpu.HBM)


def in_smem():
    return pl.BlockSpec(memory_space=pltpu.SMEM)


def params(steps=1):
    return pltpu.CompilerParams(
        dimension_semantics=("arbitrary",) * steps, vmem_limit_bytes=VMEM_BYTES
    )


def cost(micros):
    return pl.CostEstimate(flops=int(micros * 1.1e9), bytes_accessed=1 << 10, transcendentals=0)


def rows_spec(width):
    return pl.BlockSpec((ROWS, width), lambda image: (image, 0))


def part_spec(tokens):
    return pl.BlockSpec((tokens, WIDTH), lambda part: (0, part))


def fixed(shape):
    return pl.BlockSpec(shape, lambda image: (0,) * len(shape))


def normalise(rows):
    centre = rows - jnp.mean(rows, axis=-1, keepdims=True)
    root = lax.rsqrt(jnp.mean(centre * centre, axis=-1, keepdims=True) + norm_eps)
    return centre * root, root


PACK_ROWS = {"attn": 400, "ff": 768, "expand": 384, "reduce": 384}
PACK_CUTS = {"attn": 192, "ff": 384, "expand": 192, "reduce": 192}


def own_packs(wanted, matrices, vectors):
    count = len(wanted)
    needed = [
        at
        for at, users in enumerate(
            (("attn",), ("attn",), ("ff", "expand"), ("ff", "reduce"))
        )
        if any(kind in users for kind, layer in wanted)
    ]

    def kernel(*refs):
        heads_ref, merge_ref, expand_ref, reduce_ref = (
            refs[needed.index(at)] if at in needed else None for at in range(4)
        )
        vector_refs = refs[len(needed) : len(needed) + 8]
        outs, rows = refs[len(needed) + 8 : -1], refs[-1]
        for out, (kind, layer) in zip(outs, wanted):
            if kind == "attn":
                for at in range(3):
                    out[96 * at : 96 * at + 96] = heads_ref[layer, at]
                out[288:384] = merge_ref[layer]
                rows[...] = jnp.zeros_like(rows)
                rows[0:2, 0:96] = vector_refs[0][layer].astype(f32)
                for row in range(2, 8):
                    values = vector_refs[row - 1][...].astype(f32)
                    rows[row : row + 1, 0:96] = values[layer : layer + 1]
                rows[8:9, 0:384] = vector_refs[7][...].astype(f32)[layer : layer + 1]
                out[384:400] = rows[...].astype(bf16)
            if kind in ("ff", "expand"):
                out[0:384] = expand_ref[layer]
            if kind in ("ff", "reduce"):
                first = 384 if kind == "ff" else 0
                for part in range(FF_PARTS):
                    out[first + 96 * part : first + 96 * part + 96] = reduce_ref[
                        layer, :, WIDTH * part : WIDTH * (part + 1)
                    ]

    in_vmem = pl.BlockSpec(memory_space=pltpu.VMEM)
    return pl.pallas_call(
        kernel,
        in_specs=[in_vmem] * (len(needed) + 8),
        out_specs=[in_vmem] * count,
        out_shape=[
            jax.ShapeDtypeStruct((PACK_ROWS[kind], WIDTH), bf16) for kind, layer in wanted
        ],
        scratch_shapes=[pltpu.VMEM((16, WIDTH), f32)],
        compiler_params=pltpu.CompilerParams(vmem_limit_bytes=LARGE_VMEM_BYTES),
        cost_estimate=cost(0.01),
        name="own_packs",
    )(*[matrices[at] for at in needed], *vectors)


def join_rows(pieces_of):
    flat = [piece for pieces in pieces_of for piece in pieces]
    heights = [sum(rows for unused, unused_first, rows in pieces) for pieces in pieces_of]

    def kernel(*refs):
        ins, outs, sems = refs[: len(flat)], refs[len(flat) : -1], refs[-1]
        copies = []
        for out, pieces in zip(outs, pieces_of):
            into = 0
            for unused, first, rows in pieces:
                at = len(copies)
                copies.append(
                    pltpu.make_async_copy(
                        ins[at].at[pl.ds(first, rows)], out.at[pl.ds(into, rows)], sems.at[at]
                    )
                )
                into += rows
        run_all(copies, "start")
        run_all(copies, "wait")

    return pl.pallas_call(
        kernel,
        in_specs=[in_any()] * len(flat),
        out_specs=[pl.BlockSpec(memory_space=pltpu.VMEM)] * len(heights),
        out_shape=[jax.ShapeDtypeStruct((rows, WIDTH), bf16) for rows in heights],
        scratch_shapes=[pltpu.SemaphoreType.DMA((len(flat),))],
        compiler_params=pltpu.CompilerParams(vmem_limit_bytes=SMALL_VMEM_BYTES),
        cost_estimate=cost(0.01),
        name="join_rows",
    )(*[array for array, unused, unused_rows in flat])


def gathered_vectors(place, pack):
    arrays, regions = pack
    used = {}
    for array_at, delta, low, high, start in regions:
        if low <= 384 and 400 <= high:
            used[delta] = (arrays[array_at], start + 384 - low)
    deltas = sorted(used)

    def kernel(place_ref, *refs):
        ins, small_ref, expand_ref, rows, sems = refs[:8], refs[8], refs[9], refs[10], refs[11]
        copies = [
            pltpu.make_async_copy(
                ins[at].at[pl.ds(used[delta][1], 16)], rows.at[at], sems.at[at]
            )
            for at, delta in enumerate(deltas)
        ]
        run_all(copies, "start")
        here = place_ref[0]
        row = lax.broadcasted_iota(jnp.int32, (1024, WIDTH), 0)
        column = lax.broadcasted_iota(jnp.int32, (1024, WIDTH), 1)
        at = row & 127
        wanted = 96 * ((row >> 7) ^ here) + at
        chosen = jnp.where((column == wanted) & (at < 96), 1.0, 0.0).astype(bf16)
        run_all(copies, "wait")
        flat = jnp.concatenate([rows[at, 0:8, 0:128].astype(f32) for at in range(8)], axis=1)
        small_ref[...] = dot_nn(flat.astype(bf16), chosen)
        for at, delta in enumerate(deltas):
            owner = here ^ delta
            line = rows[at].astype(f32)[8:9, 0:384]

            @pl.when((owner & 1) == 0)
            def left():
                expand_ref[owner >> 1, :, 0:384] = line

            @pl.when((owner & 1) == 1)
            def right():
                expand_ref[owner >> 1, :, 384:768] = line

    shape = jax.ShapeDtypeStruct
    return pl.pallas_call(
        kernel,
        in_specs=[in_smem()] + [in_any()] * 8,
        out_specs=[pl.BlockSpec(memory_space=pltpu.VMEM)] * 2,
        out_shape=[shape((8, WIDTH), f32), shape((4, 1, WIDTH), f32)],
        scratch_shapes=[pltpu.VMEM((8, 16, WIDTH), bf16), pltpu.SemaphoreType.DMA((8,))],
        compiler_params=pltpu.CompilerParams(vmem_limit_bytes=LARGE_VMEM_BYTES),
        cost_estimate=cost(0.01),
        name="gathered_vectors",
    )(place, *[used[delta][0] for delta in deltas])


def elementwise(name, body, ins, out_shapes):
    def kernel(*refs):
        body(refs[: len(ins)], refs[len(ins) :])

    return pl.pallas_call(
        kernel,
        in_specs=[pl.BlockSpec(memory_space=pltpu.VMEM)] * len(ins),
        out_specs=[pl.BlockSpec(memory_space=pltpu.VMEM)] * len(out_shapes),
        out_shape=[jax.ShapeDtypeStruct(shape, bf16) for shape in out_shapes],
        compiler_params=pltpu.CompilerParams(vmem_limit_bytes=SMALL_VMEM_BYTES),
        cost_estimate=cost(0.01),
        name=name,
    )(*ins)


def add_low(*parts):
    total = parts[0].astype(f32)
    for part in parts[1:]:
        total = total + part.astype(f32)
    return total.astype(bf16)


def first_steps(travel):
    go_x, go_y, stay_x, stay_y = travel
    return swap_x(go_x), swap_y(go_y), stay_x, stay_y


def second_steps(state):
    def body(ins, outs):
        from_x, from_y, stay_x, stay_y = ins
        outs[0][...] = add_low(stay_x[1], from_x[1])
        outs[1][...] = add_low(stay_y[1], from_y[1])
        outs[2][...] = add_low(stay_x[0], from_x[0])
        outs[3][...] = add_low(stay_y[0], from_y[0])

    low, high = state[0].shape[1:], state[1].shape[1:]
    low_on, high_on, kept_low, kept_high = elementwise(
        "second_steps", body, state, [low, high, low, high]
    )
    return swap_y(low_on), swap_x(high_on), kept_low, kept_high


def ends(state):
    from_y, from_x, kept_low, kept_high = state
    low, high = kept_low.shape[0], kept_high.shape[0]

    def body(ins, outs):
        outs[0][0:low] = add_low(ins[2][...], ins[0][...])
        outs[0][low : low + high] = add_low(ins[3][...], ins[1][...])

    return elementwise("ends", body, state, [(low + high, WIDTH // 2)])[0]


def to_middle(part):
    return part, lax.ppermute(part, "rep", [(0, 1), (3, 2)])


def plus(parts):
    def body(ins, outs):
        outs[0][...] = add_low(ins[0][...], ins[1][...])

    return elementwise("plus", body, parts, [parts[0].shape])[0]


def across_middle(parts):
    inward = plus(parts)
    return inward, lax.ppermute(inward, "rep", [(1, 2), (2, 1)])


def to_ends(parts):
    total = plus(parts)
    return total, lax.ppermute(total, "rep", [(1, 0), (2, 3)])


SM_HB0, SM_HB1, SM_MB, SM_G1, SM_S1, SM_G2, SM_S2, SM_RB = range(8)


def unit_copies(place, refs, regions, first, blocks, sems):
    copies = []
    count = 96 * blocks.shape[0]
    for array_at, delta, low, high, start in regions:
        begin, end = max(low, first), min(high, first + count)
        if begin < end:
            units = (end - begin) // 96
            source = refs[array_at].at[pl.ds(start + begin - low, end - begin)]
            copies.append(
                pltpu.make_async_copy(
                    source.reshape(units, 96, WIDTH),
                    blocks.at[pl.ds((begin - first) // 96, units), place ^ delta],
                    sems.at[len(copies)],
                )
            )
    return copies


def attn_forward(place, hidden, small, pack):

    def kernel(place_ref, hidden_ref, small_ref, *rest):
        packs = rest[:PIECES]
        middle_ref, normed_ref, qkv_ref, mixed_ref, blocks, sems = rest[PIECES:]
        place_now = place_ref[0]
        image = pl.program_id(0)
        copies = unit_copies(place_now, packs, pack[1], 0, blocks, sems)

        @pl.when(image == 0)
        def begin():
            run_all(copies, "start")

        rows = hidden_ref[...].astype(f32)
        unit, root = normalise(rows)
        normed = (unit * small_ref[SM_G1 : SM_G1 + 1] + small_ref[SM_S1 : SM_S1 + 1]).astype(bf16)
        normed_ref[...] = normed

        @pl.when(image == 0)
        def arrive():
            run_all(copies, "wait")

        for member, bias in ((0, SM_HB0), (1, None), (2, SM_HB1)):
            block = blocks[member].reshape(WIDTH, WIDTH)
            made = dot_nt(normed, block)
            if bias is not None:
                made = made + small_ref[bias : bias + 1]
            qkv_ref[:, WIDTH * member : WIDTH * (member + 1)] = made.astype(bf16)
        lane = lax.broadcasted_iota(jnp.int32, (ROWS, 128), 1)
        for pair in range(HEADS // 2):
            q_pair = qkv_ref[:, 128 * pair : 128 * pair + 128] * HEAD_DIM**-0.5
            k_pair = qkv_ref[:, WIDTH + 128 * pair : WIDTH + 128 * pair + 128]
            v_pair = qkv_ref[:, 2 * WIDTH + 128 * pair : 2 * WIDTH + 128 * pair + 128]
            parts = []
            for half in range(2):
                here = (lane < 64) == (half == 0)
                scores = dot_nt(jnp.where(here, q_pair, jnp.zeros_like(q_pair)), k_pair)
                peak = jnp.max(scores, axis=-1, keepdims=True)
                powers = jnp.exp(scores - peak).astype(bf16)
                parts.append(dot_nn(powers, jnp.where(here, v_pair, jnp.ones_like(v_pair))))
            totals = pltpu.roll(jnp.where(lane < 64, parts[1], parts[0]), 64, 1)
            mixed_ref[:, 128 * pair : 128 * pair + 128] = (
                jnp.where(lane < 64, parts[0], parts[1]) / totals
            ).astype(bf16)
        merged = dot_nt(mixed_ref[...], blocks[3].reshape(WIDTH, WIDTH))
        middle_ref[...] = rows + (merged + small_ref[SM_MB : SM_MB + 1])

    tokens = hidden.shape[0]
    shape = jax.ShapeDtypeStruct
    return pl.pallas_call(
        kernel,
        grid=(tokens // ROWS,),
        in_specs=[in_smem(), rows_spec(WIDTH), fixed(small.shape)] + [in_any()] * PIECES,
        out_specs=[rows_spec(WIDTH), rows_spec(WIDTH), rows_spec(3 * WIDTH), rows_spec(WIDTH)],
        out_shape=[
            shape((tokens, WIDTH), f32),
            shape((tokens, WIDTH), bf16),
            shape((tokens, 3 * WIDTH), bf16),
            shape((tokens, WIDTH), bf16),
        ],
        scratch_shapes=[
            pltpu.VMEM((4, 8, 96, WIDTH), bf16),
            pltpu.SemaphoreType.DMA((PIECES,)),
        ],
        compiler_params=params(),
        cost_estimate=cost(0.01),
        name="attn_forward",
    )(place, hidden, small, *pack[0])


def expand_forward(place, middle, small, expand_bias, pack, first):
    tokens = middle.shape[0]

    def kernel(place_ref, middle_ref, small_ref, bias_ref, *rest):
        packs = rest[:PIECES]
        normed_ref, active_ref, slope_ref, block, sems = rest[PIECES:]
        part = pl.program_id(0)
        copies = block_copies(place_ref[0], packs, pack[1], first, 384, block, sems)

        @pl.when(part == 0)
        def begin():
            run_all(copies, "start")
            unit, root = normalise(middle_ref[...])
            normed_ref[...] = (
                unit * small_ref[SM_G2 : SM_G2 + 1] + small_ref[SM_S2 : SM_S2 + 1]
            ).astype(bf16)
            run_all(copies, "wait")

        weight = block[pl.ds(2 * part, 2)].reshape(WIDTH, WIDTH)
        point = dot_nt(normed_ref[...], weight) + bias_ref[part]
        square = point * point
        slant = jnp.tanh(0.7978845608028654 * point * (1.0 + 0.044715 * square))
        upper = 0.5 + 0.5 * slant
        active_ref[...] = (point * upper).astype(bf16)
        bend = point * (0.7978845608028654 + (3 * 0.044715 * 0.7978845608028654) * square)
        slope_ref[...] = (upper + 0.5 * bend * (1.0 - slant * slant)).astype(bf16)

    hidden_units = FF_PARTS * WIDTH
    shape = jax.ShapeDtypeStruct
    return pl.pallas_call(
        kernel,
        grid=(FF_PARTS,),
        in_specs=[
            in_smem(),
            fixed(middle.shape),
            fixed(small.shape),
            fixed(expand_bias.shape),
        ]
        + [in_any()] * PIECES,
        out_specs=[fixed(middle.shape), part_spec(tokens), part_spec(tokens)],
        out_shape=[
            shape((tokens, WIDTH), bf16),
            shape((tokens, hidden_units), bf16),
            shape((tokens, hidden_units), bf16),
        ],
        scratch_shapes=[
            pltpu.VMEM((8, 384, WIDTH), bf16),
            pltpu.SemaphoreType.DMA((PIECES,)),
        ],
        compiler_params=params(),
        cost_estimate=cost(0.01),
        name="expand_forward",
    )(place, middle, small, expand_bias, *pack[0])


def reduce_copies(place_now, packs, regions, first, blocks, sems):
    return [
        block_copies(
            place_now, packs, regions, first + 96 * part, 96, blocks.at[part], sems.at[part]
        )
        for part in range(FF_PARTS)
    ]


def for_part(part, groups, what):
    for at, group in enumerate(groups):

        @pl.when(part == at)
        def run():
            run_all(group, what)


def reduce_forward(place, live, middle, active, small, pack, first, last):
    tokens = middle.shape[0]

    def kernel(place_ref, live_ref, middle_ref, active_ref, small_ref, *rest):
        packs = rest[:PIECES]
        result_ref, total, blocks, sems = rest[PIECES:]
        part = pl.program_id(0)
        copies = reduce_copies(place_ref[0], packs, pack[1], first, blocks, sems)

        @pl.when(part == 0)
        def begin():
            for group in copies:
                run_all(group, "start")
            total[...] = middle_ref[...] + small_ref[SM_RB : SM_RB + 1]

        for_part(part, copies, "wait")
        total[...] += dot_nt(active_ref[...], blocks[part].reshape(WIDTH, WIDTH))

        @pl.when(part == FF_PARTS - 1)
        def end():
            if last:
                for image in range(tokens // ROWS):
                    rows = slice(ROWS * image, ROWS * (image + 1))
                    result_ref[rows] = (
                        total[rows] * live_ref[image, 0].astype(f32)
                    ).astype(result_ref.dtype)
            else:
                result_ref[...] = total[...].astype(result_ref.dtype)

    return pl.pallas_call(
        kernel,
        grid=(FF_PARTS,),
        in_specs=[
            in_smem(),
            in_smem(),
            fixed(middle.shape),
            part_spec(tokens),
            fixed(small.shape),
        ]
        + [in_any()] * PIECES,
        out_specs=fixed(middle.shape),
        out_shape=jax.ShapeDtypeStruct((tokens, WIDTH), bf16 if last else f32),
        scratch_shapes=[
            pltpu.VMEM((tokens, WIDTH), f32),
            pltpu.VMEM((FF_PARTS, 8, 96, WIDTH), bf16),
            pltpu.SemaphoreType.DMA((FF_PARTS, PIECES)),
        ],
        compiler_params=params(),
        cost_estimate=cost(0.01),
        name="reduce_forward",
    )(place, live, middle, active, small, *pack[0])


def split_owners(place_now, turned, mine_ref, theirs_ref, count, lead=()):
    core = place_now & 1
    chip = place_now >> 1
    for owner in range(4):
        mine_ref[lead + (owner ^ chip,)] = turned[2 * owner + core]
        theirs_ref[lead + (owner ^ chip,)] = turned[2 * owner + 1 - core]


def halves_spec(count):
    return pl.BlockSpec((4, count, ROWS), lambda image: (0, 0, image))


def start_grad(place, live, cotangent):
    def kernel(place_ref, live_ref, cot_ref, grad_ref, mine_ref, theirs_ref, turned):
        image = pl.program_id(0)
        grad = cot_ref[...].astype(f32) * live_ref[image, 0].astype(f32)
        grad_ref[...] = grad.astype(bf16)
        turned[...] = grad.T.astype(bf16).reshape(8, 96, ROWS)
        split_owners(place_ref[0], turned, mine_ref, theirs_ref, 96)

    tokens = cotangent.shape[0]
    shape = jax.ShapeDtypeStruct
    return pl.pallas_call(
        kernel,
        grid=(tokens // ROWS,),
        in_specs=[in_smem(), in_smem(), rows_spec(WIDTH)],
        out_specs=[rows_spec(WIDTH), halves_spec(96), halves_spec(96)],
        out_shape=[shape((tokens, WIDTH), bf16)] + [shape((4, 96, tokens), bf16)] * 2,
        scratch_shapes=[pltpu.VMEM((8, 96, ROWS), bf16)],
        compiler_params=params(),
        cost_estimate=cost(0.01),
        name="start_grad",
    )(place, live, cotangent)


def fetch(source, target, sem):
    return pltpu.make_async_copy(source, target, sem)


def ff_backward(place, grad, slope, middle, small, expand_pack, reduce_pack):
    tokens = middle.shape[0]
    (expand_arrays, expand_regions), expand_first = expand_pack
    (reduce_arrays, reduce_regions), reduce_first = reduce_pack

    def kernel(place_ref, grad_in, slope_in, middle_in, small_ref, *rest):
        expand_packs, reduce_packs = rest[:PIECES], rest[PIECES : 2 * PIECES]
        (
            out_ref,
            pre_mine,
            pre_theirs,
            attn_mine,
            attn_theirs,
            sums_ref,
            grad_ref,
            slope_ref,
            middle_ref,
            expand_block,
            reduce_blocks,
            turned_pre,
            turned_attn,
            pre_low,
            expand_sems,
            reduce_sems,
            in_sems,
            out_sems,
        ) = rest[2 * PIECES :]
        place_now = place_ref[0]
        core = place_now & 1
        chip = place_now >> 1
        copies = reduce_copies(
            place_now, reduce_packs, reduce_regions, reduce_first, reduce_blocks, reduce_sems
        )
        expand_copies = block_copies(
            place_now, expand_packs, expand_regions, expand_first, 384, expand_block, expand_sems
        )
        grad_copy = fetch(grad_in, grad_ref, in_sems.at[0])
        middle_copy = fetch(middle_in, middle_ref, in_sems.at[1])
        slope_copies = [
            fetch(
                slope_in.at[:, pl.ds(WIDTH * part, WIDTH)], slope_ref.at[part], in_sems.at[2 + part]
            )
            for part in range(FF_PARTS)
        ]
        grad_copy.start()
        for part in range(FF_PARTS):
            run_all(copies[part], "start")
            slope_copies[part].start()
        run_all(expand_copies, "start")
        middle_copy.start()

        sent = []

        def send(source, target):
            copy = pltpu.make_async_copy(source, target, out_sems.at[len(sent)])
            copy.start()
            sent.append(copy)

        grad_copy.wait()
        low = grad_ref[...].astype(bf16)
        sums_ref[2:3] = jnp.sum(low.astype(f32), axis=0, keepdims=True)
        for part in range(FF_PARTS):
            run_all(copies[part], "wait")
            slope_copies[part].wait()
            up = dot_nn(low, reduce_blocks[part].reshape(WIDTH, WIDTH))
            pre = (up * slope_ref[part].astype(f32)).astype(bf16)
            pre_low[part] = pre
            sums_ref[4 + part : 5 + part] = jnp.sum(pre.astype(f32), axis=0, keepdims=True)
            turned_pre[2 * part : 2 * part + 2] = pre.T.reshape(2, 384, tokens)
            send(turned_pre.at[2 * part + core], pre_mine.at[part ^ chip])
            send(turned_pre.at[2 * part + 1 - core], pre_theirs.at[part ^ chip])
        run_all(expand_copies, "wait")
        back = dot_nn(pre_low[0], expand_block[0:2].reshape(WIDTH, WIDTH))
        for part in range(1, FF_PARTS):
            back = back + dot_nn(
                pre_low[part], expand_block[2 * part : 2 * part + 2].reshape(WIDTH, WIDTH)
            )
        middle_copy.wait()
        unit, root = normalise(middle_ref[...])
        sums_ref[0:1] = jnp.sum(back * unit, axis=0, keepdims=True)
        sums_ref[1:2] = jnp.sum(back, axis=0, keepdims=True)
        scaled = back * small_ref[SM_G2 : SM_G2 + 1]
        result = grad_ref[...].astype(f32) + root * (
            scaled
            - jnp.mean(scaled, axis=-1, keepdims=True)
            - unit * jnp.mean(scaled * unit, axis=-1, keepdims=True)
        )
        out_ref[...] = result
        result_low = result.astype(bf16)
        sums_ref[3:4] = jnp.sum(result_low.astype(f32), axis=0, keepdims=True)
        turned_attn[...] = result_low.T.reshape(8, 96, tokens)
        for owner in range(4):
            send(turned_attn.at[2 * owner + core], attn_mine.at[owner ^ chip])
            send(turned_attn.at[2 * owner + 1 - core], attn_theirs.at[owner ^ chip])
        run_all(sent, "wait")

    shape = jax.ShapeDtypeStruct
    in_vmem = pl.BlockSpec(memory_space=pltpu.VMEM)
    return pl.pallas_call(
        kernel,
        in_specs=[in_smem()] + [in_any()] * 3 + [in_vmem] + [in_any()] * (2 * PIECES),
        out_specs=[in_vmem] + [in_any()] * 4 + [in_vmem],
        out_shape=[shape((tokens, WIDTH), f32)]
        + [shape((4, 384, tokens), bf16)] * 2
        + [shape((4, 96, tokens), bf16)] * 2
        + [shape((8, WIDTH), f32)],
        scratch_shapes=[
            pltpu.VMEM((tokens, WIDTH), grad.dtype),
            pltpu.VMEM((FF_PARTS, tokens, WIDTH), bf16),
            pltpu.VMEM((tokens, WIDTH), f32),
            pltpu.VMEM((8, 384, WIDTH), bf16),
            pltpu.VMEM((FF_PARTS, 8, 96, WIDTH), bf16),
            pltpu.VMEM((8, 384, tokens), bf16),
            pltpu.VMEM((8, 96, tokens), bf16),
            pltpu.VMEM((FF_PARTS, tokens, WIDTH), bf16),
            pltpu.SemaphoreType.DMA((PIECES,)),
            pltpu.SemaphoreType.DMA((FF_PARTS, PIECES)),
            pltpu.SemaphoreType.DMA((2 + FF_PARTS,)),
            pltpu.SemaphoreType.DMA((16,)),
        ],
        compiler_params=pltpu.CompilerParams(vmem_limit_bytes=VMEM_BYTES),
        cost_estimate=cost(0.01),
        name="ff_backward",
    )(place, grad, slope, middle, small, *expand_arrays, *reduce_arrays)


def attn_backward(place, grad, hidden, qkv, mixed, small, ff_sums, pack, last):
    tokens = grad.shape[0]

    def kernel(place_ref, grad_in, hidden_in, qkv_in, mixed_in, small_ref, ff_sums_ref, *rest):
        packs = rest[:PIECES]
        out_ref, qkv_mine, qkv_theirs, vec_mine, vec_theirs = rest[PIECES : PIECES + 5]
        if not last:
            low_mine, low_theirs = rest[PIECES + 5 : PIECES + 7]
        (
            grad_ref,
            hidden_ref,
            qkv_ref,
            mixed_ref,
            blocks,
            turned,
            sums_ref,
            sems,
            in_sems,
            out_sems,
        ) = rest[-10:]
        place_now = place_ref[0]
        core = place_now & 1
        chip = place_now >> 1
        copies = unit_copies(place_now, packs, pack[1], 0, blocks, sems)
        fetches = [
            fetch(source, target, in_sems.at[at])
            for at, (source, target) in enumerate(
                (
                    (grad_in, grad_ref),
                    (mixed_in, mixed_ref),
                    (qkv_in, qkv_ref),
                    (hidden_in, hidden_ref),
                )
            )
        ]
        fetches[0].start()
        run_all(copies, "start")
        run_all(fetches[1:], "start")
        sent = []

        def send(source, target):
            copy = pltpu.make_async_copy(source, target, out_sems.at[len(sent)])
            copy.start()
            sent.append(copy)

        fetches[0].wait()
        run_all(copies, "wait")
        grad_rows = grad_ref[...]
        mixed_back = dot_nn(grad_rows.astype(bf16), blocks[3].reshape(WIDTH, WIDTH)).astype(bf16)
        fetches[1].wait()
        product = mixed_back.astype(f32) * mixed_ref[...].astype(f32)
        product_high = product.astype(bf16)
        product_low = (product - product_high.astype(f32)).astype(bf16)
        head_row = lax.broadcasted_iota(jnp.int32, (16, WIDTH), 0)
        head_column = lax.broadcasted_iota(jnp.int32, (16, WIDTH), 1) >> 6
        of_head = jnp.where(head_row == head_column, 1.0, 0.0).astype(bf16)
        inner = dot_nt(of_head, product_high) + dot_nt(of_head, product_low)
        fetches[2].wait()
        lane = lax.broadcasted_iota(jnp.int32, (ROWS, 128), 1)
        line = lax.broadcasted_iota(jnp.int32, (128, ROWS), 0)
        scale = HEAD_DIM**-0.5
        for image in range(tokens // ROWS):
            rows = slice(ROWS * image, ROWS * (image + 1))
            for pair in range(HEADS // 2):
                q_pair = qkv_ref[rows, 128 * pair : 128 * pair + 128]
                k_pair = qkv_ref[rows, WIDTH + 128 * pair : WIDTH + 128 * pair + 128]
                v_pair = qkv_ref[rows, 2 * WIDTH + 128 * pair : 2 * WIDTH + 128 * pair + 128]
                g_pair = mixed_back[rows, 128 * pair : 128 * pair + 128]
                k_turned = k_pair.T
                weights, powers, inverses = [], [], []
                for half in range(2):
                    here = (lane < 64) == (half == 0)
                    k_one = jnp.where(here, k_pair * scale, jnp.zeros_like(k_pair))
                    v_one = jnp.where(here, v_pair, jnp.zeros_like(v_pair))
                    scores = dot_nt(k_one, q_pair)
                    power = jnp.exp(scores - jnp.max(scores, axis=0, keepdims=True))
                    inverses.append(1.0 / jnp.sum(power, axis=0, keepdims=True))
                    head = 2 * pair + half
                    back = dot_nt(v_one, g_pair) - inner[head : head + 1, rows]
                    weights.append((power * back).astype(bf16))
                    powers.append(power.astype(bf16))
                inverse = jnp.where(line < 64, inverses[0], inverses[1])
                q_turned = (q_pair.T.astype(f32) * (inverse * scale)).astype(bf16)
                g_turned = (g_pair.T.astype(f32) * inverse).astype(bf16)
                made = (
                    jnp.where(
                        line < 64, dot_nn(k_turned, weights[0]), dot_nn(k_turned, weights[1])
                    )
                    * (inverse * scale),
                    jnp.where(
                        line < 64, dot_nt(q_turned, weights[0]), dot_nt(q_turned, weights[1])
                    ),
                    jnp.where(
                        line < 64, dot_nt(g_turned, powers[0]), dot_nt(g_turned, powers[1])
                    ),
                )
                for member in range(3):
                    turned[member, 128 * pair : 128 * pair + 128, rows] = made[member].astype(bf16)
        for member in range(3):
            for owner in range(4):
                for odd in range(2):
                    target = qkv_theirs if odd else qkv_mine
                    first = pl.multiple_of(192 * owner + 96 * (core ^ odd), 96)
                    send(turned.at[member, pl.ds(first, 96)], target.at[member, owner ^ chip])
        back = jnp.zeros((tokens, WIDTH), f32)
        ones = jnp.ones((8, tokens), bf16)
        for member in range(3):
            back = back + lax.dot_general(
                turned[member],
                blocks[member].reshape(WIDTH, WIDTH),
                (((0,), (0,)), ((), ())),
                preferred_element_type=f32,
            )
        sums_ref[0:1] = dot_nt(ones, turned[0])[0:1]
        sums_ref[1:2] = dot_nt(ones, turned[2])[0:1]
        fetches[3].wait()
        unit, root = normalise(hidden_ref[...].astype(f32))
        sums_ref[3:4] = jnp.sum(back * unit, axis=0, keepdims=True)
        sums_ref[4:5] = jnp.sum(back, axis=0, keepdims=True)
        scaled = back * small_ref[SM_G1 : SM_G1 + 1]
        result = grad_ref[...] + root * (
            scaled
            - jnp.mean(scaled, axis=-1, keepdims=True)
            - unit * jnp.mean(scaled * unit, axis=-1, keepdims=True)
        )
        out_ref[...] = result.astype(out_ref.dtype)
        run_all(sent, "wait")
        sent.clear()
        if not last:
            turned[0] = result.astype(bf16).T
            for owner in range(4):
                for odd in range(2):
                    target = low_theirs if odd else low_mine
                    first = pl.multiple_of(192 * owner + 96 * (core ^ odd), 96)
                    send(turned.at[0, pl.ds(first, 96)], target.at[owner ^ chip])

        sums_ref[2:3] = ff_sums_ref[3:4]
        sums_ref[5:8] = ff_sums_ref[0:3]
        row = lax.broadcasted_iota(jnp.int32, (WIDTH, 1024), 0)
        column = lax.broadcasted_iota(jnp.int32, (WIDTH, 1024), 1)
        at = column & 127
        wanted = 96 * ((column >> 7) ^ place_now) + at
        chosen = jnp.where((row == wanted) & (at < 96), 1.0, 0.0).astype(bf16)
        rest_of = sums_ref[...]
        cut = jnp.zeros((8, 1024), f32)
        for term in range(3):
            term_low = rest_of.astype(bf16)
            rest_of = rest_of - term_low.astype(f32)
            cut = cut + dot_nn(term_low, chosen)
        for delta in range(8):
            owner = place_now ^ delta
            target = vec_theirs if delta & 1 else vec_mine
            target[delta >> 1] = jnp.zeros((16, WIDTH // 2), f32)
            target[delta >> 1, 0:8, 0:128] = cut[:, 128 * delta : 128 * delta + 128]
            values = ff_sums_ref[pl.ds(4 + (owner >> 1), 1)]
            target[delta >> 1, 8:9] = jnp.where(
                (owner & 1) == 0, values[:, : WIDTH // 2], values[:, WIDTH // 2 :]
            )
        run_all(sent, "wait")

    shape = jax.ShapeDtypeStruct
    in_vmem = pl.BlockSpec(memory_space=pltpu.VMEM)
    vector_shape = (4, 16, WIDTH // 2)
    out_specs = [in_vmem] + [in_any()] * 2 + [in_vmem] * 2
    out_shape = (
        [shape((tokens, WIDTH), bf16 if last else f32)]
        + [shape((3, 4, 96, tokens), bf16)] * 2
        + [shape(vector_shape, f32)] * 2
    )
    if not last:
        out_specs += [in_any()] * 2
        out_shape += [shape((4, 96, tokens), bf16)] * 2
    return pl.pallas_call(
        kernel,
        in_specs=[in_smem()] + [in_any()] * 4 + [in_vmem] * 2 + [in_any()] * PIECES,
        out_specs=out_specs,
        out_shape=out_shape,
        scratch_shapes=[
            pltpu.VMEM((tokens, WIDTH), grad.dtype),
            pltpu.VMEM((tokens, WIDTH), hidden.dtype),
            pltpu.VMEM((tokens, 3 * WIDTH), bf16),
            pltpu.VMEM((tokens, WIDTH), bf16),
            pltpu.VMEM((4, 8, 96, WIDTH), bf16),
            pltpu.VMEM((3, WIDTH, tokens), bf16),
            pltpu.VMEM((8, WIDTH), f32),
            pltpu.SemaphoreType.DMA((PIECES,)),
            pltpu.SemaphoreType.DMA((4,)),
            pltpu.SemaphoreType.DMA((24,)),
        ],
        compiler_params=pltpu.CompilerParams(vmem_limit_bytes=VMEM_BYTES),
        cost_estimate=cost(0.01),
        name="attn_backward",
    )(place, grad, hidden, qkv, mixed, small, ff_sums, *pack[0])


def spread(result, owner, rows, out_refs):
    go_x, go_y, stay_x, stay_y = out_refs
    half = WIDTH // 2
    low, high = result[:, :half].astype(bf16), result[:, half:].astype(bf16)
    target, at = ((stay_x, 0), (go_x, 0), (stay_x, 1), (go_x, 1))[owner]
    target[at, rows] = low
    target, at = ((stay_y, 0), (stay_y, 1), (go_y, 0), (go_y, 1))[owner]
    target[at, rows] = high


def travel_shapes(rows_low, rows_high):
    shape = jax.ShapeDtypeStruct
    half = WIDTH // 2
    return [shape((2, rows, half), bf16) for rows in (rows_low, rows_high, rows_low, rows_high)]


def owner_terms(reduce=None, expand=None, merge=None, heads=None, small_terms=None):
    given, in_specs, sections = [], [], []
    rows = 0
    tokens = (reduce or expand or heads)[1][0].shape[0]
    whole = pl.BlockSpec((tokens, WIDTH), lambda at: (0, 0))
    four = pl.BlockSpec((4, 96, tokens), lambda at: (0, 0, 0))
    for name, pair, left, right, taken in (
        ("reduce", reduce, four, pl.BlockSpec((tokens, WIDTH), lambda at: (0, at)), 384),
        ("expand", expand, pl.BlockSpec((1, 384, tokens), lambda at: (at, 0, 0)), whole, 384),
        ("merge", merge, four, whole, 96),
        (
            "heads",
            heads,
            pl.BlockSpec((1, 4, 96, tokens), lambda at: (jnp.minimum(at, 2), 0, 0, 0)),
            whole,
            288,
        ),
    ):
        if pair is not None:
            given += [*pair[0], *pair[1]]
            in_specs += [left, left, right, right]
            sections.append((name, rows))
            rows += taken
    extra = 0
    if small_terms is not None:
        given += small_terms
        in_specs += [pl.BlockSpec(small_terms[0].shape, lambda at: (0, 0, 0))] * 2
        extra = 16

    def kernel(*refs):
        ins, out_refs = refs[: len(given)], refs[len(given) :]
        go_x, go_y, stay_x, stay_y = out_refs
        part = pl.program_id(0)

        def multiply(place, first):
            left_a, left_b, right_a, right_b = ins[4 * place : 4 * place + 4]
            result = dot_nn(left_a[...].reshape(384, tokens), right_a[...]) + dot_nn(
                left_b[...].reshape(384, tokens), right_b[...]
            )
            if first is None:
                return result
            for owner in range(4):
                spread(
                    result[96 * owner : 96 * owner + 96], owner, pl.ds(first, 96), out_refs
                )

        for place, (name, first) in enumerate(sections):
            if name == "reduce":
                multiply(place, pl.multiple_of(first + 96 * part, 96))
            elif name == "heads":

                @pl.when(part < 3)
                def one_head_block():
                    multiply(place, pl.multiple_of(first + 96 * part, 96))

            elif name == "merge":

                @pl.when(part == 3)
                def merge_block():
                    multiply(place, first)

            else:
                result = multiply(place, None)
                for owner in range(4):

                    @pl.when(part == owner)
                    def keep():
                        spread(result, owner, slice(first, first + 384), out_refs)

        if small_terms is not None:

            @pl.when(part == 3)
            def vectors():
                for owner in range(4):
                    target, at = ((stay_x, 0), (go_x, 0), (stay_x, 1), (go_x, 1))[owner]
                    target[at, rows : rows + 16] = (ins[-2][owner] + ins[-1][owner]).astype(bf16)

    half = WIDTH // 2
    heights = (rows + extra, rows, rows + extra, rows)
    return pl.pallas_call(
        kernel,
        grid=(4,),
        in_specs=in_specs,
        out_specs=[pl.BlockSpec((2, height, half), lambda at: (0, 0, 0)) for height in heights],
        out_shape=[jax.ShapeDtypeStruct((2, height, half), bf16) for height in heights],
        compiler_params=params(),
        cost_estimate=cost(0.01),
        name="owner_terms",
    )(*given)


def taken(end_ref, pair, rows, scale):
    total, outward = pair
    part = jnp.where(end_ref[0] == 1, outward[rows], total[rows])
    return part.astype(f32) * scale


def put_halves(target, end_ref, pair, low, high, rows, scale):
    half = WIDTH // 2
    target[:, :half] = taken(end_ref, pair, slice(low, low + rows), scale)
    target[:, half:] = taken(end_ref, pair, slice(high, high + rows), scale)


def in_full():
    return pl.BlockSpec(memory_space=pltpu.VMEM)


def finish_most(at_end, reduce_1, em_1, both_01, scale):
    layers = 2
    half = WIDTH // 2

    def kernel(end_ref, *refs):
        r_pair, em_pair, hr_pair = refs[0:2], refs[2:4], refs[4:6]
        heads_out, merge_out, expand_out, reduce_out, vectors_out = refs[6:11]
        heads, merge, expand, reduce, sems = refs[11:]
        for layer, pair, high in ((0, hr_pair, 688), (1, r_pair, 384)):
            for part in range(FF_PARTS):
                for first, column in ((96 * part, WIDTH * part), (high + 96 * part, WIDTH * part + half)):
                    reduce[layer, :, column : column + half] = taken(
                        end_ref, pair, slice(first, first + 96), scale
                    )
        copies = [pltpu.make_async_copy(reduce, reduce_out, sems.at[0])]
        copies[0].start()
        put_halves(expand, end_ref, em_pair, 0, 480, 384, scale)
        put_halves(merge, end_ref, em_pair, 384, 864, 96, scale)
        for member in range(3):
            put_halves(
                heads.at[member],
                end_ref,
                hr_pair,
                384 + 96 * member,
                688 + 384 + 96 * member,
                96,
                scale,
            )
        last = layers - 1
        copies.append(pltpu.make_async_copy(expand, expand_out.at[last], sems.at[1]))
        copies.append(pltpu.make_async_copy(merge, merge_out.at[last], sems.at[2]))
        copies.append(pltpu.make_async_copy(heads, heads_out.at[last], sems.at[3]))
        run_all(copies[1:], "start")
        vectors_out[...] = taken(end_ref, hr_pair, slice(672, 688), scale)
        run_all(copies, "wait")

    shape = jax.ShapeDtypeStruct
    return pl.pallas_call(
        kernel,
        in_specs=[in_smem()] + [in_full()] * 6,
        out_specs=[in_any()] * 4 + [in_full()],
        out_shape=[
            shape((layers, 3, 96, WIDTH), f32),
            shape((layers, 96, WIDTH), f32),
            shape((layers, 384, WIDTH), f32),
            shape((layers, 96, FF_PARTS * WIDTH), f32),
            shape((16, half), f32),
        ],
        scratch_shapes=[
            pltpu.VMEM((3, 96, WIDTH), f32),
            pltpu.VMEM((96, WIDTH), f32),
            pltpu.VMEM((384, WIDTH), f32),
            pltpu.VMEM((layers, 96, FF_PARTS * WIDTH), f32),
            pltpu.SemaphoreType.DMA((4,)),
        ],
        compiler_params=pltpu.CompilerParams(vmem_limit_bytes=SMALL_VMEM_BYTES),
        cost_estimate=cost(0.01),
        name="finish_most",
    )(at_end, *reduce_1, *em_1, *both_01)


def finish_expand(at_end, em_0, merge_grad, expand_grad, scale):
    def kernel(end_ref, total, outward, merge_in, expand_in, merge_out, expand_out, *rest):
        merge, expand, sems = rest
        put_halves(expand, end_ref, (total, outward), 0, 480, 384, scale)
        put_halves(merge, end_ref, (total, outward), 384, 864, 96, scale)
        copies = [
            pltpu.make_async_copy(expand, expand_out.at[0], sems.at[0]),
            pltpu.make_async_copy(merge, merge_out.at[0], sems.at[1]),
        ]
        run_all(copies, "start")
        run_all(copies, "wait")

    return pl.pallas_call(
        kernel,
        in_specs=[in_smem()] + [in_full()] * 2 + [in_any()] * 2,
        out_specs=[in_any()] * 2,
        out_shape=[jax.ShapeDtypeStruct(a.shape, f32) for a in (merge_grad, expand_grad)],
        scratch_shapes=[
            pltpu.VMEM((96, WIDTH), f32),
            pltpu.VMEM((384, WIDTH), f32),
            pltpu.SemaphoreType.DMA((2,)),
        ],
        input_output_aliases={3: 0, 4: 1},
        compiler_params=pltpu.CompilerParams(vmem_limit_bytes=SMALL_VMEM_BYTES),
        cost_estimate=cost(0.01),
        name="finish_expand",
    )(at_end, *em_0, merge_grad, expand_grad)


def finish_heads(at_end, heads_0, vectors_1, heads_grad, scale):
    def kernel(end_ref, total, outward, vectors_ref, heads_in, heads_out, *rest):
        outs, (heads, sems) = rest[:8], rest[8:]
        for member in range(3):
            put_halves(
                heads.at[member],
                end_ref,
                (total, outward),
                96 * member,
                304 + 96 * member,
                96,
                scale,
            )
        copy = pltpu.make_async_copy(heads, heads_out.at[0], sems.at[0])
        copy.start()
        own = taken(end_ref, (total, outward), slice(288, 304), scale)
        for layer, values in ((0, own), (1, vectors_ref[...])):
            outs[0][layer] = values[0:2, :96]
            for row in range(2, 8):
                outs[row - 1][layer : layer + 1] = values[row : row + 1, :96]
            outs[7][layer : layer + 1] = values[8:9]
        copy.wait()

    shape = jax.ShapeDtypeStruct
    layers = heads_grad.shape[0]
    return pl.pallas_call(
        kernel,
        in_specs=[in_smem()] + [in_full()] * 3 + [in_any()],
        out_specs=[in_any()] + [in_full()] * 8,
        out_shape=[shape(heads_grad.shape, f32), shape((layers, 2, 96), f32)]
        + [shape((layers, 96), f32)] * 6
        + [shape((layers, 384), f32)],
        scratch_shapes=[pltpu.VMEM((3, 96, WIDTH), f32), pltpu.SemaphoreType.DMA((1,))],
        input_output_aliases={4: 0},
        compiler_params=pltpu.CompilerParams(vmem_limit_bytes=SMALL_VMEM_BYTES),
        cost_estimate=cost(0.01),
        name="finish_heads",
    )(at_end, *heads_0, vectors_1, heads_grad)


def shards(
    images,
    cotangent,
    slot_flags,
    heads_weight,
    heads_bias,
    merge_weight,
    merge_bias,
    first_gain,
    first_shift,
    second_gain,
    second_shift,
    expand_weight,
    expand_bias,
    reduce_weight,
    reduce_bias,
):
    micro_count, unused_slots, seq_len, width = images.shape
    layers = heads_weight.shape[0]
    tokens = micro_count * seq_len
    place_at = lax.axis_index("fsdp").astype(jnp.int32)
    place = place_at[None]

    matrices = (heads_weight, merge_weight, expand_weight, reduce_weight)
    vectors = (
        heads_bias,
        merge_bias,
        first_gain,
        first_shift,
        second_gain,
        second_shift,
        reduce_bias,
        expand_bias,
    )
    kinds = [("attn", 0), ("ff", 0), ("attn", 1), ("expand", 1), ("reduce", 1)]
    rows_of = [PACK_ROWS[kind] for kind, layer in kinds]
    cut_of = [PACK_CUTS[kind] for kind, layer in kinds]
    x_rows = [0] + cut_of
    y_rows = [0] + [rows - cut for rows, cut in zip(rows_of, cut_of)]
    count = len(kinds)

    def send_round(at, own_now, x_before, y_before):
        if at == 0:
            return swap_x(own_now), swap_y(own_now)
        rows, cut = rows_of[at - 1], cut_of[at - 1]
        to_x = [(y_before, y_rows[at - 1], cut)]
        to_y = [(x_before, x_rows[at - 1] + cut, rows - cut)]
        if at < count:
            to_x.append((own_now, 0, rows_of[at]))
            to_y.append((own_now, 0, rows_of[at]))
        to_x, to_y = join_rows([to_x, to_y])
        return swap_x(to_x), swap_y(to_y)

    def pack_of(at, own_pair, came):
        (x_0, y_0, cx_0, cy_0), (x_1, y_1, cx_1, cy_1) = came[at], came[at + 1]
        return (
            (own_pair[0], x_0, y_0, x_1, y_1, own_pair[1], cx_0, cy_0, cx_1, cy_1),
            regions_of(rows_of[at], cut_of[at], x_rows[at], y_rows[at]),
        )

    def both(values):
        return tuple(swap_core(value) for value in values)

    hidden = images.reshape(tokens, width)
    seal = lax.optimization_barrier

    came = []
    own = own_packs(kinds[:1], matrices, vectors)
    new = send_round(0, own[0], None, None)
    own_other = both(own)
    own += own_packs(kinds[1:2], matrices, vectors)
    grad, low_mine, low_theirs = start_grad(place, slot_flags, cotangent.reshape(tokens, width))
    own, own_other, new, grad, low_mine, low_theirs, matrices, vectors = seal(
        (own, own_other, new, grad, low_mine, low_theirs, matrices, vectors)
    )

    got, new = new, send_round(1, own[1], *new)
    came.append(got + both(got))
    low = (low_mine, swap_core(low_theirs))
    own += own_packs(kinds[2:], matrices, vectors)
    own_other += both(own[1:])
    own, own_other, came, new, low, grad = seal((own, own_other, came, new, low, grad))

    got, new = new, send_round(2, own[2], *new)
    came.append(got + both(got))
    pack_a0 = pack_of(0, (own[0], own_other[0]), came)
    small_0, expand_rows_0 = gathered_vectors(place, pack_a0)
    middle_0, normed_0, qkv_0, mixed_0 = attn_forward(place, hidden, small_0, pack_a0)
    own, came, new, small_0, expand_rows_0, middle_0, normed_0, qkv_0, mixed_0 = seal(
        (own, came, new, small_0, expand_rows_0, middle_0, normed_0, qkv_0, mixed_0)
    )

    got, new = new, send_round(3, own[3], *new)
    came.append(got + both(got))
    pack_f0 = pack_of(1, (own[1], own_other[1]), came)
    second_0, active_0, slope_0 = expand_forward(
        place, middle_0, small_0, expand_rows_0, pack_f0, 0
    )
    hidden_1 = reduce_forward(
        place, slot_flags, middle_0, active_0, small_0, pack_f0, 384, False
    )
    others_a0 = both((normed_0, mixed_0))
    own, came, new, second_0, active_0, slope_0, hidden_1, others_a0 = seal(
        (own, came, new, second_0, active_0, slope_0, hidden_1, others_a0)
    )

    got, new = new, send_round(4, own[4], *new)
    came.append(got + both(got))
    pack_a1 = pack_of(2, (own[2], own_other[2]), came)
    small_1, expand_rows_1 = gathered_vectors(place, pack_a1)
    middle_1, normed_1, qkv_1, mixed_1 = attn_forward(place, hidden_1, small_1, pack_a1)
    second_other_0 = swap_core(second_0)
    came, new, small_1, expand_rows_1, middle_1, normed_1, qkv_1, mixed_1, second_other_0 = seal(
        (came, new, small_1, expand_rows_1, middle_1, normed_1, qkv_1, mixed_1, second_other_0)
    )

    got, new = new, send_round(5, None, *new)
    came.append(got + both(got))
    pack_e1 = pack_of(3, (own[3], own_other[3]), came)
    second_1, active_1, slope_1 = expand_forward(
        place, middle_1, small_1, expand_rows_1, pack_e1, 0
    )
    others_a1 = both((normed_1, mixed_1))
    second_1, active_1, slope_1, others_a1, came, new = seal(
        (second_1, active_1, slope_1, others_a1, came, new)
    )
    came.append(new + both(new))
    second_1, active_1, came = seal((second_1, active_1, came))
    pack_e1 = pack_of(3, (own[3], own_other[3]), came)
    pack_r1 = pack_of(4, (own[4], own_other[4]), came)

    grad, pre_mine, pre_theirs, attn_mine, attn_theirs, ff_sums = ff_backward(
        place, grad, slope_1, middle_1, small_1, (pack_e1, 0), (pack_r1, 0)
    )
    others_f1 = both((second_1, active_1))
    made = (grad, pre_mine, pre_theirs, attn_mine, attn_theirs, ff_sums)
    made, others_f1, pack_r1_arrays = seal((made, others_f1, pack_r1[0]))
    grad, pre_mine, pre_theirs, attn_mine, attn_theirs, ff_sums = made
    pack_r1 = (pack_r1_arrays, pack_r1[1])

    travel_r1 = owner_terms(reduce=(low, (active_1, others_f1[1])))
    pre_other, attn_other = both((pre_theirs, attn_theirs))
    travel_r1, pre_other, attn_other, grad = seal((travel_r1, pre_other, attn_other, grad))

    state_r1 = first_steps(travel_r1)
    travel_em1 = owner_terms(
        expand=((pre_mine, pre_other), (second_1, others_f1[0])),
        merge=((attn_mine, attn_other), (mixed_1, others_a1[1])),
    )
    state_r1, travel_em1, grad, active_0 = seal((state_r1, travel_em1, grad, active_0))

    state_r1 = second_steps(state_r1)
    state_em1 = first_steps(travel_em1)
    grad, qkv_mine, qkv_theirs, vec_mine, vec_theirs, low_mine, low_theirs = attn_backward(
        place, grad, hidden_1, qkv_1, mixed_1, small_1, ff_sums, pack_a1, False
    )
    active_other_0 = swap_core(active_0)
    made = (grad, qkv_mine, qkv_theirs, vec_mine, vec_theirs, low_mine, low_theirs)
    state_r1, state_em1, made, active_other_0 = seal((state_r1, state_em1, made, active_other_0))
    grad, qkv_mine, qkv_theirs, vec_mine, vec_theirs, low_mine, low_theirs = made

    sum_r1 = to_middle(ends(state_r1))
    state_em1 = second_steps(state_em1)
    low_other, qkv_other, vec_other = both((low_theirs, qkv_theirs, vec_theirs))
    travel_hr = owner_terms(
        reduce=((low_mine, low_other), (active_0, active_other_0)),
        heads=((qkv_mine, qkv_other), (normed_1, others_a1[0])),
        small_terms=(vec_mine, vec_other),
    )
    sum_r1, state_em1, travel_hr, grad = seal((sum_r1, state_em1, travel_hr, grad))

    state_hr = first_steps(travel_hr)
    sum_em1 = to_middle(ends(state_em1))
    sum_r1 = across_middle(sum_r1)
    grad, pre_mine, pre_theirs, attn_mine, attn_theirs, ff_sums = ff_backward(
        place, grad, slope_0, middle_0, small_0, (pack_f0, 0), (pack_f0, 384)
    )
    made = (grad, pre_mine, pre_theirs, attn_mine, attn_theirs, ff_sums)
    state_hr, sum_em1, sum_r1, made = seal((state_hr, sum_em1, sum_r1, made))
    grad, pre_mine, pre_theirs, attn_mine, attn_theirs, ff_sums = made

    state_hr = second_steps(state_hr)
    sum_em1 = across_middle(sum_em1)
    pre_other, attn_other = both((pre_theirs, attn_theirs))
    travel_em0 = owner_terms(
        expand=((pre_mine, pre_other), (second_0, second_other_0)),
        merge=((attn_mine, attn_other), (mixed_0, others_a0[1])),
    )
    state_hr, sum_em1, travel_em0, grad = seal((state_hr, sum_em1, travel_em0, grad))

    state_em0 = first_steps(travel_em0)
    sum_hr = to_middle(ends(state_hr))
    final_r1, final_em1 = to_ends(sum_r1), to_ends(sum_em1)
    images_grad, qkv_mine, qkv_theirs, vec_mine, vec_theirs = attn_backward(
        place, grad, hidden, qkv_0, mixed_0, small_0, ff_sums, pack_a0, True
    )
    made = (images_grad, qkv_mine, qkv_theirs, vec_mine, vec_theirs)
    state_em0, sum_hr, final_r1, final_em1, made = seal(
        (state_em0, sum_hr, final_r1, final_em1, made)
    )
    images_grad, qkv_mine, qkv_theirs, vec_mine, vec_theirs = made

    state_em0 = second_steps(state_em0)
    sum_hr = across_middle(sum_hr)
    qkv_other, vec_other = both((qkv_theirs, vec_theirs))
    travel_h0 = owner_terms(
        heads=((qkv_mine, qkv_other), (normed_0, others_a0[0])), small_terms=(vec_mine, vec_other)
    )
    state_em0, travel_h0, middle_1, active_1 = seal((state_em0, travel_h0, middle_1, active_1))

    state_h0 = first_steps(travel_h0)
    sum_em0 = to_middle(ends(state_em0))
    outputs = reduce_forward(
        place, slot_flags, middle_1, active_1, small_1, pack_r1, 0, True
    ).reshape(images.shape)
    state_h0, outputs, sum_hr = seal((state_h0, outputs, sum_hr))

    state_h0 = second_steps(state_h0)
    final_hr = to_ends(sum_hr)
    state_h0, sum_em0 = seal((state_h0, sum_em0))
    sum_h0 = to_middle(ends(state_h0))
    sum_em0 = across_middle(sum_em0)
    sum_h0, final_hr, sum_em0 = seal((sum_h0, final_hr, sum_em0))
    sum_h0 = across_middle(sum_h0)
    final_em0 = to_ends(sum_em0)
    final_h0 = to_ends(sum_h0)

    images_grad = images_grad.reshape(images.shape)
    grad_scale = (
        micro_count * images.shape[1] * lax.axis_size("fsdp") * lax.axis_size("rep") * seq_len
    ) ** (-0.5)
    rep_at = lax.axis_index("rep")
    at_end = ((rep_at == 0) | (rep_at == lax.axis_size("rep") - 1)).astype(jnp.int32)[None]
    heads_grad, merge_grad, expand_grad, reduce_grad, vectors_1 = finish_most(
        at_end, final_r1, final_em1, final_hr, grad_scale
    )
    merge_grad, expand_grad = finish_expand(at_end, final_em0, merge_grad, expand_grad, grad_scale)
    heads_grad, *vector_grads = finish_heads(at_end, final_h0, vectors_1, heads_grad, grad_scale)
    return (
        outputs,
        images_grad,
        heads_grad,
        vector_grads[0],
        merge_grad,
        *vector_grads[1:6],
        expand_grad,
        vector_grads[7],
        reduce_grad,
        vector_grads[6],
    )


def solution(mesh):
    body = shards if (mesh.shape["fsdp"], mesh.shape["rep"]) == (8, 4) else plain_shards
    placed = (
        P(None, ("fsdp", "rep"), None, None),
        P(None, ("fsdp", "rep"), None, None),
        P(None, ("fsdp", "rep")),
        P(None, None, "fsdp", None),
        P(None, None, "fsdp"),
        P(None, "fsdp", None),
        P(None, "fsdp"),
        P(None, "fsdp"),
        P(None, "fsdp"),
        P(None, "fsdp"),
        P(None, "fsdp"),
        P(None, "fsdp", None),
        P(None, "fsdp"),
        P(None, "fsdp", None),
        P(None, "fsdp"),
    )
    return jax.shard_map(
        body,
        mesh=mesh,
        in_specs=placed,
        out_specs=(
            P(None, ("fsdp", "rep"), None, None),
            P(None, ("fsdp", "rep"), None, None),
            P(None, None, "fsdp", None),
            P(None, None, "fsdp"),
            P(None, "fsdp", None),
            P(None, "fsdp"),
            P(None, "fsdp"),
            P(None, "fsdp"),
            P(None, "fsdp"),
            P(None, "fsdp"),
            P(None, "fsdp", None),
            P(None, "fsdp"),
            P(None, "fsdp", None),
            P(None, "fsdp"),
        ),
        check_vma=False,
    )
```

```python
import jax
import jax.numpy as jnp
from jax import lax
from jax.experimental import pallas as pl
from jax.experimental.pallas import tpu as pltpu
from jax.sharding import PartitionSpec as P

HEADS = 12
HEAD_DIM = 64


norm_eps = 1e-06


def layer_norm(token_rows, scale_row, offset_row):
    centre = token_rows - jnp.mean(token_rows, axis=-1, keepdims=True)
    spread = jnp.mean(centre * centre, axis=-1, keepdims=True)
    return centre * lax.rsqrt(spread + norm_eps) * scale_row + offset_row


def project(token_rows, weight):
    return lax.dot_general(
        token_rows, weight, (((1,), (1,)), ((), ())), preferred_element_type=jnp.float32
    )


def outer_sum(grad_rows, token_rows):
    return lax.dot_general(
        grad_rows, token_rows, (((0,), (0,)), ((), ())), preferred_element_type=jnp.float32
    )


def carry_back(grad_rows, weight):
    return jnp.dot(grad_rows, weight, preferred_element_type=jnp.float32)


def forward_layer(hidden, params):
    (
        heads_weight,
        heads_bias,
        merge_weight,
        merge_bias,
        first_gain,
        first_shift,
        second_gain,
        second_shift,
        expand_weight,
        expand_bias,
        reduce_weight,
        reduce_bias,
    ) = params
    seq_len, model_width = hidden.shape
    shaped = (seq_len, HEADS, HEAD_DIM)
    score_scale = HEAD_DIM ** (-0.5)
    normed = layer_norm(
        hidden, first_gain.astype(jnp.float32), first_shift.astype(jnp.float32)
    ).astype(jnp.bfloat16)
    queries = (project(normed, heads_weight[0]) + heads_bias[0].astype(jnp.float32)).astype(
        jnp.bfloat16
    )
    key_rows = project(normed, heads_weight[1]).astype(jnp.bfloat16)
    values = (project(normed, heads_weight[2]) + heads_bias[1].astype(jnp.float32)).astype(
        jnp.bfloat16
    )
    scores = (
        jnp.einsum(
            "qhd,khd->hqk",
            queries.reshape(shaped),
            key_rows.reshape(shaped),
            preferred_element_type=jnp.float32,
        )
        * score_scale
    )
    row_peak = jnp.max(scores, axis=-1, keepdims=True)
    exponent = jnp.exp(scores - row_peak)
    row_total = jnp.sum(exponent, axis=-1, keepdims=True)
    attend = exponent / row_total
    log_total = row_peak + jnp.log(row_total)
    mixed_rows = jnp.einsum(
        "hqk,khd->qhd",
        attend.astype(jnp.bfloat16),
        values.reshape(shaped),
        preferred_element_type=jnp.float32,
    )
    mixed_rows = mixed_rows.reshape(seq_len, model_width).astype(jnp.bfloat16)
    middle = hidden + (project(mixed_rows, merge_weight) + merge_bias.astype(jnp.float32))
    second = layer_norm(
        middle, second_gain.astype(jnp.float32), second_shift.astype(jnp.float32)
    ).astype(jnp.bfloat16)
    pre_act = project(second, expand_weight) + expand_bias.astype(jnp.float32)
    activated = jax.nn.gelu(pre_act, approximate=True).astype(jnp.bfloat16)
    result = middle + (project(activated, reduce_weight) + reduce_bias.astype(jnp.float32))
    saved = (
        hidden,
        normed,
        queries,
        key_rows,
        values,
        log_total,
        mixed_rows,
        middle,
        second,
        pre_act,
        activated,
    )
    return (result, saved)


def backward_layer(grad_out, params, saved):
    (
        heads_weight,
        heads_bias,
        merge_weight,
        merge_bias,
        first_gain,
        first_shift,
        second_gain,
        second_shift,
        expand_weight,
        expand_bias,
        reduce_weight,
        reduce_bias,
    ) = params
    (
        hidden,
        normed,
        queries,
        key_rows,
        values,
        log_total,
        mixed_rows,
        middle,
        second,
        pre_act,
        activated,
    ) = saved
    seq_len, model_width = hidden.shape
    shaped = (seq_len, HEADS, HEAD_DIM)
    score_scale = HEAD_DIM ** (-0.5)
    branch_low = grad_out.astype(jnp.bfloat16)
    reduce_weight_term = outer_sum(branch_low, activated)
    reduce_bias_term = jnp.sum(branch_low.astype(jnp.float32), axis=0)
    grad_act = carry_back(branch_low, reduce_weight)
    unused_value, gelu_back = jax.vjp(lambda point: jax.nn.gelu(point, approximate=True), pre_act)
    grad_pre = gelu_back(grad_act)[0].astype(jnp.bfloat16)
    expand_weight_term = outer_sum(grad_pre, second)
    expand_bias_term = jnp.sum(grad_pre.astype(jnp.float32), axis=0)
    grad_second = carry_back(grad_pre, expand_weight)
    unused_norm, second_back = jax.vjp(
        layer_norm, middle, second_gain.astype(jnp.float32), second_shift.astype(jnp.float32)
    )
    middle_part, second_gain_term, second_shift_term = second_back(grad_second)
    grad_middle = grad_out + middle_part
    attn_low = grad_middle.astype(jnp.bfloat16)
    merge_weight_term = outer_sum(attn_low, mixed_rows)
    merge_bias_term = jnp.sum(attn_low.astype(jnp.float32), axis=0)
    grad_mixed = carry_back(attn_low, merge_weight).astype(jnp.bfloat16).reshape(shaped)
    queries_heads = queries.reshape(shaped)
    keys_heads = key_rows.reshape(shaped)
    values_heads = values.reshape(shaped)
    scores = (
        jnp.einsum("qhd,khd->hqk", queries_heads, keys_heads, preferred_element_type=jnp.float32)
        * score_scale
    )
    attend = jnp.exp(scores - log_total)
    grad_values = jnp.einsum(
        "hqk,qhd->khd", attend.astype(jnp.bfloat16), grad_mixed, preferred_element_type=jnp.float32
    ).astype(jnp.bfloat16)
    grad_attend = jnp.einsum(
        "qhd,khd->hqk", grad_mixed, values_heads, preferred_element_type=jnp.float32
    )
    grad_scores = attend * (grad_attend - jnp.sum(grad_attend * attend, axis=-1, keepdims=True))
    grad_scores = grad_scores.astype(jnp.bfloat16)
    grad_queries = (
        jnp.einsum("hqk,khd->qhd", grad_scores, keys_heads, preferred_element_type=jnp.float32)
        * score_scale
    ).astype(jnp.bfloat16)
    grad_keys = (
        jnp.einsum("hqk,qhd->khd", grad_scores, queries_heads, preferred_element_type=jnp.float32)
        * score_scale
    ).astype(jnp.bfloat16)
    stacked_grads = jnp.stack(
        [
            grad_queries.reshape(seq_len, model_width),
            grad_keys.reshape(seq_len, model_width),
            grad_values.reshape(seq_len, model_width),
        ]
    )
    heads_weight_term = jnp.einsum(
        "jto,ti->joi", stacked_grads, normed, preferred_element_type=jnp.float32
    )
    grad_normed = jnp.einsum(
        "jto,joi->ti", stacked_grads, heads_weight, preferred_element_type=jnp.float32
    )
    heads_bias_term = jnp.stack(
        [
            jnp.sum(stacked_grads[0].astype(jnp.float32), axis=0),
            jnp.sum(stacked_grads[2].astype(jnp.float32), axis=0),
        ]
    )
    unused_first, first_back = jax.vjp(
        layer_norm, hidden, first_gain.astype(jnp.float32), first_shift.astype(jnp.float32)
    )
    hidden_part, first_gain_term, first_shift_term = first_back(grad_normed)
    grad_hidden = grad_middle + hidden_part
    terms = (
        heads_weight_term,
        heads_bias_term,
        merge_weight_term,
        merge_bias_term,
        first_gain_term,
        first_shift_term,
        second_gain_term,
        second_shift_term,
        expand_weight_term,
        expand_bias_term,
        reduce_weight_term,
        reduce_bias_term,
    )
    return (grad_hidden, terms)


def plain_shards(
    images,
    cotangent,
    slot_flags,
    heads_weight,
    heads_bias,
    merge_weight,
    merge_bias,
    first_gain,
    first_shift,
    second_gain,
    second_shift,
    expand_weight,
    expand_bias,
    reduce_weight,
    reduce_bias,
):
    micro_count = images.shape[0]
    seq_len = images.shape[2]
    layers = heads_weight.shape[0]
    live_flags = slot_flags.astype(jnp.float32)
    states = [images[batch_at, 0].astype(jnp.float32) for batch_at in range(micro_count)]
    saved_all = []
    for layer_at in range(layers):
        saved_row = []
        for batch_at in range(micro_count):
            params = (
                lax.all_gather(heads_weight[layer_at], "fsdp", axis=1, tiled=True),
                lax.all_gather(heads_bias[layer_at], "fsdp", axis=1, tiled=True),
                lax.all_gather(merge_weight[layer_at], "fsdp", axis=0, tiled=True),
                lax.all_gather(merge_bias[layer_at], "fsdp", axis=0, tiled=True),
                lax.all_gather(first_gain[layer_at], "fsdp", axis=0, tiled=True),
                lax.all_gather(first_shift[layer_at], "fsdp", axis=0, tiled=True),
                lax.all_gather(second_gain[layer_at], "fsdp", axis=0, tiled=True),
                lax.all_gather(second_shift[layer_at], "fsdp", axis=0, tiled=True),
                lax.all_gather(expand_weight[layer_at], "fsdp", axis=0, tiled=True),
                lax.all_gather(expand_bias[layer_at], "fsdp", axis=0, tiled=True),
                lax.all_gather(reduce_weight[layer_at], "fsdp", axis=0, tiled=True),
                lax.all_gather(reduce_bias[layer_at], "fsdp", axis=0, tiled=True),
            )
            states[batch_at], saved = forward_layer(states[batch_at], params)
            saved_row.append(saved)
        saved_all.append(saved_row)
    outputs = jnp.stack(
        [live_flags[batch_at, 0] * states[batch_at] for batch_at in range(micro_count)]
    )[:, None].astype(jnp.bfloat16)
    grads_back = [
        cotangent[batch_at, 0].astype(jnp.float32) * live_flags[batch_at, 0]
        for batch_at in range(micro_count)
    ]
    collected = [None] * layers
    for layer_at in reversed(range(layers)):
        totals = None
        for batch_at in range(micro_count):
            params = (
                lax.all_gather(heads_weight[layer_at], "fsdp", axis=1, tiled=True),
                lax.all_gather(heads_bias[layer_at], "fsdp", axis=1, tiled=True),
                lax.all_gather(merge_weight[layer_at], "fsdp", axis=0, tiled=True),
                lax.all_gather(merge_bias[layer_at], "fsdp", axis=0, tiled=True),
                lax.all_gather(first_gain[layer_at], "fsdp", axis=0, tiled=True),
                lax.all_gather(first_shift[layer_at], "fsdp", axis=0, tiled=True),
                lax.all_gather(second_gain[layer_at], "fsdp", axis=0, tiled=True),
                lax.all_gather(second_shift[layer_at], "fsdp", axis=0, tiled=True),
                lax.all_gather(expand_weight[layer_at], "fsdp", axis=0, tiled=True),
                lax.all_gather(expand_bias[layer_at], "fsdp", axis=0, tiled=True),
                lax.all_gather(reduce_weight[layer_at], "fsdp", axis=0, tiled=True),
                lax.all_gather(reduce_bias[layer_at], "fsdp", axis=0, tiled=True),
            )
            grads_back[batch_at], terms = backward_layer(
                grads_back[batch_at], params, saved_all[layer_at][batch_at]
            )
            if totals is None:
                totals = terms
            else:
                totals = tuple((earlier + current for earlier, current in zip(totals, terms)))
        collected[layer_at] = totals
    images_grad = jnp.stack(grads_back)[:, None].astype(jnp.bfloat16)
    stacked = [
        jnp.stack([collected[layer_at][member] for layer_at in range(layers)])
        for member in range(12)
    ]
    shares = (
        lax.psum_scatter(
            stacked[0].astype(jnp.bfloat16), "fsdp", scatter_dimension=2, tiled=True
        ).astype(jnp.float32),
        lax.psum_scatter(
            stacked[1].astype(jnp.bfloat16), "fsdp", scatter_dimension=2, tiled=True
        ).astype(jnp.float32),
        lax.psum_scatter(
            stacked[2].astype(jnp.bfloat16), "fsdp", scatter_dimension=1, tiled=True
        ).astype(jnp.float32),
        lax.psum_scatter(
            stacked[3].astype(jnp.bfloat16), "fsdp", scatter_dimension=1, tiled=True
        ).astype(jnp.float32),
        lax.psum_scatter(
            stacked[4].astype(jnp.bfloat16), "fsdp", scatter_dimension=1, tiled=True
        ).astype(jnp.float32),
        lax.psum_scatter(
            stacked[5].astype(jnp.bfloat16), "fsdp", scatter_dimension=1, tiled=True
        ).astype(jnp.float32),
        lax.psum_scatter(
            stacked[6].astype(jnp.bfloat16), "fsdp", scatter_dimension=1, tiled=True
        ).astype(jnp.float32),
        lax.psum_scatter(
            stacked[7].astype(jnp.bfloat16), "fsdp", scatter_dimension=1, tiled=True
        ).astype(jnp.float32),
        lax.psum_scatter(
            stacked[8].astype(jnp.bfloat16), "fsdp", scatter_dimension=1, tiled=True
        ).astype(jnp.float32),
        lax.psum_scatter(
            stacked[9].astype(jnp.bfloat16), "fsdp", scatter_dimension=1, tiled=True
        ).astype(jnp.float32),
        lax.psum_scatter(
            stacked[10].astype(jnp.bfloat16), "fsdp", scatter_dimension=1, tiled=True
        ).astype(jnp.float32),
        lax.psum_scatter(
            stacked[11].astype(jnp.bfloat16), "fsdp", scatter_dimension=1, tiled=True
        ).astype(jnp.float32),
    )
    reduced = (
        lax.psum(shares[0].astype(jnp.bfloat16), "rep").astype(jnp.float32),
        lax.psum(shares[1].astype(jnp.bfloat16), "rep").astype(jnp.float32),
        lax.psum(shares[2].astype(jnp.bfloat16), "rep").astype(jnp.float32),
        lax.psum(shares[3].astype(jnp.bfloat16), "rep").astype(jnp.float32),
        lax.psum(shares[4].astype(jnp.bfloat16), "rep").astype(jnp.float32),
        lax.psum(shares[5].astype(jnp.bfloat16), "rep").astype(jnp.float32),
        lax.psum(shares[6].astype(jnp.bfloat16), "rep").astype(jnp.float32),
        lax.psum(shares[7].astype(jnp.bfloat16), "rep").astype(jnp.float32),
        lax.psum(shares[8].astype(jnp.bfloat16), "rep").astype(jnp.float32),
        lax.psum(shares[9].astype(jnp.bfloat16), "rep").astype(jnp.float32),
        lax.psum(shares[10].astype(jnp.bfloat16), "rep").astype(jnp.float32),
        lax.psum(shares[11].astype(jnp.bfloat16), "rep").astype(jnp.float32),
    )
    grad_scale = (micro_count * lax.axis_size("fsdp") * lax.axis_size("rep") * seq_len) ** (-0.5)
    finals = tuple((member_sum * grad_scale for member_sum in reduced))
    return (outputs, images_grad) + finals


ROWS = 256
WIDTH = 768
FF_PARTS = 4
f32 = jnp.float32
bf16 = jnp.bfloat16
VMEM_BYTES = 52 * 1024 * 1024
SMALL_VMEM_BYTES = 24 * 1024 * 1024
LARGE_VMEM_BYTES = 60 * 1024 * 1024


def dot_nt(left, right):
    return lax.dot_general(left, right, (((1,), (1,)), ((), ())), preferred_element_type=f32)


def dot_nn(left, right):
    return lax.dot_general(left, right, (((1,), (0,)), ((), ())), preferred_element_type=f32)


def swap_core(value):
    return lax.ppermute(value, "fsdp", [(at, at ^ 1) for at in range(8)])


def swap_x(value):
    return lax.ppermute(value, "fsdp", [(at, at ^ 2) for at in range(8)])


def swap_y(value):
    return lax.ppermute(value, "fsdp", [(at, at ^ 4) for at in range(8)])


PIECES = 10


def regions_of(rows, cut, x_row, y_row):
    return [
        region
        for odd in range(2)
        for region in (
            (5 * odd, odd, 0, rows, 0),
            (5 * odd + 1, 2 ^ odd, 0, rows, x_row),
            (5 * odd + 2, 4 ^ odd, 0, rows, y_row),
            (5 * odd + 3, 6 ^ odd, 0, cut, 0),
            (5 * odd + 4, 6 ^ odd, cut, rows, 0),
        )
    ]


def block_copies(place, refs, regions, first, count, block, sems):
    copies = []
    for array_at, delta, low, high, start in regions:
        begin, end = max(low, first), min(high, first + count)
        if begin < end:
            copies.append(
                pltpu.make_async_copy(
                    refs[array_at].at[pl.ds(start + begin - low, end - begin)],
                    block.at[place ^ delta, pl.ds(begin - first, end - begin)],
                    sems.at[len(copies)],
                )
            )
    return copies


def run_all(copies, what):
    for copy in copies:
        getattr(copy, what)()


def in_any():
    return pl.BlockSpec(memory_space=pltpu.HBM)


def in_smem():
    return pl.BlockSpec(memory_space=pltpu.SMEM)


def params(steps=1):
    return pltpu.CompilerParams(
        dimension_semantics=("arbitrary",) * steps, vmem_limit_bytes=VMEM_BYTES
    )


def cost(micros):
    return pl.CostEstimate(flops=int(micros * 1.1e9), bytes_accessed=1 << 10, transcendentals=0)


def rows_spec(width):
    return pl.BlockSpec((ROWS, width), lambda image: (image, 0))


def part_spec(tokens):
    return pl.BlockSpec((tokens, WIDTH), lambda part: (0, part))


def fixed(shape):
    return pl.BlockSpec(shape, lambda image: (0,) * len(shape))


def normalise(rows):
    centre = rows - jnp.mean(rows, axis=-1, keepdims=True)
    root = lax.rsqrt(jnp.mean(centre * centre, axis=-1, keepdims=True) + norm_eps)
    return centre * root, root


PACK_ROWS = {"attn": 400, "ff": 768, "expand": 384, "reduce": 384}
PACK_CUTS = {"attn": 192, "ff": 384, "expand": 192, "reduce": 192}


def own_packs(wanted, matrices, vectors):
    count = len(wanted)
    needed = [
        at
        for at, users in enumerate(
            (("attn",), ("attn",), ("ff", "expand"), ("ff", "reduce"))
        )
        if any(kind in users for kind, layer in wanted)
    ]

    def kernel(*refs):
        heads_ref, merge_ref, expand_ref, reduce_ref = (
            refs[needed.index(at)] if at in needed else None for at in range(4)
        )
        vector_refs = refs[len(needed) : len(needed) + 8]
        outs, rows = refs[len(needed) + 8 : -1], refs[-1]
        for out, (kind, layer) in zip(outs, wanted):
            if kind == "attn":
                for at in range(3):
                    out[96 * at : 96 * at + 96] = heads_ref[layer, at]
                out[288:384] = merge_ref[layer]
                rows[...] = jnp.zeros_like(rows)
                rows[0:2, 0:96] = vector_refs[0][layer].astype(f32)
                for row in range(2, 8):
                    values = vector_refs[row - 1][...].astype(f32)
                    rows[row : row + 1, 0:96] = values[layer : layer + 1]
                rows[8:9, 0:384] = vector_refs[7][...].astype(f32)[layer : layer + 1]
                out[384:400] = rows[...].astype(bf16)
            if kind in ("ff", "expand"):
                out[0:384] = expand_ref[layer]
            if kind in ("ff", "reduce"):
                first = 384 if kind == "ff" else 0
                for part in range(FF_PARTS):
                    out[first + 96 * part : first + 96 * part + 96] = reduce_ref[
                        layer, :, WIDTH * part : WIDTH * (part + 1)
                    ]

    in_vmem = pl.BlockSpec(memory_space=pltpu.VMEM)
    return pl.pallas_call(
        kernel,
        in_specs=[in_vmem] * (len(needed) + 8),
        out_specs=[in_vmem] * count,
        out_shape=[
            jax.ShapeDtypeStruct((PACK_ROWS[kind], WIDTH), bf16) for kind, layer in wanted
        ],
        scratch_shapes=[pltpu.VMEM((16, WIDTH), f32)],
        compiler_params=pltpu.CompilerParams(vmem_limit_bytes=LARGE_VMEM_BYTES),
        cost_estimate=cost(0.01),
        name="own_packs",
    )(*[matrices[at] for at in needed], *vectors)


def join_rows(pieces_of):
    flat = [piece for pieces in pieces_of for piece in pieces]
    heights = [sum(rows for unused, unused_first, rows in pieces) for pieces in pieces_of]

    def kernel(*refs):
        ins, outs, sems = refs[: len(flat)], refs[len(flat) : -1], refs[-1]
        copies = []
        for out, pieces in zip(outs, pieces_of):
            into = 0
            for unused, first, rows in pieces:
                at = len(copies)
                copies.append(
                    pltpu.make_async_copy(
                        ins[at].at[pl.ds(first, rows)], out.at[pl.ds(into, rows)], sems.at[at]
                    )
                )
                into += rows
        run_all(copies, "start")
        run_all(copies, "wait")

    return pl.pallas_call(
        kernel,
        in_specs=[in_any()] * len(flat),
        out_specs=[pl.BlockSpec(memory_space=pltpu.VMEM)] * len(heights),
        out_shape=[jax.ShapeDtypeStruct((rows, WIDTH), bf16) for rows in heights],
        scratch_shapes=[pltpu.SemaphoreType.DMA((len(flat),))],
        compiler_params=pltpu.CompilerParams(vmem_limit_bytes=SMALL_VMEM_BYTES),
        cost_estimate=cost(0.01),
        name="join_rows",
    )(*[array for array, unused, unused_rows in flat])


def gathered_vectors(place, pack):
    arrays, regions = pack
    used = {}
    for array_at, delta, low, high, start in regions:
        if low <= 384 and 400 <= high:
            used[delta] = (arrays[array_at], start + 384 - low)
    deltas = sorted(used)

    def kernel(place_ref, *refs):
        ins, small_ref, expand_ref, rows, sems = refs[:8], refs[8], refs[9], refs[10], refs[11]
        copies = [
            pltpu.make_async_copy(
                ins[at].at[pl.ds(used[delta][1], 16)], rows.at[at], sems.at[at]
            )
            for at, delta in enumerate(deltas)
        ]
        run_all(copies, "start")
        here = place_ref[0]
        row = lax.broadcasted_iota(jnp.int32, (1024, WIDTH), 0)
        column = lax.broadcasted_iota(jnp.int32, (1024, WIDTH), 1)
        at = row & 127
        wanted = 96 * ((row >> 7) ^ here) + at
        chosen = jnp.where((column == wanted) & (at < 96), 1.0, 0.0).astype(bf16)
        run_all(copies, "wait")
        flat = jnp.concatenate([rows[at, 0:8, 0:128].astype(f32) for at in range(8)], axis=1)
        small_ref[...] = dot_nn(flat.astype(bf16), chosen)
        for at, delta in enumerate(deltas):
            owner = here ^ delta
            line = rows[at].astype(f32)[8:9, 0:384]

            @pl.when((owner & 1) == 0)
            def left():
                expand_ref[owner >> 1, :, 0:384] = line

            @pl.when((owner & 1) == 1)
            def right():
                expand_ref[owner >> 1, :, 384:768] = line

    shape = jax.ShapeDtypeStruct
    return pl.pallas_call(
        kernel,
        in_specs=[in_smem()] + [in_any()] * 8,
        out_specs=[pl.BlockSpec(memory_space=pltpu.VMEM)] * 2,
        out_shape=[shape((8, WIDTH), f32), shape((4, 1, WIDTH), f32)],
        scratch_shapes=[pltpu.VMEM((8, 16, WIDTH), bf16), pltpu.SemaphoreType.DMA((8,))],
        compiler_params=pltpu.CompilerParams(vmem_limit_bytes=LARGE_VMEM_BYTES),
        cost_estimate=cost(0.01),
        name="gathered_vectors",
    )(place, *[used[delta][0] for delta in deltas])


def elementwise(name, body, ins, out_shapes):
    def kernel(*refs):
        body(refs[: len(ins)], refs[len(ins) :])

    return pl.pallas_call(
        kernel,
        in_specs=[pl.BlockSpec(memory_space=pltpu.VMEM)] * len(ins),
        out_specs=[pl.BlockSpec(memory_space=pltpu.VMEM)] * len(out_shapes),
        out_shape=[jax.ShapeDtypeStruct(shape, bf16) for shape in out_shapes],
        compiler_params=pltpu.CompilerParams(vmem_limit_bytes=SMALL_VMEM_BYTES),
        cost_estimate=cost(0.01),
        name=name,
    )(*ins)


def add_low(*parts):
    total = parts[0].astype(f32)
    for part in parts[1:]:
        total = total + part.astype(f32)
    return total.astype(bf16)


def first_steps(travel):
    go_x, go_y, stay_x, stay_y = travel
    return swap_x(go_x), swap_y(go_y), stay_x, stay_y


def second_steps(state):
    def body(ins, outs):
        from_x, from_y, stay_x, stay_y = ins
        outs[0][...] = add_low(stay_x[1], from_x[1])
        outs[1][...] = add_low(stay_y[1], from_y[1])
        outs[2][...] = add_low(stay_x[0], from_x[0])
        outs[3][...] = add_low(stay_y[0], from_y[0])

    low, high = state[0].shape[1:], state[1].shape[1:]
    low_on, high_on, kept_low, kept_high = elementwise(
        "second_steps", body, state, [low, high, low, high]
    )
    return swap_y(low_on), swap_x(high_on), kept_low, kept_high


def ends(state):
    from_y, from_x, kept_low, kept_high = state
    low, high = kept_low.shape[0], kept_high.shape[0]

    def body(ins, outs):
        outs[0][0:low] = add_low(ins[2][...], ins[0][...])
        outs[0][low : low + high] = add_low(ins[3][...], ins[1][...])

    return elementwise("ends", body, state, [(low + high, WIDTH // 2)])[0]


def to_middle(part):
    return part, lax.ppermute(part, "rep", [(0, 1), (3, 2)])


def plus(parts):
    def body(ins, outs):
        outs[0][...] = add_low(ins[0][...], ins[1][...])

    return elementwise("plus", body, parts, [parts[0].shape])[0]


def across_middle(parts):
    inward = plus(parts)
    return inward, lax.ppermute(inward, "rep", [(1, 2), (2, 1)])


def to_ends(parts):
    total = plus(parts)
    return total, lax.ppermute(total, "rep", [(1, 0), (2, 3)])


SM_HB0, SM_HB1, SM_MB, SM_G1, SM_S1, SM_G2, SM_S2, SM_RB = range(8)


def unit_copies(place, refs, regions, first, blocks, sems):
    copies = []
    count = 96 * blocks.shape[0]
    for array_at, delta, low, high, start in regions:
        begin, end = max(low, first), min(high, first + count)
        if begin < end:
            units = (end - begin) // 96
            source = refs[array_at].at[pl.ds(start + begin - low, end - begin)]
            copies.append(
                pltpu.make_async_copy(
                    source.reshape(units, 96, WIDTH),
                    blocks.at[pl.ds((begin - first) // 96, units), place ^ delta],
                    sems.at[len(copies)],
                )
            )
    return copies


def attn_forward(place, hidden, small, pack):

    def kernel(place_ref, hidden_ref, small_ref, *rest):
        packs = rest[:PIECES]
        middle_ref, normed_ref, qkv_ref, mixed_ref, blocks, sems = rest[PIECES:]
        place_now = place_ref[0]
        image = pl.program_id(0)
        copies = unit_copies(place_now, packs, pack[1], 0, blocks, sems)

        @pl.when(image == 0)
        def begin():
            run_all(copies, "start")

        rows = hidden_ref[...].astype(f32)
        unit, root = normalise(rows)
        normed = (unit * small_ref[SM_G1 : SM_G1 + 1] + small_ref[SM_S1 : SM_S1 + 1]).astype(bf16)
        normed_ref[...] = normed

        @pl.when(image == 0)
        def arrive():
            run_all(copies, "wait")

        for member, bias in ((0, SM_HB0), (1, None), (2, SM_HB1)):
            block = blocks[member].reshape(WIDTH, WIDTH)
            made = dot_nt(normed, block)
            if bias is not None:
                made = made + small_ref[bias : bias + 1]
            qkv_ref[:, WIDTH * member : WIDTH * (member + 1)] = made.astype(bf16)
        lane = lax.broadcasted_iota(jnp.int32, (ROWS, 128), 1)
        for pair in range(HEADS // 2):
            q_pair = qkv_ref[:, 128 * pair : 128 * pair + 128] * HEAD_DIM**-0.5
            k_pair = qkv_ref[:, WIDTH + 128 * pair : WIDTH + 128 * pair + 128]
            v_pair = qkv_ref[:, 2 * WIDTH + 128 * pair : 2 * WIDTH + 128 * pair + 128]
            parts = []
            for half in range(2):
                here = (lane < 64) == (half == 0)
                scores = dot_nt(jnp.where(here, q_pair, jnp.zeros_like(q_pair)), k_pair)
                peak = jnp.max(scores, axis=-1, keepdims=True)
                powers = jnp.exp(scores - peak).astype(bf16)
                parts.append(dot_nn(powers, jnp.where(here, v_pair, jnp.ones_like(v_pair))))
            totals = pltpu.roll(jnp.where(lane < 64, parts[1], parts[0]), 64, 1)
            mixed_ref[:, 128 * pair : 128 * pair + 128] = (
                jnp.where(lane < 64, parts[0], parts[1]) / totals
            ).astype(bf16)
        merged = dot_nt(mixed_ref[...], blocks[3].reshape(WIDTH, WIDTH))
        middle_ref[...] = rows + (merged + small_ref[SM_MB : SM_MB + 1])

    tokens = hidden.shape[0]
    shape = jax.ShapeDtypeStruct
    return pl.pallas_call(
        kernel,
        grid=(tokens // ROWS,),
        in_specs=[in_smem(), rows_spec(WIDTH), fixed(small.shape)] + [in_any()] * PIECES,
        out_specs=[rows_spec(WIDTH), rows_spec(WIDTH), rows_spec(3 * WIDTH), rows_spec(WIDTH)],
        out_shape=[
            shape((tokens, WIDTH), f32),
            shape((tokens, WIDTH), bf16),
            shape((tokens, 3 * WIDTH), bf16),
            shape((tokens, WIDTH), bf16),
        ],
        scratch_shapes=[
            pltpu.VMEM((4, 8, 96, WIDTH), bf16),
            pltpu.SemaphoreType.DMA((PIECES,)),
        ],
        compiler_params=params(),
        cost_estimate=cost(0.01),
        name="attn_forward",
    )(place, hidden, small, *pack[0])


def expand_forward(place, middle, small, expand_bias, pack, first):
    tokens = middle.shape[0]

    def kernel(place_ref, middle_ref, small_ref, bias_ref, *rest):
        packs = rest[:PIECES]
        normed_ref, active_ref, slope_ref, block, sems = rest[PIECES:]
        part = pl.program_id(0)
        copies = block_copies(place_ref[0], packs, pack[1], first, 384, block, sems)

        @pl.when(part == 0)
        def begin():
            run_all(copies, "start")
            unit, root = normalise(middle_ref[...])
            normed_ref[...] = (
                unit * small_ref[SM_G2 : SM_G2 + 1] + small_ref[SM_S2 : SM_S2 + 1]
            ).astype(bf16)
            run_all(copies, "wait")

        weight = block[pl.ds(2 * part, 2)].reshape(WIDTH, WIDTH)
        point = dot_nt(normed_ref[...], weight) + bias_ref[part]
        root, cubic = 0.7978845608028654, 0.044715
        square = point * point
        upper = 0.5 + 0.5 * jnp.tanh(point * (root + (root * cubic) * square))
        active_ref[...] = (point * upper).astype(bf16)
        bend = point * (2.0 * root + (6.0 * root * cubic) * square)
        slope_ref[...] = (upper * (1.0 + bend * (1.0 - upper))).astype(bf16)

    hidden_units = FF_PARTS * WIDTH
    shape = jax.ShapeDtypeStruct
    return pl.pallas_call(
        kernel,
        grid=(FF_PARTS,),
        in_specs=[
            in_smem(),
            fixed(middle.shape),
            fixed(small.shape),
            fixed(expand_bias.shape),
        ]
        + [in_any()] * PIECES,
        out_specs=[fixed(middle.shape), part_spec(tokens), part_spec(tokens)],
        out_shape=[
            shape((tokens, WIDTH), bf16),
            shape((tokens, hidden_units), bf16),
            shape((tokens, hidden_units), bf16),
        ],
        scratch_shapes=[
            pltpu.VMEM((8, 384, WIDTH), bf16),
            pltpu.SemaphoreType.DMA((PIECES,)),
        ],
        compiler_params=params(),
        cost_estimate=cost(0.01),
        name="expand_forward",
    )(place, middle, small, expand_bias, *pack[0])


def reduce_copies(place_now, packs, regions, first, blocks, sems):
    return [
        block_copies(
            place_now, packs, regions, first + 96 * part, 96, blocks.at[part], sems.at[part]
        )
        for part in range(FF_PARTS)
    ]


def for_part(part, groups, what):
    for at, group in enumerate(groups):

        @pl.when(part == at)
        def run():
            run_all(group, what)


def reduce_forward(place, live, middle, active, small, pack, first, last):
    tokens = middle.shape[0]

    def kernel(place_ref, live_ref, middle_ref, active_ref, small_ref, *rest):
        packs = rest[:PIECES]
        result_ref, total, blocks, sems = rest[PIECES:]
        part = pl.program_id(0)
        copies = reduce_copies(place_ref[0], packs, pack[1], first, blocks, sems)

        @pl.when(part == 0)
        def begin():
            for group in copies:
                run_all(group, "start")
            total[...] = middle_ref[...] + small_ref[SM_RB : SM_RB + 1]

        for_part(part, copies, "wait")
        total[...] += dot_nt(active_ref[...], blocks[part].reshape(WIDTH, WIDTH))

        @pl.when(part == FF_PARTS - 1)
        def end():
            if last:
                for image in range(tokens // ROWS):
                    rows = slice(ROWS * image, ROWS * (image + 1))
                    result_ref[rows] = (
                        total[rows] * live_ref[image, 0].astype(f32)
                    ).astype(result_ref.dtype)
            else:
                result_ref[...] = total[...].astype(result_ref.dtype)

    return pl.pallas_call(
        kernel,
        grid=(FF_PARTS,),
        in_specs=[
            in_smem(),
            in_smem(),
            fixed(middle.shape),
            part_spec(tokens),
            fixed(small.shape),
        ]
        + [in_any()] * PIECES,
        out_specs=fixed(middle.shape),
        out_shape=jax.ShapeDtypeStruct((tokens, WIDTH), bf16 if last else f32),
        scratch_shapes=[
            pltpu.VMEM((tokens, WIDTH), f32),
            pltpu.VMEM((FF_PARTS, 8, 96, WIDTH), bf16),
            pltpu.SemaphoreType.DMA((FF_PARTS, PIECES)),
        ],
        compiler_params=params(),
        cost_estimate=cost(0.01),
        name="reduce_forward",
    )(place, live, middle, active, small, *pack[0])


def split_owners(place_now, turned, mine_ref, theirs_ref, count, lead=()):
    core = place_now & 1
    chip = place_now >> 1
    for owner in range(4):
        mine_ref[lead + (owner ^ chip,)] = turned[2 * owner + core]
        theirs_ref[lead + (owner ^ chip,)] = turned[2 * owner + 1 - core]


def halves_spec(count):
    return pl.BlockSpec((4, count, ROWS), lambda image: (0, 0, image))


def start_grad(place, live, cotangent):
    def kernel(place_ref, live_ref, cot_ref, grad_ref, mine_ref, theirs_ref, turned):
        image = pl.program_id(0)
        grad = cot_ref[...].astype(f32) * live_ref[image, 0].astype(f32)
        grad_ref[...] = grad.astype(bf16)
        turned[...] = grad.T.astype(bf16).reshape(8, 96, ROWS)
        split_owners(place_ref[0], turned, mine_ref, theirs_ref, 96)

    tokens = cotangent.shape[0]
    shape = jax.ShapeDtypeStruct
    return pl.pallas_call(
        kernel,
        grid=(tokens // ROWS,),
        in_specs=[in_smem(), in_smem(), rows_spec(WIDTH)],
        out_specs=[rows_spec(WIDTH), halves_spec(96), halves_spec(96)],
        out_shape=[shape((tokens, WIDTH), bf16)] + [shape((4, 96, tokens), bf16)] * 2,
        scratch_shapes=[pltpu.VMEM((8, 96, ROWS), bf16)],
        compiler_params=params(),
        cost_estimate=cost(0.01),
        name="start_grad",
    )(place, live, cotangent)


def fetch(source, target, sem):
    return pltpu.make_async_copy(source, target, sem)


def ff_backward(place, grad, slope, middle, small, expand_pack, reduce_pack):
    tokens = middle.shape[0]
    (expand_arrays, expand_regions), expand_first = expand_pack
    (reduce_arrays, reduce_regions), reduce_first = reduce_pack

    def kernel(place_ref, grad_in, slope_in, middle_in, small_ref, *rest):
        expand_packs, reduce_packs = rest[:PIECES], rest[PIECES : 2 * PIECES]
        (
            out_ref,
            pre_mine,
            pre_theirs,
            attn_mine,
            attn_theirs,
            sums_ref,
            grad_ref,
            slope_ref,
            middle_ref,
            expand_block,
            reduce_blocks,
            turned_pre,
            turned_attn,
            pre_low,
            expand_sems,
            reduce_sems,
            in_sems,
            out_sems,
        ) = rest[2 * PIECES :]
        place_now = place_ref[0]
        core = place_now & 1
        chip = place_now >> 1
        copies = reduce_copies(
            place_now, reduce_packs, reduce_regions, reduce_first, reduce_blocks, reduce_sems
        )
        expand_copies = block_copies(
            place_now, expand_packs, expand_regions, expand_first, 384, expand_block, expand_sems
        )
        grad_copy = fetch(grad_in, grad_ref, in_sems.at[0])
        middle_copy = fetch(middle_in, middle_ref, in_sems.at[1])
        slope_copies = [
            fetch(
                slope_in.at[:, pl.ds(WIDTH * part, WIDTH)], slope_ref.at[part], in_sems.at[2 + part]
            )
            for part in range(FF_PARTS)
        ]
        grad_copy.start()
        for part in range(FF_PARTS):
            run_all(copies[part], "start")
            slope_copies[part].start()
        run_all(expand_copies, "start")
        middle_copy.start()

        sent = []

        def send(source, target):
            copy = pltpu.make_async_copy(source, target, out_sems.at[len(sent)])
            copy.start()
            sent.append(copy)

        grad_copy.wait()
        low = grad_ref[...].astype(bf16)
        sums_ref[2:3] = jnp.sum(low.astype(f32), axis=0, keepdims=True)
        for part in range(FF_PARTS):
            run_all(copies[part], "wait")
            slope_copies[part].wait()
            up = dot_nn(low, reduce_blocks[part].reshape(WIDTH, WIDTH))
            pre = (up * slope_ref[part].astype(f32)).astype(bf16)
            pre_low[part] = pre
            sums_ref[4 + part : 5 + part] = jnp.sum(pre.astype(f32), axis=0, keepdims=True)
            turned_pre[2 * part : 2 * part + 2] = pre.T.reshape(2, 384, tokens)
            send(turned_pre.at[2 * part + core], pre_mine.at[part ^ chip])
            send(turned_pre.at[2 * part + 1 - core], pre_theirs.at[part ^ chip])
        run_all(expand_copies, "wait")
        back = dot_nn(pre_low[0], expand_block[0:2].reshape(WIDTH, WIDTH))
        for part in range(1, FF_PARTS):
            back = back + dot_nn(
                pre_low[part], expand_block[2 * part : 2 * part + 2].reshape(WIDTH, WIDTH)
            )
        middle_copy.wait()
        unit, root = normalise(middle_ref[...])
        sums_ref[0:1] = jnp.sum(back * unit, axis=0, keepdims=True)
        sums_ref[1:2] = jnp.sum(back, axis=0, keepdims=True)
        scaled = back * small_ref[SM_G2 : SM_G2 + 1]
        result = grad_ref[...].astype(f32) + root * (
            scaled
            - jnp.mean(scaled, axis=-1, keepdims=True)
            - unit * jnp.mean(scaled * unit, axis=-1, keepdims=True)
        )
        out_ref[...] = result
        result_low = result.astype(bf16)
        sums_ref[3:4] = jnp.sum(result_low.astype(f32), axis=0, keepdims=True)
        turned_attn[...] = result_low.T.reshape(8, 96, tokens)
        for owner in range(4):
            send(turned_attn.at[2 * owner + core], attn_mine.at[owner ^ chip])
            send(turned_attn.at[2 * owner + 1 - core], attn_theirs.at[owner ^ chip])
        run_all(sent, "wait")

    shape = jax.ShapeDtypeStruct
    in_vmem = pl.BlockSpec(memory_space=pltpu.VMEM)
    return pl.pallas_call(
        kernel,
        in_specs=[in_smem()] + [in_any()] * 3 + [in_vmem] + [in_any()] * (2 * PIECES),
        out_specs=[in_vmem] + [in_any()] * 4 + [in_vmem],
        out_shape=[shape((tokens, WIDTH), f32)]
        + [shape((4, 384, tokens), bf16)] * 2
        + [shape((4, 96, tokens), bf16)] * 2
        + [shape((8, WIDTH), f32)],
        scratch_shapes=[
            pltpu.VMEM((tokens, WIDTH), grad.dtype),
            pltpu.VMEM((FF_PARTS, tokens, WIDTH), bf16),
            pltpu.VMEM((tokens, WIDTH), f32),
            pltpu.VMEM((8, 384, WIDTH), bf16),
            pltpu.VMEM((FF_PARTS, 8, 96, WIDTH), bf16),
            pltpu.VMEM((8, 384, tokens), bf16),
            pltpu.VMEM((8, 96, tokens), bf16),
            pltpu.VMEM((FF_PARTS, tokens, WIDTH), bf16),
            pltpu.SemaphoreType.DMA((PIECES,)),
            pltpu.SemaphoreType.DMA((FF_PARTS, PIECES)),
            pltpu.SemaphoreType.DMA((2 + FF_PARTS,)),
            pltpu.SemaphoreType.DMA((16,)),
        ],
        compiler_params=pltpu.CompilerParams(vmem_limit_bytes=VMEM_BYTES),
        cost_estimate=cost(0.01),
        name="ff_backward",
    )(place, grad, slope, middle, small, *expand_arrays, *reduce_arrays)


def chosen_columns(place):
    def kernel(place_ref, out_ref):
        row = lax.broadcasted_iota(jnp.int32, (WIDTH, 1024), 0)
        column = lax.broadcasted_iota(jnp.int32, (WIDTH, 1024), 1)
        at = column & 127
        wanted = 96 * ((column >> 7) ^ place_ref[0]) + at
        out_ref[...] = jnp.where((row == wanted) & (at < 96), 1.0, 0.0).astype(bf16)

    return pl.pallas_call(
        kernel,
        in_specs=[in_smem()],
        out_specs=pl.BlockSpec(memory_space=pltpu.VMEM),
        out_shape=jax.ShapeDtypeStruct((WIDTH, 1024), bf16),
        compiler_params=pltpu.CompilerParams(vmem_limit_bytes=LARGE_VMEM_BYTES),
        cost_estimate=cost(0.01),
        name="chosen_columns",
    )(place)


def attn_backward(place, grad, hidden, qkv, mixed, small, ff_sums, chosen, pack, last):
    tokens = grad.shape[0]

    def kernel(
        place_ref, grad_in, hidden_in, qkv_in, mixed_in, chosen_in, small_ref, ff_sums_ref, *rest
    ):
        packs = rest[:PIECES]
        out_ref, qkv_mine, qkv_theirs, vec_mine, vec_theirs = rest[PIECES : PIECES + 5]
        if not last:
            low_mine, low_theirs = rest[PIECES + 5 : PIECES + 7]
        (
            grad_ref,
            hidden_ref,
            qkv_ref,
            mixed_ref,
            chosen_ref,
            blocks,
            turned,
            sums_ref,
            sems,
            in_sems,
            out_sems,
        ) = rest[-11:]
        place_now = place_ref[0]
        core = place_now & 1
        chip = place_now >> 1
        merge_copies = unit_copies(
            place_now, packs, pack[1], 288, blocks.at[pl.ds(3, 1)], sems.at[0]
        )
        heads_copies = unit_copies(
            place_now, packs, pack[1], 0, blocks.at[pl.ds(0, 3)], sems.at[1]
        )
        fetches = [
            fetch(source, target, in_sems.at[at])
            for at, (source, target) in enumerate(
                (
                    (grad_in, grad_ref),
                    (mixed_in, mixed_ref),
                    (qkv_in, qkv_ref),
                    (hidden_in, hidden_ref),
                    (chosen_in, chosen_ref),
                )
            )
        ]
        fetches[0].start()
        run_all(merge_copies, "start")
        run_all(fetches[1:], "start")
        run_all(heads_copies, "start")
        sent = []

        def send(source, target):
            copy = pltpu.make_async_copy(source, target, out_sems.at[len(sent)])
            copy.start()
            sent.append(copy)

        fetches[0].wait()
        run_all(merge_copies, "wait")
        grad_rows = grad_ref[...]
        mixed_back = dot_nn(grad_rows.astype(bf16), blocks[3].reshape(WIDTH, WIDTH)).astype(bf16)
        fetches[1].wait()
        product = mixed_back.astype(f32) * mixed_ref[...].astype(f32)
        product_high = product.astype(bf16)
        product_low = (product - product_high.astype(f32)).astype(bf16)
        head_row = lax.broadcasted_iota(jnp.int32, (16, WIDTH), 0)
        head_column = lax.broadcasted_iota(jnp.int32, (16, WIDTH), 1) >> 6
        of_head = jnp.where(head_row == head_column, 1.0, 0.0).astype(bf16)
        inner = dot_nt(of_head, product_high) + dot_nt(of_head, product_low)
        fetches[2].wait()
        lane = lax.broadcasted_iota(jnp.int32, (ROWS, 128), 1)
        line = lax.broadcasted_iota(jnp.int32, (128, ROWS), 0)
        scale = HEAD_DIM**-0.5
        for image in range(tokens // ROWS):
            rows = slice(ROWS * image, ROWS * (image + 1))
            for pair in range(HEADS // 2):
                q_pair = qkv_ref[rows, 128 * pair : 128 * pair + 128]
                k_pair = qkv_ref[rows, WIDTH + 128 * pair : WIDTH + 128 * pair + 128]
                v_pair = qkv_ref[rows, 2 * WIDTH + 128 * pair : 2 * WIDTH + 128 * pair + 128]
                g_pair = mixed_back[rows, 128 * pair : 128 * pair + 128]
                k_turned = k_pair.T
                weights, powers, inverses = [], [], []
                for half in range(2):
                    here = (lane < 64) == (half == 0)
                    k_one = jnp.where(here, k_pair * scale, jnp.zeros_like(k_pair))
                    v_one = jnp.where(here, v_pair, jnp.zeros_like(v_pair))
                    scores = dot_nt(k_one, q_pair)
                    power = jnp.exp(scores - jnp.max(scores, axis=0, keepdims=True))
                    inverses.append(1.0 / jnp.sum(power, axis=0, keepdims=True))
                    head = 2 * pair + half
                    back = dot_nt(v_one, g_pair) - inner[head : head + 1, rows]
                    weights.append((power * back).astype(bf16))
                    powers.append(power.astype(bf16))
                inverse = jnp.where(line < 64, inverses[0], inverses[1])
                q_turned = (q_pair.T.astype(f32) * (inverse * scale)).astype(bf16)
                g_turned = (g_pair.T.astype(f32) * inverse).astype(bf16)
                made = (
                    jnp.where(
                        line < 64, dot_nn(k_turned, weights[0]), dot_nn(k_turned, weights[1])
                    )
                    * (inverse * scale),
                    jnp.where(
                        line < 64, dot_nt(q_turned, weights[0]), dot_nt(q_turned, weights[1])
                    ),
                    jnp.where(
                        line < 64, dot_nt(g_turned, powers[0]), dot_nt(g_turned, powers[1])
                    ),
                )
                for member in range(3):
                    turned[member, 128 * pair : 128 * pair + 128, rows] = made[member].astype(bf16)
        for member in range(3):
            for owner in range(4):
                for odd in range(2):
                    target = qkv_theirs if odd else qkv_mine
                    first = pl.multiple_of(192 * owner + 96 * (core ^ odd), 96)
                    send(turned.at[member, pl.ds(first, 96)], target.at[member, owner ^ chip])
        back = jnp.zeros((tokens, WIDTH), f32)
        ones = jnp.ones((8, tokens), bf16)
        run_all(heads_copies, "wait")
        for member in range(3):
            back = back + lax.dot_general(
                turned[member],
                blocks[member].reshape(WIDTH, WIDTH),
                (((0,), (0,)), ((), ())),
                preferred_element_type=f32,
            )
        sums_ref[0:1] = dot_nt(ones, turned[0])[0:1]
        sums_ref[1:2] = dot_nt(ones, turned[2])[0:1]
        fetches[3].wait()
        unit, root = normalise(hidden_ref[...].astype(f32))
        sums_ref[3:4] = jnp.sum(back * unit, axis=0, keepdims=True)
        sums_ref[4:5] = jnp.sum(back, axis=0, keepdims=True)
        scaled = back * small_ref[SM_G1 : SM_G1 + 1]
        result = grad_ref[...] + root * (
            scaled
            - jnp.mean(scaled, axis=-1, keepdims=True)
            - unit * jnp.mean(scaled * unit, axis=-1, keepdims=True)
        )
        out_ref[...] = result.astype(out_ref.dtype)
        run_all(sent, "wait")
        sent.clear()
        if not last:
            turned[0] = result.astype(bf16).T
            for owner in range(4):
                for odd in range(2):
                    target = low_theirs if odd else low_mine
                    first = pl.multiple_of(192 * owner + 96 * (core ^ odd), 96)
                    send(turned.at[0, pl.ds(first, 96)], target.at[owner ^ chip])

        sums_ref[2:3] = ff_sums_ref[3:4]
        sums_ref[5:8] = ff_sums_ref[0:3]
        fetches[4].wait()
        rest_of = sums_ref[...]
        cut = jnp.zeros((8, 1024), f32)
        for term in range(3):
            term_low = rest_of.astype(bf16)
            rest_of = rest_of - term_low.astype(f32)
            cut = cut + dot_nn(term_low, chosen_ref[...])
        for delta in range(8):
            owner = place_now ^ delta
            target = vec_theirs if delta & 1 else vec_mine
            target[delta >> 1] = jnp.zeros((16, WIDTH // 2), f32)
            target[delta >> 1, 0:8, 0:128] = cut[:, 128 * delta : 128 * delta + 128]
            values = ff_sums_ref[pl.ds(4 + (owner >> 1), 1)]
            target[delta >> 1, 8:9] = jnp.where(
                (owner & 1) == 0, values[:, : WIDTH // 2], values[:, WIDTH // 2 :]
            )
        run_all(sent, "wait")

    shape = jax.ShapeDtypeStruct
    in_vmem = pl.BlockSpec(memory_space=pltpu.VMEM)
    vector_shape = (4, 16, WIDTH // 2)
    out_specs = [in_vmem] + [in_any()] * 2 + [in_vmem] * 2
    out_shape = (
        [shape((tokens, WIDTH), bf16 if last else f32)]
        + [shape((3, 4, 96, tokens), bf16)] * 2
        + [shape(vector_shape, f32)] * 2
    )
    if not last:
        out_specs += [in_any()] * 2
        out_shape += [shape((4, 96, tokens), bf16)] * 2
    return pl.pallas_call(
        kernel,
        in_specs=[in_smem()] + [in_any()] * 5 + [in_vmem] * 2 + [in_any()] * PIECES,
        out_specs=out_specs,
        out_shape=out_shape,
        scratch_shapes=[
            pltpu.VMEM((tokens, WIDTH), grad.dtype),
            pltpu.VMEM((tokens, WIDTH), hidden.dtype),
            pltpu.VMEM((tokens, 3 * WIDTH), bf16),
            pltpu.VMEM((tokens, WIDTH), bf16),
            pltpu.VMEM((WIDTH, 1024), bf16),
            pltpu.VMEM((4, 8, 96, WIDTH), bf16),
            pltpu.VMEM((3, WIDTH, tokens), bf16),
            pltpu.VMEM((8, WIDTH), f32),
            pltpu.SemaphoreType.DMA((2, PIECES)),
            pltpu.SemaphoreType.DMA((5,)),
            pltpu.SemaphoreType.DMA((24,)),
        ],
        compiler_params=pltpu.CompilerParams(vmem_limit_bytes=VMEM_BYTES),
        cost_estimate=cost(0.01),
        name="attn_backward",
    )(place, grad, hidden, qkv, mixed, chosen, small, ff_sums, *pack[0])


def spread(result, owner, rows, out_refs):
    go_x, go_y, stay_x, stay_y = out_refs
    half = WIDTH // 2
    low, high = result[:, :half].astype(bf16), result[:, half:].astype(bf16)
    target, at = ((stay_x, 0), (go_x, 0), (stay_x, 1), (go_x, 1))[owner]
    target[at, rows] = low
    target, at = ((stay_y, 0), (stay_y, 1), (go_y, 0), (go_y, 1))[owner]
    target[at, rows] = high


def travel_shapes(rows_low, rows_high):
    shape = jax.ShapeDtypeStruct
    half = WIDTH // 2
    return [shape((2, rows, half), bf16) for rows in (rows_low, rows_high, rows_low, rows_high)]


def owner_terms(reduce=None, expand=None, merge=None, heads=None, small_terms=None):
    given, in_specs, sections = [], [], []
    rows = 0
    tokens = (reduce or expand or heads)[1][0].shape[0]
    whole = pl.BlockSpec((tokens, WIDTH), lambda at: (0, 0))
    four = pl.BlockSpec((4, 96, tokens), lambda at: (0, 0, 0))
    for name, pair, left, right, taken in (
        ("reduce", reduce, four, pl.BlockSpec((tokens, WIDTH), lambda at: (0, at)), 384),
        ("expand", expand, pl.BlockSpec((1, 384, tokens), lambda at: (at, 0, 0)), whole, 384),
        ("merge", merge, four, whole, 96),
        (
            "heads",
            heads,
            pl.BlockSpec((1, 4, 96, tokens), lambda at: (jnp.minimum(at, 2), 0, 0, 0)),
            whole,
            288,
        ),
    ):
        if pair is not None:
            given += [*pair[0], *pair[1]]
            in_specs += [left, left, right, right]
            sections.append((name, rows))
            rows += taken
    extra = 0
    if small_terms is not None:
        given += small_terms
        in_specs += [pl.BlockSpec(small_terms[0].shape, lambda at: (0, 0, 0))] * 2
        extra = 16

    def kernel(*refs):
        ins, out_refs = refs[: len(given)], refs[len(given) :]
        go_x, go_y, stay_x, stay_y = out_refs
        part = pl.program_id(0)

        def multiply(place, first):
            left_a, left_b, right_a, right_b = ins[4 * place : 4 * place + 4]
            result = dot_nn(left_a[...].reshape(384, tokens), right_a[...]) + dot_nn(
                left_b[...].reshape(384, tokens), right_b[...]
            )
            if first is None:
                return result
            for owner in range(4):
                spread(
                    result[96 * owner : 96 * owner + 96], owner, pl.ds(first, 96), out_refs
                )

        for place, (name, first) in enumerate(sections):
            if name == "reduce":
                multiply(place, pl.multiple_of(first + 96 * part, 96))
            elif name == "heads":

                @pl.when(part < 3)
                def one_head_block():
                    multiply(place, pl.multiple_of(first + 96 * part, 96))

            elif name == "merge":

                @pl.when(part == 3)
                def merge_block():
                    multiply(place, first)

            else:
                result = multiply(place, None)
                for owner in range(4):

                    @pl.when(part == owner)
                    def keep():
                        spread(result, owner, slice(first, first + 384), out_refs)

        if small_terms is not None:

            @pl.when(part == 3)
            def vectors():
                for owner in range(4):
                    target, at = ((stay_x, 0), (go_x, 0), (stay_x, 1), (go_x, 1))[owner]
                    target[at, rows : rows + 16] = (ins[-2][owner] + ins[-1][owner]).astype(bf16)

    half = WIDTH // 2
    heights = (rows + extra, rows, rows + extra, rows)
    return pl.pallas_call(
        kernel,
        grid=(4,),
        in_specs=in_specs,
        out_specs=[pl.BlockSpec((2, height, half), lambda at: (0, 0, 0)) for height in heights],
        out_shape=[jax.ShapeDtypeStruct((2, height, half), bf16) for height in heights],
        compiler_params=params(),
        cost_estimate=cost(0.01),
        name="owner_terms",
    )(*given)


def taken(end_ref, pair, rows, scale):
    total, outward = pair
    part = jnp.where(end_ref[0] == 1, outward[rows], total[rows])
    return part.astype(f32) * scale


def put_halves(target, end_ref, pair, low, high, rows, scale):
    half = WIDTH // 2
    target[:, :half] = taken(end_ref, pair, slice(low, low + rows), scale)
    target[:, half:] = taken(end_ref, pair, slice(high, high + rows), scale)


def in_full():
    return pl.BlockSpec(memory_space=pltpu.VMEM)


def finish_most(at_end, reduce_1, em_1, both_01, scale):
    layers = 2
    half = WIDTH // 2

    def kernel(end_ref, *refs):
        r_pair, em_pair, hr_pair = refs[0:2], refs[2:4], refs[4:6]
        heads_out, merge_out, expand_out, reduce_out, vectors_out = refs[6:11]
        heads, merge, expand, reduce, sems = refs[11:]
        for layer, pair, high in ((0, hr_pair, 688), (1, r_pair, 384)):
            for part in range(FF_PARTS):
                for first, column in ((96 * part, WIDTH * part), (high + 96 * part, WIDTH * part + half)):
                    reduce[layer, :, column : column + half] = taken(
                        end_ref, pair, slice(first, first + 96), scale
                    )
        copies = [pltpu.make_async_copy(reduce, reduce_out, sems.at[0])]
        copies[0].start()
        put_halves(expand, end_ref, em_pair, 0, 480, 384, scale)
        put_halves(merge, end_ref, em_pair, 384, 864, 96, scale)
        for member in range(3):
            put_halves(
                heads.at[member],
                end_ref,
                hr_pair,
                384 + 96 * member,
                688 + 384 + 96 * member,
                96,
                scale,
            )
        last = layers - 1
        copies.append(pltpu.make_async_copy(expand, expand_out.at[last], sems.at[1]))
        copies.append(pltpu.make_async_copy(merge, merge_out.at[last], sems.at[2]))
        copies.append(pltpu.make_async_copy(heads, heads_out.at[last], sems.at[3]))
        run_all(copies[1:], "start")
        vectors_out[...] = taken(end_ref, hr_pair, slice(672, 688), scale)
        run_all(copies, "wait")

    shape = jax.ShapeDtypeStruct
    return pl.pallas_call(
        kernel,
        in_specs=[in_smem()] + [in_full()] * 6,
        out_specs=[in_any()] * 4 + [in_full()],
        out_shape=[
            shape((layers, 3, 96, WIDTH), f32),
            shape((layers, 96, WIDTH), f32),
            shape((layers, 384, WIDTH), f32),
            shape((layers, 96, FF_PARTS * WIDTH), f32),
            shape((16, half), f32),
        ],
        scratch_shapes=[
            pltpu.VMEM((3, 96, WIDTH), f32),
            pltpu.VMEM((96, WIDTH), f32),
            pltpu.VMEM((384, WIDTH), f32),
            pltpu.VMEM((layers, 96, FF_PARTS * WIDTH), f32),
            pltpu.SemaphoreType.DMA((4,)),
        ],
        compiler_params=pltpu.CompilerParams(vmem_limit_bytes=SMALL_VMEM_BYTES),
        cost_estimate=cost(0.01),
        name="finish_most",
    )(at_end, *reduce_1, *em_1, *both_01)


def finish_expand(at_end, em_0, merge_grad, expand_grad, scale):
    def kernel(end_ref, total, outward, merge_in, expand_in, merge_out, expand_out, *rest):
        merge, expand, sems = rest
        put_halves(expand, end_ref, (total, outward), 0, 480, 384, scale)
        put_halves(merge, end_ref, (total, outward), 384, 864, 96, scale)
        copies = [
            pltpu.make_async_copy(expand, expand_out.at[0], sems.at[0]),
            pltpu.make_async_copy(merge, merge_out.at[0], sems.at[1]),
        ]
        run_all(copies, "start")
        run_all(copies, "wait")

    return pl.pallas_call(
        kernel,
        in_specs=[in_smem()] + [in_full()] * 2 + [in_any()] * 2,
        out_specs=[in_any()] * 2,
        out_shape=[jax.ShapeDtypeStruct(a.shape, f32) for a in (merge_grad, expand_grad)],
        scratch_shapes=[
            pltpu.VMEM((96, WIDTH), f32),
            pltpu.VMEM((384, WIDTH), f32),
            pltpu.SemaphoreType.DMA((2,)),
        ],
        input_output_aliases={3: 0, 4: 1},
        compiler_params=pltpu.CompilerParams(vmem_limit_bytes=SMALL_VMEM_BYTES),
        cost_estimate=cost(0.01),
        name="finish_expand",
    )(at_end, *em_0, merge_grad, expand_grad)


def finish_heads(at_end, heads_0, vectors_1, heads_grad, scale):
    def kernel(end_ref, total, outward, vectors_ref, heads_in, heads_out, *rest):
        outs, (heads, sems) = rest[:8], rest[8:]
        for member in range(3):
            put_halves(
                heads.at[member],
                end_ref,
                (total, outward),
                96 * member,
                304 + 96 * member,
                96,
                scale,
            )
        copy = pltpu.make_async_copy(heads, heads_out.at[0], sems.at[0])
        copy.start()
        own = taken(end_ref, (total, outward), slice(288, 304), scale)
        for layer, values in ((0, own), (1, vectors_ref[...])):
            outs[0][layer] = values[0:2, :96]
            for row in range(2, 8):
                outs[row - 1][layer : layer + 1] = values[row : row + 1, :96]
            outs[7][layer : layer + 1] = values[8:9]
        copy.wait()

    shape = jax.ShapeDtypeStruct
    layers = heads_grad.shape[0]
    return pl.pallas_call(
        kernel,
        in_specs=[in_smem()] + [in_full()] * 3 + [in_any()],
        out_specs=[in_any()] + [in_full()] * 8,
        out_shape=[shape(heads_grad.shape, f32), shape((layers, 2, 96), f32)]
        + [shape((layers, 96), f32)] * 6
        + [shape((layers, 384), f32)],
        scratch_shapes=[pltpu.VMEM((3, 96, WIDTH), f32), pltpu.SemaphoreType.DMA((1,))],
        input_output_aliases={4: 0},
        compiler_params=pltpu.CompilerParams(vmem_limit_bytes=SMALL_VMEM_BYTES),
        cost_estimate=cost(0.01),
        name="finish_heads",
    )(at_end, *heads_0, vectors_1, heads_grad)


def shards(
    images,
    cotangent,
    slot_flags,
    heads_weight,
    heads_bias,
    merge_weight,
    merge_bias,
    first_gain,
    first_shift,
    second_gain,
    second_shift,
    expand_weight,
    expand_bias,
    reduce_weight,
    reduce_bias,
):
    micro_count, unused_slots, seq_len, width = images.shape
    layers = heads_weight.shape[0]
    tokens = micro_count * seq_len
    place_at = lax.axis_index("fsdp").astype(jnp.int32)
    place = place_at[None]

    matrices = (heads_weight, merge_weight, expand_weight, reduce_weight)
    vectors = (
        heads_bias,
        merge_bias,
        first_gain,
        first_shift,
        second_gain,
        second_shift,
        reduce_bias,
        expand_bias,
    )
    kinds = [("attn", 0), ("ff", 0), ("attn", 1), ("expand", 1), ("reduce", 1)]
    rows_of = [PACK_ROWS[kind] for kind, layer in kinds]
    cut_of = [PACK_CUTS[kind] for kind, layer in kinds]
    x_rows = [0] + cut_of
    y_rows = [0] + [rows - cut for rows, cut in zip(rows_of, cut_of)]
    count = len(kinds)

    def send_round(at, own_now, x_before, y_before):
        if at == 0:
            return swap_x(own_now), swap_y(own_now)
        rows, cut = rows_of[at - 1], cut_of[at - 1]
        to_x = [(y_before, y_rows[at - 1], cut)]
        to_y = [(x_before, x_rows[at - 1] + cut, rows - cut)]
        if at < count:
            to_x.append((own_now, 0, rows_of[at]))
            to_y.append((own_now, 0, rows_of[at]))
        to_x, to_y = join_rows([to_x, to_y])
        return swap_x(to_x), swap_y(to_y)

    def pack_of(at, own_pair, came):
        (x_0, y_0, cx_0, cy_0), (x_1, y_1, cx_1, cy_1) = came[at], came[at + 1]
        return (
            (own_pair[0], x_0, y_0, x_1, y_1, own_pair[1], cx_0, cy_0, cx_1, cy_1),
            regions_of(rows_of[at], cut_of[at], x_rows[at], y_rows[at]),
        )

    def both(values):
        return tuple(swap_core(value) for value in values)

    hidden = images.reshape(tokens, width)
    seal = lax.optimization_barrier

    came = []
    own = own_packs(kinds[:1], matrices, vectors)
    new = send_round(0, own[0], None, None)
    own_other = both(own)
    own += own_packs(kinds[1:2], matrices, vectors)
    chosen = chosen_columns(place)
    grad, low_mine, low_theirs = start_grad(place, slot_flags, cotangent.reshape(tokens, width))
    own, own_other, new, grad, low_mine, low_theirs, matrices, vectors, chosen = seal(
        (own, own_other, new, grad, low_mine, low_theirs, matrices, vectors, chosen)
    )

    got, new = new, send_round(1, own[1], *new)
    came.append(got + both(got))
    low = (low_mine, swap_core(low_theirs))
    low, matrices = seal((low, matrices))
    own += own_packs(kinds[2:], matrices, vectors)
    own_other += both(own[1:])
    own, own_other, came, new, low, grad = seal((own, own_other, came, new, low, grad))

    got, new = new, send_round(2, own[2], *new)
    came.append(got + both(got))
    pack_a0 = pack_of(0, (own[0], own_other[0]), came)
    small_0, expand_rows_0 = gathered_vectors(place, pack_a0)
    middle_0, normed_0, qkv_0, mixed_0 = attn_forward(place, hidden, small_0, pack_a0)
    own, came, new, small_0, expand_rows_0, middle_0, normed_0, qkv_0, mixed_0 = seal(
        (own, came, new, small_0, expand_rows_0, middle_0, normed_0, qkv_0, mixed_0)
    )

    got, new = new, send_round(3, own[3], *new)
    came.append(got + both(got))
    pack_f0 = pack_of(1, (own[1], own_other[1]), came)
    second_0, active_0, slope_0 = expand_forward(
        place, middle_0, small_0, expand_rows_0, pack_f0, 0
    )
    hidden_1 = reduce_forward(
        place, slot_flags, middle_0, active_0, small_0, pack_f0, 384, False
    )
    others_a0 = both((normed_0, mixed_0))
    own, came, new, second_0, active_0, slope_0, hidden_1, others_a0 = seal(
        (own, came, new, second_0, active_0, slope_0, hidden_1, others_a0)
    )

    got, new = new, send_round(4, own[4], *new)
    came.append(got + both(got))
    pack_a1 = pack_of(2, (own[2], own_other[2]), came)
    small_1, expand_rows_1 = gathered_vectors(place, pack_a1)
    middle_1, normed_1, qkv_1, mixed_1 = attn_forward(place, hidden_1, small_1, pack_a1)
    second_other_0 = swap_core(second_0)
    came, new, small_1, expand_rows_1, middle_1, normed_1, qkv_1, mixed_1, second_other_0 = seal(
        (came, new, small_1, expand_rows_1, middle_1, normed_1, qkv_1, mixed_1, second_other_0)
    )

    got, new = new, send_round(5, None, *new)
    came.append(got + both(got))
    pack_e1 = pack_of(3, (own[3], own_other[3]), came)
    second_1, active_1, slope_1 = expand_forward(
        place, middle_1, small_1, expand_rows_1, pack_e1, 0
    )
    others_a1 = both((normed_1, mixed_1))
    second_1, active_1, slope_1, others_a1, came, new = seal(
        (second_1, active_1, slope_1, others_a1, came, new)
    )
    came.append(new + both(new))
    second_1, active_1, came = seal((second_1, active_1, came))
    pack_e1 = pack_of(3, (own[3], own_other[3]), came)
    pack_r1 = pack_of(4, (own[4], own_other[4]), came)

    grad, pre_mine, pre_theirs, attn_mine, attn_theirs, ff_sums = ff_backward(
        place, grad, slope_1, middle_1, small_1, (pack_e1, 0), (pack_r1, 0)
    )
    others_f1 = both((second_1, active_1))
    made = (grad, pre_mine, pre_theirs, attn_mine, attn_theirs, ff_sums)
    made, others_f1, pack_r1_arrays = seal((made, others_f1, pack_r1[0]))
    grad, pre_mine, pre_theirs, attn_mine, attn_theirs, ff_sums = made
    pack_r1 = (pack_r1_arrays, pack_r1[1])

    travel_r1 = owner_terms(reduce=(low, (active_1, others_f1[1])))
    pre_other, attn_other = both((pre_theirs, attn_theirs))
    travel_r1, pre_other, attn_other, grad = seal((travel_r1, pre_other, attn_other, grad))

    state_r1 = first_steps(travel_r1)
    travel_em1 = owner_terms(
        expand=((pre_mine, pre_other), (second_1, others_f1[0])),
        merge=((attn_mine, attn_other), (mixed_1, others_a1[1])),
    )
    state_r1, travel_em1, grad, active_0 = seal((state_r1, travel_em1, grad, active_0))

    state_r1 = second_steps(state_r1)
    state_em1 = first_steps(travel_em1)
    grad, qkv_mine, qkv_theirs, vec_mine, vec_theirs, low_mine, low_theirs = attn_backward(
        place, grad, hidden_1, qkv_1, mixed_1, small_1, ff_sums, chosen, pack_a1, False
    )
    active_other_0 = swap_core(active_0)
    made = (grad, qkv_mine, qkv_theirs, vec_mine, vec_theirs, low_mine, low_theirs)
    state_r1, state_em1, made, active_other_0 = seal((state_r1, state_em1, made, active_other_0))
    grad, qkv_mine, qkv_theirs, vec_mine, vec_theirs, low_mine, low_theirs = made

    sum_r1 = to_middle(ends(state_r1))
    state_em1 = second_steps(state_em1)
    low_other, qkv_other, vec_other = both((low_theirs, qkv_theirs, vec_theirs))
    travel_hr = owner_terms(
        reduce=((low_mine, low_other), (active_0, active_other_0)),
        heads=((qkv_mine, qkv_other), (normed_1, others_a1[0])),
        small_terms=(vec_mine, vec_other),
    )
    sum_r1, state_em1, travel_hr, grad = seal((sum_r1, state_em1, travel_hr, grad))

    state_hr = first_steps(travel_hr)
    sum_em1 = to_middle(ends(state_em1))
    sum_r1 = across_middle(sum_r1)
    grad, pre_mine, pre_theirs, attn_mine, attn_theirs, ff_sums = ff_backward(
        place, grad, slope_0, middle_0, small_0, (pack_f0, 0), (pack_f0, 384)
    )
    made = (grad, pre_mine, pre_theirs, attn_mine, attn_theirs, ff_sums)
    state_hr, sum_em1, sum_r1, made = seal((state_hr, sum_em1, sum_r1, made))
    grad, pre_mine, pre_theirs, attn_mine, attn_theirs, ff_sums = made

    state_hr = second_steps(state_hr)
    sum_em1 = across_middle(sum_em1)
    pre_other, attn_other = both((pre_theirs, attn_theirs))
    travel_em0 = owner_terms(
        expand=((pre_mine, pre_other), (second_0, second_other_0)),
        merge=((attn_mine, attn_other), (mixed_0, others_a0[1])),
    )
    state_hr, sum_em1, travel_em0, grad = seal((state_hr, sum_em1, travel_em0, grad))

    state_em0 = first_steps(travel_em0)
    sum_hr = to_middle(ends(state_hr))
    final_r1 = to_ends(sum_r1)
    images_grad, qkv_mine, qkv_theirs, vec_mine, vec_theirs = attn_backward(
        place, grad, hidden, qkv_0, mixed_0, small_0, ff_sums, chosen, pack_a0, True
    )
    made = (images_grad, qkv_mine, qkv_theirs, vec_mine, vec_theirs)
    state_em0, sum_hr, final_r1, sum_em1, made = seal(
        (state_em0, sum_hr, final_r1, sum_em1, made)
    )
    images_grad, qkv_mine, qkv_theirs, vec_mine, vec_theirs = made

    state_em0 = second_steps(state_em0)
    sum_hr = across_middle(sum_hr)
    final_em1 = to_ends(sum_em1)
    qkv_other, vec_other = both((qkv_theirs, vec_theirs))
    travel_h0 = owner_terms(
        heads=((qkv_mine, qkv_other), (normed_0, others_a0[0])), small_terms=(vec_mine, vec_other)
    )
    state_em0, travel_h0, final_em1, middle_1, active_1 = seal(
        (state_em0, travel_h0, final_em1, middle_1, active_1)
    )

    state_h0 = first_steps(travel_h0)
    sum_em0 = to_middle(ends(state_em0))
    state_h0, sum_hr = seal((state_h0, sum_hr))

    state_h0 = second_steps(state_h0)
    final_hr = to_ends(sum_hr)
    state_h0, sum_em0, middle_1, active_1 = seal((state_h0, sum_em0, middle_1, active_1))
    sum_h0 = to_middle(ends(state_h0))
    sum_em0 = across_middle(sum_em0)
    outputs = reduce_forward(
        place, slot_flags, middle_1, active_1, small_1, pack_r1, 0, True
    ).reshape(images.shape)
    sum_h0, final_hr, sum_em0, outputs = seal((sum_h0, final_hr, sum_em0, outputs))
    sum_h0 = across_middle(sum_h0)
    final_em0 = to_ends(sum_em0)
    final_h0 = to_ends(sum_h0)

    images_grad = images_grad.reshape(images.shape)
    grad_scale = (
        micro_count * images.shape[1] * lax.axis_size("fsdp") * lax.axis_size("rep") * seq_len
    ) ** (-0.5)
    rep_at = lax.axis_index("rep")
    at_end = ((rep_at == 0) | (rep_at == lax.axis_size("rep") - 1)).astype(jnp.int32)[None]
    heads_grad, merge_grad, expand_grad, reduce_grad, vectors_1 = finish_most(
        at_end, final_r1, final_em1, final_hr, grad_scale
    )
    merge_grad, expand_grad = finish_expand(at_end, final_em0, merge_grad, expand_grad, grad_scale)
    heads_grad, *vector_grads = finish_heads(at_end, final_h0, vectors_1, heads_grad, grad_scale)
    return (
        outputs,
        images_grad,
        heads_grad,
        vector_grads[0],
        merge_grad,
        *vector_grads[1:6],
        expand_grad,
        vector_grads[7],
        reduce_grad,
        vector_grads[6],
    )


def solution(mesh):
    body = shards if (mesh.shape["fsdp"], mesh.shape["rep"]) == (8, 4) else plain_shards
    placed = (
        P(None, ("fsdp", "rep"), None, None),
        P(None, ("fsdp", "rep"), None, None),
        P(None, ("fsdp", "rep")),
        P(None, None, "fsdp", None),
        P(None, None, "fsdp"),
        P(None, "fsdp", None),
        P(None, "fsdp"),
        P(None, "fsdp"),
        P(None, "fsdp"),
        P(None, "fsdp"),
        P(None, "fsdp"),
        P(None, "fsdp", None),
        P(None, "fsdp"),
        P(None, "fsdp", None),
        P(None, "fsdp"),
    )
    return jax.shard_map(
        body,
        mesh=mesh,
        in_specs=placed,
        out_specs=(
            P(None, ("fsdp", "rep"), None, None),
            P(None, ("fsdp", "rep"), None, None),
            P(None, None, "fsdp", None),
            P(None, None, "fsdp"),
            P(None, "fsdp", None),
            P(None, "fsdp"),
            P(None, "fsdp"),
            P(None, "fsdp"),
            P(None, "fsdp"),
            P(None, "fsdp"),
            P(None, "fsdp", None),
            P(None, "fsdp"),
            P(None, "fsdp", None),
            P(None, "fsdp"),
        ),
        check_vma=False,
    )
```

```python
import jax
import jax.numpy as jnp
from jax import lax
from jax.experimental import pallas as pl
from jax.experimental.pallas import tpu as pltpu
from jax.sharding import PartitionSpec as P

HEADS = 12
HEAD_DIM = 64


norm_eps = 1e-06


def layer_norm(token_rows, scale_row, offset_row):
    centre = token_rows - jnp.mean(token_rows, axis=-1, keepdims=True)
    spread = jnp.mean(centre * centre, axis=-1, keepdims=True)
    return centre * lax.rsqrt(spread + norm_eps) * scale_row + offset_row


def project(token_rows, weight):
    return lax.dot_general(
        token_rows, weight, (((1,), (1,)), ((), ())), preferred_element_type=jnp.float32
    )


def outer_sum(grad_rows, token_rows):
    return lax.dot_general(
        grad_rows, token_rows, (((0,), (0,)), ((), ())), preferred_element_type=jnp.float32
    )


def carry_back(grad_rows, weight):
    return jnp.dot(grad_rows, weight, preferred_element_type=jnp.float32)


def forward_layer(hidden, params):
    (
        heads_weight,
        heads_bias,
        merge_weight,
        merge_bias,
        first_gain,
        first_shift,
        second_gain,
        second_shift,
        expand_weight,
        expand_bias,
        reduce_weight,
        reduce_bias,
    ) = params
    seq_len, model_width = hidden.shape
    shaped = (seq_len, HEADS, HEAD_DIM)
    score_scale = HEAD_DIM ** (-0.5)
    normed = layer_norm(
        hidden, first_gain.astype(jnp.float32), first_shift.astype(jnp.float32)
    ).astype(jnp.bfloat16)
    queries = (project(normed, heads_weight[0]) + heads_bias[0].astype(jnp.float32)).astype(
        jnp.bfloat16
    )
    key_rows = project(normed, heads_weight[1]).astype(jnp.bfloat16)
    values = (project(normed, heads_weight[2]) + heads_bias[1].astype(jnp.float32)).astype(
        jnp.bfloat16
    )
    scores = (
        jnp.einsum(
            "qhd,khd->hqk",
            queries.reshape(shaped),
            key_rows.reshape(shaped),
            preferred_element_type=jnp.float32,
        )
        * score_scale
    )
    row_peak = jnp.max(scores, axis=-1, keepdims=True)
    exponent = jnp.exp(scores - row_peak)
    row_total = jnp.sum(exponent, axis=-1, keepdims=True)
    attend = exponent / row_total
    log_total = row_peak + jnp.log(row_total)
    mixed_rows = jnp.einsum(
        "hqk,khd->qhd",
        attend.astype(jnp.bfloat16),
        values.reshape(shaped),
        preferred_element_type=jnp.float32,
    )
    mixed_rows = mixed_rows.reshape(seq_len, model_width).astype(jnp.bfloat16)
    middle = hidden + (project(mixed_rows, merge_weight) + merge_bias.astype(jnp.float32))
    second = layer_norm(
        middle, second_gain.astype(jnp.float32), second_shift.astype(jnp.float32)
    ).astype(jnp.bfloat16)
    pre_act = project(second, expand_weight) + expand_bias.astype(jnp.float32)
    activated = jax.nn.gelu(pre_act, approximate=True).astype(jnp.bfloat16)
    result = middle + (project(activated, reduce_weight) + reduce_bias.astype(jnp.float32))
    saved = (
        hidden,
        normed,
        queries,
        key_rows,
        values,
        log_total,
        mixed_rows,
        middle,
        second,
        pre_act,
        activated,
    )
    return (result, saved)


def backward_layer(grad_out, params, saved):
    (
        heads_weight,
        heads_bias,
        merge_weight,
        merge_bias,
        first_gain,
        first_shift,
        second_gain,
        second_shift,
        expand_weight,
        expand_bias,
        reduce_weight,
        reduce_bias,
    ) = params
    (
        hidden,
        normed,
        queries,
        key_rows,
        values,
        log_total,
        mixed_rows,
        middle,
        second,
        pre_act,
        activated,
    ) = saved
    seq_len, model_width = hidden.shape
    shaped = (seq_len, HEADS, HEAD_DIM)
    score_scale = HEAD_DIM ** (-0.5)
    branch_low = grad_out.astype(jnp.bfloat16)
    reduce_weight_term = outer_sum(branch_low, activated)
    reduce_bias_term = jnp.sum(branch_low.astype(jnp.float32), axis=0)
    grad_act = carry_back(branch_low, reduce_weight)
    unused_value, gelu_back = jax.vjp(lambda point: jax.nn.gelu(point, approximate=True), pre_act)
    grad_pre = gelu_back(grad_act)[0].astype(jnp.bfloat16)
    expand_weight_term = outer_sum(grad_pre, second)
    expand_bias_term = jnp.sum(grad_pre.astype(jnp.float32), axis=0)
    grad_second = carry_back(grad_pre, expand_weight)
    unused_norm, second_back = jax.vjp(
        layer_norm, middle, second_gain.astype(jnp.float32), second_shift.astype(jnp.float32)
    )
    middle_part, second_gain_term, second_shift_term = second_back(grad_second)
    grad_middle = grad_out + middle_part
    attn_low = grad_middle.astype(jnp.bfloat16)
    merge_weight_term = outer_sum(attn_low, mixed_rows)
    merge_bias_term = jnp.sum(attn_low.astype(jnp.float32), axis=0)
    grad_mixed = carry_back(attn_low, merge_weight).astype(jnp.bfloat16).reshape(shaped)
    queries_heads = queries.reshape(shaped)
    keys_heads = key_rows.reshape(shaped)
    values_heads = values.reshape(shaped)
    scores = (
        jnp.einsum("qhd,khd->hqk", queries_heads, keys_heads, preferred_element_type=jnp.float32)
        * score_scale
    )
    attend = jnp.exp(scores - log_total)
    grad_values = jnp.einsum(
        "hqk,qhd->khd", attend.astype(jnp.bfloat16), grad_mixed, preferred_element_type=jnp.float32
    ).astype(jnp.bfloat16)
    grad_attend = jnp.einsum(
        "qhd,khd->hqk", grad_mixed, values_heads, preferred_element_type=jnp.float32
    )
    grad_scores = attend * (grad_attend - jnp.sum(grad_attend * attend, axis=-1, keepdims=True))
    grad_scores = grad_scores.astype(jnp.bfloat16)
    grad_queries = (
        jnp.einsum("hqk,khd->qhd", grad_scores, keys_heads, preferred_element_type=jnp.float32)
        * score_scale
    ).astype(jnp.bfloat16)
    grad_keys = (
        jnp.einsum("hqk,qhd->khd", grad_scores, queries_heads, preferred_element_type=jnp.float32)
        * score_scale
    ).astype(jnp.bfloat16)
    stacked_grads = jnp.stack(
        [
            grad_queries.reshape(seq_len, model_width),
            grad_keys.reshape(seq_len, model_width),
            grad_values.reshape(seq_len, model_width),
        ]
    )
    heads_weight_term = jnp.einsum(
        "jto,ti->joi", stacked_grads, normed, preferred_element_type=jnp.float32
    )
    grad_normed = jnp.einsum(
        "jto,joi->ti", stacked_grads, heads_weight, preferred_element_type=jnp.float32
    )
    heads_bias_term = jnp.stack(
        [
            jnp.sum(stacked_grads[0].astype(jnp.float32), axis=0),
            jnp.sum(stacked_grads[2].astype(jnp.float32), axis=0),
        ]
    )
    unused_first, first_back = jax.vjp(
        layer_norm, hidden, first_gain.astype(jnp.float32), first_shift.astype(jnp.float32)
    )
    hidden_part, first_gain_term, first_shift_term = first_back(grad_normed)
    grad_hidden = grad_middle + hidden_part
    terms = (
        heads_weight_term,
        heads_bias_term,
        merge_weight_term,
        merge_bias_term,
        first_gain_term,
        first_shift_term,
        second_gain_term,
        second_shift_term,
        expand_weight_term,
        expand_bias_term,
        reduce_weight_term,
        reduce_bias_term,
    )
    return (grad_hidden, terms)


def plain_shards(
    images,
    cotangent,
    slot_flags,
    heads_weight,
    heads_bias,
    merge_weight,
    merge_bias,
    first_gain,
    first_shift,
    second_gain,
    second_shift,
    expand_weight,
    expand_bias,
    reduce_weight,
    reduce_bias,
):
    micro_count = images.shape[0]
    seq_len = images.shape[2]
    layers = heads_weight.shape[0]
    live_flags = slot_flags.astype(jnp.float32)
    states = [images[batch_at, 0].astype(jnp.float32) for batch_at in range(micro_count)]
    saved_all = []
    for layer_at in range(layers):
        saved_row = []
        for batch_at in range(micro_count):
            params = (
                lax.all_gather(heads_weight[layer_at], "fsdp", axis=1, tiled=True),
                lax.all_gather(heads_bias[layer_at], "fsdp", axis=1, tiled=True),
                lax.all_gather(merge_weight[layer_at], "fsdp", axis=0, tiled=True),
                lax.all_gather(merge_bias[layer_at], "fsdp", axis=0, tiled=True),
                lax.all_gather(first_gain[layer_at], "fsdp", axis=0, tiled=True),
                lax.all_gather(first_shift[layer_at], "fsdp", axis=0, tiled=True),
                lax.all_gather(second_gain[layer_at], "fsdp", axis=0, tiled=True),
                lax.all_gather(second_shift[layer_at], "fsdp", axis=0, tiled=True),
                lax.all_gather(expand_weight[layer_at], "fsdp", axis=0, tiled=True),
                lax.all_gather(expand_bias[layer_at], "fsdp", axis=0, tiled=True),
                lax.all_gather(reduce_weight[layer_at], "fsdp", axis=0, tiled=True),
                lax.all_gather(reduce_bias[layer_at], "fsdp", axis=0, tiled=True),
            )
            states[batch_at], saved = forward_layer(states[batch_at], params)
            saved_row.append(saved)
        saved_all.append(saved_row)
    outputs = jnp.stack(
        [live_flags[batch_at, 0] * states[batch_at] for batch_at in range(micro_count)]
    )[:, None].astype(jnp.bfloat16)
    grads_back = [
        cotangent[batch_at, 0].astype(jnp.float32) * live_flags[batch_at, 0]
        for batch_at in range(micro_count)
    ]
    collected = [None] * layers
    for layer_at in reversed(range(layers)):
        totals = None
        for batch_at in range(micro_count):
            params = (
                lax.all_gather(heads_weight[layer_at], "fsdp", axis=1, tiled=True),
                lax.all_gather(heads_bias[layer_at], "fsdp", axis=1, tiled=True),
                lax.all_gather(merge_weight[layer_at], "fsdp", axis=0, tiled=True),
                lax.all_gather(merge_bias[layer_at], "fsdp", axis=0, tiled=True),
                lax.all_gather(first_gain[layer_at], "fsdp", axis=0, tiled=True),
                lax.all_gather(first_shift[layer_at], "fsdp", axis=0, tiled=True),
                lax.all_gather(second_gain[layer_at], "fsdp", axis=0, tiled=True),
                lax.all_gather(second_shift[layer_at], "fsdp", axis=0, tiled=True),
                lax.all_gather(expand_weight[layer_at], "fsdp", axis=0, tiled=True),
                lax.all_gather(expand_bias[layer_at], "fsdp", axis=0, tiled=True),
                lax.all_gather(reduce_weight[layer_at], "fsdp", axis=0, tiled=True),
                lax.all_gather(reduce_bias[layer_at], "fsdp", axis=0, tiled=True),
            )
            grads_back[batch_at], terms = backward_layer(
                grads_back[batch_at], params, saved_all[layer_at][batch_at]
            )
            if totals is None:
                totals = terms
            else:
                totals = tuple((earlier + current for earlier, current in zip(totals, terms)))
        collected[layer_at] = totals
    images_grad = jnp.stack(grads_back)[:, None].astype(jnp.bfloat16)
    stacked = [
        jnp.stack([collected[layer_at][member] for layer_at in range(layers)])
        for member in range(12)
    ]
    shares = (
        lax.psum_scatter(
            stacked[0].astype(jnp.bfloat16), "fsdp", scatter_dimension=2, tiled=True
        ).astype(jnp.float32),
        lax.psum_scatter(
            stacked[1].astype(jnp.bfloat16), "fsdp", scatter_dimension=2, tiled=True
        ).astype(jnp.float32),
        lax.psum_scatter(
            stacked[2].astype(jnp.bfloat16), "fsdp", scatter_dimension=1, tiled=True
        ).astype(jnp.float32),
        lax.psum_scatter(
            stacked[3].astype(jnp.bfloat16), "fsdp", scatter_dimension=1, tiled=True
        ).astype(jnp.float32),
        lax.psum_scatter(
            stacked[4].astype(jnp.bfloat16), "fsdp", scatter_dimension=1, tiled=True
        ).astype(jnp.float32),
        lax.psum_scatter(
            stacked[5].astype(jnp.bfloat16), "fsdp", scatter_dimension=1, tiled=True
        ).astype(jnp.float32),
        lax.psum_scatter(
            stacked[6].astype(jnp.bfloat16), "fsdp", scatter_dimension=1, tiled=True
        ).astype(jnp.float32),
        lax.psum_scatter(
            stacked[7].astype(jnp.bfloat16), "fsdp", scatter_dimension=1, tiled=True
        ).astype(jnp.float32),
        lax.psum_scatter(
            stacked[8].astype(jnp.bfloat16), "fsdp", scatter_dimension=1, tiled=True
        ).astype(jnp.float32),
        lax.psum_scatter(
            stacked[9].astype(jnp.bfloat16), "fsdp", scatter_dimension=1, tiled=True
        ).astype(jnp.float32),
        lax.psum_scatter(
            stacked[10].astype(jnp.bfloat16), "fsdp", scatter_dimension=1, tiled=True
        ).astype(jnp.float32),
        lax.psum_scatter(
            stacked[11].astype(jnp.bfloat16), "fsdp", scatter_dimension=1, tiled=True
        ).astype(jnp.float32),
    )
    reduced = (
        lax.psum(shares[0].astype(jnp.bfloat16), "rep").astype(jnp.float32),
        lax.psum(shares[1].astype(jnp.bfloat16), "rep").astype(jnp.float32),
        lax.psum(shares[2].astype(jnp.bfloat16), "rep").astype(jnp.float32),
        lax.psum(shares[3].astype(jnp.bfloat16), "rep").astype(jnp.float32),
        lax.psum(shares[4].astype(jnp.bfloat16), "rep").astype(jnp.float32),
        lax.psum(shares[5].astype(jnp.bfloat16), "rep").astype(jnp.float32),
        lax.psum(shares[6].astype(jnp.bfloat16), "rep").astype(jnp.float32),
        lax.psum(shares[7].astype(jnp.bfloat16), "rep").astype(jnp.float32),
        lax.psum(shares[8].astype(jnp.bfloat16), "rep").astype(jnp.float32),
        lax.psum(shares[9].astype(jnp.bfloat16), "rep").astype(jnp.float32),
        lax.psum(shares[10].astype(jnp.bfloat16), "rep").astype(jnp.float32),
        lax.psum(shares[11].astype(jnp.bfloat16), "rep").astype(jnp.float32),
    )
    grad_scale = (micro_count * lax.axis_size("fsdp") * lax.axis_size("rep") * seq_len) ** (-0.5)
    finals = tuple((member_sum * grad_scale for member_sum in reduced))
    return (outputs, images_grad) + finals


ROWS = 256
WIDTH = 768
FF_PARTS = 4
f32 = jnp.float32
bf16 = jnp.bfloat16
VMEM_BYTES = 52 * 1024 * 1024
SMALL_VMEM_BYTES = 24 * 1024 * 1024
LARGE_VMEM_BYTES = 60 * 1024 * 1024


def dot_nt(left, right):
    return lax.dot_general(left, right, (((1,), (1,)), ((), ())), preferred_element_type=f32)


def dot_nn(left, right):
    return lax.dot_general(left, right, (((1,), (0,)), ((), ())), preferred_element_type=f32)


def swap_core(value):
    return lax.ppermute(value, "fsdp", [(at, at ^ 1) for at in range(8)])


def swap_x(value):
    return lax.ppermute(value, "fsdp", [(at, at ^ 2) for at in range(8)])


def swap_y(value):
    return lax.ppermute(value, "fsdp", [(at, at ^ 4) for at in range(8)])


PIECES = 10


def regions_of(rows, cut, x_row, y_row):
    return [
        region
        for odd in range(2)
        for region in (
            (5 * odd, odd, 0, rows, 0),
            (5 * odd + 1, 2 ^ odd, 0, rows, x_row),
            (5 * odd + 2, 4 ^ odd, 0, rows, y_row),
            (5 * odd + 3, 6 ^ odd, 0, cut, 0),
            (5 * odd + 4, 6 ^ odd, cut, rows, 0),
        )
    ]


def block_copies(place, refs, regions, first, count, block, sems):
    copies = []
    for array_at, delta, low, high, start in regions:
        begin, end = max(low, first), min(high, first + count)
        if begin < end:
            copies.append(
                pltpu.make_async_copy(
                    refs[array_at].at[pl.ds(start + begin - low, end - begin)],
                    block.at[place ^ delta, pl.ds(begin - first, end - begin)],
                    sems.at[len(copies)],
                )
            )
    return copies


def run_all(copies, what):
    for copy in copies:
        getattr(copy, what)()


def in_any():
    return pl.BlockSpec(memory_space=pltpu.HBM)


def in_smem():
    return pl.BlockSpec(memory_space=pltpu.SMEM)


def params(steps=1):
    return pltpu.CompilerParams(
        dimension_semantics=("arbitrary",) * steps, vmem_limit_bytes=VMEM_BYTES
    )


def cost(micros):
    return pl.CostEstimate(flops=int(micros * 1.1e9), bytes_accessed=1 << 10, transcendentals=0)


def rows_spec(width):
    return pl.BlockSpec((ROWS, width), lambda image: (image, 0))


def part_spec(tokens):
    return pl.BlockSpec((tokens, WIDTH), lambda part: (0, part))


def fixed(shape):
    return pl.BlockSpec(shape, lambda image: (0,) * len(shape))


def normalise(rows):
    centre = rows - jnp.mean(rows, axis=-1, keepdims=True)
    root = lax.rsqrt(jnp.mean(centre * centre, axis=-1, keepdims=True) + norm_eps)
    return centre * root, root


PACK_ROWS = {"attn": 400, "ff": 768, "expand": 384, "reduce": 384}
PACK_CUTS = {"attn": 192, "ff": 384, "expand": 192, "reduce": 192}


def own_packs(wanted, matrices, vectors, first=False):
    count = len(wanted)
    needed = [
        at
        for at, users in enumerate(
            (("attn",), ("attn",), ("ff", "expand"), ("ff", "reduce"))
        )
        if any(kind in users for kind, layer in wanted)
    ]

    def kernel(*refs):
        heads_ref, merge_ref, expand_ref, reduce_ref = (
            refs[needed.index(at)] if at in needed else None for at in range(4)
        )
        vector_refs = refs[len(needed) : len(needed) + 8]
        outs, rows = refs[len(needed) + 8 : -1], refs[-1]
        for out, (kind, layer) in zip(outs, wanted):
            if kind == "attn":
                for at in range(3):
                    out[96 * at : 96 * at + 96] = heads_ref[layer, at]
                out[288:384] = merge_ref[layer]
                rows[...] = jnp.zeros_like(rows)
                rows[0:2, 0:96] = vector_refs[0][layer].astype(f32)
                for row in range(2, 8):
                    values = vector_refs[row - 1][...].astype(f32)
                    rows[row : row + 1, 0:96] = values[layer : layer + 1]
                rows[8:9, 0:384] = vector_refs[7][...].astype(f32)[layer : layer + 1]
                out[384:400] = rows[...].astype(bf16)
            if kind in ("ff", "expand"):
                out[0:384] = expand_ref[layer]
            if kind in ("ff", "reduce"):
                first = 384 if kind == "ff" else 0
                for part in range(FF_PARTS):
                    out[first + 96 * part : first + 96 * part + 96] = reduce_ref[
                        layer, :, WIDTH * part : WIDTH * (part + 1)
                    ]

    in_vmem = pl.BlockSpec(memory_space=pltpu.VMEM)
    return pl.pallas_call(
        kernel,
        in_specs=[in_vmem] * (len(needed) + 8),
        out_specs=[in_vmem] * count,
        out_shape=[
            jax.ShapeDtypeStruct((PACK_ROWS[kind], WIDTH), bf16) for kind, layer in wanted
        ],
        scratch_shapes=[pltpu.VMEM((16, WIDTH), f32)],
        compiler_params=pltpu.CompilerParams(vmem_limit_bytes=LARGE_VMEM_BYTES if first else SMALL_VMEM_BYTES),
        cost_estimate=cost(0.01),
        name="own_packs",
    )(*[matrices[at] for at in needed], *vectors)


def join_rows(pieces_of):
    flat = [piece for pieces in pieces_of for piece in pieces]
    heights = [sum(rows for unused, unused_first, rows in pieces) for pieces in pieces_of]

    def kernel(*refs):
        ins, outs, sems = refs[: len(flat)], refs[len(flat) : -1], refs[-1]
        copies = []
        for out, pieces in zip(outs, pieces_of):
            into = 0
            for unused, first, rows in pieces:
                at = len(copies)
                copies.append(
                    pltpu.make_async_copy(
                        ins[at].at[pl.ds(first, rows)], out.at[pl.ds(into, rows)], sems.at[at]
                    )
                )
                into += rows
        run_all(copies, "start")
        run_all(copies, "wait")

    return pl.pallas_call(
        kernel,
        in_specs=[in_any()] * len(flat),
        out_specs=[pl.BlockSpec(memory_space=pltpu.VMEM)] * len(heights),
        out_shape=[jax.ShapeDtypeStruct((rows, WIDTH), bf16) for rows in heights],
        scratch_shapes=[pltpu.SemaphoreType.DMA((len(flat),))],
        compiler_params=pltpu.CompilerParams(vmem_limit_bytes=SMALL_VMEM_BYTES),
        cost_estimate=cost(0.01),
        name="join_rows",
    )(*[array for array, unused, unused_rows in flat])


def gathered_vectors(place, pack):
    arrays, regions = pack
    used = {}
    for array_at, delta, low, high, start in regions:
        if low <= 384 and 400 <= high:
            used[delta] = (arrays[array_at], start + 384 - low)
    deltas = sorted(used)

    def kernel(place_ref, *refs):
        ins, small_ref, expand_ref, rows, sems = refs[:8], refs[8], refs[9], refs[10], refs[11]
        copies = [
            pltpu.make_async_copy(
                ins[at].at[pl.ds(used[delta][1], 16)], rows.at[at], sems.at[at]
            )
            for at, delta in enumerate(deltas)
        ]
        run_all(copies, "start")
        here = place_ref[0]
        row = lax.broadcasted_iota(jnp.int32, (1024, WIDTH), 0)
        column = lax.broadcasted_iota(jnp.int32, (1024, WIDTH), 1)
        at = row & 127
        wanted = 96 * ((row >> 7) ^ here) + at
        chosen = jnp.where((column == wanted) & (at < 96), 1.0, 0.0).astype(bf16)
        run_all(copies, "wait")
        flat = jnp.concatenate([rows[at, 0:8, 0:128].astype(f32) for at in range(8)], axis=1)
        small_ref[...] = dot_nn(flat.astype(bf16), chosen)
        for at, delta in enumerate(deltas):
            owner = here ^ delta
            line = rows[at].astype(f32)[8:9, 0:384]

            @pl.when((owner & 1) == 0)
            def left():
                expand_ref[owner >> 1, :, 0:384] = line

            @pl.when((owner & 1) == 1)
            def right():
                expand_ref[owner >> 1, :, 384:768] = line

    shape = jax.ShapeDtypeStruct
    return pl.pallas_call(
        kernel,
        in_specs=[in_smem()] + [in_any()] * 8,
        out_specs=[pl.BlockSpec(memory_space=pltpu.VMEM)] * 2,
        out_shape=[shape((8, WIDTH), f32), shape((4, 1, WIDTH), f32)],
        scratch_shapes=[pltpu.VMEM((8, 16, WIDTH), bf16), pltpu.SemaphoreType.DMA((8,))],
        compiler_params=pltpu.CompilerParams(vmem_limit_bytes=SMALL_VMEM_BYTES),
        cost_estimate=cost(0.01),
        name="gathered_vectors",
    )(place, *[used[delta][0] for delta in deltas])


def elementwise(name, body, ins, out_shapes):
    def kernel(*refs):
        body(refs[: len(ins)], refs[len(ins) :])

    return pl.pallas_call(
        kernel,
        in_specs=[pl.BlockSpec(memory_space=pltpu.VMEM)] * len(ins),
        out_specs=[pl.BlockSpec(memory_space=pltpu.VMEM)] * len(out_shapes),
        out_shape=[jax.ShapeDtypeStruct(shape, bf16) for shape in out_shapes],
        compiler_params=pltpu.CompilerParams(vmem_limit_bytes=SMALL_VMEM_BYTES),
        cost_estimate=cost(0.01),
        name=name,
    )(*ins)


def add_low(*parts):
    total = parts[0].astype(f32)
    for part in parts[1:]:
        total = total + part.astype(f32)
    return total.astype(bf16)


def first_steps(travel):
    go_x, go_y, stay_x, stay_y = travel
    return swap_x(go_x), swap_y(go_y), stay_x, stay_y


def second_steps(state):
    def body(ins, outs):
        from_x, from_y, stay_x, stay_y = ins
        outs[0][...] = add_low(stay_x[1], from_x[1])
        outs[1][...] = add_low(stay_y[1], from_y[1])
        outs[2][...] = add_low(stay_x[0], from_x[0])
        outs[3][...] = add_low(stay_y[0], from_y[0])

    low, high = state[0].shape[1:], state[1].shape[1:]
    low_on, high_on, kept_low, kept_high = elementwise(
        "second_steps", body, state, [low, high, low, high]
    )
    return swap_y(low_on), swap_x(high_on), kept_low, kept_high


def ends(state):
    from_y, from_x, kept_low, kept_high = state
    low, high = kept_low.shape[0], kept_high.shape[0]

    def body(ins, outs):
        outs[0][0:low] = add_low(ins[2][...], ins[0][...])
        outs[0][low : low + high] = add_low(ins[3][...], ins[1][...])

    return elementwise("ends", body, state, [(low + high, WIDTH // 2)])[0]


def to_middle(part):
    return part, lax.ppermute(part, "rep", [(0, 1), (3, 2)])


def plus(parts):
    def body(ins, outs):
        outs[0][...] = add_low(ins[0][...], ins[1][...])

    return elementwise("plus", body, parts, [parts[0].shape])[0]


def across_middle(parts):
    inward = plus(parts)
    return inward, lax.ppermute(inward, "rep", [(1, 2), (2, 1)])


def to_ends(parts):
    total = plus(parts)
    return total, lax.ppermute(total, "rep", [(1, 0), (2, 3)])


SM_HB0, SM_HB1, SM_MB, SM_G1, SM_S1, SM_G2, SM_S2, SM_RB = range(8)


def unit_copies(place, refs, regions, first, blocks, sems):
    copies = []
    count = 96 * blocks.shape[0]
    for array_at, delta, low, high, start in regions:
        begin, end = max(low, first), min(high, first + count)
        if begin < end:
            units = (end - begin) // 96
            source = refs[array_at].at[pl.ds(start + begin - low, end - begin)]
            copies.append(
                pltpu.make_async_copy(
                    source.reshape(units, 96, WIDTH),
                    blocks.at[pl.ds((begin - first) // 96, units), place ^ delta],
                    sems.at[len(copies)],
                )
            )
    return copies


def attn_forward(place, hidden, small, pack):

    def kernel(place_ref, hidden_ref, small_ref, *rest):
        packs = rest[:PIECES]
        middle_ref, normed_ref, qkv_ref, mixed_ref, blocks, sems = rest[PIECES:]
        place_now = place_ref[0]
        image = pl.program_id(0)
        copies = unit_copies(place_now, packs, pack[1], 0, blocks, sems)

        @pl.when(image == 0)
        def begin():
            run_all(copies, "start")

        rows = hidden_ref[...].astype(f32)
        unit, root = normalise(rows)
        normed = (unit * small_ref[SM_G1 : SM_G1 + 1] + small_ref[SM_S1 : SM_S1 + 1]).astype(bf16)
        normed_ref[...] = normed

        @pl.when(image == 0)
        def arrive():
            run_all(copies, "wait")

        for member, bias in ((0, SM_HB0), (1, None), (2, SM_HB1)):
            block = blocks[member].reshape(WIDTH, WIDTH)
            made = dot_nt(normed, block)
            if bias is not None:
                made = made + small_ref[bias : bias + 1]
            qkv_ref[:, WIDTH * member : WIDTH * (member + 1)] = made.astype(bf16)
        lane = lax.broadcasted_iota(jnp.int32, (ROWS, 128), 1)
        for pair in range(HEADS // 2):
            q_pair = qkv_ref[:, 128 * pair : 128 * pair + 128] * HEAD_DIM**-0.5
            k_pair = qkv_ref[:, WIDTH + 128 * pair : WIDTH + 128 * pair + 128]
            v_pair = qkv_ref[:, 2 * WIDTH + 128 * pair : 2 * WIDTH + 128 * pair + 128]
            parts = []
            for half in range(2):
                here = (lane < 64) == (half == 0)
                scores = dot_nt(jnp.where(here, q_pair, jnp.zeros_like(q_pair)), k_pair)
                peak = jnp.max(scores, axis=-1, keepdims=True)
                powers = jnp.exp(scores - peak).astype(bf16)
                parts.append(dot_nn(powers, jnp.where(here, v_pair, jnp.ones_like(v_pair))))
            totals = pltpu.roll(jnp.where(lane < 64, parts[1], parts[0]), 64, 1)
            mixed_ref[:, 128 * pair : 128 * pair + 128] = (
                jnp.where(lane < 64, parts[0], parts[1]) / totals
            ).astype(bf16)
        merged = dot_nt(mixed_ref[...], blocks[3].reshape(WIDTH, WIDTH))
        middle_ref[...] = rows + (merged + small_ref[SM_MB : SM_MB + 1])

    tokens = hidden.shape[0]
    shape = jax.ShapeDtypeStruct
    return pl.pallas_call(
        kernel,
        grid=(tokens // ROWS,),
        in_specs=[in_smem(), rows_spec(WIDTH), fixed(small.shape)] + [in_any()] * PIECES,
        out_specs=[rows_spec(WIDTH), rows_spec(WIDTH), rows_spec(3 * WIDTH), rows_spec(WIDTH)],
        out_shape=[
            shape((tokens, WIDTH), f32),
            shape((tokens, WIDTH), bf16),
            shape((tokens, 3 * WIDTH), bf16),
            shape((tokens, WIDTH), bf16),
        ],
        scratch_shapes=[
            pltpu.VMEM((4, 8, 96, WIDTH), bf16),
            pltpu.SemaphoreType.DMA((PIECES,)),
        ],
        compiler_params=params(),
        cost_estimate=cost(0.01),
        name="attn_forward",
    )(place, hidden, small, *pack[0])


def expand_forward(place, middle, small, expand_bias, pack, first):
    tokens = middle.shape[0]

    def kernel(place_ref, middle_ref, small_ref, bias_ref, *rest):
        packs = rest[:PIECES]
        normed_ref, active_ref, slope_ref, block, sems = rest[PIECES:]
        part = pl.program_id(0)
        copies = block_copies(place_ref[0], packs, pack[1], first, 384, block, sems)

        @pl.when(part == 0)
        def begin():
            run_all(copies, "start")
            unit, root = normalise(middle_ref[...])
            normed_ref[...] = (
                unit * small_ref[SM_G2 : SM_G2 + 1] + small_ref[SM_S2 : SM_S2 + 1]
            ).astype(bf16)
            run_all(copies, "wait")

        weight = block[pl.ds(2 * part, 2)].reshape(WIDTH, WIDTH)
        point = dot_nt(normed_ref[...], weight) + bias_ref[part]
        root, cubic = 0.7978845608028654, 0.044715
        square = point * point
        upper = 0.5 + 0.5 * jnp.tanh(point * (root + (root * cubic) * square))
        active_ref[...] = (point * upper).astype(bf16)
        bend = point * (2.0 * root + (6.0 * root * cubic) * square)
        slope_ref[...] = (upper * (1.0 + bend * (1.0 - upper))).astype(bf16)

    hidden_units = FF_PARTS * WIDTH
    shape = jax.ShapeDtypeStruct
    return pl.pallas_call(
        kernel,
        grid=(FF_PARTS,),
        in_specs=[
            in_smem(),
            fixed(middle.shape),
            fixed(small.shape),
            fixed(expand_bias.shape),
        ]
        + [in_any()] * PIECES,
        out_specs=[fixed(middle.shape), part_spec(tokens), part_spec(tokens)],
        out_shape=[
            shape((tokens, WIDTH), bf16),
            shape((tokens, hidden_units), bf16),
            shape((tokens, hidden_units), bf16),
        ],
        scratch_shapes=[
            pltpu.VMEM((8, 384, WIDTH), bf16),
            pltpu.SemaphoreType.DMA((PIECES,)),
        ],
        compiler_params=params(),
        cost_estimate=cost(0.01),
        name="expand_forward",
    )(place, middle, small, expand_bias, *pack[0])


def reduce_copies(place_now, packs, regions, first, blocks, sems):
    return [
        block_copies(
            place_now, packs, regions, first + 96 * part, 96, blocks.at[part], sems.at[part]
        )
        for part in range(FF_PARTS)
    ]


def for_part(part, groups, what):
    for at, group in enumerate(groups):

        @pl.when(part == at)
        def run():
            run_all(group, what)


def reduce_forward(place, live, middle, active, small, pack, first, last):
    tokens = middle.shape[0]

    def kernel(place_ref, live_ref, middle_ref, active_ref, small_ref, *rest):
        packs = rest[:PIECES]
        result_ref, total, blocks, sems = rest[PIECES:]
        part = pl.program_id(0)
        copies = reduce_copies(place_ref[0], packs, pack[1], first, blocks, sems)

        @pl.when(part == 0)
        def begin():
            for group in copies:
                run_all(group, "start")
            total[...] = middle_ref[...] + small_ref[SM_RB : SM_RB + 1]

        for_part(part, copies, "wait")
        total[...] += dot_nt(active_ref[...], blocks[part].reshape(WIDTH, WIDTH))

        @pl.when(part == FF_PARTS - 1)
        def end():
            if last:
                for image in range(tokens // ROWS):
                    rows = slice(ROWS * image, ROWS * (image + 1))
                    result_ref[rows] = (
                        total[rows] * live_ref[image, 0].astype(f32)
                    ).astype(result_ref.dtype)
            else:
                result_ref[...] = total[...].astype(result_ref.dtype)

    return pl.pallas_call(
        kernel,
        grid=(FF_PARTS,),
        in_specs=[
            in_smem(),
            in_smem(),
            fixed(middle.shape),
            part_spec(tokens),
            fixed(small.shape),
        ]
        + [in_any()] * PIECES,
        out_specs=fixed(middle.shape),
        out_shape=jax.ShapeDtypeStruct((tokens, WIDTH), bf16 if last else f32),
        scratch_shapes=[
            pltpu.VMEM((tokens, WIDTH), f32),
            pltpu.VMEM((FF_PARTS, 8, 96, WIDTH), bf16),
            pltpu.SemaphoreType.DMA((FF_PARTS, PIECES)),
        ],
        compiler_params=params(),
        cost_estimate=cost(0.01),
        name="reduce_forward",
    )(place, live, middle, active, small, *pack[0])


def split_owners(place_now, turned, mine_ref, theirs_ref, count, lead=()):
    core = place_now & 1
    chip = place_now >> 1
    for owner in range(4):
        mine_ref[lead + (owner ^ chip,)] = turned[2 * owner + core]
        theirs_ref[lead + (owner ^ chip,)] = turned[2 * owner + 1 - core]


def halves_spec(count):
    return pl.BlockSpec((4, count, ROWS), lambda image: (0, 0, image))


def start_grad(place, live, cotangent):
    def kernel(place_ref, live_ref, cot_ref, grad_ref, mine_ref, theirs_ref, turned):
        image = pl.program_id(0)
        grad = cot_ref[...].astype(f32) * live_ref[image, 0].astype(f32)
        grad_ref[...] = grad.astype(bf16)
        turned[...] = grad.T.astype(bf16).reshape(8, 96, ROWS)
        split_owners(place_ref[0], turned, mine_ref, theirs_ref, 96)

    tokens = cotangent.shape[0]
    shape = jax.ShapeDtypeStruct
    return pl.pallas_call(
        kernel,
        grid=(tokens // ROWS,),
        in_specs=[in_smem(), in_smem(), rows_spec(WIDTH)],
        out_specs=[rows_spec(WIDTH), halves_spec(96), halves_spec(96)],
        out_shape=[shape((tokens, WIDTH), bf16)] + [shape((4, 96, tokens), bf16)] * 2,
        scratch_shapes=[pltpu.VMEM((8, 96, ROWS), bf16)],
        compiler_params=params(),
        cost_estimate=cost(0.01),
        name="start_grad",
    )(place, live, cotangent)


def fetch(source, target, sem):
    return pltpu.make_async_copy(source, target, sem)


def ff_backward(place, grad, slope, middle, small, expand_pack, reduce_pack):
    tokens = middle.shape[0]
    (expand_arrays, expand_regions), expand_first = expand_pack
    (reduce_arrays, reduce_regions), reduce_first = reduce_pack

    def kernel(place_ref, grad_in, slope_in, middle_in, small_ref, *rest):
        expand_packs, reduce_packs = rest[:PIECES], rest[PIECES : 2 * PIECES]
        (
            out_ref,
            pre_mine,
            pre_theirs,
            attn_mine,
            attn_theirs,
            sums_ref,
            grad_ref,
            slope_ref,
            middle_ref,
            expand_block,
            reduce_blocks,
            turned_pre,
            turned_attn,
            pre_low,
            expand_sems,
            reduce_sems,
            in_sems,
            out_sems,
        ) = rest[2 * PIECES :]
        place_now = place_ref[0]
        core = place_now & 1
        chip = place_now >> 1
        copies = reduce_copies(
            place_now, reduce_packs, reduce_regions, reduce_first, reduce_blocks, reduce_sems
        )
        expand_copies = block_copies(
            place_now, expand_packs, expand_regions, expand_first, 384, expand_block, expand_sems
        )
        grad_copy = fetch(grad_in, grad_ref, in_sems.at[0])
        middle_copy = fetch(middle_in, middle_ref, in_sems.at[1])
        slope_copies = [
            fetch(
                slope_in.at[:, pl.ds(WIDTH * part, WIDTH)], slope_ref.at[part], in_sems.at[2 + part]
            )
            for part in range(FF_PARTS)
        ]
        grad_copy.start()
        for part in range(FF_PARTS):
            run_all(copies[part], "start")
            slope_copies[part].start()
        run_all(expand_copies, "start")
        middle_copy.start()

        sent = []

        def send(source, target):
            copy = pltpu.make_async_copy(source, target, out_sems.at[len(sent)])
            copy.start()
            sent.append(copy)

        grad_copy.wait()
        low = grad_ref[...].astype(bf16)
        sums_ref[2:3] = jnp.sum(low.astype(f32), axis=0, keepdims=True)
        for part in range(FF_PARTS):
            run_all(copies[part], "wait")
            slope_copies[part].wait()
            up = dot_nn(low, reduce_blocks[part].reshape(WIDTH, WIDTH))
            pre = (up * slope_ref[part].astype(f32)).astype(bf16)
            pre_low[part] = pre
            sums_ref[4 + part : 5 + part] = jnp.sum(pre.astype(f32), axis=0, keepdims=True)
            turned_pre[2 * part : 2 * part + 2] = pre.T.reshape(2, 384, tokens)
            send(turned_pre.at[2 * part + core], pre_mine.at[part ^ chip])
            send(turned_pre.at[2 * part + 1 - core], pre_theirs.at[part ^ chip])
        run_all(expand_copies, "wait")
        back = dot_nn(pre_low[0], expand_block[0:2].reshape(WIDTH, WIDTH))
        for part in range(1, FF_PARTS):
            back = back + dot_nn(
                pre_low[part], expand_block[2 * part : 2 * part + 2].reshape(WIDTH, WIDTH)
            )
        middle_copy.wait()
        unit, root = normalise(middle_ref[...])
        sums_ref[0:1] = jnp.sum(back * unit, axis=0, keepdims=True)
        sums_ref[1:2] = jnp.sum(back, axis=0, keepdims=True)
        scaled = back * small_ref[SM_G2 : SM_G2 + 1]
        result = grad_ref[...].astype(f32) + root * (
            scaled
            - jnp.mean(scaled, axis=-1, keepdims=True)
            - unit * jnp.mean(scaled * unit, axis=-1, keepdims=True)
        )
        out_ref[...] = result
        result_low = result.astype(bf16)
        sums_ref[3:4] = jnp.sum(result_low.astype(f32), axis=0, keepdims=True)
        turned_attn[...] = result_low.T.reshape(8, 96, tokens)
        for owner in range(4):
            send(turned_attn.at[2 * owner + core], attn_mine.at[owner ^ chip])
            send(turned_attn.at[2 * owner + 1 - core], attn_theirs.at[owner ^ chip])
        run_all(sent, "wait")

    shape = jax.ShapeDtypeStruct
    in_vmem = pl.BlockSpec(memory_space=pltpu.VMEM)
    return pl.pallas_call(
        kernel,
        in_specs=[in_smem()] + [in_any()] * 3 + [in_vmem] + [in_any()] * (2 * PIECES),
        out_specs=[in_vmem] + [in_any()] * 4 + [in_vmem],
        out_shape=[shape((tokens, WIDTH), f32)]
        + [shape((4, 384, tokens), bf16)] * 2
        + [shape((4, 96, tokens), bf16)] * 2
        + [shape((8, WIDTH), f32)],
        scratch_shapes=[
            pltpu.VMEM((tokens, WIDTH), grad.dtype),
            pltpu.VMEM((FF_PARTS, tokens, WIDTH), bf16),
            pltpu.VMEM((tokens, WIDTH), f32),
            pltpu.VMEM((8, 384, WIDTH), bf16),
            pltpu.VMEM((FF_PARTS, 8, 96, WIDTH), bf16),
            pltpu.VMEM((8, 384, tokens), bf16),
            pltpu.VMEM((8, 96, tokens), bf16),
            pltpu.VMEM((FF_PARTS, tokens, WIDTH), bf16),
            pltpu.SemaphoreType.DMA((PIECES,)),
            pltpu.SemaphoreType.DMA((FF_PARTS, PIECES)),
            pltpu.SemaphoreType.DMA((2 + FF_PARTS,)),
            pltpu.SemaphoreType.DMA((16,)),
        ],
        compiler_params=pltpu.CompilerParams(vmem_limit_bytes=VMEM_BYTES),
        cost_estimate=cost(0.01),
        name="ff_backward",
    )(place, grad, slope, middle, small, *expand_arrays, *reduce_arrays)


def chosen_columns(place):
    def kernel(place_ref, out_ref):
        row = lax.broadcasted_iota(jnp.int32, (WIDTH, 1024), 0)
        column = lax.broadcasted_iota(jnp.int32, (WIDTH, 1024), 1)
        at = column & 127
        wanted = 96 * ((column >> 7) ^ place_ref[0]) + at
        out_ref[...] = jnp.where((row == wanted) & (at < 96), 1.0, 0.0).astype(bf16)

    return pl.pallas_call(
        kernel,
        in_specs=[in_smem()],
        out_specs=pl.BlockSpec(memory_space=pltpu.VMEM),
        out_shape=jax.ShapeDtypeStruct((WIDTH, 1024), bf16),
        compiler_params=pltpu.CompilerParams(vmem_limit_bytes=LARGE_VMEM_BYTES),
        cost_estimate=cost(0.01),
        name="chosen_columns",
    )(place)


def attn_backward(place, grad, hidden, qkv, mixed, small, ff_sums, chosen, pack, last):
    tokens = grad.shape[0]

    def kernel(
        place_ref, grad_in, hidden_in, qkv_in, mixed_in, chosen_in, small_ref, ff_sums_ref, *rest
    ):
        packs = rest[:PIECES]
        out_ref, qkv_mine, qkv_theirs, vec_mine, vec_theirs = rest[PIECES : PIECES + 5]
        if not last:
            low_mine, low_theirs = rest[PIECES + 5 : PIECES + 7]
        (
            grad_ref,
            hidden_ref,
            qkv_ref,
            mixed_ref,
            chosen_ref,
            blocks,
            turned,
            sums_ref,
            sems,
            in_sems,
            out_sems,
        ) = rest[-11:]
        place_now = place_ref[0]
        core = place_now & 1
        chip = place_now >> 1
        merge_copies = unit_copies(
            place_now, packs, pack[1], 288, blocks.at[pl.ds(3, 1)], sems.at[0]
        )
        heads_copies = unit_copies(
            place_now, packs, pack[1], 0, blocks.at[pl.ds(0, 3)], sems.at[1]
        )
        fetches = [
            fetch(source, target, in_sems.at[at])
            for at, (source, target) in enumerate(
                (
                    (grad_in, grad_ref),
                    (mixed_in, mixed_ref),
                    (qkv_in, qkv_ref),
                    (hidden_in, hidden_ref),
                    (chosen_in, chosen_ref),
                )
            )
        ]
        fetches[0].start()
        run_all(merge_copies, "start")
        run_all(fetches[1:], "start")
        run_all(heads_copies, "start")
        sent = []

        def send(source, target):
            copy = pltpu.make_async_copy(source, target, out_sems.at[len(sent)])
            copy.start()
            sent.append(copy)

        fetches[0].wait()
        run_all(merge_copies, "wait")
        grad_rows = grad_ref[...]
        mixed_back = dot_nn(grad_rows.astype(bf16), blocks[3].reshape(WIDTH, WIDTH)).astype(bf16)
        fetches[1].wait()
        product = mixed_back.astype(f32) * mixed_ref[...].astype(f32)
        product_high = product.astype(bf16)
        product_low = (product - product_high.astype(f32)).astype(bf16)
        head_row = lax.broadcasted_iota(jnp.int32, (16, WIDTH), 0)
        head_column = lax.broadcasted_iota(jnp.int32, (16, WIDTH), 1) >> 6
        of_head = jnp.where(head_row == head_column, 1.0, 0.0).astype(bf16)
        inner = dot_nt(of_head, product_high) + dot_nt(of_head, product_low)
        fetches[2].wait()
        lane = lax.broadcasted_iota(jnp.int32, (ROWS, 128), 1)
        line = lax.broadcasted_iota(jnp.int32, (128, ROWS), 0)
        scale = HEAD_DIM**-0.5
        for image in range(tokens // ROWS):
            rows = slice(ROWS * image, ROWS * (image + 1))
            for pair in range(HEADS // 2):
                q_pair = qkv_ref[rows, 128 * pair : 128 * pair + 128]
                k_pair = qkv_ref[rows, WIDTH + 128 * pair : WIDTH + 128 * pair + 128]
                v_pair = qkv_ref[rows, 2 * WIDTH + 128 * pair : 2 * WIDTH + 128 * pair + 128]
                g_pair = mixed_back[rows, 128 * pair : 128 * pair + 128]
                k_turned = k_pair.T
                weights, powers, inverses = [], [], []
                for half in range(2):
                    here = (lane < 64) == (half == 0)
                    k_one = jnp.where(here, k_pair * scale, jnp.zeros_like(k_pair))
                    v_one = jnp.where(here, v_pair, jnp.zeros_like(v_pair))
                    scores = dot_nt(k_one, q_pair)
                    power = jnp.exp(scores - jnp.max(scores, axis=0, keepdims=True))
                    inverses.append(1.0 / jnp.sum(power, axis=0, keepdims=True))
                    head = 2 * pair + half
                    back = dot_nt(v_one, g_pair) - inner[head : head + 1, rows]
                    weights.append((power * back).astype(bf16))
                    powers.append(power.astype(bf16))
                inverse = jnp.where(line < 64, inverses[0], inverses[1])
                q_turned = (q_pair.T.astype(f32) * (inverse * scale)).astype(bf16)
                g_turned = (g_pair.T.astype(f32) * inverse).astype(bf16)
                made = (
                    jnp.where(
                        line < 64, dot_nn(k_turned, weights[0]), dot_nn(k_turned, weights[1])
                    )
                    * (inverse * scale),
                    jnp.where(
                        line < 64, dot_nt(q_turned, weights[0]), dot_nt(q_turned, weights[1])
                    ),
                    jnp.where(
                        line < 64, dot_nt(g_turned, powers[0]), dot_nt(g_turned, powers[1])
                    ),
                )
                for member in range(3):
                    turned[member, 128 * pair : 128 * pair + 128, rows] = made[member].astype(bf16)
        for member in range(3):
            for owner in range(4):
                for odd in range(2):
                    target = qkv_theirs if odd else qkv_mine
                    first = pl.multiple_of(192 * owner + 96 * (core ^ odd), 96)
                    send(turned.at[member, pl.ds(first, 96)], target.at[member, owner ^ chip])
        back = jnp.zeros((tokens, WIDTH), f32)
        ones = jnp.ones((8, tokens), bf16)
        run_all(heads_copies, "wait")
        for member in range(3):
            back = back + lax.dot_general(
                turned[member],
                blocks[member].reshape(WIDTH, WIDTH),
                (((0,), (0,)), ((), ())),
                preferred_element_type=f32,
            )
        sums_ref[0:1] = dot_nt(ones, turned[0])[0:1]
        sums_ref[1:2] = dot_nt(ones, turned[2])[0:1]
        fetches[3].wait()
        unit, root = normalise(hidden_ref[...].astype(f32))
        sums_ref[3:4] = jnp.sum(back * unit, axis=0, keepdims=True)
        sums_ref[4:5] = jnp.sum(back, axis=0, keepdims=True)
        scaled = back * small_ref[SM_G1 : SM_G1 + 1]
        result = grad_ref[...] + root * (
            scaled
            - jnp.mean(scaled, axis=-1, keepdims=True)
            - unit * jnp.mean(scaled * unit, axis=-1, keepdims=True)
        )
        out_ref[...] = result.astype(out_ref.dtype)
        run_all(sent, "wait")
        sent.clear()
        if not last:
            turned[0] = result.astype(bf16).T
            for owner in range(4):
                for odd in range(2):
                    target = low_theirs if odd else low_mine
                    first = pl.multiple_of(192 * owner + 96 * (core ^ odd), 96)
                    send(turned.at[0, pl.ds(first, 96)], target.at[owner ^ chip])

        sums_ref[2:3] = ff_sums_ref[3:4]
        sums_ref[5:8] = ff_sums_ref[0:3]
        fetches[4].wait()
        rest_of = sums_ref[...]
        cut = jnp.zeros((8, 1024), f32)
        for term in range(3):
            term_low = rest_of.astype(bf16)
            rest_of = rest_of - term_low.astype(f32)
            cut = cut + dot_nn(term_low, chosen_ref[...])
        for delta in range(8):
            owner = place_now ^ delta
            target = vec_theirs if delta & 1 else vec_mine
            target[delta >> 1] = jnp.zeros((16, WIDTH // 2), f32)
            target[delta >> 1, 0:8, 0:128] = cut[:, 128 * delta : 128 * delta + 128]
            values = ff_sums_ref[pl.ds(4 + (owner >> 1), 1)]
            target[delta >> 1, 8:9] = jnp.where(
                (owner & 1) == 0, values[:, : WIDTH // 2], values[:, WIDTH // 2 :]
            )
        run_all(sent, "wait")

    shape = jax.ShapeDtypeStruct
    in_vmem = pl.BlockSpec(memory_space=pltpu.VMEM)
    vector_shape = (4, 16, WIDTH // 2)
    out_specs = [in_vmem] + [in_any()] * 2 + [in_vmem] * 2
    out_shape = (
        [shape((tokens, WIDTH), bf16 if last else f32)]
        + [shape((3, 4, 96, tokens), bf16)] * 2
        + [shape(vector_shape, f32)] * 2
    )
    if not last:
        out_specs += [in_any()] * 2
        out_shape += [shape((4, 96, tokens), bf16)] * 2
    return pl.pallas_call(
        kernel,
        in_specs=[in_smem()] + [in_any()] * 5 + [in_vmem] * 2 + [in_any()] * PIECES,
        out_specs=out_specs,
        out_shape=out_shape,
        scratch_shapes=[
            pltpu.VMEM((tokens, WIDTH), grad.dtype),
            pltpu.VMEM((tokens, WIDTH), hidden.dtype),
            pltpu.VMEM((tokens, 3 * WIDTH), bf16),
            pltpu.VMEM((tokens, WIDTH), bf16),
            pltpu.VMEM((WIDTH, 1024), bf16),
            pltpu.VMEM((4, 8, 96, WIDTH), bf16),
            pltpu.VMEM((3, WIDTH, tokens), bf16),
            pltpu.VMEM((8, WIDTH), f32),
            pltpu.SemaphoreType.DMA((2, PIECES)),
            pltpu.SemaphoreType.DMA((5,)),
            pltpu.SemaphoreType.DMA((24,)),
        ],
        compiler_params=pltpu.CompilerParams(vmem_limit_bytes=VMEM_BYTES),
        cost_estimate=cost(0.01),
        name="attn_backward",
    )(place, grad, hidden, qkv, mixed, chosen, small, ff_sums, *pack[0])


def spread(result, owner, rows, out_refs):
    go_x, go_y, stay_x, stay_y = out_refs
    half = WIDTH // 2
    low, high = result[:, :half].astype(bf16), result[:, half:].astype(bf16)
    target, at = ((stay_x, 0), (go_x, 0), (stay_x, 1), (go_x, 1))[owner]
    target[at, rows] = low
    target, at = ((stay_y, 0), (stay_y, 1), (go_y, 0), (go_y, 1))[owner]
    target[at, rows] = high


def travel_shapes(rows_low, rows_high):
    shape = jax.ShapeDtypeStruct
    half = WIDTH // 2
    return [shape((2, rows, half), bf16) for rows in (rows_low, rows_high, rows_low, rows_high)]


def owner_terms(reduce=None, expand=None, merge=None, heads=None, small_terms=None):
    given, in_specs, sections = [], [], []
    rows = 0
    tokens = (reduce or expand or heads)[1][0].shape[0]
    whole = pl.BlockSpec((tokens, WIDTH), lambda at: (0, 0))
    four = pl.BlockSpec((4, 96, tokens), lambda at: (0, 0, 0))
    for name, pair, left, right, taken in (
        ("reduce", reduce, four, pl.BlockSpec((tokens, WIDTH), lambda at: (0, at)), 384),
        ("expand", expand, pl.BlockSpec((1, 384, tokens), lambda at: (at, 0, 0)), whole, 384),
        ("merge", merge, four, whole, 96),
        (
            "heads",
            heads,
            pl.BlockSpec((1, 4, 96, tokens), lambda at: (jnp.minimum(at, 2), 0, 0, 0)),
            whole,
            288,
        ),
    ):
        if pair is not None:
            given += [*pair[0], *pair[1]]
            in_specs += [left, left, right, right]
            sections.append((name, rows))
            rows += taken
    extra = 0
    if small_terms is not None:
        given += small_terms
        in_specs += [pl.BlockSpec(small_terms[0].shape, lambda at: (0, 0, 0))] * 2
        extra = 16

    def kernel(*refs):
        ins, out_refs = refs[: len(given)], refs[len(given) :]
        go_x, go_y, stay_x, stay_y = out_refs
        part = pl.program_id(0)

        def multiply(place, first):
            left_a, left_b, right_a, right_b = ins[4 * place : 4 * place + 4]
            result = dot_nn(left_a[...].reshape(384, tokens), right_a[...]) + dot_nn(
                left_b[...].reshape(384, tokens), right_b[...]
            )
            if first is None:
                return result
            for owner in range(4):
                spread(
                    result[96 * owner : 96 * owner + 96], owner, pl.ds(first, 96), out_refs
                )

        for place, (name, first) in enumerate(sections):
            if name == "reduce":
                multiply(place, pl.multiple_of(first + 96 * part, 96))
            elif name == "heads":

                @pl.when(part < 3)
                def one_head_block():
                    multiply(place, pl.multiple_of(first + 96 * part, 96))

            elif name == "merge":

                @pl.when(part == 3)
                def merge_block():
                    multiply(place, first)

            else:
                result = multiply(place, None)
                for owner in range(4):

                    @pl.when(part == owner)
                    def keep():
                        spread(result, owner, slice(first, first + 384), out_refs)

        if small_terms is not None:

            @pl.when(part == 3)
            def vectors():
                for owner in range(4):
                    target, at = ((stay_x, 0), (go_x, 0), (stay_x, 1), (go_x, 1))[owner]
                    target[at, rows : rows + 16] = (ins[-2][owner] + ins[-1][owner]).astype(bf16)

    half = WIDTH // 2
    heights = (rows + extra, rows, rows + extra, rows)
    return pl.pallas_call(
        kernel,
        grid=(4,),
        in_specs=in_specs,
        out_specs=[pl.BlockSpec((2, height, half), lambda at: (0, 0, 0)) for height in heights],
        out_shape=[jax.ShapeDtypeStruct((2, height, half), bf16) for height in heights],
        compiler_params=params(),
        cost_estimate=cost(0.01),
        name="owner_terms",
    )(*given)


def taken(end_ref, pair, rows, scale):
    total, outward = pair
    part = jnp.where(end_ref[0] == 1, outward[rows], total[rows])
    return part.astype(f32) * scale


def put_halves(target, end_ref, pair, low, high, rows, scale):
    half = WIDTH // 2
    target[:, :half] = taken(end_ref, pair, slice(low, low + rows), scale)
    target[:, half:] = taken(end_ref, pair, slice(high, high + rows), scale)


def in_full():
    return pl.BlockSpec(memory_space=pltpu.VMEM)


def finish_most(at_end, reduce_1, em_1, both_01, scale):
    layers = 2
    half = WIDTH // 2

    def kernel(end_ref, *refs):
        r_pair, em_pair, hr_pair = refs[0:2], refs[2:4], refs[4:6]
        heads_out, merge_out, expand_out, reduce_out, vectors_out = refs[6:11]
        heads, merge, expand, reduce, sems = refs[11:]
        for layer, pair, high in ((0, hr_pair, 688), (1, r_pair, 384)):
            for part in range(FF_PARTS):
                for first, column in ((96 * part, WIDTH * part), (high + 96 * part, WIDTH * part + half)):
                    reduce[layer, :, column : column + half] = taken(
                        end_ref, pair, slice(first, first + 96), scale
                    )
        copies = [pltpu.make_async_copy(reduce, reduce_out, sems.at[0])]
        copies[0].start()
        put_halves(expand, end_ref, em_pair, 0, 480, 384, scale)
        put_halves(merge, end_ref, em_pair, 384, 864, 96, scale)
        for member in range(3):
            put_halves(
                heads.at[member],
                end_ref,
                hr_pair,
                384 + 96 * member,
                688 + 384 + 96 * member,
                96,
                scale,
            )
        last = layers - 1
        copies.append(pltpu.make_async_copy(expand, expand_out.at[last], sems.at[1]))
        copies.append(pltpu.make_async_copy(merge, merge_out.at[last], sems.at[2]))
        copies.append(pltpu.make_async_copy(heads, heads_out.at[last], sems.at[3]))
        run_all(copies[1:], "start")
        vectors_out[...] = taken(end_ref, hr_pair, slice(672, 688), scale)
        run_all(copies, "wait")

    shape = jax.ShapeDtypeStruct
    return pl.pallas_call(
        kernel,
        in_specs=[in_smem()] + [in_full()] * 6,
        out_specs=[in_any()] * 4 + [in_full()],
        out_shape=[
            shape((layers, 3, 96, WIDTH), f32),
            shape((layers, 96, WIDTH), f32),
            shape((layers, 384, WIDTH), f32),
            shape((layers, 96, FF_PARTS * WIDTH), f32),
            shape((16, half), f32),
        ],
        scratch_shapes=[
            pltpu.VMEM((3, 96, WIDTH), f32),
            pltpu.VMEM((96, WIDTH), f32),
            pltpu.VMEM((384, WIDTH), f32),
            pltpu.VMEM((layers, 96, FF_PARTS * WIDTH), f32),
            pltpu.SemaphoreType.DMA((4,)),
        ],
        compiler_params=pltpu.CompilerParams(vmem_limit_bytes=SMALL_VMEM_BYTES),
        cost_estimate=cost(0.01),
        name="finish_most",
    )(at_end, *reduce_1, *em_1, *both_01)


def finish_expand(at_end, em_0, merge_grad, expand_grad, scale):
    def kernel(end_ref, total, outward, merge_in, expand_in, merge_out, expand_out, *rest):
        merge, expand, sems = rest
        put_halves(expand, end_ref, (total, outward), 0, 480, 384, scale)
        put_halves(merge, end_ref, (total, outward), 384, 864, 96, scale)
        copies = [
            pltpu.make_async_copy(expand, expand_out.at[0], sems.at[0]),
            pltpu.make_async_copy(merge, merge_out.at[0], sems.at[1]),
        ]
        run_all(copies, "start")
        run_all(copies, "wait")

    return pl.pallas_call(
        kernel,
        in_specs=[in_smem()] + [in_full()] * 2 + [in_any()] * 2,
        out_specs=[in_any()] * 2,
        out_shape=[jax.ShapeDtypeStruct(a.shape, f32) for a in (merge_grad, expand_grad)],
        scratch_shapes=[
            pltpu.VMEM((96, WIDTH), f32),
            pltpu.VMEM((384, WIDTH), f32),
            pltpu.SemaphoreType.DMA((2,)),
        ],
        input_output_aliases={3: 0, 4: 1},
        compiler_params=pltpu.CompilerParams(vmem_limit_bytes=SMALL_VMEM_BYTES),
        cost_estimate=cost(0.01),
        name="finish_expand",
    )(at_end, *em_0, merge_grad, expand_grad)


def finish_heads(at_end, heads_0, vectors_1, heads_grad, scale):
    def kernel(end_ref, total, outward, vectors_ref, heads_in, heads_out, *rest):
        outs, (heads, sems) = rest[:8], rest[8:]
        for member in range(3):
            put_halves(
                heads.at[member],
                end_ref,
                (total, outward),
                96 * member,
                304 + 96 * member,
                96,
                scale,
            )
        copy = pltpu.make_async_copy(heads, heads_out.at[0], sems.at[0])
        copy.start()
        own = taken(end_ref, (total, outward), slice(288, 304), scale)
        for layer, values in ((0, own), (1, vectors_ref[...])):
            outs[0][layer] = values[0:2, :96]
            for row in range(2, 8):
                outs[row - 1][layer : layer + 1] = values[row : row + 1, :96]
            outs[7][layer : layer + 1] = values[8:9]
        copy.wait()

    shape = jax.ShapeDtypeStruct
    layers = heads_grad.shape[0]
    return pl.pallas_call(
        kernel,
        in_specs=[in_smem()] + [in_full()] * 3 + [in_any()],
        out_specs=[in_any()] + [in_full()] * 8,
        out_shape=[shape(heads_grad.shape, f32), shape((layers, 2, 96), f32)]
        + [shape((layers, 96), f32)] * 6
        + [shape((layers, 384), f32)],
        scratch_shapes=[pltpu.VMEM((3, 96, WIDTH), f32), pltpu.SemaphoreType.DMA((1,))],
        input_output_aliases={4: 0},
        compiler_params=pltpu.CompilerParams(vmem_limit_bytes=SMALL_VMEM_BYTES),
        cost_estimate=cost(0.01),
        name="finish_heads",
    )(at_end, *heads_0, vectors_1, heads_grad)


def shards(
    images,
    cotangent,
    slot_flags,
    heads_weight,
    heads_bias,
    merge_weight,
    merge_bias,
    first_gain,
    first_shift,
    second_gain,
    second_shift,
    expand_weight,
    expand_bias,
    reduce_weight,
    reduce_bias,
):
    micro_count, unused_slots, seq_len, width = images.shape
    layers = heads_weight.shape[0]
    tokens = micro_count * seq_len
    place_at = lax.axis_index("fsdp").astype(jnp.int32)
    place = place_at[None]

    matrices = (heads_weight, merge_weight, expand_weight, reduce_weight)
    vectors = (
        heads_bias,
        merge_bias,
        first_gain,
        first_shift,
        second_gain,
        second_shift,
        reduce_bias,
        expand_bias,
    )
    kinds = [("attn", 0), ("ff", 0), ("attn", 1), ("expand", 1), ("reduce", 1)]
    rows_of = [PACK_ROWS[kind] for kind, layer in kinds]
    cut_of = [PACK_CUTS[kind] for kind, layer in kinds]
    x_rows = [0] + cut_of
    y_rows = [0] + [rows - cut for rows, cut in zip(rows_of, cut_of)]
    count = len(kinds)

    def send_round(at, own_now, x_before, y_before):
        if at == 0:
            return swap_x(own_now), swap_y(own_now)
        rows, cut = rows_of[at - 1], cut_of[at - 1]
        to_x = [(y_before, y_rows[at - 1], cut)]
        to_y = [(x_before, x_rows[at - 1] + cut, rows - cut)]
        if at < count:
            to_x.append((own_now, 0, rows_of[at]))
            to_y.append((own_now, 0, rows_of[at]))
        to_x, to_y = join_rows([to_x, to_y])
        return swap_x(to_x), swap_y(to_y)

    def pack_of(at, own_pair, came):
        (x_0, y_0, cx_0, cy_0), (x_1, y_1, cx_1, cy_1) = came[at], came[at + 1]
        return (
            (own_pair[0], x_0, y_0, x_1, y_1, own_pair[1], cx_0, cy_0, cx_1, cy_1),
            regions_of(rows_of[at], cut_of[at], x_rows[at], y_rows[at]),
        )

    def both(values):
        return tuple(swap_core(value) for value in values)

    hidden = images.reshape(tokens, width)
    seal = lax.optimization_barrier

    came = []
    own = own_packs(kinds[:1], matrices, vectors, True)
    new = send_round(0, own[0], None, None)
    own_other = both(own)
    own += own_packs(kinds[1:2], matrices, vectors)
    chosen = chosen_columns(place)
    grad, low_mine, low_theirs = start_grad(place, slot_flags, cotangent.reshape(tokens, width))
    own, own_other, new, grad, low_mine, low_theirs, matrices, vectors, chosen = seal(
        (own, own_other, new, grad, low_mine, low_theirs, matrices, vectors, chosen)
    )

    got, new = new, send_round(1, own[1], *new)
    came.append(got + both(got))
    low = (low_mine, swap_core(low_theirs))
    low, matrices = seal((low, matrices))
    own += own_packs(kinds[2:], matrices, vectors)
    own_other += both(own[1:])
    own, own_other, came, new, low, grad = seal((own, own_other, came, new, low, grad))

    got, new = new, send_round(2, own[2], *new)
    came.append(got + both(got))
    pack_a0 = pack_of(0, (own[0], own_other[0]), came)
    small_0, expand_rows_0 = gathered_vectors(place, pack_a0)
    middle_0, normed_0, qkv_0, mixed_0 = attn_forward(place, hidden, small_0, pack_a0)
    own, came, new, small_0, expand_rows_0, middle_0, normed_0, qkv_0, mixed_0 = seal(
        (own, came, new, small_0, expand_rows_0, middle_0, normed_0, qkv_0, mixed_0)
    )

    got, new = new, send_round(3, own[3], *new)
    came.append(got + both(got))
    pack_f0 = pack_of(1, (own[1], own_other[1]), came)
    second_0, active_0, slope_0 = expand_forward(
        place, middle_0, small_0, expand_rows_0, pack_f0, 0
    )
    hidden_1 = reduce_forward(
        place, slot_flags, middle_0, active_0, small_0, pack_f0, 384, False
    )
    others_a0 = both((normed_0, mixed_0))
    own, came, new, second_0, active_0, slope_0, hidden_1, others_a0 = seal(
        (own, came, new, second_0, active_0, slope_0, hidden_1, others_a0)
    )

    got, new = new, send_round(4, own[4], *new)
    came.append(got + both(got))
    pack_a1 = pack_of(2, (own[2], own_other[2]), came)
    small_1, expand_rows_1 = gathered_vectors(place, pack_a1)
    middle_1, normed_1, qkv_1, mixed_1 = attn_forward(place, hidden_1, small_1, pack_a1)
    second_other_0 = swap_core(second_0)
    came, new, small_1, expand_rows_1, middle_1, normed_1, qkv_1, mixed_1, second_other_0 = seal(
        (came, new, small_1, expand_rows_1, middle_1, normed_1, qkv_1, mixed_1, second_other_0)
    )

    got, new = new, send_round(5, None, *new)
    came.append(got + both(got))
    pack_e1 = pack_of(3, (own[3], own_other[3]), came)
    second_1, active_1, slope_1 = expand_forward(
        place, middle_1, small_1, expand_rows_1, pack_e1, 0
    )
    others_a1 = both((normed_1, mixed_1))
    second_1, active_1, slope_1, others_a1, came, new = seal(
        (second_1, active_1, slope_1, others_a1, came, new)
    )
    came.append(new + both(new))
    second_1, active_1, came = seal((second_1, active_1, came))
    pack_e1 = pack_of(3, (own[3], own_other[3]), came)
    pack_r1 = pack_of(4, (own[4], own_other[4]), came)

    grad, pre_mine, pre_theirs, attn_mine, attn_theirs, ff_sums = ff_backward(
        place, grad, slope_1, middle_1, small_1, (pack_e1, 0), (pack_r1, 0)
    )
    others_f1 = both((second_1, active_1))
    made = (grad, pre_mine, pre_theirs, attn_mine, attn_theirs, ff_sums)
    made, others_f1, pack_r1_arrays = seal((made, others_f1, pack_r1[0]))
    grad, pre_mine, pre_theirs, attn_mine, attn_theirs, ff_sums = made
    pack_r1 = (pack_r1_arrays, pack_r1[1])

    travel_r1 = owner_terms(reduce=(low, (active_1, others_f1[1])))
    pre_other, attn_other = both((pre_theirs, attn_theirs))
    travel_r1, pre_other, attn_other, grad = seal((travel_r1, pre_other, attn_other, grad))

    state_r1 = first_steps(travel_r1)
    travel_em1 = owner_terms(
        expand=((pre_mine, pre_other), (second_1, others_f1[0])),
        merge=((attn_mine, attn_other), (mixed_1, others_a1[1])),
    )
    state_r1, travel_em1, grad, active_0 = seal((state_r1, travel_em1, grad, active_0))

    state_r1 = second_steps(state_r1)
    state_em1 = first_steps(travel_em1)
    grad, qkv_mine, qkv_theirs, vec_mine, vec_theirs, low_mine, low_theirs = attn_backward(
        place, grad, hidden_1, qkv_1, mixed_1, small_1, ff_sums, chosen, pack_a1, False
    )
    active_other_0 = swap_core(active_0)
    made = (grad, qkv_mine, qkv_theirs, vec_mine, vec_theirs, low_mine, low_theirs)
    state_r1, state_em1, made, active_other_0 = seal((state_r1, state_em1, made, active_other_0))
    grad, qkv_mine, qkv_theirs, vec_mine, vec_theirs, low_mine, low_theirs = made

    sum_r1 = to_middle(ends(state_r1))
    state_em1 = second_steps(state_em1)
    low_other, qkv_other, vec_other = both((low_theirs, qkv_theirs, vec_theirs))
    travel_hr = owner_terms(
        reduce=((low_mine, low_other), (active_0, active_other_0)),
        heads=((qkv_mine, qkv_other), (normed_1, others_a1[0])),
        small_terms=(vec_mine, vec_other),
    )
    sum_r1, state_em1, travel_hr, grad = seal((sum_r1, state_em1, travel_hr, grad))

    state_hr = first_steps(travel_hr)
    sum_em1 = to_middle(ends(state_em1))
    sum_r1 = across_middle(sum_r1)
    grad, pre_mine, pre_theirs, attn_mine, attn_theirs, ff_sums = ff_backward(
        place, grad, slope_0, middle_0, small_0, (pack_f0, 0), (pack_f0, 384)
    )
    made = (grad, pre_mine, pre_theirs, attn_mine, attn_theirs, ff_sums)
    state_hr, sum_em1, sum_r1, made = seal((state_hr, sum_em1, sum_r1, made))
    grad, pre_mine, pre_theirs, attn_mine, attn_theirs, ff_sums = made

    state_hr = second_steps(state_hr)
    sum_em1 = across_middle(sum_em1)
    pre_other, attn_other = both((pre_theirs, attn_theirs))
    travel_em0 = owner_terms(
        expand=((pre_mine, pre_other), (second_0, second_other_0)),
        merge=((attn_mine, attn_other), (mixed_0, others_a0[1])),
    )
    state_hr, sum_em1, travel_em0, grad = seal((state_hr, sum_em1, travel_em0, grad))

    state_em0 = first_steps(travel_em0)
    sum_hr = to_middle(ends(state_hr))
    final_r1 = to_ends(sum_r1)
    images_grad, qkv_mine, qkv_theirs, vec_mine, vec_theirs = attn_backward(
        place, grad, hidden, qkv_0, mixed_0, small_0, ff_sums, chosen, pack_a0, True
    )
    made = (images_grad, qkv_mine, qkv_theirs, vec_mine, vec_theirs)
    state_em0, sum_hr, final_r1, sum_em1, made = seal(
        (state_em0, sum_hr, final_r1, sum_em1, made)
    )
    images_grad, qkv_mine, qkv_theirs, vec_mine, vec_theirs = made

    state_em0 = second_steps(state_em0)
    sum_hr = across_middle(sum_hr)
    final_em1 = to_ends(sum_em1)
    qkv_other, vec_other = both((qkv_theirs, vec_theirs))
    travel_h0 = owner_terms(
        heads=((qkv_mine, qkv_other), (normed_0, others_a0[0])), small_terms=(vec_mine, vec_other)
    )
    state_em0, travel_h0, final_em1, middle_1, active_1 = seal(
        (state_em0, travel_h0, final_em1, middle_1, active_1)
    )

    state_h0 = first_steps(travel_h0)
    sum_em0 = to_middle(ends(state_em0))
    state_h0, sum_hr = seal((state_h0, sum_hr))

    state_h0 = second_steps(state_h0)
    final_hr = to_ends(sum_hr)
    state_h0, sum_em0, middle_1, active_1 = seal((state_h0, sum_em0, middle_1, active_1))
    sum_h0 = to_middle(ends(state_h0))
    sum_em0 = across_middle(sum_em0)
    outputs = reduce_forward(
        place, slot_flags, middle_1, active_1, small_1, pack_r1, 0, True
    ).reshape(images.shape)
    sum_h0, final_hr, sum_em0, outputs = seal((sum_h0, final_hr, sum_em0, outputs))
    sum_h0 = across_middle(sum_h0)
    final_em0 = to_ends(sum_em0)
    final_h0 = to_ends(sum_h0)

    images_grad = images_grad.reshape(images.shape)
    grad_scale = (
        micro_count * images.shape[1] * lax.axis_size("fsdp") * lax.axis_size("rep") * seq_len
    ) ** (-0.5)
    rep_at = lax.axis_index("rep")
    at_end = ((rep_at == 0) | (rep_at == lax.axis_size("rep") - 1)).astype(jnp.int32)[None]
    heads_grad, merge_grad, expand_grad, reduce_grad, vectors_1 = finish_most(
        at_end, final_r1, final_em1, final_hr, grad_scale
    )
    merge_grad, expand_grad = finish_expand(at_end, final_em0, merge_grad, expand_grad, grad_scale)
    heads_grad, *vector_grads = finish_heads(at_end, final_h0, vectors_1, heads_grad, grad_scale)
    return (
        outputs,
        images_grad,
        heads_grad,
        vector_grads[0],
        merge_grad,
        *vector_grads[1:6],
        expand_grad,
        vector_grads[7],
        reduce_grad,
        vector_grads[6],
    )


def solution(mesh):
    body = shards if (mesh.shape["fsdp"], mesh.shape["rep"]) == (8, 4) else plain_shards
    placed = (
        P(None, ("fsdp", "rep"), None, None),
        P(None, ("fsdp", "rep"), None, None),
        P(None, ("fsdp", "rep")),
        P(None, None, "fsdp", None),
        P(None, None, "fsdp"),
        P(None, "fsdp", None),
        P(None, "fsdp"),
        P(None, "fsdp"),
        P(None, "fsdp"),
        P(None, "fsdp"),
        P(None, "fsdp"),
        P(None, "fsdp", None),
        P(None, "fsdp"),
        P(None, "fsdp", None),
        P(None, "fsdp"),
    )
    return jax.shard_map(
        body,
        mesh=mesh,
        in_specs=placed,
        out_specs=(
            P(None, ("fsdp", "rep"), None, None),
            P(None, ("fsdp", "rep"), None, None),
            P(None, None, "fsdp", None),
            P(None, None, "fsdp"),
            P(None, "fsdp", None),
            P(None, "fsdp"),
            P(None, "fsdp"),
            P(None, "fsdp"),
            P(None, "fsdp"),
            P(None, "fsdp"),
            P(None, "fsdp", None),
            P(None, "fsdp"),
            P(None, "fsdp", None),
            P(None, "fsdp"),
        ),
        check_vma=False,
    )
```

```python
import jax
import jax.numpy as jnp
from jax import lax
from jax.experimental import pallas as pl
from jax.experimental.pallas import tpu as pltpu
from jax.sharding import PartitionSpec as P

HEADS = 12
HEAD_DIM = 64


norm_eps = 1e-06


def layer_norm(token_rows, scale_row, offset_row):
    centre = token_rows - jnp.mean(token_rows, axis=-1, keepdims=True)
    spread = jnp.mean(centre * centre, axis=-1, keepdims=True)
    return centre * lax.rsqrt(spread + norm_eps) * scale_row + offset_row


def project(token_rows, weight):
    return lax.dot_general(
        token_rows, weight, (((1,), (1,)), ((), ())), preferred_element_type=jnp.float32
    )


def outer_sum(grad_rows, token_rows):
    return lax.dot_general(
        grad_rows, token_rows, (((0,), (0,)), ((), ())), preferred_element_type=jnp.float32
    )


def carry_back(grad_rows, weight):
    return jnp.dot(grad_rows, weight, preferred_element_type=jnp.float32)


def forward_layer(hidden, params):
    (
        heads_weight,
        heads_bias,
        merge_weight,
        merge_bias,
        first_gain,
        first_shift,
        second_gain,
        second_shift,
        expand_weight,
        expand_bias,
        reduce_weight,
        reduce_bias,
    ) = params
    seq_len, model_width = hidden.shape
    shaped = (seq_len, HEADS, HEAD_DIM)
    score_scale = HEAD_DIM ** (-0.5)
    normed = layer_norm(
        hidden, first_gain.astype(jnp.float32), first_shift.astype(jnp.float32)
    ).astype(jnp.bfloat16)
    queries = (project(normed, heads_weight[0]) + heads_bias[0].astype(jnp.float32)).astype(
        jnp.bfloat16
    )
    key_rows = project(normed, heads_weight[1]).astype(jnp.bfloat16)
    values = (project(normed, heads_weight[2]) + heads_bias[1].astype(jnp.float32)).astype(
        jnp.bfloat16
    )
    scores = (
        jnp.einsum(
            "qhd,khd->hqk",
            queries.reshape(shaped),
            key_rows.reshape(shaped),
            preferred_element_type=jnp.float32,
        )
        * score_scale
    )
    row_peak = jnp.max(scores, axis=-1, keepdims=True)
    exponent = jnp.exp(scores - row_peak)
    row_total = jnp.sum(exponent, axis=-1, keepdims=True)
    attend = exponent / row_total
    log_total = row_peak + jnp.log(row_total)
    mixed_rows = jnp.einsum(
        "hqk,khd->qhd",
        attend.astype(jnp.bfloat16),
        values.reshape(shaped),
        preferred_element_type=jnp.float32,
    )
    mixed_rows = mixed_rows.reshape(seq_len, model_width).astype(jnp.bfloat16)
    middle = hidden + (project(mixed_rows, merge_weight) + merge_bias.astype(jnp.float32))
    second = layer_norm(
        middle, second_gain.astype(jnp.float32), second_shift.astype(jnp.float32)
    ).astype(jnp.bfloat16)
    pre_act = project(second, expand_weight) + expand_bias.astype(jnp.float32)
    activated = jax.nn.gelu(pre_act, approximate=True).astype(jnp.bfloat16)
    result = middle + (project(activated, reduce_weight) + reduce_bias.astype(jnp.float32))
    saved = (
        hidden,
        normed,
        queries,
        key_rows,
        values,
        log_total,
        mixed_rows,
        middle,
        second,
        pre_act,
        activated,
    )
    return (result, saved)


def backward_layer(grad_out, params, saved):
    (
        heads_weight,
        heads_bias,
        merge_weight,
        merge_bias,
        first_gain,
        first_shift,
        second_gain,
        second_shift,
        expand_weight,
        expand_bias,
        reduce_weight,
        reduce_bias,
    ) = params
    (
        hidden,
        normed,
        queries,
        key_rows,
        values,
        log_total,
        mixed_rows,
        middle,
        second,
        pre_act,
        activated,
    ) = saved
    seq_len, model_width = hidden.shape
    shaped = (seq_len, HEADS, HEAD_DIM)
    score_scale = HEAD_DIM ** (-0.5)
    branch_low = grad_out.astype(jnp.bfloat16)
    reduce_weight_term = outer_sum(branch_low, activated)
    reduce_bias_term = jnp.sum(branch_low.astype(jnp.float32), axis=0)
    grad_act = carry_back(branch_low, reduce_weight)
    unused_value, gelu_back = jax.vjp(lambda point: jax.nn.gelu(point, approximate=True), pre_act)
    grad_pre = gelu_back(grad_act)[0].astype(jnp.bfloat16)
    expand_weight_term = outer_sum(grad_pre, second)
    expand_bias_term = jnp.sum(grad_pre.astype(jnp.float32), axis=0)
    grad_second = carry_back(grad_pre, expand_weight)
    unused_norm, second_back = jax.vjp(
        layer_norm, middle, second_gain.astype(jnp.float32), second_shift.astype(jnp.float32)
    )
    middle_part, second_gain_term, second_shift_term = second_back(grad_second)
    grad_middle = grad_out + middle_part
    attn_low = grad_middle.astype(jnp.bfloat16)
    merge_weight_term = outer_sum(attn_low, mixed_rows)
    merge_bias_term = jnp.sum(attn_low.astype(jnp.float32), axis=0)
    grad_mixed = carry_back(attn_low, merge_weight).astype(jnp.bfloat16).reshape(shaped)
    queries_heads = queries.reshape(shaped)
    keys_heads = key_rows.reshape(shaped)
    values_heads = values.reshape(shaped)
    scores = (
        jnp.einsum("qhd,khd->hqk", queries_heads, keys_heads, preferred_element_type=jnp.float32)
        * score_scale
    )
    attend = jnp.exp(scores - log_total)
    grad_values = jnp.einsum(
        "hqk,qhd->khd", attend.astype(jnp.bfloat16), grad_mixed, preferred_element_type=jnp.float32
    ).astype(jnp.bfloat16)
    grad_attend = jnp.einsum(
        "qhd,khd->hqk", grad_mixed, values_heads, preferred_element_type=jnp.float32
    )
    grad_scores = attend * (grad_attend - jnp.sum(grad_attend * attend, axis=-1, keepdims=True))
    grad_scores = grad_scores.astype(jnp.bfloat16)
    grad_queries = (
        jnp.einsum("hqk,khd->qhd", grad_scores, keys_heads, preferred_element_type=jnp.float32)
        * score_scale
    ).astype(jnp.bfloat16)
    grad_keys = (
        jnp.einsum("hqk,qhd->khd", grad_scores, queries_heads, preferred_element_type=jnp.float32)
        * score_scale
    ).astype(jnp.bfloat16)
    stacked_grads = jnp.stack(
        [
            grad_queries.reshape(seq_len, model_width),
            grad_keys.reshape(seq_len, model_width),
            grad_values.reshape(seq_len, model_width),
        ]
    )
    heads_weight_term = jnp.einsum(
        "jto,ti->joi", stacked_grads, normed, preferred_element_type=jnp.float32
    )
    grad_normed = jnp.einsum(
        "jto,joi->ti", stacked_grads, heads_weight, preferred_element_type=jnp.float32
    )
    heads_bias_term = jnp.stack(
        [
            jnp.sum(stacked_grads[0].astype(jnp.float32), axis=0),
            jnp.sum(stacked_grads[2].astype(jnp.float32), axis=0),
        ]
    )
    unused_first, first_back = jax.vjp(
        layer_norm, hidden, first_gain.astype(jnp.float32), first_shift.astype(jnp.float32)
    )
    hidden_part, first_gain_term, first_shift_term = first_back(grad_normed)
    grad_hidden = grad_middle + hidden_part
    terms = (
        heads_weight_term,
        heads_bias_term,
        merge_weight_term,
        merge_bias_term,
        first_gain_term,
        first_shift_term,
        second_gain_term,
        second_shift_term,
        expand_weight_term,
        expand_bias_term,
        reduce_weight_term,
        reduce_bias_term,
    )
    return (grad_hidden, terms)


def plain_shards(
    images,
    cotangent,
    slot_flags,
    heads_weight,
    heads_bias,
    merge_weight,
    merge_bias,
    first_gain,
    first_shift,
    second_gain,
    second_shift,
    expand_weight,
    expand_bias,
    reduce_weight,
    reduce_bias,
):
    micro_count = images.shape[0]
    seq_len = images.shape[2]
    layers = heads_weight.shape[0]
    live_flags = slot_flags.astype(jnp.float32)
    states = [images[batch_at, 0].astype(jnp.float32) for batch_at in range(micro_count)]
    saved_all = []
    for layer_at in range(layers):
        saved_row = []
        for batch_at in range(micro_count):
            params = (
                lax.all_gather(heads_weight[layer_at], "fsdp", axis=1, tiled=True),
                lax.all_gather(heads_bias[layer_at], "fsdp", axis=1, tiled=True),
                lax.all_gather(merge_weight[layer_at], "fsdp", axis=0, tiled=True),
                lax.all_gather(merge_bias[layer_at], "fsdp", axis=0, tiled=True),
                lax.all_gather(first_gain[layer_at], "fsdp", axis=0, tiled=True),
                lax.all_gather(first_shift[layer_at], "fsdp", axis=0, tiled=True),
                lax.all_gather(second_gain[layer_at], "fsdp", axis=0, tiled=True),
                lax.all_gather(second_shift[layer_at], "fsdp", axis=0, tiled=True),
                lax.all_gather(expand_weight[layer_at], "fsdp", axis=0, tiled=True),
                lax.all_gather(expand_bias[layer_at], "fsdp", axis=0, tiled=True),
                lax.all_gather(reduce_weight[layer_at], "fsdp", axis=0, tiled=True),
                lax.all_gather(reduce_bias[layer_at], "fsdp", axis=0, tiled=True),
            )
            states[batch_at], saved = forward_layer(states[batch_at], params)
            saved_row.append(saved)
        saved_all.append(saved_row)
    outputs = jnp.stack(
        [live_flags[batch_at, 0] * states[batch_at] for batch_at in range(micro_count)]
    )[:, None].astype(jnp.bfloat16)
    grads_back = [
        cotangent[batch_at, 0].astype(jnp.float32) * live_flags[batch_at, 0]
        for batch_at in range(micro_count)
    ]
    collected = [None] * layers
    for layer_at in reversed(range(layers)):
        totals = None
        for batch_at in range(micro_count):
            params = (
                lax.all_gather(heads_weight[layer_at], "fsdp", axis=1, tiled=True),
                lax.all_gather(heads_bias[layer_at], "fsdp", axis=1, tiled=True),
                lax.all_gather(merge_weight[layer_at], "fsdp", axis=0, tiled=True),
                lax.all_gather(merge_bias[layer_at], "fsdp", axis=0, tiled=True),
                lax.all_gather(first_gain[layer_at], "fsdp", axis=0, tiled=True),
                lax.all_gather(first_shift[layer_at], "fsdp", axis=0, tiled=True),
                lax.all_gather(second_gain[layer_at], "fsdp", axis=0, tiled=True),
                lax.all_gather(second_shift[layer_at], "fsdp", axis=0, tiled=True),
                lax.all_gather(expand_weight[layer_at], "fsdp", axis=0, tiled=True),
                lax.all_gather(expand_bias[layer_at], "fsdp", axis=0, tiled=True),
                lax.all_gather(reduce_weight[layer_at], "fsdp", axis=0, tiled=True),
                lax.all_gather(reduce_bias[layer_at], "fsdp", axis=0, tiled=True),
            )
            grads_back[batch_at], terms = backward_layer(
                grads_back[batch_at], params, saved_all[layer_at][batch_at]
            )
            if totals is None:
                totals = terms
            else:
                totals = tuple((earlier + current for earlier, current in zip(totals, terms)))
        collected[layer_at] = totals
    images_grad = jnp.stack(grads_back)[:, None].astype(jnp.bfloat16)
    stacked = [
        jnp.stack([collected[layer_at][member] for layer_at in range(layers)])
        for member in range(12)
    ]
    shares = (
        lax.psum_scatter(
            stacked[0].astype(jnp.bfloat16), "fsdp", scatter_dimension=2, tiled=True
        ).astype(jnp.float32),
        lax.psum_scatter(
            stacked[1].astype(jnp.bfloat16), "fsdp", scatter_dimension=2, tiled=True
        ).astype(jnp.float32),
        lax.psum_scatter(
            stacked[2].astype(jnp.bfloat16), "fsdp", scatter_dimension=1, tiled=True
        ).astype(jnp.float32),
        lax.psum_scatter(
            stacked[3].astype(jnp.bfloat16), "fsdp", scatter_dimension=1, tiled=True
        ).astype(jnp.float32),
        lax.psum_scatter(
            stacked[4].astype(jnp.bfloat16), "fsdp", scatter_dimension=1, tiled=True
        ).astype(jnp.float32),
        lax.psum_scatter(
            stacked[5].astype(jnp.bfloat16), "fsdp", scatter_dimension=1, tiled=True
        ).astype(jnp.float32),
        lax.psum_scatter(
            stacked[6].astype(jnp.bfloat16), "fsdp", scatter_dimension=1, tiled=True
        ).astype(jnp.float32),
        lax.psum_scatter(
            stacked[7].astype(jnp.bfloat16), "fsdp", scatter_dimension=1, tiled=True
        ).astype(jnp.float32),
        lax.psum_scatter(
            stacked[8].astype(jnp.bfloat16), "fsdp", scatter_dimension=1, tiled=True
        ).astype(jnp.float32),
        lax.psum_scatter(
            stacked[9].astype(jnp.bfloat16), "fsdp", scatter_dimension=1, tiled=True
        ).astype(jnp.float32),
        lax.psum_scatter(
            stacked[10].astype(jnp.bfloat16), "fsdp", scatter_dimension=1, tiled=True
        ).astype(jnp.float32),
        lax.psum_scatter(
            stacked[11].astype(jnp.bfloat16), "fsdp", scatter_dimension=1, tiled=True
        ).astype(jnp.float32),
    )
    reduced = (
        lax.psum(shares[0].astype(jnp.bfloat16), "rep").astype(jnp.float32),
        lax.psum(shares[1].astype(jnp.bfloat16), "rep").astype(jnp.float32),
        lax.psum(shares[2].astype(jnp.bfloat16), "rep").astype(jnp.float32),
        lax.psum(shares[3].astype(jnp.bfloat16), "rep").astype(jnp.float32),
        lax.psum(shares[4].astype(jnp.bfloat16), "rep").astype(jnp.float32),
        lax.psum(shares[5].astype(jnp.bfloat16), "rep").astype(jnp.float32),
        lax.psum(shares[6].astype(jnp.bfloat16), "rep").astype(jnp.float32),
        lax.psum(shares[7].astype(jnp.bfloat16), "rep").astype(jnp.float32),
        lax.psum(shares[8].astype(jnp.bfloat16), "rep").astype(jnp.float32),
        lax.psum(shares[9].astype(jnp.bfloat16), "rep").astype(jnp.float32),
        lax.psum(shares[10].astype(jnp.bfloat16), "rep").astype(jnp.float32),
        lax.psum(shares[11].astype(jnp.bfloat16), "rep").astype(jnp.float32),
    )
    grad_scale = (micro_count * lax.axis_size("fsdp") * lax.axis_size("rep") * seq_len) ** (-0.5)
    finals = tuple((member_sum * grad_scale for member_sum in reduced))
    return (outputs, images_grad) + finals


ROWS = 256
WIDTH = 768
FF_PARTS = 4
f32 = jnp.float32
bf16 = jnp.bfloat16
VMEM_BYTES = 52 * 1024 * 1024
SMALL_VMEM_BYTES = 24 * 1024 * 1024
LARGE_VMEM_BYTES = 60 * 1024 * 1024


def dot_nt(left, right):
    return lax.dot_general(left, right, (((1,), (1,)), ((), ())), preferred_element_type=f32)


def dot_nn(left, right):
    return lax.dot_general(left, right, (((1,), (0,)), ((), ())), preferred_element_type=f32)


def swap_core(value):
    return lax.ppermute(value, "fsdp", [(at, at ^ 1) for at in range(8)])


def swap_x(value):
    return lax.ppermute(value, "fsdp", [(at, at ^ 2) for at in range(8)])


def swap_y(value):
    return lax.ppermute(value, "fsdp", [(at, at ^ 4) for at in range(8)])


PIECES = 10


def regions_of(rows, cut, x_row, y_row):
    return [
        region
        for odd in range(2)
        for region in (
            (5 * odd, odd, 0, rows, 0),
            (5 * odd + 1, 2 ^ odd, 0, rows, x_row),
            (5 * odd + 2, 4 ^ odd, 0, rows, y_row),
            (5 * odd + 3, 6 ^ odd, 0, cut, 0),
            (5 * odd + 4, 6 ^ odd, cut, rows, 0),
        )
    ]


def block_copies(place, refs, regions, first, count, block, sems):
    copies = []
    for array_at, delta, low, high, start in regions:
        begin, end = max(low, first), min(high, first + count)
        if begin < end:
            copies.append(
                pltpu.make_async_copy(
                    refs[array_at].at[pl.ds(start + begin - low, end - begin)],
                    block.at[place ^ delta, pl.ds(begin - first, end - begin)],
                    sems.at[len(copies)],
                )
            )
    return copies


def run_all(copies, what):
    for copy in copies:
        getattr(copy, what)()


def in_any():
    return pl.BlockSpec(memory_space=pltpu.HBM)


def in_smem():
    return pl.BlockSpec(memory_space=pltpu.SMEM)


def params(steps=1):
    return pltpu.CompilerParams(
        dimension_semantics=("arbitrary",) * steps, vmem_limit_bytes=VMEM_BYTES
    )


def cost(micros):
    return pl.CostEstimate(flops=int(micros * 1.1e9), bytes_accessed=1 << 10, transcendentals=0)


def rows_spec(width):
    return pl.BlockSpec((ROWS, width), lambda image: (image, 0))


def part_spec(tokens):
    return pl.BlockSpec((tokens, WIDTH), lambda part: (0, part))


def fixed(shape):
    return pl.BlockSpec(shape, lambda image: (0,) * len(shape))


def normalise(rows):
    centre = rows - jnp.mean(rows, axis=-1, keepdims=True)
    root = lax.rsqrt(jnp.mean(centre * centre, axis=-1, keepdims=True) + norm_eps)
    return centre * root, root


PACK_ROWS = {"attn": 400, "ff": 768, "expand": 384, "reduce": 384}
PACK_CUTS = {"attn": 192, "ff": 384, "expand": 192, "reduce": 192}


def own_packs(wanted, matrices, vectors, first=False):
    count = len(wanted)
    needed = [
        at
        for at, users in enumerate(
            (("attn",), ("attn",), ("ff", "expand"), ("ff", "reduce"))
        )
        if any(kind in users for kind, layer in wanted)
    ]

    def kernel(*refs):
        heads_ref, merge_ref, expand_ref, reduce_ref = (
            refs[needed.index(at)] if at in needed else None for at in range(4)
        )
        vector_refs = refs[len(needed) : len(needed) + 8]
        outs, rows = refs[len(needed) + 8 : -1], refs[-1]
        for out, (kind, layer) in zip(outs, wanted):
            if kind == "attn":
                for at in range(3):
                    out[96 * at : 96 * at + 96] = heads_ref[layer, at]
                out[288:384] = merge_ref[layer]
                rows[...] = jnp.zeros_like(rows)
                rows[0:2, 0:96] = vector_refs[0][layer].astype(f32)
                for row in range(2, 8):
                    values = vector_refs[row - 1][...].astype(f32)
                    rows[row : row + 1, 0:96] = values[layer : layer + 1]
                rows[8:9, 0:384] = vector_refs[7][...].astype(f32)[layer : layer + 1]
                out[384:400] = rows[...].astype(bf16)
            if kind in ("ff", "expand"):
                out[0:384] = expand_ref[layer]
            if kind in ("ff", "reduce"):
                first = 384 if kind == "ff" else 0
                for part in range(FF_PARTS):
                    out[first + 96 * part : first + 96 * part + 96] = reduce_ref[
                        layer, :, WIDTH * part : WIDTH * (part + 1)
                    ]

    in_vmem = pl.BlockSpec(memory_space=pltpu.VMEM)
    return pl.pallas_call(
        kernel,
        in_specs=[in_vmem] * (len(needed) + 8),
        out_specs=[in_vmem] * count,
        out_shape=[
            jax.ShapeDtypeStruct((PACK_ROWS[kind], WIDTH), bf16) for kind, layer in wanted
        ],
        scratch_shapes=[pltpu.VMEM((16, WIDTH), f32)],
        compiler_params=pltpu.CompilerParams(vmem_limit_bytes=LARGE_VMEM_BYTES if first else SMALL_VMEM_BYTES),
        cost_estimate=cost(0.01),
        name="own_packs",
    )(*[matrices[at] for at in needed], *vectors)


def join_rows(pieces_of):
    flat = [piece for pieces in pieces_of for piece in pieces]
    heights = [sum(rows for unused, unused_first, rows in pieces) for pieces in pieces_of]

    def kernel(*refs):
        ins, outs, sems = refs[: len(flat)], refs[len(flat) : -1], refs[-1]
        copies = []
        for out, pieces in zip(outs, pieces_of):
            into = 0
            for unused, first, rows in pieces:
                at = len(copies)
                copies.append(
                    pltpu.make_async_copy(
                        ins[at].at[pl.ds(first, rows)], out.at[pl.ds(into, rows)], sems.at[at]
                    )
                )
                into += rows
        run_all(copies, "start")
        run_all(copies, "wait")

    return pl.pallas_call(
        kernel,
        in_specs=[in_any()] * len(flat),
        out_specs=[pl.BlockSpec(memory_space=pltpu.VMEM)] * len(heights),
        out_shape=[jax.ShapeDtypeStruct((rows, WIDTH), bf16) for rows in heights],
        scratch_shapes=[pltpu.SemaphoreType.DMA((len(flat),))],
        compiler_params=pltpu.CompilerParams(vmem_limit_bytes=SMALL_VMEM_BYTES),
        cost_estimate=cost(0.01),
        name="join_rows",
    )(*[array for array, unused, unused_rows in flat])


def gathered_vectors(place, pack):
    arrays, regions = pack
    used = {}
    for array_at, delta, low, high, start in regions:
        if low <= 384 and 400 <= high:
            used[delta] = (arrays[array_at], start + 384 - low)
    deltas = sorted(used)

    def kernel(place_ref, *refs):
        ins, small_ref, expand_ref, rows, sems = refs[:8], refs[8], refs[9], refs[10], refs[11]
        copies = [
            pltpu.make_async_copy(
                ins[at].at[pl.ds(used[delta][1], 16)], rows.at[at], sems.at[at]
            )
            for at, delta in enumerate(deltas)
        ]
        run_all(copies, "start")
        here = place_ref[0]
        row = lax.broadcasted_iota(jnp.int32, (1024, WIDTH), 0)
        column = lax.broadcasted_iota(jnp.int32, (1024, WIDTH), 1)
        at = row & 127
        wanted = 96 * ((row >> 7) ^ here) + at
        chosen = jnp.where((column == wanted) & (at < 96), 1.0, 0.0).astype(bf16)
        run_all(copies, "wait")
        flat = jnp.concatenate([rows[at, 0:8, 0:128].astype(f32) for at in range(8)], axis=1)
        small_ref[...] = dot_nn(flat.astype(bf16), chosen)
        for at, delta in enumerate(deltas):
            owner = here ^ delta
            line = rows[at].astype(f32)[8:9, 0:384]

            @pl.when((owner & 1) == 0)
            def left():
                expand_ref[owner >> 1, :, 0:384] = line

            @pl.when((owner & 1) == 1)
            def right():
                expand_ref[owner >> 1, :, 384:768] = line

    shape = jax.ShapeDtypeStruct
    return pl.pallas_call(
        kernel,
        in_specs=[in_smem()] + [in_any()] * 8,
        out_specs=[pl.BlockSpec(memory_space=pltpu.VMEM)] * 2,
        out_shape=[shape((8, WIDTH), f32), shape((4, 1, WIDTH), f32)],
        scratch_shapes=[pltpu.VMEM((8, 16, WIDTH), bf16), pltpu.SemaphoreType.DMA((8,))],
        compiler_params=pltpu.CompilerParams(vmem_limit_bytes=SMALL_VMEM_BYTES),
        cost_estimate=cost(0.01),
        name="gathered_vectors",
    )(place, *[used[delta][0] for delta in deltas])


def elementwise(name, body, ins, out_shapes):
    def kernel(*refs):
        body(refs[: len(ins)], refs[len(ins) :])

    return pl.pallas_call(
        kernel,
        in_specs=[pl.BlockSpec(memory_space=pltpu.VMEM)] * len(ins),
        out_specs=[pl.BlockSpec(memory_space=pltpu.VMEM)] * len(out_shapes),
        out_shape=[jax.ShapeDtypeStruct(shape, bf16) for shape in out_shapes],
        compiler_params=pltpu.CompilerParams(vmem_limit_bytes=SMALL_VMEM_BYTES),
        cost_estimate=cost(0.01),
        name=name,
    )(*ins)


def add_low(*parts):
    total = parts[0].astype(f32)
    for part in parts[1:]:
        total = total + part.astype(f32)
    return total.astype(bf16)


def first_steps(travel):
    go_x, go_y, stay_x, stay_y = travel
    return swap_x(go_x), swap_y(go_y), stay_x, stay_y


def second_steps(state):
    def body(ins, outs):
        from_x, from_y, stay_x, stay_y = ins
        outs[0][...] = add_low(stay_x[1], from_x[1])
        outs[1][...] = add_low(stay_y[1], from_y[1])
        outs[2][...] = add_low(stay_x[0], from_x[0])
        outs[3][...] = add_low(stay_y[0], from_y[0])

    low, high = state[0].shape[1:], state[1].shape[1:]
    low_on, high_on, kept_low, kept_high = elementwise(
        "second_steps", body, state, [low, high, low, high]
    )
    return swap_y(low_on), swap_x(high_on), kept_low, kept_high


def ends(state):
    from_y, from_x, kept_low, kept_high = state
    low, high = kept_low.shape[0], kept_high.shape[0]

    def body(ins, outs):
        outs[0][0:low] = add_low(ins[2][...], ins[0][...])
        outs[0][low : low + high] = add_low(ins[3][...], ins[1][...])

    return elementwise("ends", body, state, [(low + high, WIDTH // 2)])[0]


def to_middle(part):
    return part, lax.ppermute(part, "rep", [(0, 1), (3, 2)])


def plus(parts):
    def body(ins, outs):
        outs[0][...] = add_low(ins[0][...], ins[1][...])

    return elementwise("plus", body, parts, [parts[0].shape])[0]


def across_middle(parts):
    inward = plus(parts)
    return inward, lax.ppermute(inward, "rep", [(1, 2), (2, 1)])


def to_ends(parts):
    total = plus(parts)
    return total, lax.ppermute(total, "rep", [(1, 0), (2, 3)])


SM_HB0, SM_HB1, SM_MB, SM_G1, SM_S1, SM_G2, SM_S2, SM_RB = range(8)


def unit_copies(place, refs, regions, first, blocks, sems):
    copies = []
    count = 96 * blocks.shape[0]
    for array_at, delta, low, high, start in regions:
        begin, end = max(low, first), min(high, first + count)
        if begin < end:
            units = (end - begin) // 96
            source = refs[array_at].at[pl.ds(start + begin - low, end - begin)]
            copies.append(
                pltpu.make_async_copy(
                    source.reshape(units, 96, WIDTH),
                    blocks.at[pl.ds((begin - first) // 96, units), place ^ delta],
                    sems.at[len(copies)],
                )
            )
    return copies


def attn_forward(place, hidden, small, pack):

    def kernel(place_ref, hidden_ref, small_ref, *rest):
        packs = rest[:PIECES]
        middle_ref, normed_ref, qkv_ref, mixed_ref, blocks, sems = rest[PIECES:]
        place_now = place_ref[0]
        image = pl.program_id(0)
        copies = unit_copies(place_now, packs, pack[1], 0, blocks, sems)

        @pl.when(image == 0)
        def begin():
            run_all(copies, "start")

        rows = hidden_ref[...].astype(f32)
        unit, root = normalise(rows)
        normed = (unit * small_ref[SM_G1 : SM_G1 + 1] + small_ref[SM_S1 : SM_S1 + 1]).astype(bf16)
        normed_ref[...] = normed

        @pl.when(image == 0)
        def arrive():
            run_all(copies, "wait")

        for member, bias in ((0, SM_HB0), (1, None), (2, SM_HB1)):
            block = blocks[member].reshape(WIDTH, WIDTH)
            made = dot_nt(normed, block)
            if bias is not None:
                made = made + small_ref[bias : bias + 1]
            qkv_ref[:, WIDTH * member : WIDTH * (member + 1)] = made.astype(bf16)
        lane = lax.broadcasted_iota(jnp.int32, (ROWS, 128), 1)
        for pair in range(HEADS // 2):
            q_pair = qkv_ref[:, 128 * pair : 128 * pair + 128] * HEAD_DIM**-0.5
            k_pair = qkv_ref[:, WIDTH + 128 * pair : WIDTH + 128 * pair + 128]
            v_pair = qkv_ref[:, 2 * WIDTH + 128 * pair : 2 * WIDTH + 128 * pair + 128]
            parts = []
            for half in range(2):
                here = (lane < 64) == (half == 0)
                scores = dot_nt(jnp.where(here, q_pair, jnp.zeros_like(q_pair)), k_pair)
                peak = jnp.max(scores, axis=-1, keepdims=True)
                powers = jnp.exp(scores - peak).astype(bf16)
                parts.append(dot_nn(powers, jnp.where(here, v_pair, jnp.ones_like(v_pair))))
            totals = pltpu.roll(jnp.where(lane < 64, parts[1], parts[0]), 64, 1)
            mixed_ref[:, 128 * pair : 128 * pair + 128] = (
                jnp.where(lane < 64, parts[0], parts[1]) / totals
            ).astype(bf16)
        merged = dot_nt(mixed_ref[...], blocks[3].reshape(WIDTH, WIDTH))
        middle_ref[...] = rows + (merged + small_ref[SM_MB : SM_MB + 1])

    tokens = hidden.shape[0]
    shape = jax.ShapeDtypeStruct
    return pl.pallas_call(
        kernel,
        grid=(tokens // ROWS,),
        in_specs=[in_smem(), rows_spec(WIDTH), fixed(small.shape)] + [in_any()] * PIECES,
        out_specs=[rows_spec(WIDTH), rows_spec(WIDTH), rows_spec(3 * WIDTH), rows_spec(WIDTH)],
        out_shape=[
            shape((tokens, WIDTH), f32),
            shape((tokens, WIDTH), bf16),
            shape((tokens, 3 * WIDTH), bf16),
            shape((tokens, WIDTH), bf16),
        ],
        scratch_shapes=[
            pltpu.VMEM((4, 8, 96, WIDTH), bf16),
            pltpu.SemaphoreType.DMA((PIECES,)),
        ],
        compiler_params=params(),
        cost_estimate=cost(0.01),
        name="attn_forward",
    )(place, hidden, small, *pack[0])


def expand_forward(place, middle, small, expand_bias, pack, first):
    tokens = middle.shape[0]

    def kernel(place_ref, middle_ref, small_ref, bias_ref, *rest):
        packs = rest[:PIECES]
        normed_ref, active_ref, slope_ref, block, sems = rest[PIECES:]
        part = pl.program_id(0)
        copies = block_copies(place_ref[0], packs, pack[1], first, 384, block, sems)

        @pl.when(part == 0)
        def begin():
            run_all(copies, "start")
            unit, root = normalise(middle_ref[...])
            normed_ref[...] = (
                unit * small_ref[SM_G2 : SM_G2 + 1] + small_ref[SM_S2 : SM_S2 + 1]
            ).astype(bf16)
            run_all(copies, "wait")

        weight = block[pl.ds(2 * part, 2)].reshape(WIDTH, WIDTH)
        point = dot_nt(normed_ref[...], weight) + bias_ref[part]
        root, cubic = 0.7978845608028654, 0.044715
        square = point * point
        upper = 0.5 + 0.5 * jnp.tanh(point * (root + (root * cubic) * square))
        active_ref[...] = (point * upper).astype(bf16)
        bend = point * (2.0 * root + (6.0 * root * cubic) * square)
        slope_ref[...] = (upper * (1.0 + bend * (1.0 - upper))).astype(bf16)

    hidden_units = FF_PARTS * WIDTH
    shape = jax.ShapeDtypeStruct
    return pl.pallas_call(
        kernel,
        grid=(FF_PARTS,),
        in_specs=[
            in_smem(),
            fixed(middle.shape),
            fixed(small.shape),
            fixed(expand_bias.shape),
        ]
        + [in_any()] * PIECES,
        out_specs=[fixed(middle.shape), part_spec(tokens), part_spec(tokens)],
        out_shape=[
            shape((tokens, WIDTH), bf16),
            shape((tokens, hidden_units), bf16),
            shape((tokens, hidden_units), bf16),
        ],
        scratch_shapes=[
            pltpu.VMEM((8, 384, WIDTH), bf16),
            pltpu.SemaphoreType.DMA((PIECES,)),
        ],
        compiler_params=params(),
        cost_estimate=cost(0.01),
        name="expand_forward",
    )(place, middle, small, expand_bias, *pack[0])


def reduce_copies(place_now, packs, regions, first, blocks, sems):
    return [
        block_copies(
            place_now, packs, regions, first + 96 * part, 96, blocks.at[part], sems.at[part]
        )
        for part in range(FF_PARTS)
    ]


def for_part(part, groups, what):
    for at, group in enumerate(groups):

        @pl.when(part == at)
        def run():
            run_all(group, what)


def reduce_forward(place, live, middle, active, small, pack, first, last):
    tokens = middle.shape[0]

    def kernel(place_ref, live_ref, middle_ref, active_ref, small_ref, *rest):
        packs = rest[:PIECES]
        result_ref, total, blocks, sems = rest[PIECES:]
        part = pl.program_id(0)
        copies = reduce_copies(place_ref[0], packs, pack[1], first, blocks, sems)

        @pl.when(part == 0)
        def begin():
            for group in copies:
                run_all(group, "start")
            total[...] = middle_ref[...] + small_ref[SM_RB : SM_RB + 1]

        for_part(part, copies, "wait")
        total[...] += dot_nt(active_ref[...], blocks[part].reshape(WIDTH, WIDTH))

        @pl.when(part == FF_PARTS - 1)
        def end():
            if last:
                for image in range(tokens // ROWS):
                    rows = slice(ROWS * image, ROWS * (image + 1))
                    result_ref[rows] = (
                        total[rows] * live_ref[image, 0].astype(f32)
                    ).astype(result_ref.dtype)
            else:
                result_ref[...] = total[...].astype(result_ref.dtype)

    return pl.pallas_call(
        kernel,
        grid=(FF_PARTS,),
        in_specs=[
            in_smem(),
            in_smem(),
            fixed(middle.shape),
            part_spec(tokens),
            fixed(small.shape),
        ]
        + [in_any()] * PIECES,
        out_specs=fixed(middle.shape),
        out_shape=jax.ShapeDtypeStruct((tokens, WIDTH), bf16 if last else f32),
        scratch_shapes=[
            pltpu.VMEM((tokens, WIDTH), f32),
            pltpu.VMEM((FF_PARTS, 8, 96, WIDTH), bf16),
            pltpu.SemaphoreType.DMA((FF_PARTS, PIECES)),
        ],
        compiler_params=params(),
        cost_estimate=cost(0.01),
        name="reduce_forward",
    )(place, live, middle, active, small, *pack[0])


def split_owners(place_now, turned, mine_ref, theirs_ref, count, lead=()):
    core = place_now & 1
    chip = place_now >> 1
    for owner in range(4):
        mine_ref[lead + (owner ^ chip,)] = turned[2 * owner + core]
        theirs_ref[lead + (owner ^ chip,)] = turned[2 * owner + 1 - core]


def halves_spec(count):
    return pl.BlockSpec((4, count, ROWS), lambda image: (0, 0, image))


def start_grad(place, live, cotangent):
    def kernel(place_ref, live_ref, cot_ref, grad_ref, mine_ref, theirs_ref, turned):
        image = pl.program_id(0)
        grad = cot_ref[...].astype(f32) * live_ref[image, 0].astype(f32)
        grad_ref[...] = grad.astype(bf16)
        turned[...] = grad.T.astype(bf16).reshape(8, 96, ROWS)
        split_owners(place_ref[0], turned, mine_ref, theirs_ref, 96)

    tokens = cotangent.shape[0]
    shape = jax.ShapeDtypeStruct
    return pl.pallas_call(
        kernel,
        grid=(tokens // ROWS,),
        in_specs=[in_smem(), in_smem(), rows_spec(WIDTH)],
        out_specs=[rows_spec(WIDTH), halves_spec(96), halves_spec(96)],
        out_shape=[shape((tokens, WIDTH), bf16)] + [shape((4, 96, tokens), bf16)] * 2,
        scratch_shapes=[pltpu.VMEM((8, 96, ROWS), bf16)],
        compiler_params=params(),
        cost_estimate=cost(0.01),
        name="start_grad",
    )(place, live, cotangent)


def fetch(source, target, sem):
    return pltpu.make_async_copy(source, target, sem)


def ff_backward(place, grad, slope, middle, small, expand_pack, reduce_pack):
    tokens = middle.shape[0]
    (expand_arrays, expand_regions), expand_first = expand_pack
    (reduce_arrays, reduce_regions), reduce_first = reduce_pack

    def kernel(place_ref, grad_in, slope_in, middle_in, small_ref, *rest):
        expand_packs, reduce_packs = rest[:PIECES], rest[PIECES : 2 * PIECES]
        (
            out_ref,
            pre_mine,
            pre_theirs,
            attn_mine,
            attn_theirs,
            sums_ref,
            grad_ref,
            slope_ref,
            middle_ref,
            expand_block,
            reduce_blocks,
            turned_pre,
            turned_attn,
            pre_low,
            expand_sems,
            reduce_sems,
            in_sems,
            out_sems,
        ) = rest[2 * PIECES :]
        place_now = place_ref[0]
        core = place_now & 1
        chip = place_now >> 1
        copies = reduce_copies(
            place_now, reduce_packs, reduce_regions, reduce_first, reduce_blocks, reduce_sems
        )
        expand_copies = block_copies(
            place_now, expand_packs, expand_regions, expand_first, 384, expand_block, expand_sems
        )
        grad_copy = fetch(grad_in, grad_ref, in_sems.at[0])
        middle_copy = fetch(middle_in, middle_ref, in_sems.at[1])
        slope_copies = [
            fetch(
                slope_in.at[:, pl.ds(WIDTH * part, WIDTH)], slope_ref.at[part], in_sems.at[2 + part]
            )
            for part in range(FF_PARTS)
        ]
        grad_copy.start()
        for part in range(FF_PARTS):
            run_all(copies[part], "start")
            slope_copies[part].start()
        run_all(expand_copies, "start")
        middle_copy.start()

        sent = []

        def send(source, target):
            copy = pltpu.make_async_copy(source, target, out_sems.at[len(sent)])
            copy.start()
            sent.append(copy)

        grad_copy.wait()
        low = grad_ref[...].astype(bf16)
        sums_ref[2:3] = jnp.sum(low.astype(f32), axis=0, keepdims=True)
        for part in range(FF_PARTS):
            run_all(copies[part], "wait")
            slope_copies[part].wait()
            up = dot_nn(low, reduce_blocks[part].reshape(WIDTH, WIDTH))
            pre = (up * slope_ref[part].astype(f32)).astype(bf16)
            pre_low[part] = pre
            sums_ref[4 + part : 5 + part] = jnp.sum(pre.astype(f32), axis=0, keepdims=True)
            turned_pre[2 * part : 2 * part + 2] = pre.T.reshape(2, 384, tokens)
            send(turned_pre.at[2 * part + core], pre_mine.at[part ^ chip])
            send(turned_pre.at[2 * part + 1 - core], pre_theirs.at[part ^ chip])
        run_all(expand_copies, "wait")
        back = dot_nn(pre_low[0], expand_block[0:2].reshape(WIDTH, WIDTH))
        for part in range(1, FF_PARTS):
            back = back + dot_nn(
                pre_low[part], expand_block[2 * part : 2 * part + 2].reshape(WIDTH, WIDTH)
            )
        middle_copy.wait()
        unit, root = normalise(middle_ref[...])
        sums_ref[0:1] = jnp.sum(back * unit, axis=0, keepdims=True)
        sums_ref[1:2] = jnp.sum(back, axis=0, keepdims=True)
        scaled = back * small_ref[SM_G2 : SM_G2 + 1]
        result = grad_ref[...].astype(f32) + root * (
            scaled
            - jnp.mean(scaled, axis=-1, keepdims=True)
            - unit * jnp.mean(scaled * unit, axis=-1, keepdims=True)
        )
        out_ref[...] = result
        result_low = result.astype(bf16)
        sums_ref[3:4] = jnp.sum(result_low.astype(f32), axis=0, keepdims=True)
        turned_attn[...] = result_low.T.reshape(8, 96, tokens)
        for owner in range(4):
            send(turned_attn.at[2 * owner + core], attn_mine.at[owner ^ chip])
            send(turned_attn.at[2 * owner + 1 - core], attn_theirs.at[owner ^ chip])
        run_all(sent, "wait")

    shape = jax.ShapeDtypeStruct
    in_vmem = pl.BlockSpec(memory_space=pltpu.VMEM)
    return pl.pallas_call(
        kernel,
        in_specs=[in_smem()] + [in_any()] * 3 + [in_vmem] + [in_any()] * (2 * PIECES),
        out_specs=[in_vmem] + [in_any()] * 4 + [in_vmem],
        out_shape=[shape((tokens, WIDTH), f32)]
        + [shape((4, 384, tokens), bf16)] * 2
        + [shape((4, 96, tokens), bf16)] * 2
        + [shape((8, WIDTH), f32)],
        scratch_shapes=[
            pltpu.VMEM((tokens, WIDTH), grad.dtype),
            pltpu.VMEM((FF_PARTS, tokens, WIDTH), bf16),
            pltpu.VMEM((tokens, WIDTH), f32),
            pltpu.VMEM((8, 384, WIDTH), bf16),
            pltpu.VMEM((FF_PARTS, 8, 96, WIDTH), bf16),
            pltpu.VMEM((8, 384, tokens), bf16),
            pltpu.VMEM((8, 96, tokens), bf16),
            pltpu.VMEM((FF_PARTS, tokens, WIDTH), bf16),
            pltpu.SemaphoreType.DMA((PIECES,)),
            pltpu.SemaphoreType.DMA((FF_PARTS, PIECES)),
            pltpu.SemaphoreType.DMA((2 + FF_PARTS,)),
            pltpu.SemaphoreType.DMA((16,)),
        ],
        compiler_params=pltpu.CompilerParams(vmem_limit_bytes=VMEM_BYTES),
        cost_estimate=cost(0.01),
        name="ff_backward",
    )(place, grad, slope, middle, small, *expand_arrays, *reduce_arrays)


def chosen_columns(place):
    def kernel(place_ref, out_ref):
        row = lax.broadcasted_iota(jnp.int32, (WIDTH, 1024), 0)
        column = lax.broadcasted_iota(jnp.int32, (WIDTH, 1024), 1)
        at = column & 127
        wanted = 96 * ((column >> 7) ^ place_ref[0]) + at
        out_ref[...] = jnp.where((row == wanted) & (at < 96), 1.0, 0.0).astype(bf16)

    return pl.pallas_call(
        kernel,
        in_specs=[in_smem()],
        out_specs=pl.BlockSpec(memory_space=pltpu.VMEM),
        out_shape=jax.ShapeDtypeStruct((WIDTH, 1024), bf16),
        compiler_params=pltpu.CompilerParams(vmem_limit_bytes=LARGE_VMEM_BYTES),
        cost_estimate=cost(0.01),
        name="chosen_columns",
    )(place)


def attn_backward(place, grad, hidden, qkv, mixed, small, ff_sums, chosen, pack, last):
    tokens = grad.shape[0]

    def kernel(
        place_ref, grad_in, hidden_in, qkv_in, mixed_in, chosen_in, small_ref, ff_sums_ref, *rest
    ):
        packs = rest[:PIECES]
        out_ref, qkv_mine, qkv_theirs, vec_mine, vec_theirs = rest[PIECES : PIECES + 5]
        if not last:
            low_mine, low_theirs = rest[PIECES + 5 : PIECES + 7]
        (
            grad_ref,
            hidden_ref,
            qkv_ref,
            mixed_ref,
            chosen_ref,
            blocks,
            turned,
            sums_ref,
            sems,
            in_sems,
            out_sems,
        ) = rest[-11:]
        place_now = place_ref[0]
        core = place_now & 1
        chip = place_now >> 1
        merge_copies = unit_copies(
            place_now, packs, pack[1], 288, blocks.at[pl.ds(3, 1)], sems.at[0]
        )
        heads_copies = unit_copies(
            place_now, packs, pack[1], 0, blocks.at[pl.ds(0, 3)], sems.at[1]
        )
        fetches = [
            fetch(source, target, in_sems.at[at])
            for at, (source, target) in enumerate(
                (
                    (grad_in, grad_ref),
                    (mixed_in, mixed_ref),
                    (qkv_in, qkv_ref),
                    (hidden_in, hidden_ref),
                    (chosen_in, chosen_ref),
                )
            )
        ]
        fetches[0].start()
        run_all(merge_copies, "start")
        run_all(fetches[1:], "start")
        run_all(heads_copies, "start")
        sent = []

        def send(source, target):
            copy = pltpu.make_async_copy(source, target, out_sems.at[len(sent)])
            copy.start()
            sent.append(copy)

        fetches[0].wait()
        run_all(merge_copies, "wait")
        grad_rows = grad_ref[...]
        mixed_back = dot_nn(grad_rows.astype(bf16), blocks[3].reshape(WIDTH, WIDTH)).astype(bf16)
        fetches[1].wait()
        product = mixed_back.astype(f32) * mixed_ref[...].astype(f32)
        product_high = product.astype(bf16)
        product_low = (product - product_high.astype(f32)).astype(bf16)
        head_row = lax.broadcasted_iota(jnp.int32, (16, WIDTH), 0)
        head_column = lax.broadcasted_iota(jnp.int32, (16, WIDTH), 1) >> 6
        of_head = jnp.where(head_row == head_column, 1.0, 0.0).astype(bf16)
        inner = dot_nt(of_head, product_high) + dot_nt(of_head, product_low)
        fetches[2].wait()
        lane = lax.broadcasted_iota(jnp.int32, (ROWS, 128), 1)
        line = lax.broadcasted_iota(jnp.int32, (128, ROWS), 0)
        scale = HEAD_DIM**-0.5
        for image in range(tokens // ROWS):
            rows = slice(ROWS * image, ROWS * (image + 1))
            for pair in range(HEADS // 2):
                q_pair = qkv_ref[rows, 128 * pair : 128 * pair + 128]
                k_pair = qkv_ref[rows, WIDTH + 128 * pair : WIDTH + 128 * pair + 128]
                v_pair = qkv_ref[rows, 2 * WIDTH + 128 * pair : 2 * WIDTH + 128 * pair + 128]
                g_pair = mixed_back[rows, 128 * pair : 128 * pair + 128]
                k_turned = k_pair.T
                weights, powers, inverses = [], [], []
                for half in range(2):
                    here = (lane < 64) == (half == 0)
                    k_one = jnp.where(here, k_pair * scale, jnp.zeros_like(k_pair))
                    v_one = jnp.where(here, v_pair, jnp.zeros_like(v_pair))
                    scores = dot_nt(k_one, q_pair)
                    power = jnp.exp(scores - jnp.max(scores, axis=0, keepdims=True))
                    inverses.append(1.0 / jnp.sum(power, axis=0, keepdims=True))
                    head = 2 * pair + half
                    back = dot_nt(v_one, g_pair) - inner[head : head + 1, rows]
                    weights.append((power * back).astype(bf16))
                    powers.append(power.astype(bf16))
                inverse = jnp.where(line < 64, inverses[0], inverses[1])
                q_turned = (q_pair.T.astype(f32) * (inverse * scale)).astype(bf16)
                g_turned = (g_pair.T.astype(f32) * inverse).astype(bf16)
                made = (
                    jnp.where(
                        line < 64, dot_nn(k_turned, weights[0]), dot_nn(k_turned, weights[1])
                    )
                    * (inverse * scale),
                    jnp.where(
                        line < 64, dot_nt(q_turned, weights[0]), dot_nt(q_turned, weights[1])
                    ),
                    jnp.where(
                        line < 64, dot_nt(g_turned, powers[0]), dot_nt(g_turned, powers[1])
                    ),
                )
                for member in range(3):
                    turned[member, 128 * pair : 128 * pair + 128, rows] = made[member].astype(bf16)
        for member in range(3):
            for owner in range(4):
                for odd in range(2):
                    target = qkv_theirs if odd else qkv_mine
                    first = pl.multiple_of(192 * owner + 96 * (core ^ odd), 96)
                    send(turned.at[member, pl.ds(first, 96)], target.at[member, owner ^ chip])
        back = jnp.zeros((tokens, WIDTH), f32)
        ones = jnp.ones((8, tokens), bf16)
        run_all(heads_copies, "wait")
        for member in range(3):
            back = back + lax.dot_general(
                turned[member],
                blocks[member].reshape(WIDTH, WIDTH),
                (((0,), (0,)), ((), ())),
                preferred_element_type=f32,
            )
        sums_ref[0:1] = dot_nt(ones, turned[0])[0:1]
        sums_ref[1:2] = dot_nt(ones, turned[2])[0:1]
        fetches[3].wait()
        unit, root = normalise(hidden_ref[...].astype(f32))
        sums_ref[3:4] = jnp.sum(back * unit, axis=0, keepdims=True)
        sums_ref[4:5] = jnp.sum(back, axis=0, keepdims=True)
        scaled = back * small_ref[SM_G1 : SM_G1 + 1]
        result = grad_ref[...] + root * (
            scaled
            - jnp.mean(scaled, axis=-1, keepdims=True)
            - unit * jnp.mean(scaled * unit, axis=-1, keepdims=True)
        )
        out_ref[...] = result.astype(out_ref.dtype)
        run_all(sent, "wait")
        sent.clear()
        if not last:
            turned[0] = result.astype(bf16).T
            for owner in range(4):
                for odd in range(2):
                    target = low_theirs if odd else low_mine
                    first = pl.multiple_of(192 * owner + 96 * (core ^ odd), 96)
                    send(turned.at[0, pl.ds(first, 96)], target.at[owner ^ chip])

        sums_ref[2:3] = ff_sums_ref[3:4]
        sums_ref[5:8] = ff_sums_ref[0:3]
        fetches[4].wait()
        rest_of = sums_ref[...]
        cut = jnp.zeros((8, 1024), f32)
        for term in range(3):
            term_low = rest_of.astype(bf16)
            rest_of = rest_of - term_low.astype(f32)
            cut = cut + dot_nn(term_low, chosen_ref[...])
        for delta in range(8):
            owner = place_now ^ delta
            target = vec_theirs if delta & 1 else vec_mine
            target[delta >> 1] = jnp.zeros((16, WIDTH // 2), f32)
            target[delta >> 1, 0:8, 0:128] = cut[:, 128 * delta : 128 * delta + 128]
            values = ff_sums_ref[pl.ds(4 + (owner >> 1), 1)]
            target[delta >> 1, 8:9] = jnp.where(
                (owner & 1) == 0, values[:, : WIDTH // 2], values[:, WIDTH // 2 :]
            )
        run_all(sent, "wait")

    shape = jax.ShapeDtypeStruct
    in_vmem = pl.BlockSpec(memory_space=pltpu.VMEM)
    vector_shape = (4, 16, WIDTH // 2)
    out_specs = [in_vmem] + [in_any()] * 2 + [in_vmem] * 2
    out_shape = (
        [shape((tokens, WIDTH), bf16 if last else f32)]
        + [shape((3, 4, 96, tokens), bf16)] * 2
        + [shape(vector_shape, f32)] * 2
    )
    if not last:
        out_specs += [in_any()] * 2
        out_shape += [shape((4, 96, tokens), bf16)] * 2
    return pl.pallas_call(
        kernel,
        in_specs=[in_smem()] + [in_any()] * 5 + [in_vmem] * 2 + [in_any()] * PIECES,
        out_specs=out_specs,
        out_shape=out_shape,
        scratch_shapes=[
            pltpu.VMEM((tokens, WIDTH), grad.dtype),
            pltpu.VMEM((tokens, WIDTH), hidden.dtype),
            pltpu.VMEM((tokens, 3 * WIDTH), bf16),
            pltpu.VMEM((tokens, WIDTH), bf16),
            pltpu.VMEM((WIDTH, 1024), bf16),
            pltpu.VMEM((4, 8, 96, WIDTH), bf16),
            pltpu.VMEM((3, WIDTH, tokens), bf16),
            pltpu.VMEM((8, WIDTH), f32),
            pltpu.SemaphoreType.DMA((2, PIECES)),
            pltpu.SemaphoreType.DMA((5,)),
            pltpu.SemaphoreType.DMA((24,)),
        ],
        compiler_params=pltpu.CompilerParams(vmem_limit_bytes=VMEM_BYTES),
        cost_estimate=cost(0.01),
        name="attn_backward",
    )(place, grad, hidden, qkv, mixed, chosen, small, ff_sums, *pack[0])


def spread(result, owner, rows, out_refs):
    go_x, go_y, stay_x, stay_y = out_refs
    half = WIDTH // 2
    low, high = result[:, :half].astype(bf16), result[:, half:].astype(bf16)
    target, at = ((stay_x, 0), (go_x, 0), (stay_x, 1), (go_x, 1))[owner]
    target[at, rows] = low
    target, at = ((stay_y, 0), (stay_y, 1), (go_y, 0), (go_y, 1))[owner]
    target[at, rows] = high


def travel_shapes(rows_low, rows_high):
    shape = jax.ShapeDtypeStruct
    half = WIDTH // 2
    return [shape((2, rows, half), bf16) for rows in (rows_low, rows_high, rows_low, rows_high)]


def owner_terms(reduce=None, expand=None, merge=None, heads=None, small_terms=None):
    given, in_specs, sections = [], [], []
    rows = 0
    tokens = (reduce or expand or heads)[1][0].shape[0]
    whole = pl.BlockSpec((tokens, WIDTH), lambda at: (0, 0))
    four = pl.BlockSpec((4, 96, tokens), lambda at: (0, 0, 0))
    for name, pair, left, right, taken in (
        ("reduce", reduce, four, pl.BlockSpec((tokens, WIDTH), lambda at: (0, at)), 384),
        ("expand", expand, pl.BlockSpec((1, 384, tokens), lambda at: (at, 0, 0)), whole, 384),
        ("merge", merge, four, whole, 96),
        (
            "heads",
            heads,
            pl.BlockSpec((1, 4, 96, tokens), lambda at: (jnp.minimum(at, 2), 0, 0, 0)),
            whole,
            288,
        ),
    ):
        if pair is not None:
            given += [*pair[0], *pair[1]]
            in_specs += [left, left, right, right]
            sections.append((name, rows))
            rows += taken
    extra = 0
    if small_terms is not None:
        given += small_terms
        in_specs += [pl.BlockSpec(small_terms[0].shape, lambda at: (0, 0, 0))] * 2
        extra = 16

    def kernel(*refs):
        ins, out_refs = refs[: len(given)], refs[len(given) :]
        go_x, go_y, stay_x, stay_y = out_refs
        part = pl.program_id(0)

        def multiply(place, first):
            left_a, left_b, right_a, right_b = ins[4 * place : 4 * place + 4]
            result = dot_nn(left_a[...].reshape(384, tokens), right_a[...]) + dot_nn(
                left_b[...].reshape(384, tokens), right_b[...]
            )
            if first is None:
                return result
            for owner in range(4):
                spread(
                    result[96 * owner : 96 * owner + 96], owner, pl.ds(first, 96), out_refs
                )

        for place, (name, first) in enumerate(sections):
            if name == "reduce":
                multiply(place, pl.multiple_of(first + 96 * part, 96))
            elif name == "heads":

                @pl.when(part < 3)
                def one_head_block():
                    multiply(place, pl.multiple_of(first + 96 * part, 96))

            elif name == "merge":

                @pl.when(part == 3)
                def merge_block():
                    multiply(place, first)

            else:
                result = multiply(place, None)
                for owner in range(4):

                    @pl.when(part == owner)
                    def keep():
                        spread(result, owner, slice(first, first + 384), out_refs)

        if small_terms is not None:

            @pl.when(part == 3)
            def vectors():
                for owner in range(4):
                    target, at = ((stay_x, 0), (go_x, 0), (stay_x, 1), (go_x, 1))[owner]
                    target[at, rows : rows + 16] = (ins[-2][owner] + ins[-1][owner]).astype(bf16)

    half = WIDTH // 2
    heights = (rows + extra, rows, rows + extra, rows)
    return pl.pallas_call(
        kernel,
        grid=(4,),
        in_specs=in_specs,
        out_specs=[pl.BlockSpec((2, height, half), lambda at: (0, 0, 0)) for height in heights],
        out_shape=[jax.ShapeDtypeStruct((2, height, half), bf16) for height in heights],
        compiler_params=params(),
        cost_estimate=cost(0.01),
        name="owner_terms",
    )(*given)


def taken(end_ref, pair, rows, scale):
    total, outward = pair
    part = jnp.where(end_ref[0] == 1, outward[rows], total[rows])
    return part.astype(f32) * scale


def put_halves(target, end_ref, pair, low, high, rows, scale):
    half = WIDTH // 2
    target[:, :half] = taken(end_ref, pair, slice(low, low + rows), scale)
    target[:, half:] = taken(end_ref, pair, slice(high, high + rows), scale)


def in_full():
    return pl.BlockSpec(memory_space=pltpu.VMEM)


def finish_most(at_end, reduce_1, em_1, both_01, scale):
    layers = 2
    half = WIDTH // 2

    def kernel(end_ref, *refs):
        r_pair, em_pair, hr_pair = refs[0:2], refs[2:4], refs[4:6]
        heads_out, merge_out, expand_out, reduce_out, vectors_out = refs[6:11]
        heads, merge, expand, reduce, sems = refs[11:]
        for layer, pair, high in ((0, hr_pair, 688), (1, r_pair, 384)):
            for part in range(FF_PARTS):
                for first, column in ((96 * part, WIDTH * part), (high + 96 * part, WIDTH * part + half)):
                    reduce[layer, :, column : column + half] = taken(
                        end_ref, pair, slice(first, first + 96), scale
                    )
        copies = [pltpu.make_async_copy(reduce, reduce_out, sems.at[0])]
        copies[0].start()
        put_halves(expand, end_ref, em_pair, 0, 480, 384, scale)
        put_halves(merge, end_ref, em_pair, 384, 864, 96, scale)
        for member in range(3):
            put_halves(
                heads.at[member],
                end_ref,
                hr_pair,
                384 + 96 * member,
                688 + 384 + 96 * member,
                96,
                scale,
            )
        last = layers - 1
        copies.append(pltpu.make_async_copy(expand, expand_out.at[last], sems.at[1]))
        copies.append(pltpu.make_async_copy(merge, merge_out.at[last], sems.at[2]))
        copies.append(pltpu.make_async_copy(heads, heads_out.at[last], sems.at[3]))
        run_all(copies[1:], "start")
        vectors_out[...] = taken(end_ref, hr_pair, slice(672, 688), scale)
        run_all(copies, "wait")

    shape = jax.ShapeDtypeStruct
    return pl.pallas_call(
        kernel,
        in_specs=[in_smem()] + [in_full()] * 6,
        out_specs=[in_any()] * 4 + [in_full()],
        out_shape=[
            shape((layers, 3, 96, WIDTH), f32),
            shape((layers, 96, WIDTH), f32),
            shape((layers, 384, WIDTH), f32),
            shape((layers, 96, FF_PARTS * WIDTH), f32),
            shape((16, half), f32),
        ],
        scratch_shapes=[
            pltpu.VMEM((3, 96, WIDTH), f32),
            pltpu.VMEM((96, WIDTH), f32),
            pltpu.VMEM((384, WIDTH), f32),
            pltpu.VMEM((layers, 96, FF_PARTS * WIDTH), f32),
            pltpu.SemaphoreType.DMA((4,)),
        ],
        compiler_params=pltpu.CompilerParams(vmem_limit_bytes=SMALL_VMEM_BYTES),
        cost_estimate=cost(0.01),
        name="finish_most",
    )(at_end, *reduce_1, *em_1, *both_01)


def finish_expand(at_end, em_0, merge_grad, expand_grad, scale):
    def kernel(end_ref, total, outward, merge_in, expand_in, merge_out, expand_out, *rest):
        merge, expand, sems = rest
        put_halves(expand, end_ref, (total, outward), 0, 480, 384, scale)
        put_halves(merge, end_ref, (total, outward), 384, 864, 96, scale)
        copies = [
            pltpu.make_async_copy(expand, expand_out.at[0], sems.at[0]),
            pltpu.make_async_copy(merge, merge_out.at[0], sems.at[1]),
        ]
        run_all(copies, "start")
        run_all(copies, "wait")

    return pl.pallas_call(
        kernel,
        in_specs=[in_smem()] + [in_full()] * 2 + [in_any()] * 2,
        out_specs=[in_any()] * 2,
        out_shape=[jax.ShapeDtypeStruct(a.shape, f32) for a in (merge_grad, expand_grad)],
        scratch_shapes=[
            pltpu.VMEM((96, WIDTH), f32),
            pltpu.VMEM((384, WIDTH), f32),
            pltpu.SemaphoreType.DMA((2,)),
        ],
        input_output_aliases={3: 0, 4: 1},
        compiler_params=pltpu.CompilerParams(vmem_limit_bytes=SMALL_VMEM_BYTES),
        cost_estimate=cost(0.01),
        name="finish_expand",
    )(at_end, *em_0, merge_grad, expand_grad)


def finish_heads(at_end, heads_0, vectors_1, heads_grad, scale):
    def kernel(end_ref, total, outward, vectors_ref, heads_in, heads_out, *rest):
        outs, (heads, sems) = rest[:8], rest[8:]
        for member in range(3):
            put_halves(
                heads.at[member],
                end_ref,
                (total, outward),
                96 * member,
                304 + 96 * member,
                96,
                scale,
            )
        copy = pltpu.make_async_copy(heads, heads_out.at[0], sems.at[0])
        copy.start()
        own = taken(end_ref, (total, outward), slice(288, 304), scale)
        for layer, values in ((0, own), (1, vectors_ref[...])):
            outs[0][layer] = values[0:2, :96]
            for row in range(2, 8):
                outs[row - 1][layer : layer + 1] = values[row : row + 1, :96]
            outs[7][layer : layer + 1] = values[8:9]
        copy.wait()

    shape = jax.ShapeDtypeStruct
    layers = heads_grad.shape[0]
    return pl.pallas_call(
        kernel,
        in_specs=[in_smem()] + [in_full()] * 3 + [in_any()],
        out_specs=[in_any()] + [in_full()] * 8,
        out_shape=[shape(heads_grad.shape, f32), shape((layers, 2, 96), f32)]
        + [shape((layers, 96), f32)] * 6
        + [shape((layers, 384), f32)],
        scratch_shapes=[pltpu.VMEM((3, 96, WIDTH), f32), pltpu.SemaphoreType.DMA((1,))],
        input_output_aliases={4: 0},
        compiler_params=pltpu.CompilerParams(vmem_limit_bytes=SMALL_VMEM_BYTES),
        cost_estimate=cost(0.01),
        name="finish_heads",
    )(at_end, *heads_0, vectors_1, heads_grad)


def shards(
    images,
    cotangent,
    slot_flags,
    heads_weight,
    heads_bias,
    merge_weight,
    merge_bias,
    first_gain,
    first_shift,
    second_gain,
    second_shift,
    expand_weight,
    expand_bias,
    reduce_weight,
    reduce_bias,
):
    micro_count, unused_slots, seq_len, width = images.shape
    layers = heads_weight.shape[0]
    tokens = micro_count * seq_len
    place_at = lax.axis_index("fsdp").astype(jnp.int32)
    place = place_at[None]

    matrices = (heads_weight, merge_weight, expand_weight, reduce_weight)
    vectors = (
        heads_bias,
        merge_bias,
        first_gain,
        first_shift,
        second_gain,
        second_shift,
        reduce_bias,
        expand_bias,
    )
    kinds = [("attn", 0), ("ff", 0), ("attn", 1), ("expand", 1), ("reduce", 1)]
    rows_of = [PACK_ROWS[kind] for kind, layer in kinds]
    cut_of = [PACK_CUTS[kind] for kind, layer in kinds]
    x_rows = [0] + cut_of
    y_rows = [0] + [rows - cut for rows, cut in zip(rows_of, cut_of)]
    count = len(kinds)

    def send_round(at, own_now, x_before, y_before):
        if at == 0:
            return swap_x(own_now), swap_y(own_now)
        rows, cut = rows_of[at - 1], cut_of[at - 1]
        to_x = [(y_before, y_rows[at - 1], cut)]
        to_y = [(x_before, x_rows[at - 1] + cut, rows - cut)]
        if at < count:
            to_x.append((own_now, 0, rows_of[at]))
            to_y.append((own_now, 0, rows_of[at]))
        to_x, to_y = join_rows([to_x, to_y])
        return swap_x(to_x), swap_y(to_y)

    def pack_of(at, own_pair, came):
        (x_0, y_0, cx_0, cy_0), (x_1, y_1, cx_1, cy_1) = came[at], came[at + 1]
        return (
            (own_pair[0], x_0, y_0, x_1, y_1, own_pair[1], cx_0, cy_0, cx_1, cy_1),
            regions_of(rows_of[at], cut_of[at], x_rows[at], y_rows[at]),
        )

    def both(values):
        return tuple(swap_core(value) for value in values)

    hidden = images.reshape(tokens, width)
    seal = lax.optimization_barrier

    came = []
    own = own_packs(kinds[:1], matrices, vectors, True)
    new = send_round(0, own[0], None, None)
    own_other = both(own)
    own += own_packs(kinds[1:2], matrices, vectors)
    chosen = chosen_columns(place)
    grad, low_mine, low_theirs = start_grad(place, slot_flags, cotangent.reshape(tokens, width))
    own, own_other, new, grad, low_mine, low_theirs, matrices, vectors, chosen = seal(
        (own, own_other, new, grad, low_mine, low_theirs, matrices, vectors, chosen)
    )

    got, new = new, send_round(1, own[1], *new)
    came.append(got + both(got))
    low = (low_mine, swap_core(low_theirs))
    low, matrices = seal((low, matrices))
    own += own_packs(kinds[2:], matrices, vectors)
    own_other += both(own[1:])
    own, own_other, came, new, low, grad = seal((own, own_other, came, new, low, grad))

    got, new = new, send_round(2, own[2], *new)
    came.append(got + both(got))
    pack_a0 = pack_of(0, (own[0], own_other[0]), came)
    small_0, expand_rows_0 = gathered_vectors(place, pack_a0)
    middle_0, normed_0, qkv_0, mixed_0 = attn_forward(place, hidden, small_0, pack_a0)
    own, came, new, small_0, expand_rows_0, middle_0, normed_0, qkv_0, mixed_0 = seal(
        (own, came, new, small_0, expand_rows_0, middle_0, normed_0, qkv_0, mixed_0)
    )

    got, new = new, send_round(3, own[3], *new)
    came.append(got + both(got))
    pack_f0 = pack_of(1, (own[1], own_other[1]), came)
    second_0, active_0, slope_0 = expand_forward(
        place, middle_0, small_0, expand_rows_0, pack_f0, 0
    )
    hidden_1 = reduce_forward(
        place, slot_flags, middle_0, active_0, small_0, pack_f0, 384, False
    )
    others_a0 = both((normed_0, mixed_0))
    own, came, new, second_0, active_0, slope_0, hidden_1, others_a0 = seal(
        (own, came, new, second_0, active_0, slope_0, hidden_1, others_a0)
    )

    got, new = new, send_round(4, own[4], *new)
    came.append(got + both(got))
    pack_a1 = pack_of(2, (own[2], own_other[2]), came)
    small_1, expand_rows_1 = gathered_vectors(place, pack_a1)
    middle_1, normed_1, qkv_1, mixed_1 = attn_forward(place, hidden_1, small_1, pack_a1)
    second_other_0 = swap_core(second_0)
    came, new, small_1, expand_rows_1, middle_1, normed_1, qkv_1, mixed_1, second_other_0 = seal(
        (came, new, small_1, expand_rows_1, middle_1, normed_1, qkv_1, mixed_1, second_other_0)
    )

    got, new = new, send_round(5, None, *new)
    came.append(got + both(got))
    pack_e1 = pack_of(3, (own[3], own_other[3]), came)
    second_1, active_1, slope_1 = expand_forward(
        place, middle_1, small_1, expand_rows_1, pack_e1, 0
    )
    others_a1 = both((normed_1, mixed_1))
    second_1, active_1, slope_1, others_a1, came, new = seal(
        (second_1, active_1, slope_1, others_a1, came, new)
    )
    came.append(new + both(new))
    second_1, active_1, came = seal((second_1, active_1, came))
    pack_e1 = pack_of(3, (own[3], own_other[3]), came)
    pack_r1 = pack_of(4, (own[4], own_other[4]), came)

    grad, pre_mine, pre_theirs, attn_mine, attn_theirs, ff_sums = ff_backward(
        place, grad, slope_1, middle_1, small_1, (pack_e1, 0), (pack_r1, 0)
    )
    others_f1 = both((second_1, active_1))
    made = (grad, pre_mine, pre_theirs, attn_mine, attn_theirs, ff_sums)
    made, others_f1, pack_r1_arrays = seal((made, others_f1, pack_r1[0]))
    grad, pre_mine, pre_theirs, attn_mine, attn_theirs, ff_sums = made
    pack_r1 = (pack_r1_arrays, pack_r1[1])

    travel_r1 = owner_terms(reduce=(low, (active_1, others_f1[1])))
    pre_other, attn_other = both((pre_theirs, attn_theirs))
    travel_r1, pre_other, attn_other, grad = seal((travel_r1, pre_other, attn_other, grad))

    state_r1 = first_steps(travel_r1)
    travel_em1 = owner_terms(
        expand=((pre_mine, pre_other), (second_1, others_f1[0])),
        merge=((attn_mine, attn_other), (mixed_1, others_a1[1])),
    )
    state_r1, travel_em1, grad, active_0 = seal((state_r1, travel_em1, grad, active_0))

    state_r1 = second_steps(state_r1)
    state_em1 = first_steps(travel_em1)
    grad, qkv_mine, qkv_theirs, vec_mine, vec_theirs, low_mine, low_theirs = attn_backward(
        place, grad, hidden_1, qkv_1, mixed_1, small_1, ff_sums, chosen, pack_a1, False
    )
    active_other_0 = swap_core(active_0)
    made = (grad, qkv_mine, qkv_theirs, vec_mine, vec_theirs, low_mine, low_theirs)
    state_r1, state_em1, made, active_other_0 = seal((state_r1, state_em1, made, active_other_0))
    grad, qkv_mine, qkv_theirs, vec_mine, vec_theirs, low_mine, low_theirs = made

    sum_r1 = to_middle(ends(state_r1))
    state_em1 = second_steps(state_em1)
    low_other, qkv_other, vec_other = both((low_theirs, qkv_theirs, vec_theirs))
    travel_hr = owner_terms(
        reduce=((low_mine, low_other), (active_0, active_other_0)),
        heads=((qkv_mine, qkv_other), (normed_1, others_a1[0])),
        small_terms=(vec_mine, vec_other),
    )
    sum_r1, state_em1, travel_hr, grad = seal((sum_r1, state_em1, travel_hr, grad))

    state_hr = first_steps(travel_hr)
    sum_em1 = to_middle(ends(state_em1))
    sum_r1 = across_middle(sum_r1)
    grad, pre_mine, pre_theirs, attn_mine, attn_theirs, ff_sums = ff_backward(
        place, grad, slope_0, middle_0, small_0, (pack_f0, 0), (pack_f0, 384)
    )
    made = (grad, pre_mine, pre_theirs, attn_mine, attn_theirs, ff_sums)
    state_hr, sum_em1, sum_r1, made = seal((state_hr, sum_em1, sum_r1, made))
    grad, pre_mine, pre_theirs, attn_mine, attn_theirs, ff_sums = made

    state_hr = second_steps(state_hr)
    sum_em1 = across_middle(sum_em1)
    pre_other, attn_other = both((pre_theirs, attn_theirs))
    travel_em0 = owner_terms(
        expand=((pre_mine, pre_other), (second_0, second_other_0)),
        merge=((attn_mine, attn_other), (mixed_0, others_a0[1])),
    )
    state_hr, sum_em1, travel_em0, grad = seal((state_hr, sum_em1, travel_em0, grad))

    state_em0 = first_steps(travel_em0)
    sum_hr = to_middle(ends(state_hr))
    final_r1 = to_ends(sum_r1)
    images_grad, qkv_mine, qkv_theirs, vec_mine, vec_theirs = attn_backward(
        place, grad, hidden, qkv_0, mixed_0, small_0, ff_sums, chosen, pack_a0, True
    )
    made = (images_grad, qkv_mine, qkv_theirs, vec_mine, vec_theirs)
    state_em0, sum_hr, final_r1, sum_em1, made = seal(
        (state_em0, sum_hr, final_r1, sum_em1, made)
    )
    images_grad, qkv_mine, qkv_theirs, vec_mine, vec_theirs = made

    state_em0 = second_steps(state_em0)
    sum_hr = across_middle(sum_hr)
    final_em1 = to_ends(sum_em1)
    qkv_other, vec_other = both((qkv_theirs, vec_theirs))
    travel_h0 = owner_terms(
        heads=((qkv_mine, qkv_other), (normed_0, others_a0[0])), small_terms=(vec_mine, vec_other)
    )
    state_em0, travel_h0, final_em1, middle_1, active_1 = seal(
        (state_em0, travel_h0, final_em1, middle_1, active_1)
    )

    state_h0 = first_steps(travel_h0)
    sum_em0 = to_middle(ends(state_em0))
    state_h0, sum_hr = seal((state_h0, sum_hr))

    state_h0 = second_steps(state_h0)
    kept_h0, sum_hr = seal((state_h0[2:], sum_hr))
    state_h0 = state_h0[:2] + kept_h0
    final_hr = to_ends(sum_hr)
    state_h0, sum_em0, middle_1, active_1 = seal((state_h0, sum_em0, middle_1, active_1))
    sum_h0 = to_middle(ends(state_h0))
    sum_em0 = across_middle(sum_em0)
    outputs = reduce_forward(
        place, slot_flags, middle_1, active_1, small_1, pack_r1, 0, True
    ).reshape(images.shape)
    sum_h0, final_hr, sum_em0, outputs = seal((sum_h0, final_hr, sum_em0, outputs))
    sum_h0 = across_middle(sum_h0)
    final_em0 = to_ends(sum_em0)
    final_h0 = to_ends(sum_h0)

    images_grad = images_grad.reshape(images.shape)
    grad_scale = (
        micro_count * images.shape[1] * lax.axis_size("fsdp") * lax.axis_size("rep") * seq_len
    ) ** (-0.5)
    rep_at = lax.axis_index("rep")
    at_end = ((rep_at == 0) | (rep_at == lax.axis_size("rep") - 1)).astype(jnp.int32)[None]
    heads_grad, merge_grad, expand_grad, reduce_grad, vectors_1 = finish_most(
        at_end, final_r1, final_em1, final_hr, grad_scale
    )
    merge_grad, expand_grad = finish_expand(at_end, final_em0, merge_grad, expand_grad, grad_scale)
    heads_grad, *vector_grads = finish_heads(at_end, final_h0, vectors_1, heads_grad, grad_scale)
    return (
        outputs,
        images_grad,
        heads_grad,
        vector_grads[0],
        merge_grad,
        *vector_grads[1:6],
        expand_grad,
        vector_grads[7],
        reduce_grad,
        vector_grads[6],
    )


def solution(mesh):
    body = shards if (mesh.shape["fsdp"], mesh.shape["rep"]) == (8, 4) else plain_shards
    placed = (
        P(None, ("fsdp", "rep"), None, None),
        P(None, ("fsdp", "rep"), None, None),
        P(None, ("fsdp", "rep")),
        P(None, None, "fsdp", None),
        P(None, None, "fsdp"),
        P(None, "fsdp", None),
        P(None, "fsdp"),
        P(None, "fsdp"),
        P(None, "fsdp"),
        P(None, "fsdp"),
        P(None, "fsdp"),
        P(None, "fsdp", None),
        P(None, "fsdp"),
        P(None, "fsdp", None),
        P(None, "fsdp"),
    )
    return jax.shard_map(
        body,
        mesh=mesh,
        in_specs=placed,
        out_specs=(
            P(None, ("fsdp", "rep"), None, None),
            P(None, ("fsdp", "rep"), None, None),
            P(None, None, "fsdp", None),
            P(None, None, "fsdp"),
            P(None, "fsdp", None),
            P(None, "fsdp"),
            P(None, "fsdp"),
            P(None, "fsdp"),
            P(None, "fsdp"),
            P(None, "fsdp"),
            P(None, "fsdp", None),
            P(None, "fsdp"),
            P(None, "fsdp", None),
            P(None, "fsdp"),
        ),
        check_vma=False,
    )
```
